128 devices in a mesh: dp: 8 (over z, core), seq: 2 (over x_lo), tensor: 8 (over y, x_hi).
Axes of the slice: x: 4 (x_hi: 2, x_lo: 2; x = x_hi * 2 + x_lo), y: 4, z: 4, core: 2. Of those that a mesh axis runs over, the one named last changes fastest.
Arguments:
- tokens: bfloat16 [16, 1536, 1024], P('dp', ('seq', 'tensor')), may hold values from -6 to 6
- w_query: bfloat16 [1024, 1024], P(('dp', 'seq'), 'tensor'), may hold values from -0.375 to 0.375
- w_key: bfloat16 [1024, 1024], P(('dp', 'seq'), 'tensor'), may hold values from -0.1875 to 0.1875
- w_value: bfloat16 [1024, 1024], P(('dp', 'seq'), 'tensor'), may hold values from -0.1875 to 0.1875
- w_out: bfloat16 [1024, 1024], P('tensor', ('dp', 'seq')), may hold values from -1 to 1
- w_up: bfloat16 [1024, 4096], P(('dp', 'seq'), 'tensor'), may hold values from -0.1875 to 0.1875
- w_down: bfloat16 [4096, 1024], P('tensor', ('dp', 'seq')), may hold values from -0.09375 to 0.09375
- b_query: bfloat16 [1024], P(('dp', 'seq')), may hold values from -3 to 3
- b_value: bfloat16 [1024], P(('dp', 'seq')), may hold values from -3 to 3
- b_out: bfloat16 [1024], P(('dp', 'seq')), may hold values from -3 to 3
- b_up: bfloat16 [4096], P(('dp', 'seq')), may hold values from -3 to 3
- b_down: bfloat16 [1024], P(('dp', 'seq')), may hold values from -3 to 3
- gain_attn: bfloat16 [1024], P(('dp', 'seq')), may hold values from 0.25 to 1.75
- shift_attn: bfloat16 [1024], P(('dp', 'seq')), may hold values from -3 to 3
- gain_mlp: bfloat16 [1024], P(('dp', 'seq')), may hold values from 0.25 to 1.75
- shift_mlp: bfloat16 [1024], P(('dp', 'seq')), may hold values from -3 to 3
- cotangent: bfloat16 [16, 1536, 1024], P('dp', ('seq', 'tensor')), may hold values from -6 to 6
Outputs:
- output: bfloat16 [16, 1536, 1024], P('dp', ('seq', 'tensor'))
- grad_tokens: float32 [16, 1536, 1024], P('dp', ('seq', 'tensor'))
- grad_w_query: float32 [1024, 1024], P(('dp', 'seq'), 'tensor')
- grad_w_key: float32 [1024, 1024], P(('dp', 'seq'), 'tensor')
- grad_w_value: float32 [1024, 1024], P(('dp', 'seq'), 'tensor')
- grad_w_out: float32 [1024, 1024], P('tensor', ('dp', 'seq'))
- grad_w_up: float32 [1024, 4096], P(('dp', 'seq'), 'tensor')
- grad_w_down: float32 [4096, 1024], P('tensor', ('dp', 'seq'))
- grad_b_query: float32 [1024], P(('dp', 'seq'))
- grad_b_value: float32 [1024], P(('dp', 'seq'))
- grad_b_out: float32 [1024], P(('dp', 'seq'))
- grad_b_up: float32 [4096], P(('dp', 'seq'))
- grad_b_down: float32 [1024], P(('dp', 'seq'))
- grad_gain_attn: float32 [1024], P(('dp', 'seq'))
- grad_shift_attn: float32 [1024], P(('dp', 'seq'))
- grad_gain_mlp: float32 [1024], P(('dp', 'seq'))
- grad_shift_mlp: float32 [1024], P(('dp', 'seq'))
The draws below stay inside these ranges and needn't reach their ends.
All inputs are finite; a program needn't handle non-finite values.
Results may differ from the reference program's by a relative error of at most 0.025.
Values may be sent and summed in bfloat16 or wider, within the bound.
No kernel may reach another device: no remote copies, remote signals or barrier semaphores. Data moves between devices by JAX's collectives and lax.ppermute only.
A program may use at most 192 MiB of HBM per device.

```python
import jax
import jax.numpy as jnp
from jax import lax

D = 1024
H = 16
HD = 64
FF = 4096
LEN = 1536
SEQS = 16


def block_scale(key, extent, split, low, largest):
    level = 1.0
    for position, shards_of in split:
        steps = jax.random.uniform(jax.random.fold_in(jax.random.fold_in(key, 6), position), (shards_of,), jnp.float32, low / len(split), largest / len(split))
        level = level * jnp.repeat(jnp.exp(steps), extent[position] // shards_of).reshape((-1,) + (1,) * (len(extent) - 1 - position))
    return level


def centred(key, shape, scale, reach, pieces=(), kind=jnp.bfloat16):
    factor_of = block_scale(key, shape, pieces, -0.22, 0.18) if pieces else 1.0
    drawn = jax.random.normal(key, shape, jnp.float32) * scale * factor_of
    return jnp.minimum(jnp.maximum(drawn, -reach), reach).astype(kind)


def setup_inputs(seed: int = 0) -> dict:
    keys = jax.random.split(jax.random.key(seed), 18)
    tokens = centred(keys[0], (SEQS, LEN, D), 1.0, 6.0, ((0, 8), (1, 16)))
    w_query = centred(keys[1], (D, D), (D // 4) ** -0.5, 0.375, ((0, 16), (1, 8)))
    w_key = centred(keys[2], (D, D), D ** -0.5, 0.1875, ((0, 16), (1, 8)))
    w_value = centred(keys[3], (D, D), D ** -0.5, 0.1875, ((0, 16), (1, 8)))
    w_out = centred(keys[4], (D, D), (D // 32) ** -0.5, 1.0, ((0, 8), (1, 16)))
    w_up = centred(keys[5], (D, FF), D ** -0.5, 0.1875, ((0, 16), (1, 8)))
    w_down = centred(keys[6], (FF, D), FF ** -0.5, 0.09375, ((0, 8), (1, 16)))
    b_query = centred(keys[7], (D,), 0.5, 3.0, ((0, 16),))
    b_value = centred(keys[8], (D,), 0.5, 3.0, ((0, 16),))
    b_out = centred(keys[9], (D,), 0.3, 3.0, ((0, 16),))
    b_up = centred(keys[10], (FF,), 0.5, 3.0, ((0, 16),))
    b_down = centred(keys[11], (D,), 0.3, 3.0, ((0, 16),))
    gain_attn = jnp.clip(1.0 + 0.15 * jax.random.normal(keys[12], (D,), jnp.float32), 0.25, 1.75).astype(jnp.bfloat16)
    shift_attn = centred(keys[13], (D,), 0.3, 3.0, ((0, 16),))
    gain_mlp = jnp.clip(1.0 + 0.15 * jax.random.normal(keys[14], (D,), jnp.float32), 0.25, 1.75).astype(jnp.bfloat16)
    shift_mlp = centred(keys[15], (D,), 0.3, 3.0, ((0, 16),))
    cotangent = centred(keys[16], (SEQS, LEN, D), 1.0, 6.0, ((0, 8), (1, 16)))
    return dict(tokens=tokens, w_query=w_query, w_key=w_key, w_value=w_value, w_out=w_out, w_up=w_up, w_down=w_down, b_query=b_query, b_value=b_value, b_out=b_out, b_up=b_up, b_down=b_down, gain_attn=gain_attn, shift_attn=shift_attn, gain_mlp=gain_mlp, shift_mlp=shift_mlp, cotangent=cotangent)


EPS = 1e-05
HIGHEST = lax.Precision.HIGHEST

@jax.custom_vjp
def low(v):
    return lax.optimization_barrier(v.astype(jnp.bfloat16)).astype(jnp.float32)

@jax.custom_vjp
def low_back(v):
    return v

def low_keep(v):
    return (low(v), None)

def low_pass(kept, grad):
    return (grad,)

def back_keep(v):
    return (v, None)

def back_low(kept, grad):
    return (low(grad),)
low.defvjp(low_keep, low_pass)
low_back.defvjp(back_keep, back_low)

def product(left, right):
    return jnp.dot(left, right, precision=HIGHEST, preferred_element_type=jnp.float32)

def norm_rows(hidden, gain, shift):
    centre = lax.optimization_barrier(jnp.mean(hidden, axis=-1, keepdims=True))
    centered = hidden - centre
    spread = lax.optimization_barrier(jnp.mean(centered * centered, axis=-1, keepdims=True))
    return centered * lax.rsqrt(spread + EPS) * gain + shift

def attend_block(queries, key_rows, value_rows):
    scores = low_back(jnp.einsum('qhe,khe->hqk', queries, key_rows, precision=HIGHEST) * HD ** (-0.5))
    highest = lax.optimization_barrier(jnp.max(scores, axis=-1, keepdims=True))
    weights = jnp.exp(scores - highest)
    probs = low(weights / lax.optimization_barrier(jnp.sum(weights, axis=-1, keepdims=True)))
    return jnp.einsum('hqk,khe->qhe', probs, value_rows, precision=HIGHEST)

def layer_sequence(inputs, w_query, w_key, w_value, w_out, w_up, w_down, b_query, b_value, b_out, b_up, b_down, gain_attn, shift_attn, gain_mlp, shift_mlp):
    length = inputs.shape[0]
    model_width = inputs.shape[1]
    queries = low(low_back(product(inputs, w_query) + b_query)).reshape(length, H, HD)
    key_rows = low(low_back(product(inputs, w_key))).reshape(length, H, HD)
    value_rows = low(low_back(product(inputs, w_value) + b_value)).reshape(length, H, HD)
    span = min(512, length)
    query_blocks = queries.reshape(length // span, span, H, HD)
    attend_saved = jax.checkpoint(attend_block)
    context = lax.map(lambda piece_rows: attend_saved(piece_rows, key_rows, value_rows), query_blocks)
    context = low(low_back(context.reshape(length, model_width)))
    attended = low_back(product(context, w_out)) + b_out
    normed = norm_rows(inputs + attended, gain_attn, shift_attn)
    pre_act = low_back(product(low(normed), w_up)) + b_up
    active = low(jax.nn.gelu(pre_act, approximate=False))
    mixed = low_back(product(active, w_down)) + b_down
    return norm_rows(normed + mixed, gain_mlp, shift_mlp)

def reference(tokens, w_query, w_key, w_value, w_out, w_up, w_down, b_query, b_value, b_out, b_up, b_down, gain_attn, shift_attn, gain_mlp, shift_mlp, cotangent):
    params = tuple((array.astype(jnp.float32) for array in (w_query, w_key, w_value, w_out, w_up, w_down, b_query, b_value, b_out, b_up, b_down, gain_attn, shift_attn, gain_mlp, shift_mlp)))

    def whole_layer(inputs, *weights):
        return lax.map(lambda sequence: layer_sequence(sequence, *weights), inputs)
    result, pullback = jax.vjp(whole_layer, tokens.astype(jnp.float32), *params)
    grads = pullback(cotangent.astype(jnp.float32))
    return (result.astype(jnp.bfloat16), grads[0], grads[1], grads[2], grads[3], grads[4], grads[5], grads[6], grads[7], grads[8], grads[9], grads[10], grads[11], grads[12], grads[13], grads[14], grads[15])
```

```python
import functools

import jax
import jax.numpy as jnp
from jax import lax
from jax.experimental import pallas as pl
from jax.experimental.pallas import tpu as pltpu
from jax.sharding import Mesh, PartitionSpec as P

HD = 64
EPS = 1e-05
F32 = jnp.float32
BF16 = jnp.bfloat16
HIGHEST = lax.Precision.HIGHEST
VMEM_LIMIT = 56 * 1024 * 1024
Q_BLOCKS = 4
PLANE = ("seq", "y", "xhi")


def dims(a, b, ca, cb):
    return lax.dot_general(a, b, (((ca,), (cb,)), ((), ())), preferred_element_type=F32)


def shift4(by):
    return [(i, (i + by) % 4) for i in range(4)]


def flip(which):
    out = []
    for seq in range(2):
        for xhi in range(2):
            to = (seq ^ which[0]) * 2 + (xhi ^ which[1])
            out.append((seq * 2 + xhi, to))
    return out


FLIP_S, FLIP_B, FLIP_H = flip((1, 0)), flip((1, 1)), flip((0, 1))


def halves(block):
    for dim in range(4):
        if block.shape[dim] % 2 == 0:
            half = block.shape[dim] // 2
            return (
                lax.slice_in_dim(block, 0, half, axis=dim),
                lax.slice_in_dim(block, half, 2 * half, axis=dim),
                dim,
            )
    return None


def gather_axis(block, axis, direct):
    if axis == "x":
        names = ("seq", "xhi")
        one, two = FLIP_S, FLIP_B
    else:
        names = axis
        one, two = shift4(-1), shift4(1)
    first = lax.ppermute(block, names, one)
    second = lax.ppermute(block, names, two)
    if direct:
        far = lax.ppermute(block, names, FLIP_H if axis == "x" else shift4(2))
    elif axis == "x":
        head, _, dim = halves(second)
        _, tail, _ = halves(first)
        far = lax.concatenate(
            [lax.ppermute(head, names, one), lax.ppermute(tail, names, two)], dim
        )
    else:
        head, _, dim = halves(first)
        _, tail, _ = halves(second)
        far = lax.concatenate(
            [lax.ppermute(head, names, one), lax.ppermute(tail, names, two)], dim
        )
    if axis == "x":
        near = lax.concatenate([block, far], 3)
        other = lax.concatenate([first, second], 3)
        return lax.concatenate([near, other], 1)
    return lax.concatenate([block, first, far, second], 0 if axis == "z" else 2)


def gather_weight(block, order, direct):
    for axis, straight in zip(order, direct):
        block = gather_axis(block, axis, straight)
    return block


def add(*terms):
    total = terms[0].astype(F32)
    for term in terms[1:]:
        total = total + term.astype(F32)
    return total.astype(BF16)


def reduce_axis(block, axis, direct):
    if axis == "x":
        names = ("seq", "xhi")
        to_first, to_second = FLIP_S, FLIP_B
        pick = lambda s, h: block[:, s : s + 1, :, h : h + 1]
        own, first, far, second = pick(0, 0), pick(1, 0), pick(0, 1), pick(1, 1)
    else:
        names = axis
        dim = 0 if axis == "z" else 2
        to_first, to_second = shift4(1), shift4(-1)
        own, first, far, second = (
            lax.slice_in_dim(block, i, i + 1, axis=dim) for i in range(4)
        )
    if direct:
        return add(
            own,
            lax.ppermute(first, names, to_first),
            lax.ppermute(second, names, to_second),
            lax.ppermute(far, names, FLIP_H if axis == "x" else shift4(2)),
        )
    head, tail, dim = halves(far)
    head_in = lax.ppermute(head, names, to_first)
    tail_in = lax.ppermute(tail, names, to_second)
    first_head, first_tail, _ = halves(first)
    second_head, second_tail, _ = halves(second)
    if axis == "x":
        second = lax.concatenate([add(second_head, head_in), second_tail], dim)
        first = lax.concatenate([first_head, add(first_tail, tail_in)], dim)
    else:
        first = lax.concatenate([add(first_head, head_in), first_tail], dim)
        second = lax.concatenate([second_head, add(second_tail, tail_in)], dim)
    return add(
        own,
        lax.ppermute(first, names, to_first),
        lax.ppermute(second, names, to_second),
    )


def reduce_weight(block, order, direct):
    for axis, straight in zip(order, direct):
        block = reduce_axis(block, axis, straight)
    return block


def other_core(block):
    return lax.ppermute(block, "core", [(0, 1), (1, 0)])


def params(*semantics):
    return pltpu.CompilerParams(
        vmem_limit_bytes=VMEM_LIMIT,
        dimension_semantics=semantics if semantics else None,
    )


def vmem():
    return pl.BlockSpec(memory_space=pltpu.VMEM)


def smem():
    return pl.BlockSpec(memory_space=pltpu.SMEM)


def wide(ref, y, x, rows=None):
    return jnp.concatenate(
        [
            ref[z, s, y, x] if rows is None else ref[z, s, y, x, 0:rows]
            for z in range(4)
            for s in range(2)
        ],
        axis=1,
    )


def spread(ref, y, x, value):
    for z in range(4):
        for s in range(2):
            at = (z * 2 + s) * 128
            ref[z, s, y, x] = value[:, at : at + 128].astype(BF16)


def place(me_ref, y, x):
    return lax.rem(me_ref[1] + y, 4) * 2 + (me_ref[2] ^ x)


def qkv_kernel(me_ref, x_ref, wq_ref, wk_ref, wv_ref, bias_ref, out_ref):
    core = me_ref[0]
    rows = x_ref[...]
    span = rows.shape[0] // 4
    for y in range(4):
        for x in range(2):
            weight = jnp.concatenate(
                [wide(wq_ref, y, x, HD), wide(wk_ref, y, x), wide(wv_ref, y, x)], axis=0
            )
            made = dims(rows, weight, 1, 1) + bias_ref[y * 2 + x]
            made = made.astype(BF16)
            to = place(me_ref, y, x)
            for half in range(2):
                top = made[half * 2 * span : half * 2 * span + span]
                low = made[half * 2 * span + span : (half + 1) * 2 * span]
                packed = jnp.concatenate(
                    [
                        jnp.concatenate(
                            [top[:, i * HD : (i + 1) * HD], low[:, i * HD : (i + 1) * HD]],
                            axis=1,
                        )
                        for i in range(3)
                    ],
                    axis=0,
                )
                out_ref[core ^ half, to] = packed


def attend_kernel(q_ref, kv_ref, ctx_ref, lse_ref, *, rows):
    chunk = q_ref.shape[0] * rows
    length = kv_ref.shape[0] * rows
    queries = q_ref[:, 0:rows].reshape(chunk, 2 * HD) * jnp.bfloat16(0.125)
    keys = kv_ref[:, rows : 2 * rows].reshape(length, 2 * HD)
    values = kv_ref[:, 2 * rows : 3 * rows].reshape(length, 2 * HD)
    lane = lax.broadcasted_iota(jnp.int32, (chunk, 2 * HD), 1)
    parts = []
    for s in range(2):
        mine = (lane < HD) if s == 0 else (lane >= HD)
        picked = jnp.where(mine, queries, jnp.bfloat16(0))
        scores = dims(picked, keys, 1, 1)
        top = jnp.max(scores, axis=1, keepdims=True)
        weights = jnp.exp(scores - top)
        total = jnp.sum(weights, axis=1, keepdims=True)
        mixed = dims(weights.astype(BF16), values, 1, 0)
        parts.append(mixed / total)
        lse = jnp.broadcast_to(top + jnp.log(total), (chunk, 128))
        lse_ref[s] = jnp.transpose(lse)[0:8]
    ctx = jnp.where(lane < HD, parts[0], parts[1])
    ctx_ref[...] = ctx.astype(BF16).reshape(ctx_ref.shape)


def attend_back_kernel(
    q_ref, kv_ref, ctx_ref, dctx_ref, lse_ref, dq_ref, dkv_ref, dk_acc, dv_acc, *, rows
):
    step = pl.program_id(0)
    chunk = q_ref.shape[0] * rows
    length = kv_ref.shape[0] * rows
    queries = q_ref[:, 0:rows].reshape(chunk, 2 * HD) * jnp.bfloat16(0.125)
    grads = dctx_ref[...].reshape(chunk, 2 * HD)
    context = ctx_ref[...].reshape(chunk, 2 * HD)
    keys = kv_ref[:, rows : 2 * rows].reshape(length, 2 * HD)
    values = kv_ref[:, 2 * rows : 3 * rows].reshape(length, 2 * HD)
    lane = lax.broadcasted_iota(jnp.int32, (chunk, 2 * HD), 1)
    long_lane = lax.broadcasted_iota(jnp.int32, (length, 2 * HD), 1)
    both = grads.astype(F32) * context.astype(F32)

    @pl.when(step == 0)
    def _():
        dk_acc[...] = jnp.zeros_like(dk_acc)
        dv_acc[...] = jnp.zeros_like(dv_acc)

    dq_parts, dk_parts, dv_parts = [], [], []
    for s in range(2):
        mine = (lane < HD) if s == 0 else (lane >= HD)
        q_mine = jnp.where(mine, queries, jnp.bfloat16(0))
        g_mine = jnp.where(mine, grads, jnp.bfloat16(0))
        delta = jnp.sum(jnp.where(mine, both, 0.0), axis=1, keepdims=True)
        delta = jnp.transpose(jnp.broadcast_to(delta, (chunk, 128)))[0:1]
        scores = dims(keys, q_mine, 1, 1)
        exact = jnp.exp(scores - lse_ref[s, 0:1])
        grad_probs = dims(values, g_mine, 1, 1)
        grad_scores = (exact * (grad_probs - delta)).astype(BF16)
        dq_parts.append(dims(grad_scores, keys, 0, 0))
        dk_parts.append(dims(grad_scores, queries, 1, 0))
        dv_parts.append(dims(exact.astype(BF16), grads, 1, 0))
    dq = jnp.where(lane < HD, dq_parts[0], dq_parts[1]) * 0.125
    dq_ref[...] = dq.astype(BF16).reshape(dq_ref.shape)
    dk_acc[...] += jnp.where(long_lane < HD, dk_parts[0], dk_parts[1])
    dv_acc[...] += jnp.where(long_lane < HD, dv_parts[0], dv_parts[1])

    @pl.when(step == pl.num_programs(0) - 1)
    def _():
        shape = (kv_ref.shape[0], rows, 2 * HD)
        dkv_ref[:, 0:rows] = dk_acc[...].astype(BF16).reshape(shape)
        dkv_ref[:, rows : 2 * rows] = dv_acc[...].astype(BF16).reshape(shape)


def unpack_rows(top, low):
    return jnp.concatenate([top[:, 0:HD], top[:, HD:], low[:, 0:HD], low[:, HD:]], axis=0)


def out_kernel(me_ref, recv_ref, wo_ref, ctx_ref, own_ref, other_ref):
    core = me_ref[0]
    pieces, weights = [], []
    for y in range(4):
        for x in range(2):
            at = place(me_ref, y, x)
            pieces.append(unpack_rows(recv_ref[core, at], recv_ref[1 - core, at]))
            weights.append(wide(wo_ref, y, x))
    ctx = jnp.concatenate(pieces, axis=1)
    ctx_ref[...] = ctx
    made = dims(ctx, jnp.concatenate(weights, axis=0), 1, 0)
    half = made.shape[0] // 2
    own_ref[...] = made[0:half]
    other_ref[...] = made[half:].astype(BF16)


def ffn_kernel(n_ref, wup_ref, wdown_ref, bias_ref, active_ref, slope_ref, own_ref, other_ref, acc):
    step = pl.program_id(0)
    rows = n_ref[...]
    pre = dims(rows, wide(wup_ref, 0, 0), 1, 1) + bias_ref[0]
    cdf = 0.5 * (1.0 + lax.erf(pre * 0.7071067811865476))
    pdf = jnp.exp(-0.5 * pre * pre) * 0.3989422804014327
    active = (pre * cdf).astype(BF16)
    active_ref[...] = active
    slope_ref[...] = (cdf + pre * pdf).astype(BF16)
    made = dims(active, wide(wdown_ref, 0, 0), 1, 0)

    @pl.when(step == 0)
    def _():
        acc[...] = made

    @pl.when(step > 0)
    def _():
        acc[...] += made

    @pl.when(step == pl.num_programs(0) - 1)
    def _():
        half = acc.shape[0] // 2
        own_ref[...] = acc[0:half]
        other_ref[...] = acc[half:].astype(BF16)


def ffn_back_kernel(
    n_ref, g_ref, wup_ref, wdown_ref, active_ref, slope_ref,
    dup_ref, ddown_ref, bias_ref, own_ref, other_ref, acc,
):
    step = pl.program_id(0)
    grads = g_ref[...]
    active = active_ref[...]
    spread(ddown_ref, 0, 0, dims(active, grads, 0, 0))
    grad_pre = dims(grads, wide(wdown_ref, 0, 0), 1, 1) * slope_ref[...].astype(F32)
    bias_ref[0] = jnp.sum(grad_pre, axis=0, keepdims=True)
    low = grad_pre.astype(BF16)
    spread(dup_ref, 0, 0, dims(low, n_ref[...], 0, 0))
    made = dims(low, wide(wup_ref, 0, 0), 1, 0)

    @pl.when(step == 0)
    def _():
        acc[...] = made

    @pl.when(step > 0)
    def _():
        acc[...] += made

    @pl.when(step == pl.num_programs(0) - 1)
    def _():
        half = acc.shape[0] // 2
        own_ref[...] = acc[0:half]
        other_ref[...] = acc[half:].astype(BF16)


def out_back_kernel(me_ref, g_ref, ctx_ref, wo_ref, dctx_ref, dwo_ref):
    core = me_ref[0]
    grads = g_ref[...]
    span = grads.shape[0] // 4
    weights = jnp.concatenate([wide(wo_ref, y, x) for y in range(4) for x in range(2)], axis=0)
    made = dims(grads, weights, 1, 1).astype(BF16)
    for y in range(4):
        for x in range(2):
            at = (y * 2 + x) * HD
            piece = made[:, at : at + HD]
            to = place(me_ref, y, x)
            for half in range(2):
                base = half * 2 * span
                dctx_ref[core ^ half, to] = jnp.concatenate(
                    [piece[base : base + span], piece[base + span : base + 2 * span]], axis=1
                )
    grad = dims(ctx_ref[...], grads, 0, 0)
    for y in range(4):
        for x in range(2):
            at = (y * 2 + x) * HD
            spread(dwo_ref, y, x, grad[at : at + HD])


def qkv_back_kernel(
    me_ref, recv_ref, x_ref, wq_ref, wk_ref, wv_ref,
    dq_ref, dk_ref, dv_ref, bias_ref, own_ref, other_ref,
):
    core = me_ref[0]
    rows = x_ref[...]
    span = rows.shape[0] // 4
    total = jnp.zeros(rows.shape, F32)
    for y in range(4):
        for x in range(2):
            at = place(me_ref, y, x)
            top, low = recv_ref[core, at], recv_ref[1 - core, at]
            made = jnp.concatenate(
                [
                    unpack_rows(
                        top[i * span : (i + 1) * span], low[i * span : (i + 1) * span]
                    )
                    for i in range(3)
                ],
                axis=1,
            )
            bias_ref[y * 2 + x] = jnp.sum(made.astype(F32), axis=0, keepdims=True)
            grad = dims(made, rows, 0, 0)
            spread(dq_ref, y, x, grad[0:HD])
            spread(dk_ref, y, x, grad[HD : 2 * HD])
            spread(dv_ref, y, x, grad[2 * HD :])
            weight = jnp.concatenate(
                [wide(wq_ref, y, x, HD), wide(wk_ref, y, x), wide(wv_ref, y, x)], axis=0
            )
            total = total + dims(made, weight, 1, 0)
    half = total.shape[0] // 2
    own_ref[...] = total[0:half]
    other_ref[...] = total[half:].astype(BF16)


def norm_forward(hidden, gain, shift):
    centre = jnp.mean(hidden, axis=-1, keepdims=True)
    centered = hidden - centre
    inverse = lax.rsqrt(jnp.mean(centered * centered, axis=-1, keepdims=True) + EPS)
    normed = centered * inverse
    return (normed * gain + shift, normed, inverse)


def norm_backward(grad_in, normed, inverse, gain):
    scaled = grad_in * gain
    inner_term = (
        scaled
        - jnp.mean(scaled, axis=-1, keepdims=True)
        - normed * jnp.mean(scaled * normed, axis=-1, keepdims=True)
    )
    return (
        inverse * inner_term,
        jnp.sum(grad_in * normed, axis=0),
        jnp.sum(grad_in, axis=0),
    )


def sds(shape, dtype=BF16):
    return jax.ShapeDtypeStruct(shape, dtype)


def cost(flops, size, trans=0):
    return pl.CostEstimate(flops=flops, bytes_accessed=size, transcendentals=trans)


def local(
    tokens, w_query, w_key, w_value, w_out, w_up, w_down,
    b_query, b_value, b_out, b_up, b_down,
    gain_attn, shift_attn, gain_mlp, shift_mlp, cotangent,
):
    core = lax.axis_index("core")
    me_z, me_s = lax.axis_index("z"), lax.axis_index("seq")
    me_y, me_x = lax.axis_index("y"), lax.axis_index("xhi")
    first_core = core == 0
    me = jnp.stack([core, me_y, me_x]).astype(jnp.int32)
    seqs, span, width = tokens.shape
    rows = seqs * span
    hidden = w_up.shape[1] // 2

    at = jnp.arange(width, dtype=jnp.int32)
    z_of, c_of, s_of, i_of = at // 256, (at // 128) % 2, (at // 64) % 2, at % 64
    stored = ((z_of - me_z) % 4) * 256 + (s_of ^ me_s) * 128 + c_of * 64 + i_of
    order = (stored[:, None] == at[None, :]).astype(BF16)

    def by_core(piece):
        half = piece.shape[0] // 2
        return piece[0:half], piece[half:]

    split = [by_core(p) for p in (w_query.T, w_key.T, w_value.T, w_out, w_up.T, w_down)]
    small = jnp.stack(
        [b_query, b_value, b_out, b_down, gain_attn, shift_attn, gain_mlp, shift_mlp]
    )
    small = jnp.concatenate([small, b_up.reshape(4, HD), jnp.zeros((4, HD), BF16)], axis=0)
    lower = jnp.concatenate([s[0] for s in split] + [small], axis=0)
    upper = jnp.concatenate([s[1] for s in split] + [small], axis=0)
    keep = jnp.where(first_core, lower, upper)
    give = jnp.where(first_core, upper, lower)
    got = other_core(give)
    shard = jnp.where(
        first_core,
        jnp.concatenate([keep, got], axis=1),
        jnp.concatenate([got, keep], axis=1),
    )[None, None, None, None]
    cut = lambda a, b: shard[..., a:b, :]
    at_o, at_up, at_down, at_vec = 3 * HD, 4 * HD, 4 * HD + hidden, 4 * HD + 2 * hidden
    q_piece = jnp.concatenate([cut(0, HD), cut(at_vec, at_vec + 16)], axis=4)
    quick, slow = (True, True, False), (True, False, False)
    wq = gather_weight(q_piece, "yzx", quick)
    wk = gather_weight(cut(HD, 2 * HD), "zxy", quick)
    wv = gather_weight(cut(2 * HD, 3 * HD), "xyz", quick)
    wo = gather_weight(cut(at_o, at_up), "yzx", quick)
    wup = gather_weight(cut(at_up, at_down), "zxy", slow)
    wdown = gather_weight(cut(at_down, at_vec), "xyz", slow)

    both_in = jnp.concatenate([tokens.reshape(rows, width), cotangent.reshape(rows, width)], axis=0)
    both_in = dims(both_in, order, 1, 0)
    mine = both_in[0:rows]
    grad_final = both_in[rows:]
    mine_low = mine.astype(BF16)
    x_rows = jnp.concatenate([mine_low, other_core(mine_low)], axis=0)

    vec = wq[:, :, 0, 0, HD:, :]
    feature = lambda i: vec[:, :, i, :].reshape(width).astype(F32)
    heads = jnp.arange(8, dtype=jnp.int32)
    t_abs = ((me_y + heads // 2) % 4) * 2 + (me_x ^ (heads % 2))
    owner = ((t_abs // 2 - me_z) % 4) * 4 + (core ^ me_s) * 2 + t_abs % 2
    pick = (owner[:, None] == jnp.arange(16, dtype=jnp.int32)[None, :]).astype(F32)
    six = jnp.concatenate([vec[:, :, 0:2], vec[:, :, 8:12]], axis=2)
    six = six.reshape(8, 6, 2, HD).transpose(0, 2, 1, 3).reshape(16, 6 * HD).astype(F32)
    chosen = jnp.dot(pick, six, precision=HIGHEST)
    zeros = jnp.zeros((8, HD), F32)
    bias_qkv = jnp.concatenate([chosen[:, 0:HD], zeros, chosen[:, HD : 2 * HD]], axis=1)
    bias_qkv = bias_qkv[:, None, :]
    bias_up = chosen[:, 2 * HD :][:, None, :]
    gain_one, gain_two = feature(4), feature(6)

    with jax.named_scope("project"):
        packed = pl.pallas_call(
            qkv_kernel,
            out_shape=sds((2, 8, 3 * span, 2 * HD)),
            in_specs=[smem()] + [vmem()] * 5,
            out_specs=vmem(),
            compiler_params=params(),
            cost_estimate=cost(2 * 2 * rows * width * 1536, 6 << 20),
        )(me, x_rows, wq, wk, wv, bias_qkv)

    def exchange(block):
        flat = block.reshape((16,) + block.shape[2:])
        return lax.all_to_all(flat, PLANE, 0, 0, tiled=False)

    qkv = exchange(packed)
    per = Q_BLOCKS
    chunk = per * span
    steps = 16 // per
    length = 16 * span
    with jax.named_scope("attend"):
        ctx_heads, lse = pl.pallas_call(
            functools.partial(attend_kernel, rows=span),
            grid=(steps,),
            out_shape=(sds((16, span, 2 * HD)), sds((2, 8, length), F32)),
            in_specs=[
                pl.BlockSpec((per, 3 * span, 2 * HD), lambda i: (i, 0, 0)),
                pl.BlockSpec((16, 3 * span, 2 * HD), lambda i: (0, 0, 0)),
            ],
            out_specs=(
                pl.BlockSpec((per, span, 2 * HD), lambda i: (i, 0, 0)),
                pl.BlockSpec((2, 8, chunk), lambda i: (0, 0, i)),
            ),
            compiler_params=params("arbitrary"),
            cost_estimate=cost(8 * length * length * HD, 4 << 20, 2 * length * length),
        )(qkv, qkv)
    recv = lax.all_to_all(ctx_heads, PLANE, 0, 0, tiled=False)
    recv = recv.reshape(2, 8, span, 2 * HD)
    with jax.named_scope("out_project"):
        ctx, own, other = pl.pallas_call(
            out_kernel,
            out_shape=(sds((2 * rows, 8 * HD)), sds((rows, width), F32), sds((rows, width))),
            in_specs=[smem(), vmem(), vmem()],
            out_specs=(vmem(), vmem(), vmem()),
            compiler_params=params(),
            cost_estimate=cost(2 * 2 * rows * width * 512, 3 << 20),
        )(me, recv, wo)
    attended = own + other_core(other).astype(F32)
    resid_one = mine + attended + feature(2)
    normed_one, norm_first, inverse_first = norm_forward(resid_one, gain_one, feature(5))
    normed_low = normed_one.astype(BF16)
    n_rows = jnp.concatenate([normed_low, other_core(normed_low)], axis=0)

    weight_spec = pl.BlockSpec(
        (4, 2, 1, 1, hidden, 2 * HD), lambda t: (0, 0, t // 2, t % 2, 0, 0)
    )
    whole_spec = pl.BlockSpec((2 * rows, width), lambda t: (0, 0))
    cols_spec = pl.BlockSpec((2 * rows, hidden), lambda t: (0, t))
    half_spec = pl.BlockSpec((rows, width), lambda t: (0, 0))
    bias_spec = pl.BlockSpec((1, 1, hidden), lambda t: (t, 0, 0))
    with jax.named_scope("feed_forward"):
        active, slope, own, other = pl.pallas_call(
            ffn_kernel,
            grid=(8,),
            out_shape=(
                sds((2 * rows, 8 * hidden)),
                sds((2 * rows, 8 * hidden)),
                sds((rows, width), F32),
                sds((rows, width)),
            ),
            in_specs=[whole_spec, weight_spec, weight_spec, bias_spec],
            out_specs=(cols_spec, cols_spec, half_spec, half_spec),
            scratch_shapes=[pltpu.VMEM((2 * rows, width), F32)],
            compiler_params=params("arbitrary"),
            cost_estimate=cost(4 * 2 * rows * width * 2048, 12 << 20, 4 * rows * 2048),
        )(n_rows, wup, wdown, bias_up)
    mixed = own + other_core(other).astype(F32)
    resid_two = normed_one + mixed + feature(3)
    final, norm_second, inverse_second = norm_forward(resid_two, gain_two, feature(7))
    output = dims(final.astype(BF16), order, 1, 1).astype(BF16)
    grad_two, part_gain_mlp, part_shift_mlp = norm_backward(
        grad_final, norm_second, inverse_second, gain_two
    )
    grad_low = grad_two.astype(BF16)
    g_rows = jnp.concatenate([grad_low, other_core(grad_low)], axis=0)
    with jax.named_scope("feed_forward_back"):
        grad_up, grad_down, part_up, own, other = pl.pallas_call(
            ffn_back_kernel,
            grid=(8,),
            out_shape=(
                sds((4, 2, 4, 2, hidden, 2 * HD)),
                sds((4, 2, 4, 2, hidden, 2 * HD)),
                sds((8, 1, hidden), F32),
                sds((rows, width), F32),
                sds((rows, width)),
            ),
            in_specs=[whole_spec, whole_spec, weight_spec, weight_spec, cols_spec, cols_spec],
            out_specs=(weight_spec, weight_spec, bias_spec, half_spec, half_spec),
            scratch_shapes=[pltpu.VMEM((2 * rows, width), F32)],
            compiler_params=params("arbitrary"),
            cost_estimate=cost(8 * 2 * rows * width * 2048, 20 << 20),
        )(n_rows, g_rows, wup, wdown, active, slope)
    got_up = reduce_weight(grad_up, "yxz", (False, False, True))
    got_down = reduce_weight(grad_down, "zyx", (False, False, True))
    grad_mid = grad_two + (own + other_core(other).astype(F32))
    grad_one, part_gain_attn, part_shift_attn = norm_backward(
        grad_mid, norm_first, inverse_first, gain_one
    )
    grad_low = grad_one.astype(BF16)
    g_rows = jnp.concatenate([grad_low, other_core(grad_low)], axis=0)
    with jax.named_scope("out_project_back"):
        dctx, grad_o = pl.pallas_call(
            out_back_kernel,
            out_shape=(sds((2, 8, span, 2 * HD)), sds((4, 2, 4, 2, HD, 2 * HD))),
            in_specs=[smem(), vmem(), vmem(), vmem()],
            out_specs=(vmem(), vmem()),
            compiler_params=params(),
            cost_estimate=cost(4 * 2 * rows * width * 512, 4 << 20),
        )(me, g_rows, ctx, wo)
    got_o = reduce_weight(grad_o, "xzy", (False, True, True))
    dctx = exchange(dctx)
    with jax.named_scope("attend_back"):
        dq, dkv = pl.pallas_call(
            functools.partial(attend_back_kernel, rows=span),
            grid=(steps,),
            out_shape=(sds((16, span, 2 * HD)), sds((16, 2 * span, 2 * HD))),
            in_specs=[
                pl.BlockSpec((per, 3 * span, 2 * HD), lambda i: (i, 0, 0)),
                pl.BlockSpec((16, 3 * span, 2 * HD), lambda i: (0, 0, 0)),
                pl.BlockSpec((per, span, 2 * HD), lambda i: (i, 0, 0)),
                pl.BlockSpec((per, span, 2 * HD), lambda i: (i, 0, 0)),
                pl.BlockSpec((2, 8, chunk), lambda i: (0, 0, i)),
            ],
            out_specs=(
                pl.BlockSpec((per, span, 2 * HD), lambda i: (i, 0, 0)),
                pl.BlockSpec((16, 2 * span, 2 * HD), lambda i: (0, 0, 0)),
            ),
            scratch_shapes=[pltpu.VMEM((length, 2 * HD), F32)] * 2,
            compiler_params=params("arbitrary"),
            cost_estimate=cost(20 * length * length * HD, 6 << 20, 2 * length * length),
        )(qkv, qkv, ctx_heads, dctx, lse)
    dqkv = exchange(jnp.concatenate([dq, dkv], axis=1)[None]).reshape(2, 8, 3 * span, 2 * HD)
    with jax.named_scope("project_back"):
        piece = sds((4, 2, 4, 2, HD, 2 * HD))
        grad_q, grad_k, grad_v, part_qkv, own, other = pl.pallas_call(
            qkv_back_kernel,
            out_shape=(
                piece, piece, piece,
                sds((8, 1, 3 * HD), F32),
                sds((rows, width), F32),
                sds((rows, width)),
            ),
            in_specs=[smem()] + [vmem()] * 5,
            out_specs=(vmem(),) * 6,
            compiler_params=params(),
            cost_estimate=cost(4 * 2 * rows * width * 1536, 10 << 20),
        )(me, dqkv, x_rows, wq, wk, wv)

    six = jnp.concatenate([part_qkv[:, 0, 0:HD], part_qkv[:, 0, 2 * HD :], part_up[:, 0]], axis=1)
    six = lax.dot_general(pick, six, (((0,), (0,)), ((), ())), precision=HIGHEST)
    six = six.reshape(8, 2, 6, HD).transpose(0, 2, 1, 3).reshape(4, 2, 6, 2 * HD)
    eight = jnp.stack(
        [
            jnp.sum(grad_one, axis=0), jnp.sum(grad_two, axis=0),
            part_gain_attn, part_shift_attn, part_gain_mlp, part_shift_mlp,
        ]
    ).reshape(6, 4, 2, 2 * HD).transpose(1, 2, 0, 3)
    vec_rows = jnp.concatenate(
        [six[:, :, 0:2], eight, six[:, :, 2:], jnp.zeros((4, 2, 4, 2 * HD), F32)], axis=2
    ).astype(BF16)
    vec_rows = jnp.broadcast_to(vec_rows[:, :, None, None], (4, 2, 4, 2, 16, 2 * HD))
    grad_q = jnp.concatenate([grad_q, vec_rows], axis=4)
    got_q = reduce_weight(grad_q, "xzy", (False, True, True))
    got_k = reduce_weight(grad_k, "yxz", (False, True, True))
    got_v = reduce_weight(grad_v, "zyx", (False, True, True))
    input_sum = own + other_core(other).astype(F32)
    grad_tokens = lax.dot_general(
        grad_one + input_sum, order.astype(F32), (((1,), (1,)), ((), ())), precision=HIGHEST
    )

    got = [p.reshape(p.shape[-2:]) for p in (got_q, got_k, got_v, got_o, got_up, got_down)]
    final_rows = jnp.concatenate(got, axis=0)
    swapped = other_core(final_rows)
    lanes = lambda a: jnp.where(first_core, a[:, 0:HD], a[:, HD:]).astype(F32)
    mine_f, other_f = lanes(final_rows), lanes(swapped)
    from_zero = jnp.where(first_core, mine_f, other_f)
    from_one = jnp.where(first_core, other_f, mine_f)
    ends = []
    at_row = 0
    for p in got:
        ends.append((at_row, at_row + p.shape[0]))
        at_row += p.shape[0]

    def joined(i, size):
        start = ends[i][0]
        return jnp.concatenate(
            [from_zero[start : start + size], from_one[start : start + size]], axis=0
        )

    vecs = from_zero[HD : HD + 16] + from_one[HD : HD + 16]
    return (
        output.reshape(seqs, span, width),
        grad_tokens.reshape(seqs, span, width),
        joined(0, HD).T,
        joined(1, HD).T,
        joined(2, HD).T,
        joined(3, HD),
        joined(4, hidden).T,
        joined(5, hidden),
        vecs[0],
        vecs[1],
        vecs[2],
        vecs[8:12].reshape(4 * HD),
        vecs[3],
        vecs[4],
        vecs[5],
        vecs[6],
        vecs[7],
    )


def solution(mesh):
    fine = Mesh(mesh.devices.reshape(4, 2, 2, 4, 2), ("z", "core", "seq", "y", "xhi"))
    owners, tensor = ("z", "core", "seq"), ("y", "xhi")
    tokens = P(("z", "core"), ("seq", "y", "xhi"), None)
    columns, by_rows, vector = P(owners, tensor), P(tensor, owners), P(owners)
    weights = (columns, columns, columns, by_rows, columns, by_rows)
    return jax.shard_map(
        local,
        mesh=fine,
        in_specs=(tokens,) + weights + (vector,) * 9 + (tokens,),
        out_specs=(tokens, tokens) + weights + (vector,) * 9,
        check_vma=False,
    )
```

```python
import functools

import jax
import jax.numpy as jnp
from jax import lax
from jax.experimental import pallas as pl
from jax.experimental.pallas import tpu as pltpu
from jax.sharding import Mesh, PartitionSpec as P

HD = 64
EPS = 1e-05
F32 = jnp.float32
BF16 = jnp.bfloat16
HIGHEST = lax.Precision.HIGHEST
VMEM_LIMIT = 56 * 1024 * 1024
Q_BLOCKS = 4
PLANE = ("seq", "y", "xhi")


def dims(a, b, ca, cb):
    return lax.dot_general(a, b, (((ca,), (cb,)), ((), ())), preferred_element_type=F32)


def shift4(by):
    return [(i, (i + by) % 4) for i in range(4)]


def flip(seq_too, xhi_too):
    return [
        (seq * 2 + xhi, (seq ^ seq_too) * 2 + (xhi ^ xhi_too))
        for seq in range(2)
        for xhi in range(2)
    ]


def links(axis):
    if axis == "x":
        return ("seq", "xhi"), flip(1, 0), flip(1, 1)
    return axis, shift4(-1), shift4(1)


def halves(block):
    half = block.shape[0] // 2
    return block[0:half], block[half:]


def ring_gather(block, axis):
    names, one, two = links(axis)
    first = lax.ppermute(block, names, one)
    second = lax.ppermute(block, names, two)
    if axis == "x":
        head, tail = halves(second)[0], halves(first)[1]
    else:
        head, tail = halves(first)[0], halves(second)[1]
    head = lax.ppermute(head, names, one)
    tail = lax.ppermute(tail, names, two)
    if axis == "x":
        whole = jnp.concatenate([block, head, tail, first, second], axis=0)
        return whole.reshape((2, 2) + block.shape)
    whole = jnp.concatenate([block, first, head, tail, second], axis=0)
    return whole.reshape((4,) + block.shape)


def add(*terms):
    total = terms[0].astype(F32)
    for term in terms[1:]:
        total = total + term.astype(F32)
    return total.astype(BF16)


def ring_reduce(block, axis):
    names, one, two = links(axis)
    if axis == "x":
        own, far, first, second = block[0, 0], block[0, 1], block[1, 0], block[1, 1]
        to_first, to_second = one, two
    else:
        own, first, far, second = block[0], block[1], block[2], block[3]
        to_first, to_second = two, one
    head, tail = halves(far)
    head = lax.ppermute(head, names, to_first)
    tail = lax.ppermute(tail, names, to_second)
    first_head, first_tail = halves(first)
    second_head, second_tail = halves(second)
    if axis == "x":
        second = jnp.concatenate([add(second_head, head), second_tail], axis=0)
        first = jnp.concatenate([first_head, add(first_tail, tail)], axis=0)
    else:
        first = jnp.concatenate([add(first_head, head), first_tail], axis=0)
        second = jnp.concatenate([second_head, add(second_tail, tail)], axis=0)
    return add(
        own,
        lax.ppermute(first, names, to_first),
        lax.ppermute(second, names, to_second),
    )


SIZES = {"z": 4, "seq": 2, "y": 4, "xhi": 2}


def plane_gather(shard, names):
    copies = jnp.broadcast_to(shard[None], (16,) + shard.shape)
    got = lax.all_to_all(copies, names, 0, 0, tiled=False)
    return got.reshape(tuple(SIZES[n] for n in names) + shard.shape)


def plane_reduce(block, names):
    flat = block.reshape((16,) + block.shape[-2:])
    got = lax.all_to_all(flat, names, 0, 0, tiled=False)
    return jnp.sum(got.astype(F32), axis=0)


PLANE_QKV, PLANE_UP, PLANE_DOWN = PLANE, ("z", "seq", "xhi"), ("z", "y")


def other_core(block):
    return lax.ppermute(block, "core", [(0, 1), (1, 0)])


def params(*semantics):
    return pltpu.CompilerParams(
        vmem_limit_bytes=VMEM_LIMIT,
        dimension_semantics=semantics if semantics else None,
    )


def vmem():
    return pl.BlockSpec(memory_space=pltpu.VMEM)


def smem():
    return pl.BlockSpec(memory_space=pltpu.SMEM)


CORE, Z, SEQ, Y, XHI = range(5)


def qkv_at(me, z, s, y, x):
    return lax.rem(z + 4 - me[Z], 4), s, y, x


def up_at(me, z, s, y, x):
    return lax.rem(y + 4 - me[Y], 4), z, s, x


def wide(ref, at, me, y, x, start, stop):
    return jnp.concatenate(
        [ref[(*at(me, z, s, y, x), slice(start, stop))] for z in range(4) for s in range(2)],
        axis=1,
    )


def spread(ref, at, me, y, x, start, value):
    for z in range(4):
        for s in range(2):
            lanes = (z * 2 + s) * 128
            ref[(*at(me, z, s, y, x), slice(start, start + value.shape[0]))] = value[
                :, lanes : lanes + 128
            ].astype(BF16)


def qkv_kernel(me_ref, x_ref, w_ref, bias_ref, out_ref):
    core = me_ref[CORE]
    rows = x_ref[...]
    span = rows.shape[0] // 4
    for y in range(4):
        for x in range(2):
            weight = wide(w_ref, qkv_at, me_ref, y, x, 0, 3 * HD)
            made = dims(rows, weight, 1, 1) + bias_ref[y * 2 + x]
            made = made.astype(BF16)
            to = y * 2 + x
            for half in range(2):
                top = made[half * 2 * span : half * 2 * span + span]
                low = made[half * 2 * span + span : (half + 1) * 2 * span]
                packed = jnp.concatenate(
                    [
                        jnp.concatenate(
                            [top[:, i * HD : (i + 1) * HD], low[:, i * HD : (i + 1) * HD]],
                            axis=1,
                        )
                        for i in range(3)
                    ],
                    axis=0,
                )
                out_ref[core ^ half, to] = packed


def attend_kernel(q_ref, kv_ref, ctx_ref, lse_ref, *, rows):
    chunk = q_ref.shape[0] * rows
    length = kv_ref.shape[0] * rows
    queries = q_ref[:, 0:rows].reshape(chunk, 2 * HD) * jnp.bfloat16(0.125)
    keys = kv_ref[:, rows : 2 * rows].reshape(length, 2 * HD)
    values = kv_ref[:, 2 * rows : 3 * rows].reshape(length, 2 * HD)
    lane = lax.broadcasted_iota(jnp.int32, (chunk, 2 * HD), 1)
    parts = []
    for s in range(2):
        mine = (lane < HD) if s == 0 else (lane >= HD)
        picked = jnp.where(mine, queries, jnp.bfloat16(0))
        scores = dims(picked, keys, 1, 1)
        top = jnp.max(scores, axis=1, keepdims=True)
        weights = jnp.exp(scores - top)
        total = jnp.sum(weights, axis=1, keepdims=True)
        mixed = dims(weights.astype(BF16), values, 1, 0)
        parts.append(mixed / total)
        lse = jnp.broadcast_to(top + jnp.log(total), (chunk, 128))
        lse_ref[s] = jnp.transpose(lse)[0:8]
    ctx = jnp.where(lane < HD, parts[0], parts[1])
    ctx_ref[...] = ctx.astype(BF16).reshape(ctx_ref.shape)


def attend_back_kernel(
    q_ref, kv_ref, ctx_ref, dctx_ref, lse_ref, dq_ref, dkv_ref, dk_acc, dv_acc, *, rows
):
    step = pl.program_id(0)
    chunk = q_ref.shape[0] * rows
    length = kv_ref.shape[0] * rows
    queries = q_ref[:, 0:rows].reshape(chunk, 2 * HD) * jnp.bfloat16(0.125)
    grads = dctx_ref[...].reshape(chunk, 2 * HD)
    context = ctx_ref[...].reshape(chunk, 2 * HD)
    keys = kv_ref[:, rows : 2 * rows].reshape(length, 2 * HD)
    values = kv_ref[:, 2 * rows : 3 * rows].reshape(length, 2 * HD)
    lane = lax.broadcasted_iota(jnp.int32, (chunk, 2 * HD), 1)
    long_lane = lax.broadcasted_iota(jnp.int32, (length, 2 * HD), 1)
    both = grads.astype(F32) * context.astype(F32)

    @pl.when(step == 0)
    def _():
        dk_acc[...] = jnp.zeros_like(dk_acc)
        dv_acc[...] = jnp.zeros_like(dv_acc)

    dq_parts, dk_parts, dv_parts = [], [], []
    for s in range(2):
        mine = (lane < HD) if s == 0 else (lane >= HD)
        q_mine = jnp.where(mine, queries, jnp.bfloat16(0))
        g_mine = jnp.where(mine, grads, jnp.bfloat16(0))
        delta = jnp.sum(jnp.where(mine, both, 0.0), axis=1, keepdims=True)
        delta = jnp.transpose(jnp.broadcast_to(delta, (chunk, 128)))[0:1]
        scores = dims(keys, q_mine, 1, 1)
        exact = jnp.exp(scores - lse_ref[s, 0:1])
        grad_probs = dims(values, g_mine, 1, 1)
        grad_scores = (exact * (grad_probs - delta)).astype(BF16)
        dq_parts.append(dims(grad_scores, keys, 0, 0))
        dk_parts.append(dims(grad_scores, queries, 1, 0))
        dv_parts.append(dims(exact.astype(BF16), grads, 1, 0))
    dq = jnp.where(lane < HD, dq_parts[0], dq_parts[1]) * 0.125
    dq_ref[...] = dq.astype(BF16).reshape(dq_ref.shape)
    dk_acc[...] += jnp.where(long_lane < HD, dk_parts[0], dk_parts[1])
    dv_acc[...] += jnp.where(long_lane < HD, dv_parts[0], dv_parts[1])

    @pl.when(step == pl.num_programs(0) - 1)
    def _():
        shape = (kv_ref.shape[0], rows, 2 * HD)
        dkv_ref[:, 0:rows] = dk_acc[...].astype(BF16).reshape(shape)
        dkv_ref[:, rows : 2 * rows] = dv_acc[...].astype(BF16).reshape(shape)


def unpack_rows(top, low):
    return jnp.concatenate([top[:, 0:HD], top[:, HD:], low[:, 0:HD], low[:, HD:]], axis=0)


def out_kernel(me_ref, recv_ref, wo_ref, ctx_ref, own_ref, other_ref):
    core = me_ref[CORE]
    pieces, weights = [], []
    for y in range(4):
        for x in range(2):
            at = y * 2 + x
            pieces.append(unpack_rows(recv_ref[core, at], recv_ref[1 - core, at]))
            weights.append(wide(wo_ref, up_at, me_ref, y, x, 0, HD))
    ctx = jnp.concatenate(pieces, axis=1)
    ctx_ref[...] = ctx
    made = dims(ctx, jnp.concatenate(weights, axis=0), 1, 0)
    half = made.shape[0] // 2
    own_ref[...] = made[0:half]
    other_ref[...] = made[half:].astype(BF16)


def wide_up(ref):
    return jnp.concatenate([ref[0, z, s, 0] for z in range(4) for s in range(2)], axis=1)


def wide_down(ref, me):
    return jnp.concatenate(
        [ref[s ^ me[SEQ], 0, z, 0] for z in range(4) for s in range(2)], axis=1
    )


def ffn_kernel(
    me_ref, n_ref, wup_ref, wdown_ref, bias_ref, active_ref, slope_ref, own_ref, other_ref, acc
):
    step = pl.program_id(0)
    rows = n_ref[...]
    pre = dims(rows, wide_up(wup_ref), 1, 1) + bias_ref[0]
    cdf = 0.5 * (1.0 + lax.erf(pre * 0.7071067811865476))
    pdf = jnp.exp(-0.5 * pre * pre) * 0.3989422804014327
    active = (pre * cdf).astype(BF16)
    active_ref[...] = active
    slope_ref[...] = (cdf + pre * pdf).astype(BF16)
    made = dims(active, wide_down(wdown_ref, me_ref), 1, 0)

    @pl.when(step == 0)
    def _():
        acc[...] = made

    @pl.when(step > 0)
    def _():
        acc[...] += made

    @pl.when(step == pl.num_programs(0) - 1)
    def _():
        half = acc.shape[0] // 2
        own_ref[...] = acc[0:half]
        other_ref[...] = acc[half:].astype(BF16)


def ffn_back_kernel(
    me_ref, n_ref, g_ref, wup_ref, wdown_ref, active_ref, slope_ref,
    dup_ref, ddown_ref, bias_ref, own_ref, other_ref, acc,
):
    step = pl.program_id(0)
    grads = g_ref[...]
    active = active_ref[...]
    grad = dims(active, grads, 0, 0).astype(BF16)
    for z in range(4):
        for s in range(2):
            at = (z * 2 + s) * 128
            ddown_ref[s ^ me_ref[SEQ], 0, z, 0] = grad[:, at : at + 128]
    grad_pre = dims(grads, wide_down(wdown_ref, me_ref), 1, 1) * slope_ref[...].astype(F32)
    bias_ref[0] = jnp.sum(grad_pre, axis=0, keepdims=True)
    low = grad_pre.astype(BF16)
    grad = dims(low, n_ref[...], 0, 0).astype(BF16)
    for z in range(4):
        for s in range(2):
            at = (z * 2 + s) * 128
            dup_ref[0, z, s, 0] = grad[:, at : at + 128]
    made = dims(low, wide_up(wup_ref), 1, 0)

    @pl.when(step == 0)
    def _():
        acc[...] = made

    @pl.when(step > 0)
    def _():
        acc[...] += made

    @pl.when(step == pl.num_programs(0) - 1)
    def _():
        half = acc.shape[0] // 2
        own_ref[...] = acc[0:half]
        other_ref[...] = acc[half:].astype(BF16)


def out_back_kernel(me_ref, g_ref, ctx_ref, wo_ref, dctx_ref, dwo_ref):
    core = me_ref[CORE]
    grads = g_ref[...]
    span = grads.shape[0] // 4
    weights = jnp.concatenate(
        [wide(wo_ref, up_at, me_ref, y, x, 0, HD) for y in range(4) for x in range(2)], axis=0
    )
    made = dims(grads, weights, 1, 1).astype(BF16)
    for y in range(4):
        for x in range(2):
            at = (y * 2 + x) * HD
            piece = made[:, at : at + HD]
            to = y * 2 + x
            for half in range(2):
                base = half * 2 * span
                dctx_ref[core ^ half, to] = jnp.concatenate(
                    [piece[base : base + span], piece[base + span : base + 2 * span]], axis=1
                )
    grad = dims(ctx_ref[...], grads, 0, 0)
    for y in range(4):
        for x in range(2):
            at = (y * 2 + x) * HD
            spread(dwo_ref, up_at, me_ref, y, x, 0, grad[at : at + HD])


def qkv_back_kernel(me_ref, recv_ref, x_ref, w_ref, vec_ref, dw_ref, own_ref, other_ref):
    core = me_ref[CORE]
    rows = x_ref[...]
    span = rows.shape[0] // 4
    total = jnp.zeros(rows.shape, F32)
    sums = []
    for y in range(4):
        for x in range(2):
            at = y * 2 + x
            top, low = recv_ref[core, at], recv_ref[1 - core, at]
            made = jnp.concatenate(
                [
                    unpack_rows(
                        top[i * span : (i + 1) * span], low[i * span : (i + 1) * span]
                    )
                    for i in range(3)
                ],
                axis=1,
            )
            sums.append(jnp.sum(made.astype(F32), axis=0, keepdims=True))
            spread(dw_ref, qkv_at, me_ref, y, x, 0, dims(made, rows, 0, 0))
            weight = wide(w_ref, qkv_at, me_ref, y, x, 0, 3 * HD)
            total = total + dims(made, weight, 1, 0)
    for z in range(4):
        a, b = sums[2 * z], sums[2 * z + 1]
        bias_q = jnp.concatenate([a[:, 0:HD], b[:, 0:HD]], axis=1)
        bias_v = jnp.concatenate([a[:, 2 * HD :], b[:, 2 * HD :]], axis=1)
        two = jnp.concatenate([bias_q, bias_v, jnp.zeros((14, 2 * HD), F32)], axis=0)
        for s in range(2):
            block = vec_ref[z, s] + jnp.where(core == s, two, 0.0)
            for y in range(4):
                for x in range(2):
                    dw_ref[(*qkv_at(me_ref, z, s, y, x), slice(3 * HD, 3 * HD + 16))] = (
                        block.astype(BF16)
                    )
    half = total.shape[0] // 2
    own_ref[...] = total[0:half]
    other_ref[...] = total[half:].astype(BF16)


def norm_forward(hidden, gain, shift):
    centre = jnp.mean(hidden, axis=-1, keepdims=True)
    centered = hidden - centre
    inverse = lax.rsqrt(jnp.mean(centered * centered, axis=-1, keepdims=True) + EPS)
    normed = centered * inverse
    return (normed * gain + shift, normed, inverse)


def norm_backward(grad_in, normed, inverse, gain):
    scaled = grad_in * gain
    inner_term = (
        scaled
        - jnp.mean(scaled, axis=-1, keepdims=True)
        - normed * jnp.mean(scaled * normed, axis=-1, keepdims=True)
    )
    return (
        inverse * inner_term,
        jnp.sum(grad_in * normed, axis=0),
        jnp.sum(grad_in, axis=0),
    )


def sds(shape, dtype=BF16):
    return jax.ShapeDtypeStruct(shape, dtype)


def cost(flops, size, trans=0):
    return pl.CostEstimate(flops=flops, bytes_accessed=size, transcendentals=trans)


def local(
    tokens, w_query, w_key, w_value, w_out, w_up, w_down,
    b_query, b_value, b_out, b_up, b_down,
    gain_attn, shift_attn, gain_mlp, shift_mlp, cotangent,
):
    core = lax.axis_index("core")
    me_z, me_s = lax.axis_index("z"), lax.axis_index("seq")
    me_y, me_x = lax.axis_index("y"), lax.axis_index("xhi")
    first_core = core == 0
    me = jnp.stack([core, me_z, me_s, me_y, me_x]).astype(jnp.int32)
    seqs, span, width = tokens.shape
    rows = seqs * span
    hidden = w_up.shape[1] // 2

    at = jnp.arange(width, dtype=jnp.int32)
    z_of, c_of, s_of, i_of = at // 256, (at // 128) % 2, (at // 64) % 2, at % 64
    stored = z_of * 256 + s_of * 128 + c_of * 64 + i_of
    order = (stored[:, None] == at[None, :]).astype(BF16)

    def by_core(piece):
        half = piece.shape[0] // 2
        return piece[0:half], piece[half:]

    split = [by_core(p) for p in (w_query.T, w_key.T, w_value.T, w_out, w_up.T, w_down)]
    small = jnp.stack(
        [b_query, b_value, b_out, b_down, gain_attn, shift_attn, gain_mlp, shift_mlp]
    )
    small = jnp.concatenate([small, b_up.reshape(4, HD), jnp.zeros((4, HD), BF16)], axis=0)
    lower = jnp.concatenate([s[0] for s in split] + [small], axis=0)
    upper = jnp.concatenate([s[1] for s in split] + [small], axis=0)
    keep = jnp.where(first_core, lower, upper)
    give = jnp.where(first_core, upper, lower)
    got = other_core(give)
    shard = jnp.where(
        first_core,
        jnp.concatenate([keep, got], axis=1),
        jnp.concatenate([got, keep], axis=1),
    )
    at_o, at_up, at_down, at_vec = 3 * HD, 4 * HD, 4 * HD + hidden, 4 * HD + 2 * hidden
    qkv_shard = jnp.concatenate([shard[0:at_o], shard[at_vec:]], axis=0)
    up_shard = jnp.concatenate([shard[at_up:at_down], shard[at_o:at_up]], axis=0)
    w_qkv = ring_gather(plane_gather(qkv_shard, PLANE_QKV), "z")
    w_upo = ring_gather(plane_gather(up_shard, PLANE_UP), "y")
    wdown = ring_gather(plane_gather(shard[at_down:at_vec], PLANE_DOWN), "x")

    both_in = jnp.concatenate([tokens.reshape(rows, width), cotangent.reshape(rows, width)], axis=0)
    both_in = dims(both_in, order, 1, 0)
    mine = both_in[0:rows]
    grad_final = both_in[rows:]
    mine_low = mine.astype(BF16)
    x_rows = jnp.concatenate([mine_low, other_core(mine_low)], axis=0)

    fours = jnp.arange(4, dtype=jnp.int32)
    turn = ((fours[:, None] - me_z) % 4 == fours[None, :]).astype(F32)
    vec = w_qkv[:, :, 0, 0, 3 * HD :, :].reshape(4, 4096).astype(F32)
    vec = jnp.dot(turn, vec, precision=HIGHEST).reshape(4, 2, 16, 2 * HD)
    feature = lambda i: vec[:, :, i, :].reshape(width)
    chosen = jnp.where(first_core, vec[:, 0], vec[:, 1])
    chosen = chosen.reshape(4, 16, 2, HD).transpose(0, 2, 1, 3).reshape(8, 16 * HD)
    zeros = jnp.zeros((8, HD), F32)
    bias_qkv = jnp.concatenate([chosen[:, 0:HD], zeros, chosen[:, HD : 2 * HD]], axis=1)
    bias_qkv = bias_qkv[:, None, :]
    bias_up = chosen[:, 8 * HD : 12 * HD][:, None, :]
    gain_one, gain_two = feature(4), feature(6)

    with jax.named_scope("project"):
        packed = pl.pallas_call(
            qkv_kernel,
            out_shape=sds((2, 8, 3 * span, 2 * HD)),
            in_specs=[smem()] + [vmem()] * 3,
            out_specs=vmem(),
            compiler_params=params(),
            cost_estimate=cost(2 * 2 * rows * width * 1536, 6 << 20),
        )(me, x_rows, w_qkv, bias_qkv)

    def exchange(block):
        flat = block.reshape((16,) + block.shape[2:])
        return lax.all_to_all(flat, PLANE, 0, 0, tiled=False)

    qkv = exchange(packed)
    per = Q_BLOCKS
    chunk = per * span
    steps = 16 // per
    length = 16 * span
    with jax.named_scope("attend"):
        ctx_heads, lse = pl.pallas_call(
            functools.partial(attend_kernel, rows=span),
            grid=(steps,),
            out_shape=(sds((16, span, 2 * HD)), sds((2, 8, length), F32)),
            in_specs=[
                pl.BlockSpec((per, 3 * span, 2 * HD), lambda i: (i, 0, 0)),
                pl.BlockSpec((16, 3 * span, 2 * HD), lambda i: (0, 0, 0)),
            ],
            out_specs=(
                pl.BlockSpec((per, span, 2 * HD), lambda i: (i, 0, 0)),
                pl.BlockSpec((2, 8, chunk), lambda i: (0, 0, i)),
            ),
            compiler_params=params("arbitrary"),
            cost_estimate=cost(8 * length * length * HD, 4 << 20, 2 * length * length),
        )(qkv, qkv)
    recv = lax.all_to_all(ctx_heads, PLANE, 0, 0, tiled=False)
    recv = recv.reshape(2, 8, span, 2 * HD)
    out_spec = pl.BlockSpec((4, 4, 2, 2, HD, 2 * HD), lambda i: (0, 0, 0, 0, hidden // HD, 0))
    with jax.named_scope("out_project"):
        ctx, own, other = pl.pallas_call(
            out_kernel,
            out_shape=(sds((2 * rows, 8 * HD)), sds((rows, width), F32), sds((rows, width))),
            grid=(1,),
            in_specs=[smem(), vmem(), out_spec],
            out_specs=(vmem(), vmem(), vmem()),
            compiler_params=params("arbitrary"),
            cost_estimate=cost(2 * 2 * rows * width * 512, 3 << 20),
        )(me, recv, w_upo)
    attended = own + other_core(other).astype(F32)
    resid_one = mine + attended + feature(2)
    normed_one, norm_first, inverse_first = norm_forward(resid_one, gain_one, feature(5))
    normed_low = normed_one.astype(BF16)
    n_rows = jnp.concatenate([normed_low, other_core(normed_low)], axis=0)

    up_spec = pl.BlockSpec(
        (1, 4, 2, 1, hidden, 2 * HD),
        lambda t, at: (lax.rem(t // 2 + 4 - at[Y], 4), 0, 0, t % 2, 0, 0),
    )
    down_spec = pl.BlockSpec(
        (2, 1, 4, 1, hidden, 2 * HD), lambda t, at: (0, (t % 2) ^ at[XHI], 0, t // 2, 0, 0)
    )
    whole_spec = pl.BlockSpec((2 * rows, width), lambda t, at: (0, 0))
    cols_spec = pl.BlockSpec((2 * rows, hidden), lambda t, at: (0, t))
    half_spec = pl.BlockSpec((rows, width), lambda t, at: (0, 0))
    bias_spec = pl.BlockSpec((1, 1, hidden), lambda t, at: (t, 0, 0))
    with jax.named_scope("feed_forward"):
        active, slope, own, other = pl.pallas_call(
            ffn_kernel,
            grid_spec=pltpu.PrefetchScalarGridSpec(
                num_scalar_prefetch=1,
                grid=(8,),
                in_specs=[whole_spec, up_spec, down_spec, bias_spec],
                out_specs=(cols_spec, cols_spec, half_spec, half_spec),
                scratch_shapes=[pltpu.VMEM((2 * rows, width), F32)],
            ),
            out_shape=(
                sds((2 * rows, 8 * hidden)),
                sds((2 * rows, 8 * hidden)),
                sds((rows, width), F32),
                sds((rows, width)),
            ),
            compiler_params=params("arbitrary"),
            cost_estimate=cost(4 * 2 * rows * width * 2048, 12 << 20, 4 * rows * 2048),
        )(me, n_rows, w_upo, wdown, bias_up)
    mixed = own + other_core(other).astype(F32)
    resid_two = normed_one + mixed + feature(3)
    final, norm_second, inverse_second = norm_forward(resid_two, gain_two, feature(7))
    output = dims(final.astype(BF16), order, 1, 1).astype(BF16)
    grad_two, part_gain_mlp, part_shift_mlp = norm_backward(
        grad_final, norm_second, inverse_second, gain_two
    )
    grad_low = grad_two.astype(BF16)
    g_rows = jnp.concatenate([grad_low, other_core(grad_low)], axis=0)
    with jax.named_scope("feed_forward_back"):
        grad_up, grad_down, part_up, own, other = pl.pallas_call(
            ffn_back_kernel,
            grid_spec=pltpu.PrefetchScalarGridSpec(
                num_scalar_prefetch=1,
                grid=(8,),
                in_specs=[whole_spec, whole_spec, up_spec, down_spec, cols_spec, cols_spec],
                out_specs=(up_spec, down_spec, bias_spec, half_spec, half_spec),
                scratch_shapes=[pltpu.VMEM((2 * rows, width), F32)],
            ),
            out_shape=(
                sds((4, 4, 2, 2, hidden, 2 * HD)),
                sds((2, 2, 4, 4, hidden, 2 * HD)),
                sds((8, 1, hidden), F32),
                sds((rows, width), F32),
                sds((rows, width)),
            ),
            compiler_params=params("arbitrary"),
            cost_estimate=cost(8 * 2 * rows * width * 2048, 20 << 20),
        )(me, n_rows, g_rows, w_upo, wdown, active, slope)
    got_down = plane_reduce(ring_reduce(grad_down, "x"), PLANE_DOWN)
    grad_mid = grad_two + (own + other_core(other).astype(F32))
    grad_one, part_gain_attn, part_shift_attn = norm_backward(
        grad_mid, norm_first, inverse_first, gain_one
    )
    grad_low = grad_one.astype(BF16)
    g_rows = jnp.concatenate([grad_low, other_core(grad_low)], axis=0)
    with jax.named_scope("out_project_back"):
        dctx, grad_o = pl.pallas_call(
            out_back_kernel,
            grid=(1,),
            out_shape=(sds((2, 8, span, 2 * HD)), sds((4, 4, 2, 2, HD, 2 * HD))),
            in_specs=[smem(), vmem(), vmem(), out_spec],
            out_specs=(vmem(), vmem()),
            compiler_params=params("arbitrary"),
            cost_estimate=cost(4 * 2 * rows * width * 512, 4 << 20),
        )(me, g_rows, ctx, w_upo)
    grad_upo = jnp.concatenate([grad_up, grad_o], axis=4)
    got_upo = plane_reduce(ring_reduce(grad_upo, "y"), PLANE_UP)
    dctx = exchange(dctx)
    with jax.named_scope("attend_back"):
        dq, dkv = pl.pallas_call(
            functools.partial(attend_back_kernel, rows=span),
            grid=(steps,),
            out_shape=(sds((16, span, 2 * HD)), sds((16, 2 * span, 2 * HD))),
            in_specs=[
                pl.BlockSpec((per, 3 * span, 2 * HD), lambda i: (i, 0, 0)),
                pl.BlockSpec((16, 3 * span, 2 * HD), lambda i: (0, 0, 0)),
                pl.BlockSpec((per, span, 2 * HD), lambda i: (i, 0, 0)),
                pl.BlockSpec((per, span, 2 * HD), lambda i: (i, 0, 0)),
                pl.BlockSpec((2, 8, chunk), lambda i: (0, 0, i)),
            ],
            out_specs=(
                pl.BlockSpec((per, span, 2 * HD), lambda i: (i, 0, 0)),
                pl.BlockSpec((16, 2 * span, 2 * HD), lambda i: (0, 0, 0)),
            ),
            scratch_shapes=[pltpu.VMEM((length, 2 * HD), F32)] * 2,
            compiler_params=params("arbitrary"),
            cost_estimate=cost(20 * length * length * HD, 6 << 20, 2 * length * length),
        )(qkv, qkv, ctx_heads, dctx, lse)
    dqkv = exchange(jnp.concatenate([dq, dkv], axis=1)[None]).reshape(2, 8, 3 * span, 2 * HD)
    ups = part_up.reshape(4, 2, 4, HD).transpose(0, 2, 1, 3).reshape(4, 1, 4, 2 * HD)
    nothing = jnp.zeros_like(ups)
    ups = jnp.concatenate(
        [jnp.where(first_core, ups, nothing), jnp.where(first_core, nothing, ups)], axis=1
    )
    six = jnp.stack(
        [
            jnp.sum(grad_one, axis=0), jnp.sum(grad_two, axis=0),
            part_gain_attn, part_shift_attn, part_gain_mlp, part_shift_mlp,
        ]
    ).reshape(6, 4, 2, 2 * HD).transpose(1, 2, 0, 3)
    vec_rows = jnp.concatenate(
        [jnp.zeros((4, 2, 2, 2 * HD), F32), six, ups, jnp.zeros((4, 2, 4, 2 * HD), F32)], axis=2
    )
    with jax.named_scope("project_back"):
        grad_qkv, own, other = pl.pallas_call(
            qkv_back_kernel,
            out_shape=(
                sds((4, 2, 4, 2, 3 * HD + 16, 2 * HD)),
                sds((rows, width), F32),
                sds((rows, width)),
            ),
            in_specs=[smem()] + [vmem()] * 4,
            out_specs=(vmem(),) * 3,
            compiler_params=params(),
            cost_estimate=cost(4 * 2 * rows * width * 1536, 10 << 20),
        )(me, dqkv, x_rows, w_qkv, vec_rows)
    got_qkv = plane_reduce(ring_reduce(grad_qkv, "z"), PLANE_QKV)
    input_sum = own + other_core(other).astype(F32)
    grad_tokens = lax.dot_general(
        grad_one + input_sum, order.astype(F32), (((1,), (1,)), ((), ())), precision=HIGHEST
    )

    final_rows = jnp.concatenate([got_qkv, got_upo, got_down], axis=0).astype(BF16)
    swapped = other_core(final_rows)
    lanes = lambda a: jnp.where(first_core, a[:, 0:HD], a[:, HD:]).astype(F32)
    mine_f, other_f = lanes(final_rows), lanes(swapped)
    from_zero = jnp.where(first_core, mine_f, other_f)
    from_one = jnp.where(first_core, other_f, mine_f)

    def joined(start, size):
        return jnp.concatenate(
            [from_zero[start : start + size], from_one[start : start + size]], axis=0
        )

    vecs = from_zero[3 * HD : 3 * HD + 16] + from_one[3 * HD : 3 * HD + 16]
    up_from = 3 * HD + 16
    o_from = up_from + hidden
    return (
        output.reshape(seqs, span, width),
        grad_tokens.reshape(seqs, span, width),
        joined(0, HD).T,
        joined(HD, HD).T,
        joined(2 * HD, HD).T,
        joined(o_from, HD),
        joined(up_from, hidden).T,
        joined(o_from + HD, hidden),
        vecs[0],
        vecs[1],
        vecs[2],
        vecs[8:12].reshape(4 * HD),
        vecs[3],
        vecs[4],
        vecs[5],
        vecs[6],
        vecs[7],
    )


def solution(mesh):
    fine = Mesh(mesh.devices.reshape(4, 2, 2, 4, 2), ("z", "core", "seq", "y", "xhi"))
    owners, tensor = ("z", "core", "seq"), ("y", "xhi")
    tokens = P(("z", "core"), ("seq", "y", "xhi"), None)
    columns, by_rows, vector = P(owners, tensor), P(tensor, owners), P(owners)
    weights = (columns, columns, columns, by_rows, columns, by_rows)
    return jax.shard_map(
        local,
        mesh=fine,
        in_specs=(tokens,) + weights + (vector,) * 9 + (tokens,),
        out_specs=(tokens, tokens) + weights + (vector,) * 9,
        check_vma=False,
    )
```

```python
import functools

import jax
import jax.numpy as jnp
from jax import lax
from jax.experimental import pallas as pl
from jax.experimental.pallas import tpu as pltpu
from jax.sharding import Mesh, PartitionSpec as P

HD = 64
EPS = 1e-05
F32 = jnp.float32
BF16 = jnp.bfloat16
HIGHEST = lax.Precision.HIGHEST
VMEM_LIMIT = 56 * 1024 * 1024
Q_BLOCKS = 4
PLANE = ("seq", "y", "xhi")


def dims(a, b, ca, cb):
    return lax.dot_general(a, b, (((ca,), (cb,)), ((), ())), preferred_element_type=F32)


def shift4(by):
    return [(i, (i + by) % 4) for i in range(4)]


def flip(seq_too, xhi_too):
    return [
        (seq * 2 + xhi, (seq ^ seq_too) * 2 + (xhi ^ xhi_too))
        for seq in range(2)
        for xhi in range(2)
    ]


def links(axis):
    if axis == "x":
        return ("seq", "xhi"), flip(1, 0), flip(1, 1)
    return axis, shift4(-1), shift4(1)


def halves(block):
    half = block.shape[0] // 2
    return block[0:half], block[half:]


def ring_gather(block, axis):
    names, one, two = links(axis)
    first = lax.ppermute(block, names, one)
    second = lax.ppermute(block, names, two)
    if axis == "x":
        head, tail = halves(second)[0], halves(first)[1]
    else:
        head, tail = halves(first)[0], halves(second)[1]
    head = lax.ppermute(head, names, one)
    tail = lax.ppermute(tail, names, two)
    if axis == "x":
        whole = jnp.concatenate([block, head, tail, first, second], axis=0)
        return whole.reshape((2, 2) + block.shape)
    whole = jnp.concatenate([block, first, head, tail, second], axis=0)
    return whole.reshape((4,) + block.shape)


def add(*terms):
    total = terms[0].astype(F32)
    for term in terms[1:]:
        total = total + term.astype(F32)
    return total.astype(BF16)


def reduce_start(block, axis):
    names, one, two = links(axis)
    if axis == "x":
        own, far, first, second = block[0, 0], block[0, 1], block[1, 0], block[1, 1]
        to_first, to_second = one, two
    else:
        own, first, far, second = block[0], block[1], block[2], block[3]
        to_first, to_second = two, one
    head, tail = halves(far)
    head = lax.ppermute(head, names, to_first)
    tail = lax.ppermute(tail, names, to_second)
    return own, first, second, head, tail


def reduce_middle(begun, axis):
    own, first, second, head, tail = begun
    first_head, first_tail = halves(first)
    second_head, second_tail = halves(second)
    if axis == "x":
        second = jnp.concatenate([add(second_head, head), second_tail], axis=0)
        first = jnp.concatenate([first_head, add(first_tail, tail)], axis=0)
    else:
        first = jnp.concatenate([add(first_head, head), first_tail], axis=0)
        second = jnp.concatenate([second_head, add(second_tail, tail)], axis=0)
    return own, first, second


def reduce_end(middle, axis):
    own, first, second = middle
    names, one, two = links(axis)
    to_first, to_second = (one, two) if axis == "x" else (two, one)
    return add(
        own,
        lax.ppermute(first, names, to_first),
        lax.ppermute(second, names, to_second),
    )


def tie(*values):
    return lax.optimization_barrier(values)


SIZES = {"z": 4, "seq": 2, "y": 4, "xhi": 2}


def plane_gather(shard, names):
    copies = jnp.broadcast_to(shard[None], (16,) + shard.shape)
    got = lax.all_to_all(copies, names, 0, 0, tiled=False)
    return got.reshape(tuple(SIZES[n] for n in names) + shard.shape)


def plane_reduce(block, names):
    flat = block.reshape((16,) + block.shape[-2:])
    got = lax.all_to_all(flat, names, 0, 0, tiled=False)
    return jnp.sum(got.astype(F32), axis=0)


PLANE_QKV, PLANE_UP, PLANE_DOWN = PLANE, ("z", "seq", "xhi"), ("z", "y")


def other_core(block):
    return lax.ppermute(block, "core", [(0, 1), (1, 0)])


def params(*semantics):
    return pltpu.CompilerParams(
        vmem_limit_bytes=VMEM_LIMIT,
        dimension_semantics=semantics if semantics else None,
    )


def vmem():
    return pl.BlockSpec(memory_space=pltpu.VMEM)


def smem():
    return pl.BlockSpec(memory_space=pltpu.SMEM)


CORE, Z, SEQ, Y, XHI = range(5)


def qkv_at(me, z, s, y, x):
    return lax.rem(z + 4 - me[Z], 4), s, y, x


def up_at(me, z, s, y, x):
    return lax.rem(y + 4 - me[Y], 4), z, s, x


def wide(ref, at, me, y, x, start, stop):
    return jnp.concatenate(
        [ref[(*at(me, z, s, y, x), slice(start, stop))] for z in range(4) for s in range(2)],
        axis=1,
    )


def spread(ref, at, me, y, x, start, value):
    for z in range(4):
        for s in range(2):
            lanes = (z * 2 + s) * 128
            ref[(*at(me, z, s, y, x), slice(start, start + value.shape[0]))] = value[
                :, lanes : lanes + 128
            ].astype(BF16)


def flipped(value):
    return jnp.transpose(value.astype(F32))


def split_kernel(me_ref, wq, wk, wv, wo, wup, wdown, small, keep_ref, give_ref):
    first = me_ref[CORE] == 0
    at = 0
    for ref, turn in ((wq, 1), (wk, 1), (wv, 1), (wo, 0), (wup, 1), (wdown, 0)):
        value = flipped(ref[...]) if turn else ref[...].astype(F32)
        half = value.shape[0] // 2
        a, b = value[0:half], value[half:]
        keep_ref[at : at + half] = jnp.where(first, a, b).astype(BF16)
        give_ref[at : at + half] = jnp.where(first, b, a).astype(BF16)
        at += half
    keep_ref[at:] = small[...]
    give_ref[at:] = small[...]


def join_kernel(me_ref, mine_ref, other_ref, dq, dk, dv, do, dup, ddown, vec_ref):
    first = me_ref[CORE] == 0
    hidden = ddown.shape[0] // 2

    def rows(start, size):
        a = mine_ref[start : start + size].astype(F32)
        b = other_ref[start : start + size].astype(F32)
        zero, one = jnp.where(first, a, b), jnp.where(first, b, a)
        zero = jnp.where(first, zero[:, 0:HD], zero[:, HD:])
        one = jnp.where(first, one[:, 0:HD], one[:, HD:])
        return zero, one

    at = 0
    plan = ((dq, HD, 1), (dk, HD, 1), (dv, HD, 1), (vec_ref, 16, 2))
    for ref, size, turn in plan + ((dup, hidden, 1), (do, HD, 0), (ddown, hidden, 0)):
        zero, one = rows(at, size)
        at += size
        if turn == 2:
            ref[...] = zero + one
        elif turn:
            ref[...] = jnp.transpose(jnp.concatenate([zero, one], axis=0))
        else:
            ref[0:size] = zero
            ref[size:] = one


def qkv_kernel(me_ref, x_ref, w_ref, bias_ref, out_ref):
    core = me_ref[CORE]
    rows = x_ref[...]
    span = rows.shape[0] // 4
    for y in range(4):
        for x in range(2):
            weight = wide(w_ref, qkv_at, me_ref, y, x, 0, 3 * HD)
            made = dims(rows, weight, 1, 1) + bias_ref[y * 2 + x]
            made = made.astype(BF16)
            to = y * 2 + x
            for half in range(2):
                top = made[half * 2 * span : half * 2 * span + span]
                low = made[half * 2 * span + span : (half + 1) * 2 * span]
                packed = jnp.concatenate(
                    [
                        jnp.concatenate(
                            [top[:, i * HD : (i + 1) * HD], low[:, i * HD : (i + 1) * HD]],
                            axis=1,
                        )
                        for i in range(3)
                    ],
                    axis=0,
                )
                out_ref[core ^ half, to] = packed


def attend_kernel(q_ref, kv_ref, ctx_ref, lse_ref, *, rows):
    chunk = q_ref.shape[0] * rows
    length = kv_ref.shape[0] * rows
    queries = q_ref[:, 0:rows].reshape(chunk, 2 * HD) * jnp.bfloat16(0.125)
    keys = kv_ref[:, rows : 2 * rows].reshape(length, 2 * HD)
    values = kv_ref[:, 2 * rows : 3 * rows].reshape(length, 2 * HD)
    lane = lax.broadcasted_iota(jnp.int32, (chunk, 2 * HD), 1)
    parts = []
    for s in range(2):
        mine = (lane < HD) if s == 0 else (lane >= HD)
        picked = jnp.where(mine, queries, jnp.bfloat16(0))
        scores = dims(picked, keys, 1, 1)
        top = jnp.max(scores, axis=1, keepdims=True)
        weights = jnp.exp(scores - top)
        total = jnp.sum(weights, axis=1, keepdims=True)
        mixed = dims(weights.astype(BF16), values, 1, 0)
        parts.append(mixed / total)
        lse = jnp.broadcast_to(top + jnp.log(total), (chunk, 128))
        lse_ref[s] = jnp.transpose(lse)[0:8]
    ctx = jnp.where(lane < HD, parts[0], parts[1])
    ctx_ref[...] = ctx.astype(BF16).reshape(ctx_ref.shape)


def attend_back_kernel(
    q_ref, kv_ref, ctx_ref, dctx_ref, lse_ref, dq_ref, dkv_ref, dk_acc, dv_acc, *, rows
):
    step = pl.program_id(0)
    chunk = q_ref.shape[0] * rows
    length = kv_ref.shape[0] * rows
    queries = q_ref[:, 0:rows].reshape(chunk, 2 * HD) * jnp.bfloat16(0.125)
    grads = dctx_ref[...].reshape(chunk, 2 * HD)
    context = ctx_ref[...].reshape(chunk, 2 * HD)
    keys = kv_ref[:, rows : 2 * rows].reshape(length, 2 * HD)
    values = kv_ref[:, 2 * rows : 3 * rows].reshape(length, 2 * HD)
    lane = lax.broadcasted_iota(jnp.int32, (chunk, 2 * HD), 1)
    long_lane = lax.broadcasted_iota(jnp.int32, (length, 2 * HD), 1)
    both = grads.astype(F32) * context.astype(F32)

    @pl.when(step == 0)
    def _():
        dk_acc[...] = jnp.zeros_like(dk_acc)
        dv_acc[...] = jnp.zeros_like(dv_acc)

    dq_parts, dk_parts, dv_parts = [], [], []
    for s in range(2):
        mine = (lane < HD) if s == 0 else (lane >= HD)
        q_mine = jnp.where(mine, queries, jnp.bfloat16(0))
        g_mine = jnp.where(mine, grads, jnp.bfloat16(0))
        delta = jnp.sum(jnp.where(mine, both, 0.0), axis=1, keepdims=True)
        delta = jnp.transpose(jnp.broadcast_to(delta, (chunk, 128)))[0:1]
        scores = dims(keys, q_mine, 1, 1)
        exact = jnp.exp(scores - lse_ref[s, 0:1])
        grad_probs = dims(values, g_mine, 1, 1)
        grad_scores = (exact * (grad_probs - delta)).astype(BF16)
        dq_parts.append(dims(grad_scores, keys, 0, 0))
        dk_parts.append(dims(grad_scores, queries, 1, 0))
        dv_parts.append(dims(exact.astype(BF16), grads, 1, 0))
    dq = jnp.where(lane < HD, dq_parts[0], dq_parts[1]) * 0.125
    dq_ref[...] = dq.astype(BF16).reshape(dq_ref.shape)
    dk_acc[...] += jnp.where(long_lane < HD, dk_parts[0], dk_parts[1])
    dv_acc[...] += jnp.where(long_lane < HD, dv_parts[0], dv_parts[1])

    @pl.when(step == pl.num_programs(0) - 1)
    def _():
        shape = (kv_ref.shape[0], rows, 2 * HD)
        dkv_ref[:, 0:rows] = dk_acc[...].astype(BF16).reshape(shape)
        dkv_ref[:, rows : 2 * rows] = dv_acc[...].astype(BF16).reshape(shape)


def unpack_rows(top, low):
    return jnp.concatenate([top[:, 0:HD], top[:, HD:], low[:, 0:HD], low[:, HD:]], axis=0)


def out_kernel(me_ref, recv_ref, wo_ref, ctx_ref, own_ref, other_ref):
    core = me_ref[CORE]
    pieces, weights = [], []
    for y in range(4):
        for x in range(2):
            at = y * 2 + x
            pieces.append(unpack_rows(recv_ref[core, at], recv_ref[1 - core, at]))
            weights.append(wide(wo_ref, up_at, me_ref, y, x, 0, HD))
    ctx = jnp.concatenate(pieces, axis=1)
    ctx_ref[...] = ctx
    made = dims(ctx, jnp.concatenate(weights, axis=0), 1, 0)
    half = made.shape[0] // 2
    own_ref[...] = made[0:half]
    other_ref[...] = made[half:].astype(BF16)


def wide_up(ref):
    return jnp.concatenate([ref[0, z, s, 0] for z in range(4) for s in range(2)], axis=1)


def wide_down(ref, me):
    return jnp.concatenate(
        [ref[s ^ me[SEQ], 0, z, 0] for z in range(4) for s in range(2)], axis=1
    )


def ffn_kernel(
    me_ref, n_ref, wup_ref, wdown_ref, bias_ref, active_ref, slope_ref, own_ref, other_ref, acc
):
    step = pl.program_id(0)
    rows = n_ref[...]
    pre = dims(rows, wide_up(wup_ref), 1, 1) + bias_ref[0]
    cdf = 0.5 * (1.0 + lax.erf(pre * 0.7071067811865476))
    pdf = jnp.exp(-0.5 * pre * pre) * 0.3989422804014327
    active = (pre * cdf).astype(BF16)
    active_ref[...] = active
    slope_ref[...] = (cdf + pre * pdf).astype(BF16)
    made = dims(active, wide_down(wdown_ref, me_ref), 1, 0)

    @pl.when(step == 0)
    def _():
        acc[...] = made

    @pl.when(step > 0)
    def _():
        acc[...] += made

    @pl.when(step == pl.num_programs(0) - 1)
    def _():
        half = acc.shape[0] // 2
        own_ref[...] = acc[0:half]
        other_ref[...] = acc[half:].astype(BF16)


def ffn_back_kernel(
    me_ref, n_ref, g_ref, wup_ref, wdown_ref, active_ref, slope_ref,
    dup_ref, ddown_ref, bias_ref, own_ref, other_ref, acc,
):
    step = pl.program_id(0)
    grads = g_ref[...]
    active = active_ref[...]
    grad = dims(active, grads, 0, 0).astype(BF16)
    for z in range(4):
        for s in range(2):
            at = (z * 2 + s) * 128
            ddown_ref[s ^ me_ref[SEQ], 0, z, 0] = grad[:, at : at + 128]
    grad_pre = dims(grads, wide_down(wdown_ref, me_ref), 1, 1) * slope_ref[...].astype(F32)
    bias_ref[0] = jnp.sum(grad_pre, axis=0, keepdims=True)
    low = grad_pre.astype(BF16)
    grad = dims(low, n_ref[...], 0, 0).astype(BF16)
    for z in range(4):
        for s in range(2):
            at = (z * 2 + s) * 128
            dup_ref[0, z, s, 0] = grad[:, at : at + 128]
    made = dims(low, wide_up(wup_ref), 1, 0)

    @pl.when(step == 0)
    def _():
        acc[...] = made

    @pl.when(step > 0)
    def _():
        acc[...] += made

    @pl.when(step == pl.num_programs(0) - 1)
    def _():
        half = acc.shape[0] // 2
        own_ref[...] = acc[0:half]
        other_ref[...] = acc[half:].astype(BF16)


def out_back_kernel(me_ref, g_ref, ctx_ref, wo_ref, up_ref, dctx_ref, dwo_ref):
    core = me_ref[CORE]
    grads = g_ref[...]
    span = grads.shape[0] // 4
    weights = jnp.concatenate(
        [wide(wo_ref, up_at, me_ref, y, x, 0, HD) for y in range(4) for x in range(2)], axis=0
    )
    made = dims(grads, weights, 1, 1).astype(BF16)
    for y in range(4):
        for x in range(2):
            at = (y * 2 + x) * HD
            piece = made[:, at : at + HD]
            to = y * 2 + x
            for half in range(2):
                base = half * 2 * span
                dctx_ref[core ^ half, to] = jnp.concatenate(
                    [piece[base : base + span], piece[base + span : base + 2 * span]], axis=1
                )
    grad = dims(ctx_ref[...], grads, 0, 0)
    for y in range(4):
        for x in range(2):
            at = (y * 2 + x) * HD
            spread(dwo_ref, up_at, me_ref, y, x, 0, grad[at : at + HD])


def qkv_back_kernel(me_ref, recv_ref, x_ref, w_ref, vec_ref, dw_ref, own_ref, other_ref):
    core = me_ref[CORE]
    rows = x_ref[...]
    span = rows.shape[0] // 4
    total = jnp.zeros(rows.shape, F32)
    sums = []
    for y in range(4):
        for x in range(2):
            at = y * 2 + x
            top, low = recv_ref[core, at], recv_ref[1 - core, at]
            made = jnp.concatenate(
                [
                    unpack_rows(
                        top[i * span : (i + 1) * span], low[i * span : (i + 1) * span]
                    )
                    for i in range(3)
                ],
                axis=1,
            )
            sums.append(jnp.sum(made.astype(F32), axis=0, keepdims=True))
            spread(dw_ref, qkv_at, me_ref, y, x, 0, dims(made, rows, 0, 0))
            weight = wide(w_ref, qkv_at, me_ref, y, x, 0, 3 * HD)
            total = total + dims(made, weight, 1, 0)
    for z in range(4):
        a, b = sums[2 * z], sums[2 * z + 1]
        bias_q = jnp.concatenate([a[:, 0:HD], b[:, 0:HD]], axis=1)
        bias_v = jnp.concatenate([a[:, 2 * HD :], b[:, 2 * HD :]], axis=1)
        two = jnp.concatenate([bias_q, bias_v, jnp.zeros((14, 2 * HD), F32)], axis=0)
        for s in range(2):
            block = vec_ref[z, s] + jnp.where(core == s, two, 0.0)
            for y in range(4):
                for x in range(2):
                    dw_ref[(*qkv_at(me_ref, z, s, y, x), slice(3 * HD, 3 * HD + 16))] = (
                        block.astype(BF16)
                    )
    half = total.shape[0] // 2
    own_ref[...] = total[0:half]
    other_ref[...] = total[half:].astype(BF16)


def norm_forward(hidden, gain, shift):
    centre = jnp.mean(hidden, axis=-1, keepdims=True)
    centered = hidden - centre
    inverse = lax.rsqrt(jnp.mean(centered * centered, axis=-1, keepdims=True) + EPS)
    normed = centered * inverse
    return (normed * gain + shift, normed, inverse)


def norm_backward(grad_in, normed, inverse, gain):
    scaled = grad_in * gain
    inner_term = (
        scaled
        - jnp.mean(scaled, axis=-1, keepdims=True)
        - normed * jnp.mean(scaled * normed, axis=-1, keepdims=True)
    )
    return (
        inverse * inner_term,
        jnp.sum(grad_in * normed, axis=0),
        jnp.sum(grad_in, axis=0),
    )


def sds(shape, dtype=BF16):
    return jax.ShapeDtypeStruct(shape, dtype)


def took(us):
    return pl.CostEstimate(flops=int(us * 1.15e9), bytes_accessed=1 << 20, transcendentals=0)


def local(
    tokens, w_query, w_key, w_value, w_out, w_up, w_down,
    b_query, b_value, b_out, b_up, b_down,
    gain_attn, shift_attn, gain_mlp, shift_mlp, cotangent,
):
    core = lax.axis_index("core")
    me_z, me_s = lax.axis_index("z"), lax.axis_index("seq")
    me_y, me_x = lax.axis_index("y"), lax.axis_index("xhi")
    first_core = core == 0
    me = jnp.stack([core, me_z, me_s, me_y, me_x]).astype(jnp.int32)
    seqs, span, width = tokens.shape
    rows = seqs * span
    hidden = w_up.shape[1] // 2

    at = jnp.arange(width, dtype=jnp.int32)
    z_of, c_of, s_of, i_of = at // 256, (at // 128) % 2, (at // 64) % 2, at % 64
    stored = z_of * 256 + s_of * 128 + c_of * 64 + i_of
    order = (stored[:, None] == at[None, :]).astype(BF16)

    small = jnp.stack(
        [b_query, b_value, b_out, b_down, gain_attn, shift_attn, gain_mlp, shift_mlp]
    )
    small = jnp.concatenate([small, b_up.reshape(4, HD), jnp.zeros((4, HD), BF16)], axis=0)
    shard_rows = 4 * HD + 2 * hidden + 16
    with jax.named_scope("split"):
        keep, give = pl.pallas_call(
            split_kernel,
            out_shape=(sds((shard_rows, HD)),) * 2,
            in_specs=[smem()] + [vmem()] * 7,
            out_specs=(vmem(), vmem()),
            compiler_params=params(),
            cost_estimate=took(2),
        )(me, w_query, w_key, w_value, w_out, w_up, w_down, small)
    got = other_core(give)
    shard = jnp.where(
        first_core,
        jnp.concatenate([keep, got], axis=1),
        jnp.concatenate([got, keep], axis=1),
    )
    at_o, at_up, at_down, at_vec = 3 * HD, 4 * HD, 4 * HD + hidden, 4 * HD + 2 * hidden
    qkv_shard = jnp.concatenate([shard[0:at_o], shard[at_vec:]], axis=0)
    up_shard = jnp.concatenate([shard[at_up:at_down], shard[at_o:at_up]], axis=0)
    qkv_block = plane_gather(qkv_shard, PLANE_QKV)
    qkv_block, up_shard = tie(qkv_block, up_shard)
    up_block = plane_gather(up_shard, PLANE_UP)
    up_block, down_shard = tie(up_block, shard[at_down:at_vec])
    down_block = plane_gather(down_shard, PLANE_DOWN)
    w_qkv = ring_gather(qkv_block, "z")
    w_upo = ring_gather(up_block, "y")
    wdown = ring_gather(down_block, "x")

    both_in = jnp.concatenate([tokens.reshape(rows, width), cotangent.reshape(rows, width)], axis=0)
    both_in = dims(both_in, order, 1, 0)
    mine = both_in[0:rows]
    grad_final = both_in[rows:]
    mine_low = mine.astype(BF16)
    x_rows = jnp.concatenate([mine_low, other_core(mine_low)], axis=0)

    fours = jnp.arange(4, dtype=jnp.int32)
    turn = ((fours[:, None] - me_z) % 4 == fours[None, :]).astype(F32)
    vec = w_qkv[:, :, 0, 0, 3 * HD :, :].reshape(4, 4096).astype(F32)
    vec = jnp.dot(turn, vec, precision=HIGHEST).reshape(4, 2, 16, 2 * HD)
    feature = lambda i: vec[:, :, i, :].reshape(width)
    chosen = jnp.where(first_core, vec[:, 0], vec[:, 1])
    chosen = chosen.reshape(4, 16, 2, HD).transpose(0, 2, 1, 3).reshape(8, 16 * HD)
    zeros = jnp.zeros((8, HD), F32)
    bias_qkv = jnp.concatenate([chosen[:, 0:HD], zeros, chosen[:, HD : 2 * HD]], axis=1)
    bias_qkv = bias_qkv[:, None, :]
    bias_up = chosen[:, 8 * HD : 12 * HD][:, None, :]
    gain_one, gain_two = feature(4), feature(6)

    with jax.named_scope("project"):
        packed = pl.pallas_call(
            qkv_kernel,
            out_shape=sds((2, 8, 3 * span, 2 * HD)),
            in_specs=[smem()] + [vmem()] * 3,
            out_specs=vmem(),
            compiler_params=params(),
            cost_estimate=took(5),
        )(me, x_rows, w_qkv, bias_qkv)

    def exchange(block):
        flat = block.reshape((16,) + block.shape[2:])
        return lax.all_to_all(flat, PLANE, 0, 0, tiled=False)

    qkv = exchange(packed)
    per = Q_BLOCKS
    chunk = per * span
    steps = 16 // per
    length = 16 * span
    with jax.named_scope("attend"):
        ctx_heads, lse = pl.pallas_call(
            functools.partial(attend_kernel, rows=span),
            grid=(steps,),
            out_shape=(sds((16, span, 2 * HD)), sds((2, 8, length), F32)),
            in_specs=[
                pl.BlockSpec((per, 3 * span, 2 * HD), lambda i: (i, 0, 0)),
                pl.BlockSpec((16, 3 * span, 2 * HD), lambda i: (0, 0, 0)),
            ],
            out_specs=(
                pl.BlockSpec((per, span, 2 * HD), lambda i: (i, 0, 0)),
                pl.BlockSpec((2, 8, chunk), lambda i: (0, 0, i)),
            ),
            compiler_params=params("arbitrary"),
            cost_estimate=took(11),
        )(qkv, qkv)
    recv = lax.all_to_all(ctx_heads, PLANE, 0, 0, tiled=False)
    recv = recv.reshape(2, 8, span, 2 * HD)
    out_spec = pl.BlockSpec((4, 4, 2, 2, HD, 2 * HD), lambda i: (0, 0, 0, 0, hidden // HD, 0))
    with jax.named_scope("out_project"):
        ctx, own, other = pl.pallas_call(
            out_kernel,
            out_shape=(sds((2 * rows, 8 * HD)), sds((rows, width), F32), sds((rows, width))),
            grid=(1,),
            in_specs=[smem(), vmem(), out_spec],
            out_specs=(vmem(), vmem(), vmem()),
            compiler_params=params("arbitrary"),
            cost_estimate=took(3),
        )(me, recv, w_upo)
    attended = own + other_core(other).astype(F32)
    resid_one = mine + attended + feature(2)
    normed_one, norm_first, inverse_first = norm_forward(resid_one, gain_one, feature(5))
    normed_low = normed_one.astype(BF16)
    n_rows = jnp.concatenate([normed_low, other_core(normed_low)], axis=0)

    up_spec = pl.BlockSpec(
        (1, 4, 2, 1, hidden, 2 * HD),
        lambda t, at: (lax.rem(t // 2 + 4 - at[Y], 4), 0, 0, t % 2, 0, 0),
    )
    down_spec = pl.BlockSpec(
        (2, 1, 4, 1, hidden, 2 * HD), lambda t, at: (0, (t % 2) ^ at[XHI], 0, t // 2, 0, 0)
    )
    whole_spec = pl.BlockSpec((2 * rows, width), lambda t, at: (0, 0))
    cols_spec = pl.BlockSpec((2 * rows, hidden), lambda t, at: (0, t))
    half_spec = pl.BlockSpec((rows, width), lambda t, at: (0, 0))
    bias_spec = pl.BlockSpec((1, 1, hidden), lambda t, at: (t, 0, 0))
    with jax.named_scope("feed_forward"):
        active, slope, own, other = pl.pallas_call(
            ffn_kernel,
            grid_spec=pltpu.PrefetchScalarGridSpec(
                num_scalar_prefetch=1,
                grid=(8,),
                in_specs=[whole_spec, up_spec, down_spec, bias_spec],
                out_specs=(cols_spec, cols_spec, half_spec, half_spec),
                scratch_shapes=[pltpu.VMEM((2 * rows, width), F32)],
            ),
            out_shape=(
                sds((2 * rows, 8 * hidden)),
                sds((2 * rows, 8 * hidden)),
                sds((rows, width), F32),
                sds((rows, width)),
            ),
            compiler_params=params("arbitrary"),
            cost_estimate=took(14),
        )(me, n_rows, w_upo, wdown, bias_up)
    mixed = own + other_core(other).astype(F32)
    resid_two = normed_one + mixed + feature(3)
    final, norm_second, inverse_second = norm_forward(resid_two, gain_two, feature(7))
    output = dims(final.astype(BF16), order, 1, 1).astype(BF16)
    grad_two, part_gain_mlp, part_shift_mlp = norm_backward(
        grad_final, norm_second, inverse_second, gain_two
    )
    grad_low = grad_two.astype(BF16)
    g_rows = jnp.concatenate([grad_low, other_core(grad_low)], axis=0)
    with jax.named_scope("feed_forward_back"):
        grad_up, grad_down, part_up, own, other = pl.pallas_call(
            ffn_back_kernel,
            grid_spec=pltpu.PrefetchScalarGridSpec(
                num_scalar_prefetch=1,
                grid=(8,),
                in_specs=[whole_spec, whole_spec, up_spec, down_spec, cols_spec, cols_spec],
                out_specs=(up_spec, down_spec, bias_spec, half_spec, half_spec),
                scratch_shapes=[pltpu.VMEM((2 * rows, width), F32)],
            ),
            out_shape=(
                sds((4, 4, 2, 2, hidden + HD, 2 * HD)),
                sds((2, 2, 4, 4, hidden, 2 * HD)),
                sds((8, 1, hidden), F32),
                sds((rows, width), F32),
                sds((rows, width)),
            ),
            compiler_params=params("arbitrary"),
            cost_estimate=took(20),
        )(me, n_rows, g_rows, w_upo, wdown, active, slope)
    down_begun = reduce_start(grad_down, "x")
    grad_mid = grad_two + (own + other_core(other).astype(F32))
    grad_one, part_gain_attn, part_shift_attn = norm_backward(
        grad_mid, norm_first, inverse_first, gain_one
    )
    grad_low = grad_one.astype(BF16)
    g_rows = jnp.concatenate([grad_low, other_core(grad_low)], axis=0)
    with jax.named_scope("out_project_back"):
        dctx, grad_upo = pl.pallas_call(
            out_back_kernel,
            grid=(1,),
            out_shape=(sds((2, 8, span, 2 * HD)), sds(grad_up.shape)),
            in_specs=[smem(), vmem(), vmem(), out_spec, pl.BlockSpec(memory_space=pl.ANY)],
            out_specs=(vmem(), out_spec),
            input_output_aliases={4: 1},
            compiler_params=params("arbitrary"),
            cost_estimate=took(4),
        )(me, g_rows, ctx, w_upo, grad_up)
    up_begun = reduce_start(grad_upo, "y")
    dctx, *down_middle = tie(exchange(dctx), *reduce_middle(down_begun, "x"))
    down_sum = reduce_end(down_middle, "x")
    with jax.named_scope("attend_back"):
        dq, dkv = pl.pallas_call(
            functools.partial(attend_back_kernel, rows=span),
            grid=(steps,),
            out_shape=(sds((16, span, 2 * HD)), sds((16, 2 * span, 2 * HD))),
            in_specs=[
                pl.BlockSpec((per, 3 * span, 2 * HD), lambda i: (i, 0, 0)),
                pl.BlockSpec((16, 3 * span, 2 * HD), lambda i: (0, 0, 0)),
                pl.BlockSpec((per, span, 2 * HD), lambda i: (i, 0, 0)),
                pl.BlockSpec((per, span, 2 * HD), lambda i: (i, 0, 0)),
                pl.BlockSpec((2, 8, chunk), lambda i: (0, 0, i)),
            ],
            out_specs=(
                pl.BlockSpec((per, span, 2 * HD), lambda i: (i, 0, 0)),
                pl.BlockSpec((16, 2 * span, 2 * HD), lambda i: (0, 0, 0)),
            ),
            scratch_shapes=[pltpu.VMEM((length, 2 * HD), F32)] * 2,
            compiler_params=params("arbitrary"),
            cost_estimate=took(18),
        )(qkv, qkv, ctx_heads, dctx, lse)
    dqkv = exchange(jnp.concatenate([dq, dkv], axis=1)[None])
    dqkv, down_sum, *up_middle = tie(dqkv, down_sum, *reduce_middle(up_begun, "y"))
    dqkv = dqkv.reshape(2, 8, 3 * span, 2 * HD)
    got_down = plane_reduce(down_sum, PLANE_DOWN)
    got_upo = plane_reduce(reduce_end(up_middle, "y"), PLANE_UP)
    ups = part_up.reshape(4, 2, 4, HD).transpose(0, 2, 1, 3).reshape(4, 1, 4, 2 * HD)
    nothing = jnp.zeros_like(ups)
    ups = jnp.concatenate(
        [jnp.where(first_core, ups, nothing), jnp.where(first_core, nothing, ups)], axis=1
    )
    six = jnp.stack(
        [
            jnp.sum(grad_one, axis=0), jnp.sum(grad_two, axis=0),
            part_gain_attn, part_shift_attn, part_gain_mlp, part_shift_mlp,
        ]
    ).reshape(6, 4, 2, 2 * HD).transpose(1, 2, 0, 3)
    vec_rows = jnp.concatenate(
        [jnp.zeros((4, 2, 2, 2 * HD), F32), six, ups, jnp.zeros((4, 2, 4, 2 * HD), F32)], axis=2
    )
    with jax.named_scope("project_back"):
        grad_qkv, own, other = pl.pallas_call(
            qkv_back_kernel,
            out_shape=(
                sds((4, 2, 4, 2, 3 * HD + 16, 2 * HD)),
                sds((rows, width), F32),
                sds((rows, width)),
            ),
            in_specs=[smem()] + [vmem()] * 4,
            out_specs=(vmem(),) * 3,
            compiler_params=params(),
            cost_estimate=took(8),
        )(me, dqkv, x_rows, w_qkv, vec_rows)
    qkv_middle = reduce_middle(reduce_start(grad_qkv, "z"), "z")
    got_qkv = plane_reduce(reduce_end(qkv_middle, "z"), PLANE_QKV)
    input_sum = own + other_core(other).astype(F32)
    grad_tokens = lax.dot_general(
        grad_one + input_sum, order.astype(F32), (((1,), (1,)), ((), ())), precision=HIGHEST
    )

    final_rows = jnp.concatenate([got_qkv, got_upo, got_down], axis=0).astype(BF16)
    swapped = other_core(final_rows)
    with jax.named_scope("join"):
        square = sds((HD, 2 * HD), F32)
        *weights, vecs = pl.pallas_call(
            join_kernel,
            out_shape=(
                square, square, square,
                sds((2 * HD, HD), F32),
                sds((HD, 2 * hidden), F32),
                sds((2 * hidden, HD), F32),
                sds((16, HD), F32),
            ),
            in_specs=[smem(), vmem(), vmem()],
            out_specs=(vmem(),) * 7,
            compiler_params=params(),
            cost_estimate=took(2),
        )(me, final_rows, swapped)
    return (
        output.reshape(seqs, span, width),
        grad_tokens.reshape(seqs, span, width),
        *weights,
        vecs[0],
        vecs[1],
        vecs[2],
        vecs[8:12].reshape(4 * HD),
        vecs[3],
        vecs[4],
        vecs[5],
        vecs[6],
        vecs[7],
    )


def solution(mesh):
    fine = Mesh(mesh.devices.reshape(4, 2, 2, 4, 2), ("z", "core", "seq", "y", "xhi"))
    owners, tensor = ("z", "core", "seq"), ("y", "xhi")
    tokens = P(("z", "core"), ("seq", "y", "xhi"), None)
    columns, by_rows, vector = P(owners, tensor), P(tensor, owners), P(owners)
    weights = (columns, columns, columns, by_rows, columns, by_rows)
    return jax.shard_map(
        local,
        mesh=fine,
        in_specs=(tokens,) + weights + (vector,) * 9 + (tokens,),
        out_specs=(tokens, tokens) + weights + (vector,) * 9,
        check_vma=False,
    )
```

```python
import functools

import jax
import jax.numpy as jnp
from jax import lax
from jax.experimental import pallas as pl
from jax.experimental.pallas import tpu as pltpu
from jax.sharding import Mesh, PartitionSpec as P

HD = 64
EPS = 1e-05
F32 = jnp.float32
BF16 = jnp.bfloat16
HIGHEST = lax.Precision.HIGHEST
VMEM_LIMIT = 56 * 1024 * 1024
Q_BLOCKS = 4
PLANE = ("seq", "y", "xhi")


def dims(a, b, ca, cb):
    return lax.dot_general(a, b, (((ca,), (cb,)), ((), ())), preferred_element_type=F32)


def shift4(by):
    return [(i, (i + by) % 4) for i in range(4)]


def flip(seq_too, xhi_too):
    return [
        (seq * 2 + xhi, (seq ^ seq_too) * 2 + (xhi ^ xhi_too))
        for seq in range(2)
        for xhi in range(2)
    ]


def links(axis):
    if axis == "x":
        return ("seq", "xhi"), flip(1, 0), flip(1, 1)
    return axis, shift4(-1), shift4(1)


def halves(block):
    half = block.shape[0] // 2
    return block[0:half], block[half:]


def ring_parts(block, axis):
    names, one, two = links(axis)
    first = lax.ppermute(block, names, one)
    second = lax.ppermute(block, names, two)
    if axis == "x":
        head, tail = halves(second)[0], halves(first)[1]
    else:
        head, tail = halves(first)[0], halves(second)[1]
    head = lax.ppermute(head, names, one)
    tail = lax.ppermute(tail, names, two)
    return block, first, second, head, tail


def ring_gather(block, axis):
    block, first, second, head, tail = ring_parts(block, axis)
    if axis == "x":
        whole = jnp.concatenate([block, head, tail, first, second], axis=0)
        return whole.reshape((2, 2) + block.shape)
    whole = jnp.concatenate([block, first, head, tail, second], axis=0)
    return whole.reshape((4,) + block.shape)


def direct_gather(block):
    parts = [block] + [lax.ppermute(block, "z", shift4(-i)) for i in (1, 2, 3)]
    return jnp.stack(parts)


def direct_reduce(block):
    parts = [block[0]] + [lax.ppermute(block[i], "z", shift4(i)) for i in (1, 2, 3)]
    return add(*parts)


def add(*terms):
    total = terms[0].astype(F32)
    for term in terms[1:]:
        total = total + term.astype(F32)
    return total.astype(BF16)


def reduce_parts(block, axis):
    if axis == "x":
        own, far, first, second = block[0, 0], block[0, 1], block[1, 0], block[1, 1]
    else:
        own, first, far, second = block[0], block[1], block[2], block[3]
    return (own, first, second) + halves(far)


def reduce_start(parts, axis):
    names, one, two = links(axis)
    to_first, to_second = (one, two) if axis == "x" else (two, one)
    own, first, second, head, tail = parts
    head = lax.ppermute(head, names, to_first)
    tail = lax.ppermute(tail, names, to_second)
    return own, first, second, head, tail


def reduce_middle(begun, axis):
    own, first, second, head, tail = begun
    first_head, first_tail = halves(first)
    second_head, second_tail = halves(second)
    if axis == "x":
        second = jnp.concatenate([add(second_head, head), second_tail], axis=0)
        first = jnp.concatenate([first_head, add(first_tail, tail)], axis=0)
    else:
        first = jnp.concatenate([add(first_head, head), first_tail], axis=0)
        second = jnp.concatenate([second_head, add(second_tail, tail)], axis=0)
    return own, first, second


def reduce_end(middle, axis):
    own, first, second = middle
    names, one, two = links(axis)
    to_first, to_second = (one, two) if axis == "x" else (two, one)
    return add(
        own,
        lax.ppermute(first, names, to_first),
        lax.ppermute(second, names, to_second),
    )


def tie(*values):
    return lax.optimization_barrier(values)


def plane_gather(shard):
    copies = jnp.broadcast_to(shard[None], (16,) + shard.shape)
    got = lax.all_to_all(copies, PLANE, 0, 0, tiled=False)
    return got.reshape((2, 4, 2) + shard.shape)


def plane_reduce(block):
    flat = block.reshape((16,) + block.shape[-2:])
    got = lax.all_to_all(flat, PLANE, 0, 0, tiled=False)
    return jnp.sum(got.astype(F32), axis=0)


def other_core(block):
    return lax.ppermute(block, "core", [(0, 1), (1, 0)])


def params(*semantics):
    return pltpu.CompilerParams(
        vmem_limit_bytes=VMEM_LIMIT,
        dimension_semantics=semantics if semantics else None,
    )


def vmem():
    return pl.BlockSpec(memory_space=pltpu.VMEM)


def smem():
    return pl.BlockSpec(memory_space=pltpu.SMEM)


CORE, Z, SEQ, Y, XHI = range(5)


def away(me, axis, at):
    return lax.rem(at + 4 - me[axis], 4)


def up_at(me, z, s, y, x):
    return away(me, Y, y), s ^ me[SEQ], x ^ me[XHI], away(me, Z, z)


def ring_rows(parts, step, y, x, size):
    if step == 2:
        a, b = parts[3][0, y, x, 0:size], parts[4][0, y, x, 0:size]
    else:
        ref = parts[{0: 0, 1: 1, 3: 2}[step]]
        a, b = ref[0, y, x, 0:size], ref[1, y, x, 0:size]
    return jnp.concatenate([a, b], axis=1)


def features_of(me, step):
    return pl.ds(pl.multiple_of(lax.rem(me[Z] + step, 4) * 256, 256), 256)


def wide(ref, at, me, y, x, start, stop):
    return jnp.concatenate(
        [ref[(*at(me, z, s, y, x), slice(start, stop))] for z in range(4) for s in range(2)],
        axis=1,
    )


def spread(ref, at, me, y, x, start, value):
    for z in range(4):
        for s in range(2):
            lanes = (z * 2 + s) * 128
            ref[(*at(me, z, s, y, x), slice(start, start + value.shape[0]))] = value[
                :, lanes : lanes + 128
            ].astype(BF16)


def flipped(value):
    return jnp.transpose(value.astype(F32))


def split_kernel(me_ref, wq, wk, wv, wo, wup, wdown, small, keep_ref, give_ref):
    first = me_ref[CORE] == 0
    at = 0
    for ref, turn in ((wq, 1), (wk, 1), (wv, 1), (wo, 0), (wup, 1), (wdown, 0)):
        value = flipped(ref[...]) if turn else ref[...].astype(F32)
        half = value.shape[0] // 2
        a, b = value[0:half], value[half:]
        keep_ref[at : at + half] = jnp.where(first, a, b).astype(BF16)
        give_ref[at : at + half] = jnp.where(first, b, a).astype(BF16)
        at += half
    keep_ref[at:] = small[...]
    give_ref[at:] = small[...]


def join_kernel(me_ref, mine_ref, other_ref, dq, dk, dv, do, dup, ddown, vec_ref):
    first = me_ref[CORE] == 0
    hidden = ddown.shape[0] // 2

    def rows(start, size):
        a = mine_ref[start : start + size].astype(F32)
        b = other_ref[start : start + size].astype(F32)
        zero, one = jnp.where(first, a, b), jnp.where(first, b, a)
        zero = jnp.where(first, zero[:, 0:HD], zero[:, HD:])
        one = jnp.where(first, one[:, 0:HD], one[:, HD:])
        return zero, one

    at = 0
    plan = ((dq, HD, 1), (dk, HD, 1), (dv, HD, 1), (vec_ref, 16, 2))
    for ref, size, turn in plan + ((dup, hidden, 1), (do, HD, 0), (ddown, hidden, 0)):
        zero, one = rows(at, size)
        at += size
        if turn == 2:
            ref[...] = zero + one
        elif turn:
            ref[...] = jnp.transpose(jnp.concatenate([zero, one], axis=0))
        else:
            ref[0:size] = zero
            ref[size:] = one


def qkv_kernel(me_ref, x_ref, bias_ref, w0, w1, w2, w3, w4, out_ref):
    parts = (w0, w1, w2, w3, w4)
    core = me_ref[CORE]
    rows = [x_ref[:, features_of(me_ref, step)] for step in range(4)]
    span = x_ref.shape[0] // 4
    for y in range(4):
        for x in range(2):
            made = bias_ref[y * 2 + x]
            for step in range(4):
                made = made + dims(rows[step], ring_rows(parts, step, y, x, 3 * HD), 1, 1)
            made = made.astype(BF16)
            to = y * 2 + x
            for half in range(2):
                top = made[half * 2 * span : half * 2 * span + span]
                low = made[half * 2 * span + span : (half + 1) * 2 * span]
                packed = jnp.concatenate(
                    [
                        jnp.concatenate(
                            [top[:, i * HD : (i + 1) * HD], low[:, i * HD : (i + 1) * HD]],
                            axis=1,
                        )
                        for i in range(3)
                    ],
                    axis=0,
                )
                out_ref[core ^ half, to] = packed


def attend_kernel(q_ref, kv_ref, ctx_ref, lse_ref, *, rows):
    chunk = q_ref.shape[0] * rows
    length = kv_ref.shape[0] * rows
    queries = q_ref[:, 0:rows].reshape(chunk, 2 * HD) * jnp.bfloat16(0.125)
    keys = kv_ref[:, rows : 2 * rows].reshape(length, 2 * HD)
    values = kv_ref[:, 2 * rows : 3 * rows].reshape(length, 2 * HD)
    lane = lax.broadcasted_iota(jnp.int32, (chunk, 2 * HD), 1)
    parts = []
    for s in range(2):
        mine = (lane < HD) if s == 0 else (lane >= HD)
        picked = jnp.where(mine, queries, jnp.bfloat16(0))
        scores = dims(picked, keys, 1, 1)
        top = jnp.max(scores, axis=1, keepdims=True)
        weights = jnp.exp(scores - top)
        total = jnp.sum(weights, axis=1, keepdims=True)
        mixed = dims(weights.astype(BF16), values, 1, 0)
        parts.append(mixed / total)
        lse = jnp.broadcast_to(top + jnp.log(total), (chunk, 128))
        lse_ref[s] = jnp.transpose(lse)[0:8]
    ctx = jnp.where(lane < HD, parts[0], parts[1])
    ctx_ref[...] = ctx.astype(BF16).reshape(ctx_ref.shape)


def attend_back_kernel(
    q_ref, kv_ref, ctx_ref, dctx_ref, lse_ref, dq_ref, dkv_ref, dk_acc, dv_acc, *, rows
):
    step = pl.program_id(0)
    chunk = q_ref.shape[0] * rows
    length = kv_ref.shape[0] * rows
    queries = q_ref[:, 0:rows].reshape(chunk, 2 * HD) * jnp.bfloat16(0.125)
    grads = dctx_ref[...].reshape(chunk, 2 * HD)
    context = ctx_ref[...].reshape(chunk, 2 * HD)
    keys = kv_ref[:, rows : 2 * rows].reshape(length, 2 * HD)
    values = kv_ref[:, 2 * rows : 3 * rows].reshape(length, 2 * HD)
    lane = lax.broadcasted_iota(jnp.int32, (chunk, 2 * HD), 1)
    long_lane = lax.broadcasted_iota(jnp.int32, (length, 2 * HD), 1)
    both = grads.astype(F32) * context.astype(F32)

    @pl.when(step == 0)
    def _():
        dk_acc[...] = jnp.zeros_like(dk_acc)
        dv_acc[...] = jnp.zeros_like(dv_acc)

    dq_parts, dk_parts, dv_parts = [], [], []
    for s in range(2):
        mine = (lane < HD) if s == 0 else (lane >= HD)
        q_mine = jnp.where(mine, queries, jnp.bfloat16(0))
        g_mine = jnp.where(mine, grads, jnp.bfloat16(0))
        delta = jnp.sum(jnp.where(mine, both, 0.0), axis=1, keepdims=True)
        delta = jnp.transpose(jnp.broadcast_to(delta, (chunk, 128)))[0:1]
        scores = dims(keys, q_mine, 1, 1)
        exact = jnp.exp(scores - lse_ref[s, 0:1])
        grad_probs = dims(values, g_mine, 1, 1)
        grad_scores = (exact * (grad_probs - delta)).astype(BF16)
        dq_parts.append(dims(grad_scores, keys, 0, 0))
        dk_parts.append(dims(grad_scores, queries, 1, 0))
        dv_parts.append(dims(exact.astype(BF16), grads, 1, 0))
    dq = jnp.where(lane < HD, dq_parts[0], dq_parts[1]) * 0.125
    dq_ref[...] = dq.astype(BF16).reshape(dq_ref.shape)
    dk_acc[...] += jnp.where(long_lane < HD, dk_parts[0], dk_parts[1])
    dv_acc[...] += jnp.where(long_lane < HD, dv_parts[0], dv_parts[1])

    @pl.when(step == pl.num_programs(0) - 1)
    def _():
        shape = (kv_ref.shape[0], rows, 2 * HD)
        dkv_ref[:, 0:rows] = dk_acc[...].astype(BF16).reshape(shape)
        dkv_ref[:, rows : 2 * rows] = dv_acc[...].astype(BF16).reshape(shape)


def unpack_rows(top, low):
    return jnp.concatenate([top[:, 0:HD], top[:, HD:], low[:, 0:HD], low[:, HD:]], axis=0)


def out_kernel(me_ref, recv_ref, wo_ref, ctx_ref, own_ref, other_ref):
    core = me_ref[CORE]
    pieces, weights = [], []
    for y in range(4):
        for x in range(2):
            at = y * 2 + x
            pieces.append(unpack_rows(recv_ref[core, at], recv_ref[1 - core, at]))
            weights.append(wide(wo_ref, up_at, me_ref, y, x, 0, HD))
    ctx = jnp.concatenate(pieces, axis=1)
    ctx_ref[...] = ctx
    made = dims(ctx, jnp.concatenate(weights, axis=0), 1, 0)
    half = made.shape[0] // 2
    own_ref[...] = made[0:half]
    other_ref[...] = made[half:].astype(BF16)


def wide_up(ref, me):
    return jnp.concatenate(
        [ref[0, s ^ me[SEQ], 0, away(me, Z, z)] for z in range(4) for s in range(2)], axis=1
    )


def wide_down(ref, me):
    return jnp.concatenate(
        [ref[s ^ me[SEQ], 0, 0, away(me, Z, z)] for z in range(4) for s in range(2)], axis=1
    )


def ffn_kernel(
    me_ref, n_ref, wup_ref, wdown_ref, bias_ref, active_ref, slope_ref, own_ref, other_ref, acc
):
    step = pl.program_id(0)
    rows = n_ref[...]
    pre = dims(rows, wide_up(wup_ref, me_ref), 1, 1) + bias_ref[0]
    cdf = 0.5 * (1.0 + lax.erf(pre * 0.7071067811865476))
    pdf = jnp.exp(-0.5 * pre * pre) * 0.3989422804014327
    active = (pre * cdf).astype(BF16)
    active_ref[...] = active
    slope_ref[...] = (cdf + pre * pdf).astype(BF16)
    made = dims(active, wide_down(wdown_ref, me_ref), 1, 0)

    @pl.when(step == 0)
    def _():
        acc[...] = made

    @pl.when(step > 0)
    def _():
        acc[...] += made

    @pl.when(step == pl.num_programs(0) - 1)
    def _():
        half = acc.shape[0] // 2
        own_ref[...] = acc[0:half]
        other_ref[...] = acc[half:].astype(BF16)


def ffn_back_kernel(
    me_ref, n_ref, g_ref, wup_ref, wdown_ref, active_ref, slope_ref,
    dup_ref, ddown_ref, bias_ref, own_ref, other_ref, acc,
):
    step = pl.program_id(0)
    grads = g_ref[...]
    active = active_ref[...]
    grad = dims(active, grads, 0, 0).astype(BF16)
    for z in range(4):
        for s in range(2):
            at = (z * 2 + s) * 128
            ddown_ref[s ^ me_ref[SEQ], 0, 0, away(me_ref, Z, z)] = grad[:, at : at + 128]
    grad_pre = dims(grads, wide_down(wdown_ref, me_ref), 1, 1) * slope_ref[...].astype(F32)
    bias_ref[0] = jnp.sum(grad_pre, axis=0, keepdims=True)
    low = grad_pre.astype(BF16)
    grad = dims(low, n_ref[...], 0, 0).astype(BF16)
    for z in range(4):
        for s in range(2):
            at = (z * 2 + s) * 128
            dup_ref[0, s ^ me_ref[SEQ], 0, away(me_ref, Z, z)] = grad[:, at : at + 128]
    made = dims(low, wide_up(wup_ref, me_ref), 1, 0)

    @pl.when(step == 0)
    def _():
        acc[...] = made

    @pl.when(step > 0)
    def _():
        acc[...] += made

    @pl.when(step == pl.num_programs(0) - 1)
    def _():
        half = acc.shape[0] // 2
        own_ref[...] = acc[0:half]
        other_ref[...] = acc[half:].astype(BF16)


def out_back_kernel(me_ref, g_ref, ctx_ref, wo_ref, up_ref, dctx_ref, dwo_ref):
    core = me_ref[CORE]
    grads = g_ref[...]
    span = grads.shape[0] // 4
    weights = jnp.concatenate(
        [wide(wo_ref, up_at, me_ref, y, x, 0, HD) for y in range(4) for x in range(2)], axis=0
    )
    made = dims(grads, weights, 1, 1).astype(BF16)
    for y in range(4):
        for x in range(2):
            at = (y * 2 + x) * HD
            piece = made[:, at : at + HD]
            to = y * 2 + x
            for half in range(2):
                base = half * 2 * span
                dctx_ref[core ^ half, to] = jnp.concatenate(
                    [piece[base : base + span], piece[base + span : base + 2 * span]], axis=1
                )
    grad = dims(ctx_ref[...], grads, 0, 0)
    for y in range(4):
        for x in range(2):
            at = (y * 2 + x) * HD
            spread(dwo_ref, up_at, me_ref, y, x, 0, grad[at : at + HD])


def qkv_back_kernel(
    me_ref, recv_ref, x_ref, vec_ref, w0, w1, w2, w3, w4,
    d0, d1, d2, d3, d4, own_ref, other_ref, acc,
):
    core = me_ref[CORE]
    parts, grads = (w0, w1, w2, w3, w4), (d0, d1, d2, d3, d4)
    rows = [x_ref[:, features_of(me_ref, step)] for step in range(4)]
    span = x_ref.shape[0] // 4
    half = x_ref.shape[0] // 2

    def put(step, y, x, start, value):
        stop = start + value.shape[0]
        for s in range(2):
            if step == 2:
                ref, at = grads[3 + s], 0
            else:
                ref, at = grads[{0: 0, 1: 1, 3: 2}[step]], s
            ref[at, y, x, start:stop] = value[:, s * 128 : (s + 1) * 128].astype(BF16)

    sums = []
    totals = [None] * 4
    for y in range(4):
        for x in range(2):
            at = y * 2 + x
            top, low = recv_ref[core, at], recv_ref[1 - core, at]
            made = jnp.concatenate(
                [
                    unpack_rows(
                        top[i * span : (i + 1) * span], low[i * span : (i + 1) * span]
                    )
                    for i in range(3)
                ],
                axis=1,
            )
            sums.append(jnp.sum(made.astype(F32), axis=0, keepdims=True))
            for step in range(4):
                put(step, y, x, 0, dims(made, rows[step], 0, 0))
                part = dims(made, ring_rows(parts, step, y, x, 3 * HD), 1, 0)
                totals[step] = part if totals[step] is None else totals[step] + part
    for step in range(4):
        acc[:, features_of(me_ref, step)] = totals[step]
    own_ref[...] = acc[0:half]
    other_ref[...] = acc[half:].astype(BF16)
    zeros = jnp.zeros((14, 2 * HD), F32)
    twos = []
    for z in range(4):
        a, b = sums[2 * z], sums[2 * z + 1]
        bias_q = jnp.concatenate([a[:, 0:HD], b[:, 0:HD]], axis=1)
        bias_v = jnp.concatenate([a[:, 2 * HD :], b[:, 2 * HD :]], axis=1)
        twos.append(jnp.concatenate([bias_q, bias_v, zeros], axis=0))
    for step in range(4):
        z_abs = lax.rem(me_ref[Z] + step, 4)
        two = twos[3]
        for z in range(3):
            two = jnp.where(z_abs == z, twos[z], two)
        block = jnp.concatenate(
            [vec_ref[z_abs, s] + jnp.where(core == s, two, 0.0) for s in range(2)], axis=1
        )
        for y in range(4):
            for x in range(2):
                put(step, y, x, 3 * HD, block)


def norm_forward(hidden, gain, shift):
    centre = jnp.mean(hidden, axis=-1, keepdims=True)
    centered = hidden - centre
    inverse = lax.rsqrt(jnp.mean(centered * centered, axis=-1, keepdims=True) + EPS)
    normed = centered * inverse
    return (normed * gain + shift, normed, inverse)


def norm_backward(grad_in, normed, inverse, gain):
    scaled = grad_in * gain
    inner_term = (
        scaled
        - jnp.mean(scaled, axis=-1, keepdims=True)
        - normed * jnp.mean(scaled * normed, axis=-1, keepdims=True)
    )
    return (
        inverse * inner_term,
        jnp.sum(grad_in * normed, axis=0),
        jnp.sum(grad_in, axis=0),
    )


def sds(shape, dtype=BF16):
    return jax.ShapeDtypeStruct(shape, dtype)


def took(us):
    return pl.CostEstimate(flops=int(us * 1.15e9), bytes_accessed=1 << 20, transcendentals=0)


def local(
    tokens, w_query, w_key, w_value, w_out, w_up, w_down,
    b_query, b_value, b_out, b_up, b_down,
    gain_attn, shift_attn, gain_mlp, shift_mlp, cotangent,
):
    core = lax.axis_index("core")
    me_z, me_s = lax.axis_index("z"), lax.axis_index("seq")
    me_y, me_x = lax.axis_index("y"), lax.axis_index("xhi")
    first_core = core == 0
    me = jnp.stack([core, me_z, me_s, me_y, me_x]).astype(jnp.int32)
    seqs, span, width = tokens.shape
    rows = seqs * span
    hidden = w_up.shape[1] // 2

    at = jnp.arange(width, dtype=jnp.int32)
    z_of, c_of, s_of, i_of = at // 256, (at // 128) % 2, (at // 64) % 2, at % 64
    stored = z_of * 256 + s_of * 128 + c_of * 64 + i_of
    order = (stored[:, None] == at[None, :]).astype(BF16)

    small = jnp.stack(
        [b_query, b_value, b_out, b_down, gain_attn, shift_attn, gain_mlp, shift_mlp]
    )
    small = jnp.concatenate([small, b_up.reshape(4, HD), jnp.zeros((4, HD), BF16)], axis=0)
    shard_rows = 4 * HD + 2 * hidden + 16
    with jax.named_scope("split"):
        keep, give = pl.pallas_call(
            split_kernel,
            out_shape=(sds((shard_rows, HD)),) * 2,
            in_specs=[smem()] + [vmem()] * 7,
            out_specs=(vmem(), vmem()),
            compiler_params=params(),
            cost_estimate=took(2),
        )(me, w_query, w_key, w_value, w_out, w_up, w_down, small)
    got = other_core(give)
    shard = jnp.where(
        first_core,
        jnp.concatenate([keep, got], axis=1),
        jnp.concatenate([got, keep], axis=1),
    )
    at_o, at_up, at_down, at_vec = 3 * HD, 4 * HD, 4 * HD + hidden, 4 * HD + 2 * hidden
    qkv_shard = jnp.concatenate([shard[0:at_o], shard[at_vec:]], axis=0)
    slow_shard = jnp.concatenate([shard[at_up:at_down], shard[at_o:at_up], shard[at_down:at_vec]])
    qkv_parts = ring_parts(plane_gather(qkv_shard), "z")
    slow = direct_gather(slow_shard)
    up_rows = hidden + HD
    w_upo = ring_gather(ring_gather(slow[:, 0:up_rows], "x"), "y")
    wdown = ring_gather(ring_gather(slow[:, up_rows:], "y"), "x")

    both_in = jnp.concatenate([tokens.reshape(rows, width), cotangent.reshape(rows, width)], axis=0)
    both_in = dims(both_in, order, 1, 0)
    mine = both_in[0:rows]
    grad_final = both_in[rows:]
    mine_low = mine.astype(BF16)
    x_rows = jnp.concatenate([mine_low, other_core(mine_low)], axis=0)

    fours = jnp.arange(4, dtype=jnp.int32)
    turn = ((fours[:, None] - me_z) % 4 == fours[None, :]).astype(F32)
    ring = [p[:, 0, 0, 3 * HD :, :].reshape(-1) for p in qkv_parts]
    vec = jnp.concatenate([ring[0], ring[1], ring[3], ring[4], ring[2]])
    vec = vec.reshape(4, 4096).astype(F32)
    vec = jnp.dot(turn, vec, precision=HIGHEST).reshape(4, 2, 16, 2 * HD)
    feature = lambda i: vec[:, :, i, :].reshape(width)
    chosen = jnp.where(first_core, vec[:, 0], vec[:, 1])
    chosen = chosen.reshape(4, 16, 2, HD).transpose(0, 2, 1, 3).reshape(8, 16 * HD)
    zeros = jnp.zeros((8, HD), F32)
    bias_qkv = jnp.concatenate([chosen[:, 0:HD], zeros, chosen[:, HD : 2 * HD]], axis=1)
    bias_qkv = bias_qkv[:, None, :]
    bias_up = chosen[:, 8 * HD : 12 * HD][:, None, :]
    gain_one, gain_two = feature(4), feature(6)

    with jax.named_scope("project"):
        packed = pl.pallas_call(
            qkv_kernel,
            out_shape=sds((2, 8, 3 * span, 2 * HD)),
            in_specs=[smem()] + [vmem()] * 7,
            out_specs=vmem(),
            compiler_params=params(),
            cost_estimate=took(5),
        )(me, x_rows, bias_qkv, *qkv_parts)

    def exchange(block):
        flat = block.reshape((16,) + block.shape[2:])
        return lax.all_to_all(flat, PLANE, 0, 0, tiled=False)

    qkv = exchange(packed)
    per = Q_BLOCKS
    chunk = per * span
    steps = 16 // per
    length = 16 * span
    with jax.named_scope("attend"):
        ctx_heads, lse = pl.pallas_call(
            functools.partial(attend_kernel, rows=span),
            grid=(steps,),
            out_shape=(sds((16, span, 2 * HD)), sds((2, 8, length), F32)),
            in_specs=[
                pl.BlockSpec((per, 3 * span, 2 * HD), lambda i: (i, 0, 0)),
                pl.BlockSpec((16, 3 * span, 2 * HD), lambda i: (0, 0, 0)),
            ],
            out_specs=(
                pl.BlockSpec((per, span, 2 * HD), lambda i: (i, 0, 0)),
                pl.BlockSpec((2, 8, chunk), lambda i: (0, 0, i)),
            ),
            compiler_params=params("arbitrary"),
            cost_estimate=took(11),
        )(qkv, qkv)
    recv = lax.all_to_all(ctx_heads, PLANE, 0, 0, tiled=False)
    recv = recv.reshape(2, 8, span, 2 * HD)
    out_spec = pl.BlockSpec((4, 2, 2, 4, HD, 2 * HD), lambda i: (0, 0, 0, 0, hidden // HD, 0))
    with jax.named_scope("out_project"):
        ctx, own, other = pl.pallas_call(
            out_kernel,
            out_shape=(sds((2 * rows, 8 * HD)), sds((rows, width), F32), sds((rows, width))),
            grid=(1,),
            in_specs=[smem(), vmem(), out_spec],
            out_specs=(vmem(), vmem(), vmem()),
            compiler_params=params("arbitrary"),
            cost_estimate=took(3),
        )(me, recv, w_upo)
    attended = own + other_core(other).astype(F32)
    resid_one = mine + attended + feature(2)
    normed_one, norm_first, inverse_first = norm_forward(resid_one, gain_one, feature(5))
    normed_low = normed_one.astype(BF16)
    n_rows = jnp.concatenate([normed_low, other_core(normed_low)], axis=0)

    up_spec = pl.BlockSpec(
        (1, 2, 1, 4, hidden, 2 * HD),
        lambda t, at: (away(at, Y, t // 2), 0, (t % 2) ^ at[XHI], 0, 0, 0),
    )
    down_spec = pl.BlockSpec(
        (2, 1, 1, 4, hidden, 2 * HD),
        lambda t, at: (0, (t % 2) ^ at[XHI], away(at, Y, t // 2), 0, 0, 0),
    )
    whole_spec = pl.BlockSpec((2 * rows, width), lambda t, at: (0, 0))
    cols_spec = pl.BlockSpec((2 * rows, hidden), lambda t, at: (0, t))
    half_spec = pl.BlockSpec((rows, width), lambda t, at: (0, 0))
    bias_spec = pl.BlockSpec((1, 1, hidden), lambda t, at: (t, 0, 0))
    with jax.named_scope("feed_forward"):
        active, slope, own, other = pl.pallas_call(
            ffn_kernel,
            grid_spec=pltpu.PrefetchScalarGridSpec(
                num_scalar_prefetch=1,
                grid=(8,),
                in_specs=[whole_spec, up_spec, down_spec, bias_spec],
                out_specs=(cols_spec, cols_spec, half_spec, half_spec),
                scratch_shapes=[pltpu.VMEM((2 * rows, width), F32)],
            ),
            out_shape=(
                sds((2 * rows, 8 * hidden)),
                sds((2 * rows, 8 * hidden)),
                sds((rows, width), F32),
                sds((rows, width)),
            ),
            compiler_params=params("arbitrary"),
            cost_estimate=took(14),
        )(me, n_rows, w_upo, wdown, bias_up)
    mixed = own + other_core(other).astype(F32)
    resid_two = normed_one + mixed + feature(3)
    final, norm_second, inverse_second = norm_forward(resid_two, gain_two, feature(7))
    output = dims(final.astype(BF16), order, 1, 1).astype(BF16)
    grad_two, part_gain_mlp, part_shift_mlp = norm_backward(
        grad_final, norm_second, inverse_second, gain_two
    )
    grad_low = grad_two.astype(BF16)
    g_rows = jnp.concatenate([grad_low, other_core(grad_low)], axis=0)
    with jax.named_scope("feed_forward_back"):
        grad_up, grad_down, part_up, own, other = pl.pallas_call(
            ffn_back_kernel,
            grid_spec=pltpu.PrefetchScalarGridSpec(
                num_scalar_prefetch=1,
                grid=(8,),
                in_specs=[whole_spec, whole_spec, up_spec, down_spec, cols_spec, cols_spec],
                out_specs=(up_spec, down_spec, bias_spec, half_spec, half_spec),
                scratch_shapes=[pltpu.VMEM((2 * rows, width), F32)],
            ),
            out_shape=(
                sds(w_upo.shape),
                sds(wdown.shape),
                sds((8, 1, hidden), F32),
                sds((rows, width), F32),
                sds((rows, width)),
            ),
            compiler_params=params("arbitrary"),
            cost_estimate=took(20),
        )(me, n_rows, g_rows, w_upo, wdown, active, slope)
    down_begun = reduce_start(reduce_parts(grad_down, "x"), "x")
    grad_mid = grad_two + (own + other_core(other).astype(F32))
    grad_one, part_gain_attn, part_shift_attn = norm_backward(
        grad_mid, norm_first, inverse_first, gain_one
    )
    grad_low = grad_one.astype(BF16)
    g_rows = jnp.concatenate([grad_low, other_core(grad_low)], axis=0)
    with jax.named_scope("out_project_back"):
        dctx, grad_upo = pl.pallas_call(
            out_back_kernel,
            grid=(1,),
            out_shape=(sds((2, 8, span, 2 * HD)), sds(grad_up.shape)),
            in_specs=[smem(), vmem(), vmem(), out_spec, pl.BlockSpec(memory_space=pl.ANY)],
            out_specs=(vmem(), out_spec),
            input_output_aliases={4: 1},
            compiler_params=params("arbitrary"),
            cost_estimate=took(4),
        )(me, g_rows, ctx, w_upo, grad_up)
    up_begun = reduce_start(reduce_parts(grad_upo, "y"), "y")
    dctx, *down_middle = tie(exchange(dctx), *reduce_middle(down_begun, "x"))
    down_sum = reduce_end(down_middle, "x")
    with jax.named_scope("attend_back"):
        dq, dkv = pl.pallas_call(
            functools.partial(attend_back_kernel, rows=span),
            grid=(steps,),
            out_shape=(sds((16, span, 2 * HD)), sds((16, 2 * span, 2 * HD))),
            in_specs=[
                pl.BlockSpec((per, 3 * span, 2 * HD), lambda i: (i, 0, 0)),
                pl.BlockSpec((16, 3 * span, 2 * HD), lambda i: (0, 0, 0)),
                pl.BlockSpec((per, span, 2 * HD), lambda i: (i, 0, 0)),
                pl.BlockSpec((per, span, 2 * HD), lambda i: (i, 0, 0)),
                pl.BlockSpec((2, 8, chunk), lambda i: (0, 0, i)),
            ],
            out_specs=(
                pl.BlockSpec((per, span, 2 * HD), lambda i: (i, 0, 0)),
                pl.BlockSpec((16, 2 * span, 2 * HD), lambda i: (0, 0, 0)),
            ),
            scratch_shapes=[pltpu.VMEM((length, 2 * HD), F32)] * 2,
            compiler_params=params("arbitrary"),
            cost_estimate=took(18),
        )(qkv, qkv, ctx_heads, dctx, lse)
    dqkv = exchange(jnp.concatenate([dq, dkv], axis=1)[None])
    dqkv, down_sum, *up_middle = tie(dqkv, down_sum, *reduce_middle(up_begun, "y"))
    dqkv = dqkv.reshape(2, 8, 3 * span, 2 * HD)
    down_begun = reduce_start(reduce_parts(down_sum, "y"), "y")
    ups = part_up.reshape(4, 2, 4, HD).transpose(0, 2, 1, 3).reshape(4, 1, 4, 2 * HD)
    nothing = jnp.zeros_like(ups)
    ups = jnp.concatenate(
        [jnp.where(first_core, ups, nothing), jnp.where(first_core, nothing, ups)], axis=1
    )
    six = jnp.stack(
        [
            jnp.sum(grad_one, axis=0), jnp.sum(grad_two, axis=0),
            part_gain_attn, part_shift_attn, part_gain_mlp, part_shift_mlp,
        ]
    ).reshape(6, 4, 2, 2 * HD).transpose(1, 2, 0, 3)
    vec_rows = jnp.concatenate(
        [jnp.zeros((4, 2, 2, 2 * HD), F32), six, ups, jnp.zeros((4, 2, 4, 2 * HD), F32)], axis=2
    )
    with jax.named_scope("project_back"):
        part, far = sds((2, 4, 2, 3 * HD + 16, 2 * HD)), sds((1, 4, 2, 3 * HD + 16, 2 * HD))
        *grad_qkv, own, other = pl.pallas_call(
            qkv_back_kernel,
            out_shape=(
                part, part, part, far, far, sds((rows, width), F32), sds((rows, width)),
            ),
            in_specs=[smem()] + [vmem()] * 8,
            out_specs=(vmem(),) * 7,
            scratch_shapes=[pltpu.VMEM((2 * rows, width), F32)],
            compiler_params=params(),
            cost_estimate=took(8),
        )(me, dqkv, x_rows, vec_rows, *qkv_parts)
    qkv_middle = reduce_middle(reduce_start(grad_qkv, "z"), "z")
    qkv_sum = reduce_end(qkv_middle, "z")
    down_sum = reduce_end(reduce_middle(down_begun, "y"), "y")
    up_begun = reduce_start(reduce_parts(reduce_end(up_middle, "y"), "x"), "x")
    up_sum = reduce_end(reduce_middle(up_begun, "x"), "x")
    got_slow = direct_reduce(jnp.concatenate([up_sum, down_sum], axis=1))
    got_qkv = plane_reduce(qkv_sum)
    input_sum = own + other_core(other).astype(F32)
    grad_tokens = lax.dot_general(
        grad_one + input_sum, order.astype(F32), (((1,), (1,)), ((), ())), precision=HIGHEST
    )

    final_rows = jnp.concatenate([got_qkv.astype(BF16), got_slow], axis=0)
    swapped = other_core(final_rows)
    with jax.named_scope("join"):
        square = sds((HD, 2 * HD), F32)
        *weights, vecs = pl.pallas_call(
            join_kernel,
            out_shape=(
                square, square, square,
                sds((2 * HD, HD), F32),
                sds((HD, 2 * hidden), F32),
                sds((2 * hidden, HD), F32),
                sds((16, HD), F32),
            ),
            in_specs=[smem(), vmem(), vmem()],
            out_specs=(vmem(),) * 7,
            compiler_params=params(),
            cost_estimate=took(2),
        )(me, final_rows, swapped)
    return (
        output.reshape(seqs, span, width),
        grad_tokens.reshape(seqs, span, width),
        *weights,
        vecs[0],
        vecs[1],
        vecs[2],
        vecs[8:12].reshape(4 * HD),
        vecs[3],
        vecs[4],
        vecs[5],
        vecs[6],
        vecs[7],
    )


def solution(mesh):
    fine = Mesh(mesh.devices.reshape(4, 2, 2, 4, 2), ("z", "core", "seq", "y", "xhi"))
    owners, tensor = ("z", "core", "seq"), ("y", "xhi")
    tokens = P(("z", "core"), ("seq", "y", "xhi"), None)
    columns, by_rows, vector = P(owners, tensor), P(tensor, owners), P(owners)
    weights = (columns, columns, columns, by_rows, columns, by_rows)
    return jax.shard_map(
        local,
        mesh=fine,
        in_specs=(tokens,) + weights + (vector,) * 9 + (tokens,),
        out_specs=(tokens, tokens) + weights + (vector,) * 9,
        check_vma=False,
    )
```

```python
import functools

import jax
import jax.numpy as jnp
from jax import lax
from jax.experimental import pallas as pl
from jax.experimental.pallas import tpu as pltpu
from jax.sharding import Mesh, PartitionSpec as P

HD = 64
EPS = 1e-05
F32 = jnp.float32
BF16 = jnp.bfloat16
HIGHEST = lax.Precision.HIGHEST
VMEM_LIMIT = 56 * 1024 * 1024
Q_BLOCKS = 4
PLANE = ("seq", "y", "xhi")


def dims(a, b, ca, cb):
    return lax.dot_general(a, b, (((ca,), (cb,)), ((), ())), preferred_element_type=F32)


def shift4(by):
    return [(i, (i + by) % 4) for i in range(4)]


def flip(seq_too, xhi_too):
    return [
        (seq * 2 + xhi, (seq ^ seq_too) * 2 + (xhi ^ xhi_too))
        for seq in range(2)
        for xhi in range(2)
    ]


def links(axis):
    if axis == "x":
        return ("seq", "xhi"), flip(1, 0), flip(1, 1)
    return axis, shift4(-1), shift4(1)


def halves(block):
    half = block.shape[0] // 2
    return block[0:half], block[half:]


def ring_parts(block, axis):
    names, one, two = links(axis)
    first = lax.ppermute(block, names, one)
    second = lax.ppermute(block, names, two)
    if axis == "x":
        head, tail = halves(second)[0], halves(first)[1]
    else:
        head, tail = halves(first)[0], halves(second)[1]
    head = lax.ppermute(head, names, one)
    tail = lax.ppermute(tail, names, two)
    return block, first, second, head, tail


def ring_gather(block, axis):
    block, first, second, head, tail = ring_parts(block, axis)
    if axis == "x":
        whole = jnp.concatenate([block, head, tail, first, second], axis=0)
        return whole.reshape((2, 2) + block.shape)
    whole = jnp.concatenate([block, first, head, tail, second], axis=0)
    return whole.reshape((4,) + block.shape)


def direct_gather(block, axis):
    parts = [block] + [lax.ppermute(block, axis, shift4(-i)) for i in (1, 2, 3)]
    return jnp.stack(parts)


def direct_reduce(block, axis):
    parts = [block[0]] + [lax.ppermute(block[i], axis, shift4(i)) for i in (1, 2, 3)]
    return add(*parts)


def add(*terms):
    total = terms[0].astype(F32)
    for term in terms[1:]:
        total = total + term.astype(F32)
    return total.astype(BF16)


def reduce_parts(block, axis):
    if axis == "x":
        own, far, first, second = block[0, 0], block[0, 1], block[1, 0], block[1, 1]
    else:
        own, first, far, second = block[0], block[1], block[2], block[3]
    return (own, first, second) + halves(far)


def reduce_start(parts, axis):
    names, one, two = links(axis)
    to_first, to_second = (one, two) if axis == "x" else (two, one)
    own, first, second, head, tail = parts
    head = lax.ppermute(head, names, to_first)
    tail = lax.ppermute(tail, names, to_second)
    return own, first, second, head, tail


def reduce_middle(begun, axis):
    own, first, second, head, tail = begun
    first_head, first_tail = halves(first)
    second_head, second_tail = halves(second)
    if axis == "x":
        second = jnp.concatenate([add(second_head, head), second_tail], axis=0)
        first = jnp.concatenate([first_head, add(first_tail, tail)], axis=0)
    else:
        first = jnp.concatenate([add(first_head, head), first_tail], axis=0)
        second = jnp.concatenate([second_head, add(second_tail, tail)], axis=0)
    return own, first, second


def reduce_end(middle, axis):
    own, first, second = middle
    names, one, two = links(axis)
    to_first, to_second = (one, two) if axis == "x" else (two, one)
    return add(
        own,
        lax.ppermute(first, names, to_first),
        lax.ppermute(second, names, to_second),
    )


def tie(*values):
    return lax.optimization_barrier(values)


def plane_gather(copies):
    got = lax.all_to_all(copies, PLANE, 0, 0, tiled=False)
    return got.reshape((2, 4, 2) + copies.shape[1:])


def plane_reduce(block):
    flat = block.reshape((16,) + block.shape[-2:])
    got = lax.all_to_all(flat, PLANE, 0, 0, tiled=False)
    return jnp.sum(got.astype(F32), axis=0)


def other_core(block):
    return lax.ppermute(block, "core", [(0, 1), (1, 0)])


def params(*semantics):
    return pltpu.CompilerParams(
        vmem_limit_bytes=VMEM_LIMIT,
        dimension_semantics=semantics if semantics else None,
    )


def vmem():
    return pl.BlockSpec(memory_space=pltpu.VMEM)


def smem():
    return pl.BlockSpec(memory_space=pltpu.SMEM)


CORE, Z, SEQ, Y, XHI = range(5)


def away(me, axis, at):
    return lax.rem(at + 4 - me[axis], 4)


def up_at(me, z, s, y, x):
    return away(me, Z, z), s ^ me[SEQ], x ^ me[XHI], away(me, Y, y)


def ring_rows(parts, step, y, x, size):
    if step == 2:
        a, b = parts[3][0, y, x, 0:size], parts[4][0, y, x, 0:size]
    else:
        ref = parts[{0: 0, 1: 1, 3: 2}[step]]
        a, b = ref[0, y, x, 0:size], ref[1, y, x, 0:size]
    return jnp.concatenate([a, b], axis=1)


def features_of(me, step):
    return pl.ds(pl.multiple_of(lax.rem(me[Z] + step, 4) * 256, 256), 256)


def wide(ref, at, me, y, x, start, stop):
    return jnp.concatenate(
        [ref[(*at(me, z, s, y, x), slice(start, stop))] for z in range(4) for s in range(2)],
        axis=1,
    )


def spread(ref, at, me, y, x, start, value):
    for z in range(4):
        for s in range(2):
            lanes = (z * 2 + s) * 128
            ref[(*at(me, z, s, y, x), slice(start, start + value.shape[0]))] = value[
                :, lanes : lanes + 128
            ].astype(BF16)


def split_kernel(me_ref, wq, wk, wv, wo, wup, wdown, small, keep_ref, give_ref):
    first = me_ref[CORE] == 0
    at = 0
    for ref in (wq, wk, wv, wo, wup, wdown):
        value = jnp.transpose(ref[...].astype(F32))
        half = value.shape[0] // 2
        a, b = value[0:half], value[half:]
        keep_ref[at : at + half] = jnp.where(first, a, b).astype(BF16)
        give_ref[at : at + half] = jnp.where(first, b, a).astype(BF16)
        at += half
    keep_ref[at:] = small[...]
    give_ref[at:] = small[...]


def join_kernel(me_ref, mine_ref, other_ref, dq, dk, dv, do, dup, ddown, vec_ref):
    first = me_ref[CORE] == 0
    hidden = ddown.shape[1] // 2

    def rows(start, size):
        a = mine_ref[start : start + size].astype(F32)
        b = other_ref[start : start + size].astype(F32)
        zero, one = jnp.where(first, a, b), jnp.where(first, b, a)
        zero = jnp.where(first, zero[:, 0:HD], zero[:, HD:])
        one = jnp.where(first, one[:, 0:HD], one[:, HD:])
        return zero, one

    at = 0
    plan = ((dq, HD), (dk, HD), (dv, HD), (vec_ref, 16), (dup, hidden), (do, HD), (ddown, hidden))
    for ref, size in plan:
        zero, one = rows(at, size)
        at += size
        if size == 16:
            ref[...] = zero + one
        else:
            ref[...] = jnp.transpose(jnp.concatenate([zero, one], axis=0))


def qkv_kernel(me_ref, x_ref, bias_ref, w0, w1, w2, w3, w4, out_ref):
    parts = (w0, w1, w2, w3, w4)
    core = me_ref[CORE]
    rows = [x_ref[:, features_of(me_ref, step)] for step in range(4)]
    span = x_ref.shape[0] // 4
    for y in range(4):
        for x in range(2):
            made = bias_ref[y * 2 + x]
            for step in range(4):
                made = made + dims(rows[step], ring_rows(parts, step, y, x, 3 * HD), 1, 1)
            made = made.astype(BF16)
            to = y * 2 + x
            for half in range(2):
                top = made[half * 2 * span : half * 2 * span + span]
                low = made[half * 2 * span + span : (half + 1) * 2 * span]
                packed = jnp.concatenate(
                    [
                        jnp.concatenate(
                            [top[:, i * HD : (i + 1) * HD], low[:, i * HD : (i + 1) * HD]],
                            axis=1,
                        )
                        for i in range(3)
                    ],
                    axis=0,
                )
                out_ref[core ^ half, to] = packed


def attend_kernel(q_ref, kv_ref, ctx_ref, lse_ref, *, rows):
    chunk = q_ref.shape[0] * rows
    length = kv_ref.shape[0] * rows
    queries = q_ref[:, 0:rows].reshape(chunk, 2 * HD) * jnp.bfloat16(0.125)
    keys = kv_ref[:, rows : 2 * rows].reshape(length, 2 * HD)
    values = kv_ref[:, 2 * rows : 3 * rows].reshape(length, 2 * HD)
    lane = lax.broadcasted_iota(jnp.int32, (chunk, 2 * HD), 1)
    parts = []
    for s in range(2):
        mine = (lane < HD) if s == 0 else (lane >= HD)
        picked = jnp.where(mine, queries, jnp.bfloat16(0))
        scores = dims(picked, keys, 1, 1)
        top = jnp.max(scores, axis=1, keepdims=True)
        weights = jnp.exp(scores - top)
        total = jnp.sum(weights, axis=1, keepdims=True)
        mixed = dims(weights.astype(BF16), values, 1, 0)
        parts.append(mixed / total)
        lse = jnp.broadcast_to(top + jnp.log(total), (chunk, 128))
        lse_ref[s] = jnp.transpose(lse)[0:8]
    ctx = jnp.where(lane < HD, parts[0], parts[1])
    ctx_ref[...] = ctx.astype(BF16).reshape(ctx_ref.shape)


def attend_back_kernel(
    q_ref, kv_ref, ctx_ref, dctx_ref, lse_ref, dq_ref, dkv_ref, dk_acc, dv_acc, *, rows
):
    step = pl.program_id(0)
    chunk = q_ref.shape[0] * rows
    length = kv_ref.shape[0] * rows
    queries = q_ref[:, 0:rows].reshape(chunk, 2 * HD) * jnp.bfloat16(0.125)
    grads = dctx_ref[...].reshape(chunk, 2 * HD)
    context = ctx_ref[...].reshape(chunk, 2 * HD)
    keys = kv_ref[:, rows : 2 * rows].reshape(length, 2 * HD)
    values = kv_ref[:, 2 * rows : 3 * rows].reshape(length, 2 * HD)
    lane = lax.broadcasted_iota(jnp.int32, (chunk, 2 * HD), 1)
    long_lane = lax.broadcasted_iota(jnp.int32, (length, 2 * HD), 1)
    both = grads.astype(F32) * context.astype(F32)

    @pl.when(step == 0)
    def _():
        dk_acc[...] = jnp.zeros_like(dk_acc)
        dv_acc[...] = jnp.zeros_like(dv_acc)

    dq_parts, dk_parts, dv_parts = [], [], []
    for s in range(2):
        mine = (lane < HD) if s == 0 else (lane >= HD)
        q_mine = jnp.where(mine, queries, jnp.bfloat16(0))
        g_mine = jnp.where(mine, grads, jnp.bfloat16(0))
        delta = jnp.sum(jnp.where(mine, both, 0.0), axis=1, keepdims=True)
        delta = jnp.transpose(jnp.broadcast_to(delta, (chunk, 128)))[0:1]
        scores = dims(keys, q_mine, 1, 1)
        exact = jnp.exp(scores - lse_ref[s, 0:1])
        grad_probs = dims(values, g_mine, 1, 1)
        grad_scores = (exact * (grad_probs - delta)).astype(BF16)
        dq_parts.append(dims(grad_scores, keys, 0, 0))
        dk_parts.append(dims(grad_scores, queries, 1, 0))
        dv_parts.append(dims(exact.astype(BF16), grads, 1, 0))
    dq = jnp.where(lane < HD, dq_parts[0], dq_parts[1]) * 0.125
    dq_ref[...] = dq.astype(BF16).reshape(dq_ref.shape)
    dk_acc[...] += jnp.where(long_lane < HD, dk_parts[0], dk_parts[1])
    dv_acc[...] += jnp.where(long_lane < HD, dv_parts[0], dv_parts[1])

    @pl.when(step == pl.num_programs(0) - 1)
    def _():
        shape = (kv_ref.shape[0], rows, 2 * HD)
        dkv_ref[:, 0:rows] = dk_acc[...].astype(BF16).reshape(shape)
        dkv_ref[:, rows : 2 * rows] = dv_acc[...].astype(BF16).reshape(shape)


def unpack_rows(top, low):
    return jnp.concatenate([top[:, 0:HD], top[:, HD:], low[:, 0:HD], low[:, HD:]], axis=0)


def out_kernel(me_ref, recv_ref, wo_ref, ctx_ref, own_ref, other_ref):
    core = me_ref[CORE]
    pieces, weights = [], []
    for y in range(4):
        for x in range(2):
            at = y * 2 + x
            pieces.append(unpack_rows(recv_ref[core, at], recv_ref[1 - core, at]))
            weights.append(wide(wo_ref, up_at, me_ref, y, x, 0, HD))
    ctx = jnp.concatenate(pieces, axis=1)
    ctx_ref[...] = ctx
    made = dims(ctx, jnp.concatenate(weights, axis=0), 1, 0)
    half = made.shape[0] // 2
    own_ref[...] = made[0:half]
    other_ref[...] = made[half:].astype(BF16)


def wide_up(ref, me):
    return jnp.concatenate(
        [ref[away(me, Z, z), s ^ me[SEQ], 0, 0] for z in range(4) for s in range(2)], axis=1
    )


def wide_down(ref, me):
    return jnp.concatenate(
        [ref[s ^ me[SEQ], 0, 0, away(me, Z, z)] for z in range(4) for s in range(2)], axis=1
    )


def ffn_kernel(
    me_ref, n_ref, wup_ref, wdown_ref, bias_ref, active_ref, slope_ref, own_ref, other_ref, acc
):
    step = pl.program_id(0)
    rows = n_ref[...]
    pre = dims(rows, wide_up(wup_ref, me_ref), 1, 1) + bias_ref[0]
    cdf = 0.5 * (1.0 + lax.erf(pre * 0.7071067811865476))
    pdf = jnp.exp(-0.5 * pre * pre) * 0.3989422804014327
    active = (pre * cdf).astype(BF16)
    active_ref[...] = active
    slope_ref[...] = (cdf + pre * pdf).astype(BF16)
    made = dims(active, wide_down(wdown_ref, me_ref), 1, 0)

    @pl.when(step == 0)
    def _():
        acc[...] = made

    @pl.when(step > 0)
    def _():
        acc[...] += made

    @pl.when(step == pl.num_programs(0) - 1)
    def _():
        half = acc.shape[0] // 2
        own_ref[...] = acc[0:half]
        other_ref[...] = acc[half:].astype(BF16)


def ffn_back_kernel(
    me_ref, n_ref, g_ref, wup_ref, wdown_ref, active_ref, slope_ref,
    dup_ref, ddown_ref, bias_ref, own_ref, other_ref, acc,
):
    step = pl.program_id(0)
    grads = g_ref[...]
    active = active_ref[...]
    grad = dims(active, grads, 0, 0).astype(BF16)
    for z in range(4):
        for s in range(2):
            at = (z * 2 + s) * 128
            ddown_ref[s ^ me_ref[SEQ], 0, 0, away(me_ref, Z, z)] = grad[:, at : at + 128]
    grad_pre = dims(grads, wide_down(wdown_ref, me_ref), 1, 1) * slope_ref[...].astype(F32)
    bias_ref[0] = jnp.sum(grad_pre, axis=0, keepdims=True)
    low = grad_pre.astype(BF16)
    grad = dims(low, n_ref[...], 0, 0).astype(BF16)
    for z in range(4):
        for s in range(2):
            at = (z * 2 + s) * 128
            dup_ref[away(me_ref, Z, z), s ^ me_ref[SEQ], 0, 0] = grad[:, at : at + 128]
    made = dims(low, wide_up(wup_ref, me_ref), 1, 0)

    @pl.when(step == 0)
    def _():
        acc[...] = made

    @pl.when(step > 0)
    def _():
        acc[...] += made

    @pl.when(step == pl.num_programs(0) - 1)
    def _():
        half = acc.shape[0] // 2
        own_ref[...] = acc[0:half]
        other_ref[...] = acc[half:].astype(BF16)


def out_back_kernel(me_ref, g_ref, ctx_ref, wo_ref, up_ref, dctx_ref, dwo_ref):
    core = me_ref[CORE]
    grads = g_ref[...]
    span = grads.shape[0] // 4
    weights = jnp.concatenate(
        [wide(wo_ref, up_at, me_ref, y, x, 0, HD) for y in range(4) for x in range(2)], axis=0
    )
    made = dims(grads, weights, 1, 1).astype(BF16)
    for y in range(4):
        for x in range(2):
            at = (y * 2 + x) * HD
            piece = made[:, at : at + HD]
            to = y * 2 + x
            for half in range(2):
                base = half * 2 * span
                dctx_ref[core ^ half, to] = jnp.concatenate(
                    [piece[base : base + span], piece[base + span : base + 2 * span]], axis=1
                )
    grad = dims(ctx_ref[...], grads, 0, 0)
    for y in range(4):
        for x in range(2):
            at = (y * 2 + x) * HD
            spread(dwo_ref, up_at, me_ref, y, x, 0, grad[at : at + HD])


def qkv_back_kernel(
    me_ref, recv_ref, x_ref, vec_ref, w0, w1, w2, w3, w4,
    d0, d1, d2, d3, d4, own_ref, other_ref, acc,
):
    core = me_ref[CORE]
    parts, grads = (w0, w1, w2, w3, w4), (d0, d1, d2, d3, d4)
    rows = [x_ref[:, features_of(me_ref, step)] for step in range(4)]
    span = x_ref.shape[0] // 4
    half = x_ref.shape[0] // 2

    def put(step, y, x, start, value):
        stop = start + value.shape[0]
        for s in range(2):
            if step == 2:
                ref, at = grads[3 + s], 0
            else:
                ref, at = grads[{0: 0, 1: 1, 3: 2}[step]], s
            ref[at, y, x, start:stop] = value[:, s * 128 : (s + 1) * 128].astype(BF16)

    sums = []
    totals = [None] * 4
    for y in range(4):
        for x in range(2):
            at = y * 2 + x
            top, low = recv_ref[core, at], recv_ref[1 - core, at]
            made = jnp.concatenate(
                [
                    unpack_rows(
                        top[i * span : (i + 1) * span], low[i * span : (i + 1) * span]
                    )
                    for i in range(3)
                ],
                axis=1,
            )
            sums.append(jnp.sum(made.astype(F32), axis=0, keepdims=True))
            for step in range(4):
                put(step, y, x, 0, dims(made, rows[step], 0, 0))
                part = dims(made, ring_rows(parts, step, y, x, 3 * HD), 1, 0)
                totals[step] = part if totals[step] is None else totals[step] + part
    for step in range(4):
        acc[:, features_of(me_ref, step)] = totals[step]
    own_ref[...] = acc[0:half]
    other_ref[...] = acc[half:].astype(BF16)
    zeros = jnp.zeros((14, 2 * HD), F32)
    twos = []
    for z in range(4):
        a, b = sums[2 * z], sums[2 * z + 1]
        bias_q = jnp.concatenate([a[:, 0:HD], b[:, 0:HD]], axis=1)
        bias_v = jnp.concatenate([a[:, 2 * HD :], b[:, 2 * HD :]], axis=1)
        twos.append(jnp.concatenate([bias_q, bias_v, zeros], axis=0))
    for step in range(4):
        z_abs = lax.rem(me_ref[Z] + step, 4)
        two = twos[3]
        for z in range(3):
            two = jnp.where(z_abs == z, twos[z], two)
        block = jnp.concatenate(
            [vec_ref[z_abs, s] + jnp.where(core == s, two, 0.0) for s in range(2)], axis=1
        )
        for y in range(4):
            for x in range(2):
                put(step, y, x, 3 * HD, block)


def norm_forward(hidden, gain, shift):
    centre = jnp.mean(hidden, axis=-1, keepdims=True)
    centered = hidden - centre
    inverse = lax.rsqrt(jnp.mean(centered * centered, axis=-1, keepdims=True) + EPS)
    normed = centered * inverse
    return (normed * gain + shift, normed, inverse)


def norm_backward(grad_in, normed, inverse, gain):
    scaled = grad_in * gain
    inner_term = (
        scaled
        - jnp.mean(scaled, axis=-1, keepdims=True)
        - normed * jnp.mean(scaled * normed, axis=-1, keepdims=True)
    )
    return (
        inverse * inner_term,
        jnp.sum(grad_in * normed, axis=0),
        jnp.sum(grad_in, axis=0),
    )


def sds(shape, dtype=BF16):
    return jax.ShapeDtypeStruct(shape, dtype)


def took(us):
    return pl.CostEstimate(flops=int(us * 1.15e9), bytes_accessed=1 << 20, transcendentals=0)


def local(
    tokens, w_query, w_key, w_value, w_out, w_up, w_down,
    b_query, b_value, b_out, b_up, b_down,
    gain_attn, shift_attn, gain_mlp, shift_mlp, cotangent,
):
    core = lax.axis_index("core")
    me_z, me_s = lax.axis_index("z"), lax.axis_index("seq")
    me_y, me_x = lax.axis_index("y"), lax.axis_index("xhi")
    first_core = core == 0
    me = jnp.stack([core, me_z, me_s, me_y, me_x]).astype(jnp.int32)
    seqs, span, width = tokens.shape
    rows = seqs * span
    hidden = w_up.shape[1] // 2

    at = jnp.arange(width, dtype=jnp.int32)
    z_of, c_of, s_of, i_of = at // 256, (at // 128) % 2, (at // 64) % 2, at % 64
    stored = z_of * 256 + s_of * 128 + c_of * 64 + i_of
    order = (stored[:, None] == at[None, :]).astype(BF16)

    small = jnp.stack(
        [b_query, b_value, b_out, b_down, gain_attn, shift_attn, gain_mlp, shift_mlp]
    )
    small = jnp.concatenate([small, b_up.reshape(4, HD), jnp.zeros((4, HD), BF16)], axis=0)
    shard_rows = 4 * HD + 2 * hidden + 16
    with jax.named_scope("split"):
        keep, give = pl.pallas_call(
            split_kernel,
            out_shape=(sds((shard_rows, HD)),) * 2,
            in_specs=[smem()] + [vmem()] * 7,
            out_specs=(vmem(), vmem()),
            compiler_params=params(),
            cost_estimate=took(2),
        )(me, w_query, w_key, w_value, w_out.T, w_up, w_down.T, small)
    got = other_core(give)
    shard = jnp.where(
        first_core,
        jnp.concatenate([keep, got], axis=1),
        jnp.concatenate([got, keep], axis=1),
    )
    at_o, at_up, at_down, at_vec = 3 * HD, 4 * HD, 4 * HD + hidden, 4 * HD + 2 * hidden
    qkv_shard = jnp.concatenate([shard[0:at_o], shard[at_vec:]], axis=0)
    up_shard = jnp.concatenate([shard[at_up:at_down], shard[at_o:at_up]])
    copies = jnp.broadcast_to(qkv_shard[None], (16,) + qkv_shard.shape)
    copies, up_shard, down_shard = tie(copies, up_shard, shard[at_down:at_vec])
    *near, head, tail = ring_parts(plane_gather(copies), "z")
    up_block = ring_gather(direct_gather(up_shard, "y"), "x")
    down_block = ring_gather(direct_gather(down_shard, "z"), "y")
    head, tail, up_block, down_block = tie(head, tail, up_block, down_block)
    qkv_parts = (*near, head, tail)
    w_upo = ring_gather(up_block, "z")
    wdown = ring_gather(down_block, "x")

    both_in = jnp.concatenate([tokens.reshape(rows, width), cotangent.reshape(rows, width)], axis=0)
    both_in = dims(both_in, order, 1, 0)
    mine = both_in[0:rows]
    grad_final = both_in[rows:]
    mine_low = mine.astype(BF16)
    x_rows = jnp.concatenate([mine_low, other_core(mine_low)], axis=0)

    fours = jnp.arange(4, dtype=jnp.int32)
    turn = ((fours[:, None] - me_z) % 4 == fours[None, :]).astype(F32)
    ring = [p[:, 0, 0, 3 * HD :, :].reshape(-1) for p in qkv_parts]
    vec = jnp.concatenate([ring[0], ring[1], ring[3], ring[4], ring[2]])
    vec = vec.reshape(4, 4096).astype(F32)
    vec = jnp.dot(turn, vec, precision=HIGHEST).reshape(4, 2, 16, 2 * HD)
    feature = lambda i: vec[:, :, i, :].reshape(width)
    chosen = jnp.where(first_core, vec[:, 0], vec[:, 1])
    chosen = chosen.reshape(4, 16, 2, HD).transpose(0, 2, 1, 3).reshape(8, 16 * HD)
    zeros = jnp.zeros((8, HD), F32)
    bias_qkv = jnp.concatenate([chosen[:, 0:HD], zeros, chosen[:, HD : 2 * HD]], axis=1)
    bias_qkv = bias_qkv[:, None, :]
    bias_up = chosen[:, 8 * HD : 12 * HD][:, None, :]
    gain_one, gain_two = feature(4), feature(6)

    with jax.named_scope("project"):
        packed = pl.pallas_call(
            qkv_kernel,
            out_shape=sds((2, 8, 3 * span, 2 * HD)),
            in_specs=[smem()] + [vmem()] * 7,
            out_specs=vmem(),
            compiler_params=params(),
            cost_estimate=took(5),
        )(me, x_rows, bias_qkv, *qkv_parts)

    def exchange(block):
        flat = block.reshape((16,) + block.shape[2:])
        return lax.all_to_all(flat, PLANE, 0, 0, tiled=False)

    qkv = exchange(packed)
    per = Q_BLOCKS
    chunk = per * span
    steps = 16 // per
    length = 16 * span
    with jax.named_scope("attend"):
        ctx_heads, lse = pl.pallas_call(
            functools.partial(attend_kernel, rows=span),
            grid=(steps,),
            out_shape=(sds((16, span, 2 * HD)), sds((2, 8, length), F32)),
            in_specs=[
                pl.BlockSpec((per, 3 * span, 2 * HD), lambda i: (i, 0, 0)),
                pl.BlockSpec((16, 3 * span, 2 * HD), lambda i: (0, 0, 0)),
            ],
            out_specs=(
                pl.BlockSpec((per, span, 2 * HD), lambda i: (i, 0, 0)),
                pl.BlockSpec((2, 8, chunk), lambda i: (0, 0, i)),
            ),
            compiler_params=params("arbitrary"),
            cost_estimate=took(11),
        )(qkv, qkv)
    recv = lax.all_to_all(ctx_heads, PLANE, 0, 0, tiled=False)
    recv = recv.reshape(2, 8, span, 2 * HD)
    out_spec = pl.BlockSpec((4, 2, 2, 4, HD, 2 * HD), lambda i: (0, 0, 0, 0, hidden // HD, 0))
    with jax.named_scope("out_project"):
        ctx, own, other = pl.pallas_call(
            out_kernel,
            out_shape=(sds((2 * rows, 8 * HD)), sds((rows, width), F32), sds((rows, width))),
            grid=(1,),
            in_specs=[smem(), vmem(), out_spec],
            out_specs=(vmem(), vmem(), vmem()),
            compiler_params=params("arbitrary"),
            cost_estimate=took(3),
        )(me, recv, w_upo)
    attended = own + other_core(other).astype(F32)
    resid_one = mine + attended + feature(2)
    normed_one, norm_first, inverse_first = norm_forward(resid_one, gain_one, feature(5))
    normed_low = normed_one.astype(BF16)
    n_rows = jnp.concatenate([normed_low, other_core(normed_low)], axis=0)

    up_spec = pl.BlockSpec(
        (4, 2, 1, 1, hidden, 2 * HD),
        lambda t, at: (0, 0, (t % 2) ^ at[XHI], away(at, Y, t // 2), 0, 0),
    )
    down_spec = pl.BlockSpec(
        (2, 1, 1, 4, hidden, 2 * HD),
        lambda t, at: (0, (t % 2) ^ at[XHI], away(at, Y, t // 2), 0, 0, 0),
    )
    whole_spec = pl.BlockSpec((2 * rows, width), lambda t, at: (0, 0))
    cols_spec = pl.BlockSpec((2 * rows, hidden), lambda t, at: (0, t))
    half_spec = pl.BlockSpec((rows, width), lambda t, at: (0, 0))
    bias_spec = pl.BlockSpec((1, 1, hidden), lambda t, at: (t, 0, 0))
    with jax.named_scope("feed_forward"):
        active, slope, own, other = pl.pallas_call(
            ffn_kernel,
            grid_spec=pltpu.PrefetchScalarGridSpec(
                num_scalar_prefetch=1,
                grid=(8,),
                in_specs=[whole_spec, up_spec, down_spec, bias_spec],
                out_specs=(cols_spec, cols_spec, half_spec, half_spec),
                scratch_shapes=[pltpu.VMEM((2 * rows, width), F32)],
            ),
            out_shape=(
                sds((2 * rows, 8 * hidden)),
                sds((2 * rows, 8 * hidden)),
                sds((rows, width), F32),
                sds((rows, width)),
            ),
            compiler_params=params("arbitrary"),
            cost_estimate=took(14),
        )(me, n_rows, w_upo, wdown, bias_up)
    mixed = own + other_core(other).astype(F32)
    resid_two = normed_one + mixed + feature(3)
    final, norm_second, inverse_second = norm_forward(resid_two, gain_two, feature(7))
    output = dims(final.astype(BF16), order, 1, 1).astype(BF16)
    grad_two, part_gain_mlp, part_shift_mlp = norm_backward(
        grad_final, norm_second, inverse_second, gain_two
    )
    grad_low = grad_two.astype(BF16)
    g_rows = jnp.concatenate([grad_low, other_core(grad_low)], axis=0)
    with jax.named_scope("feed_forward_back"):
        grad_up, grad_down, part_up, own, other = pl.pallas_call(
            ffn_back_kernel,
            grid_spec=pltpu.PrefetchScalarGridSpec(
                num_scalar_prefetch=1,
                grid=(8,),
                in_specs=[whole_spec, whole_spec, up_spec, down_spec, cols_spec, cols_spec],
                out_specs=(up_spec, down_spec, bias_spec, half_spec, half_spec),
                scratch_shapes=[pltpu.VMEM((2 * rows, width), F32)],
            ),
            out_shape=(
                sds(w_upo.shape),
                sds(wdown.shape),
                sds((8, 1, hidden), F32),
                sds((rows, width), F32),
                sds((rows, width)),
            ),
            compiler_params=params("arbitrary"),
            cost_estimate=took(20),
        )(me, n_rows, g_rows, w_upo, wdown, active, slope)
    grad_mid = grad_two + (own + other_core(other).astype(F32))
    grad_one, part_gain_attn, part_shift_attn = norm_backward(
        grad_mid, norm_first, inverse_first, gain_one
    )
    grad_low = grad_one.astype(BF16)
    g_rows = jnp.concatenate([grad_low, other_core(grad_low)], axis=0)
    with jax.named_scope("out_project_back"):
        dctx, grad_upo = pl.pallas_call(
            out_back_kernel,
            grid=(1,),
            out_shape=(sds((2, 8, span, 2 * HD)), sds(grad_up.shape)),
            in_specs=[smem(), vmem(), vmem(), out_spec, pl.BlockSpec(memory_space=pl.ANY)],
            out_specs=(vmem(), out_spec),
            input_output_aliases={4: 1},
            compiler_params=params("arbitrary"),
            cost_estimate=took(4),
        )(me, g_rows, ctx, w_upo, grad_up)
    dctx, grad_down = tie(dctx, grad_down)
    down_begun = reduce_start(reduce_parts(grad_down, "x"), "x")
    up_begun = reduce_start(reduce_parts(grad_upo, "z"), "z")
    dctx, *middles = tie(
        exchange(dctx), *reduce_middle(down_begun, "x"), *reduce_middle(up_begun, "z")
    )
    down_sum = reduce_end(middles[0:3], "x")
    up_sum = reduce_end(middles[3:6], "z")
    with jax.named_scope("attend_back"):
        dq, dkv = pl.pallas_call(
            functools.partial(attend_back_kernel, rows=span),
            grid=(steps,),
            out_shape=(sds((16, span, 2 * HD)), sds((16, 2 * span, 2 * HD))),
            in_specs=[
                pl.BlockSpec((per, 3 * span, 2 * HD), lambda i: (i, 0, 0)),
                pl.BlockSpec((16, 3 * span, 2 * HD), lambda i: (0, 0, 0)),
                pl.BlockSpec((per, span, 2 * HD), lambda i: (i, 0, 0)),
                pl.BlockSpec((per, span, 2 * HD), lambda i: (i, 0, 0)),
                pl.BlockSpec((2, 8, chunk), lambda i: (0, 0, i)),
            ],
            out_specs=(
                pl.BlockSpec((per, span, 2 * HD), lambda i: (i, 0, 0)),
                pl.BlockSpec((16, 2 * span, 2 * HD), lambda i: (0, 0, 0)),
            ),
            scratch_shapes=[pltpu.VMEM((length, 2 * HD), F32)] * 2,
            compiler_params=params("arbitrary"),
            cost_estimate=took(18),
        )(qkv, qkv, ctx_heads, dctx, lse)
    dqkv = exchange(jnp.concatenate([dq, dkv], axis=1)[None])
    dqkv, up_sum, down_sum = tie(dqkv, up_sum, down_sum)
    dqkv = dqkv.reshape(2, 8, 3 * span, 2 * HD)
    down_begun = reduce_start(reduce_parts(down_sum, "y"), "y")
    ups = part_up.reshape(4, 2, 4, HD).transpose(0, 2, 1, 3).reshape(4, 1, 4, 2 * HD)
    nothing = jnp.zeros_like(ups)
    ups = jnp.concatenate(
        [jnp.where(first_core, ups, nothing), jnp.where(first_core, nothing, ups)], axis=1
    )
    six = jnp.stack(
        [
            jnp.sum(grad_one, axis=0), jnp.sum(grad_two, axis=0),
            part_gain_attn, part_shift_attn, part_gain_mlp, part_shift_mlp,
        ]
    ).reshape(6, 4, 2, 2 * HD).transpose(1, 2, 0, 3)
    vec_rows = jnp.concatenate(
        [jnp.zeros((4, 2, 2, 2 * HD), F32), six, ups, jnp.zeros((4, 2, 4, 2 * HD), F32)], axis=2
    )
    with jax.named_scope("project_back"):
        part, far = sds((2, 4, 2, 3 * HD + 16, 2 * HD)), sds((1, 4, 2, 3 * HD + 16, 2 * HD))
        *grad_qkv, own, other = pl.pallas_call(
            qkv_back_kernel,
            out_shape=(
                part, part, part, far, far, sds((rows, width), F32), sds((rows, width)),
            ),
            in_specs=[smem()] + [vmem()] * 8,
            out_specs=(vmem(),) * 7,
            scratch_shapes=[pltpu.VMEM((2 * rows, width), F32)],
            compiler_params=params(),
            cost_estimate=took(8),
        )(me, dqkv, x_rows, vec_rows, *qkv_parts)
    qkv_middle = reduce_middle(reduce_start(grad_qkv, "z"), "z")
    qkv_sum = reduce_end(qkv_middle, "z")
    down_sum = reduce_end(reduce_middle(down_begun, "y"), "y")
    up_begun = reduce_start(reduce_parts(up_sum, "x"), "x")
    up_sum = reduce_end(reduce_middle(up_begun, "x"), "x")
    got_up = direct_reduce(up_sum, "y")
    got_down = direct_reduce(down_sum, "z")
    got_qkv = plane_reduce(qkv_sum)
    input_sum = own + other_core(other).astype(F32)
    grad_tokens = lax.dot_general(
        grad_one + input_sum, order.astype(F32), (((1,), (1,)), ((), ())), precision=HIGHEST
    )

    final_rows = jnp.concatenate([got_qkv.astype(BF16), got_up, got_down], axis=0)
    swapped = other_core(final_rows)
    with jax.named_scope("join"):
        square = sds((HD, 2 * HD), F32)
        *weights, g_out, g_up, g_down, vecs = pl.pallas_call(
            join_kernel,
            out_shape=(
                square, square, square, square,
                sds((HD, 2 * hidden), F32),
                sds((HD, 2 * hidden), F32),
                sds((16, HD), F32),
            ),
            in_specs=[smem(), vmem(), vmem()],
            out_specs=(vmem(),) * 7,
            compiler_params=params(),
            cost_estimate=took(2),
        )(me, final_rows, swapped)
    return (
        output.reshape(seqs, span, width),
        grad_tokens.reshape(seqs, span, width),
        *weights,
        g_out.T,
        g_up,
        g_down.T,
        vecs[0],
        vecs[1],
        vecs[2],
        vecs[8:12].reshape(4 * HD),
        vecs[3],
        vecs[4],
        vecs[5],
        vecs[6],
        vecs[7],
    )


def solution(mesh):
    fine = Mesh(mesh.devices.reshape(4, 2, 2, 4, 2), ("z", "core", "seq", "y", "xhi"))
    owners, tensor = ("z", "core", "seq"), ("y", "xhi")
    tokens = P(("z", "core"), ("seq", "y", "xhi"), None)
    columns, by_rows, vector = P(owners, tensor), P(tensor, owners), P(owners)
    weights = (columns, columns, columns, by_rows, columns, by_rows)
    return jax.shard_map(
        local,
        mesh=fine,
        in_specs=(tokens,) + weights + (vector,) * 9 + (tokens,),
        out_specs=(tokens, tokens) + weights + (vector,) * 9,
        check_vma=False,
    )
```

```python
import functools

import jax
import jax.numpy as jnp
from jax import lax
from jax.experimental import pallas as pl
from jax.experimental.pallas import tpu as pltpu
from jax.sharding import Mesh, PartitionSpec as P

HD = 64
EPS = 1e-05
F32 = jnp.float32
BF16 = jnp.bfloat16
HIGHEST = lax.Precision.HIGHEST
VMEM_LIMIT = 56 * 1024 * 1024
Q_BLOCKS = 4
PLANE = ("seq", "y", "xhi")


def dims(a, b, ca, cb):
    return lax.dot_general(a, b, (((ca,), (cb,)), ((), ())), preferred_element_type=F32)


def shift4(by):
    return [(i, (i + by) % 4) for i in range(4)]


def flip(seq_too, xhi_too):
    return [
        (seq * 2 + xhi, (seq ^ seq_too) * 2 + (xhi ^ xhi_too))
        for seq in range(2)
        for xhi in range(2)
    ]


def links(axis):
    if axis == "x":
        return ("seq", "xhi"), flip(1, 0), flip(1, 1)
    return axis, shift4(-1), shift4(1)


def halves(block):
    half = block.shape[0] // 2
    return block[0:half], block[half:]


def ring_begin(block, axis):
    names, one, two = links(axis)
    return lax.ppermute(block, names, one), lax.ppermute(block, names, two)


def ring_finish(block, first, second, axis):
    names, one, two = links(axis)
    if axis == "x":
        head, tail = halves(second)[0], halves(first)[1]
    else:
        head, tail = halves(first)[0], halves(second)[1]
    head = lax.ppermute(head, names, one)
    tail = lax.ppermute(tail, names, two)
    return block, first, second, head, tail


def ring_joined(block, first, second, axis):
    block, first, second, head, tail = ring_finish(block, first, second, axis)
    if axis == "x":
        whole = jnp.concatenate([block, head, tail, first, second], axis=0)
        return whole.reshape((2, 2) + block.shape)
    whole = jnp.concatenate([block, first, head, tail, second], axis=0)
    return whole.reshape((4,) + block.shape)


def ring_gather(block, axis):
    return ring_joined(block, *ring_begin(block, axis), axis)


def direct_gather(block, axis):
    parts = [block] + [lax.ppermute(block, axis, shift4(-i)) for i in (1, 2, 3)]
    return jnp.stack(parts)


def direct_reduce(block, axis):
    parts = [block[0]] + [lax.ppermute(block[i], axis, shift4(i)) for i in (1, 2, 3)]
    return add(*parts)


def add(*terms):
    total = terms[0].astype(F32)
    for term in terms[1:]:
        total = total + term.astype(F32)
    return total.astype(BF16)


def reduce_parts(block, axis):
    if axis == "x":
        own, far, first, second = block[0, 0], block[0, 1], block[1, 0], block[1, 1]
    else:
        own, first, far, second = block[0], block[1], block[2], block[3]
    return (own, first, second) + halves(far)


def reduce_start(parts, axis):
    names, one, two = links(axis)
    to_first, to_second = (one, two) if axis == "x" else (two, one)
    own, first, second, head, tail = parts
    head = lax.ppermute(head, names, to_first)
    tail = lax.ppermute(tail, names, to_second)
    return own, first, second, head, tail


def reduce_middle(begun, axis):
    own, first, second, head, tail = begun
    first_head, first_tail = halves(first)
    second_head, second_tail = halves(second)
    if axis == "x":
        second = jnp.concatenate([add(second_head, head), second_tail], axis=0)
        first = jnp.concatenate([first_head, add(first_tail, tail)], axis=0)
    else:
        first = jnp.concatenate([add(first_head, head), first_tail], axis=0)
        second = jnp.concatenate([second_head, add(second_tail, tail)], axis=0)
    return own, first, second


def reduce_end(middle, axis):
    own, first, second = middle
    names, one, two = links(axis)
    to_first, to_second = (one, two) if axis == "x" else (two, one)
    return add(
        own,
        lax.ppermute(first, names, to_first),
        lax.ppermute(second, names, to_second),
    )


def tie(*values):
    return lax.optimization_barrier(values)


def plane_gather(copies):
    got = lax.all_to_all(copies, PLANE, 0, 0, tiled=False)
    return got.reshape((2, 4, 2) + copies.shape[1:])


def plane_reduce(block):
    flat = block.reshape((16,) + block.shape[-2:])
    got = lax.all_to_all(flat, PLANE, 0, 0, tiled=False)
    return jnp.sum(got.astype(F32), axis=0)


def other_core(block):
    return lax.ppermute(block, "core", [(0, 1), (1, 0)])


def params(*semantics):
    return pltpu.CompilerParams(
        vmem_limit_bytes=VMEM_LIMIT,
        dimension_semantics=semantics if semantics else None,
    )


def vmem():
    return pl.BlockSpec(memory_space=pltpu.VMEM)


def smem():
    return pl.BlockSpec(memory_space=pltpu.SMEM)


CORE, Z, SEQ, Y, XHI = range(5)


def away(me, axis, at):
    return lax.rem(at + 4 - me[axis], 4)


def up_at(me, z, s, y, x):
    return away(me, Z, z), s, y, x


def ring_rows(parts, step, y, x, size):
    if step == 2:
        a, b = parts[3][0, y, x, 0:size], parts[4][0, y, x, 0:size]
    else:
        ref = parts[{0: 0, 1: 1, 3: 2}[step]]
        a, b = ref[0, y, x, 0:size], ref[1, y, x, 0:size]
    return jnp.concatenate([a, b], axis=1)


def features_of(me, step):
    return pl.ds(pl.multiple_of(lax.rem(me[Z] + step, 4) * 256, 256), 256)


def wide(ref, at, me, y, x, start, stop):
    return jnp.concatenate(
        [ref[(*at(me, z, s, y, x), slice(start, stop))] for z in range(4) for s in range(2)],
        axis=1,
    )


def spread(ref, at, me, y, x, start, value):
    for z in range(4):
        for s in range(2):
            lanes = (z * 2 + s) * 128
            ref[(*at(me, z, s, y, x), slice(start, start + value.shape[0]))] = value[
                :, lanes : lanes + 128
            ].astype(BF16)


def split_kernel(me_ref, wq, wk, wv, wo, wup, wdown, small, keep_ref, give_ref):
    first = me_ref[CORE] == 0
    at = 0
    for ref in (wq, wk, wv, wo, wup, wdown):
        value = jnp.transpose(ref[...].astype(F32))
        half = value.shape[0] // 2
        a, b = value[0:half], value[half:]
        keep_ref[at : at + half] = jnp.where(first, a, b).astype(BF16)
        give_ref[at : at + half] = jnp.where(first, b, a).astype(BF16)
        at += half
    keep_ref[at:] = small[...]
    give_ref[at:] = small[...]


def join_kernel(me_ref, mine_ref, other_ref, dq, dk, dv, do, dup, ddown, vec_ref):
    first = me_ref[CORE] == 0
    hidden = ddown.shape[1] // 2

    def rows(start, size):
        a = mine_ref[start : start + size].astype(F32)
        b = other_ref[start : start + size].astype(F32)
        zero, one = jnp.where(first, a, b), jnp.where(first, b, a)
        zero = jnp.where(first, zero[:, 0:HD], zero[:, HD:])
        one = jnp.where(first, one[:, 0:HD], one[:, HD:])
        return zero, one

    at = 0
    plan = ((dq, HD), (dk, HD), (dv, HD), (vec_ref, 16), (dup, hidden), (do, HD), (ddown, hidden))
    for ref, size in plan:
        zero, one = rows(at, size)
        at += size
        if size == 16:
            ref[...] = zero + one
        else:
            ref[...] = jnp.transpose(jnp.concatenate([zero, one], axis=0))


def qkv_kernel(me_ref, x_ref, bias_ref, w0, w1, w2, w3, w4, out_ref):
    parts = (w0, w1, w2, w3, w4)
    core = me_ref[CORE]
    rows = [x_ref[:, features_of(me_ref, step)] for step in range(4)]
    span = x_ref.shape[0] // 4
    for y in range(4):
        for x in range(2):
            made = bias_ref[y * 2 + x]
            for step in range(4):
                made = made + dims(rows[step], ring_rows(parts, step, y, x, 3 * HD), 1, 1)
            made = made.astype(BF16)
            to = y * 2 + x
            for half in range(2):
                top = made[half * 2 * span : half * 2 * span + span]
                low = made[half * 2 * span + span : (half + 1) * 2 * span]
                packed = jnp.concatenate(
                    [
                        jnp.concatenate(
                            [top[:, i * HD : (i + 1) * HD], low[:, i * HD : (i + 1) * HD]],
                            axis=1,
                        )
                        for i in range(3)
                    ],
                    axis=0,
                )
                out_ref[core ^ half, to] = packed


def attend_kernel(q_ref, kv_ref, ctx_ref, lse_ref, *, rows):
    chunk = q_ref.shape[0] * rows
    length = kv_ref.shape[0] * rows
    queries = q_ref[:, 0:rows].reshape(chunk, 2 * HD) * jnp.bfloat16(0.125)
    keys = kv_ref[:, rows : 2 * rows].reshape(length, 2 * HD)
    values = kv_ref[:, 2 * rows : 3 * rows].reshape(length, 2 * HD)
    lane = lax.broadcasted_iota(jnp.int32, (chunk, 2 * HD), 1)
    parts = []
    for s in range(2):
        mine = (lane < HD) if s == 0 else (lane >= HD)
        picked = jnp.where(mine, queries, jnp.bfloat16(0))
        scores = dims(picked, keys, 1, 1)
        top = jnp.max(scores, axis=1, keepdims=True)
        weights = jnp.exp(scores - top)
        total = jnp.sum(weights, axis=1, keepdims=True)
        mixed = dims(weights.astype(BF16), values, 1, 0)
        parts.append(mixed / total)
        lse = jnp.broadcast_to(top + jnp.log(total), (chunk, 128))
        lse_ref[s] = jnp.transpose(lse)[0:8]
    ctx = jnp.where(lane < HD, parts[0], parts[1])
    ctx_ref[...] = ctx.astype(BF16).reshape(ctx_ref.shape)


def attend_back_kernel(
    q_ref, kv_ref, ctx_ref, dctx_ref, lse_ref, dq_ref, dkv_ref, dk_acc, dv_acc, *, rows
):
    step = pl.program_id(0)
    chunk = q_ref.shape[0] * rows
    length = kv_ref.shape[0] * rows
    queries = q_ref[:, 0:rows].reshape(chunk, 2 * HD) * jnp.bfloat16(0.125)
    grads = dctx_ref[...].reshape(chunk, 2 * HD)
    context = ctx_ref[...].reshape(chunk, 2 * HD)
    keys = kv_ref[:, rows : 2 * rows].reshape(length, 2 * HD)
    values = kv_ref[:, 2 * rows : 3 * rows].reshape(length, 2 * HD)
    lane = lax.broadcasted_iota(jnp.int32, (chunk, 2 * HD), 1)
    long_lane = lax.broadcasted_iota(jnp.int32, (length, 2 * HD), 1)
    both = grads.astype(F32) * context.astype(F32)

    @pl.when(step == 0)
    def _():
        dk_acc[...] = jnp.zeros_like(dk_acc)
        dv_acc[...] = jnp.zeros_like(dv_acc)

    dq_parts, dk_parts, dv_parts = [], [], []
    for s in range(2):
        mine = (lane < HD) if s == 0 else (lane >= HD)
        q_mine = jnp.where(mine, queries, jnp.bfloat16(0))
        g_mine = jnp.where(mine, grads, jnp.bfloat16(0))
        delta = jnp.sum(jnp.where(mine, both, 0.0), axis=1, keepdims=True)
        delta = jnp.transpose(jnp.broadcast_to(delta, (chunk, 128)))[0:1]
        scores = dims(keys, q_mine, 1, 1)
        exact = jnp.exp(scores - lse_ref[s, 0:1])
        grad_probs = dims(values, g_mine, 1, 1)
        grad_scores = (exact * (grad_probs - delta)).astype(BF16)
        dq_parts.append(dims(grad_scores, keys, 0, 0))
        dk_parts.append(dims(grad_scores, queries, 1, 0))
        dv_parts.append(dims(exact.astype(BF16), grads, 1, 0))
    dq = jnp.where(lane < HD, dq_parts[0], dq_parts[1]) * 0.125
    dq_ref[...] = dq.astype(BF16).reshape(dq_ref.shape)
    dk_acc[...] += jnp.where(long_lane < HD, dk_parts[0], dk_parts[1])
    dv_acc[...] += jnp.where(long_lane < HD, dv_parts[0], dv_parts[1])

    @pl.when(step == pl.num_programs(0) - 1)
    def _():
        shape = (kv_ref.shape[0], rows, 2 * HD)
        dkv_ref[:, 0:rows] = dk_acc[...].astype(BF16).reshape(shape)
        dkv_ref[:, rows : 2 * rows] = dv_acc[...].astype(BF16).reshape(shape)


def unpack_rows(top, low):
    return jnp.concatenate([top[:, 0:HD], top[:, HD:], low[:, 0:HD], low[:, HD:]], axis=0)


def out_kernel(me_ref, recv_ref, wo_ref, ctx_ref, own_ref, other_ref):
    core = me_ref[CORE]
    pieces, weights = [], []
    for y in range(4):
        for x in range(2):
            at = y * 2 + x
            pieces.append(unpack_rows(recv_ref[core, at], recv_ref[1 - core, at]))
            weights.append(wide(wo_ref, up_at, me_ref, y, x, 0, HD))
    ctx = jnp.concatenate(pieces, axis=1)
    ctx_ref[...] = ctx
    made = dims(ctx, jnp.concatenate(weights, axis=0), 1, 0)
    half = made.shape[0] // 2
    own_ref[...] = made[0:half]
    other_ref[...] = made[half:].astype(BF16)


def wide_up(ref, me):
    return jnp.concatenate(
        [ref[away(me, Z, z), s, 0, 0] for z in range(4) for s in range(2)], axis=1
    )


def wide_down(ref, me):
    return jnp.concatenate(
        [ref[s ^ me[SEQ], 0, 0, away(me, Z, z)] for z in range(4) for s in range(2)], axis=1
    )


def ffn_kernel(
    me_ref, n_ref, wup_ref, wdown_ref, bias_ref, active_ref, slope_ref, own_ref, other_ref, acc
):
    step = pl.program_id(0)
    rows = n_ref[...]
    pre = dims(rows, wide_up(wup_ref, me_ref), 1, 1) + bias_ref[0]
    cdf = 0.5 * (1.0 + lax.erf(pre * 0.7071067811865476))
    pdf = jnp.exp(-0.5 * pre * pre) * 0.3989422804014327
    active = (pre * cdf).astype(BF16)
    active_ref[...] = active
    slope_ref[...] = (cdf + pre * pdf).astype(BF16)
    made = dims(active, wide_down(wdown_ref, me_ref), 1, 0)

    @pl.when(step == 0)
    def _():
        acc[...] = made

    @pl.when(step > 0)
    def _():
        acc[...] += made

    @pl.when(step == pl.num_programs(0) - 1)
    def _():
        half = acc.shape[0] // 2
        own_ref[...] = acc[0:half]
        other_ref[...] = acc[half:].astype(BF16)


def ffn_back_kernel(
    me_ref, n_ref, g_ref, wup_ref, wdown_ref, active_ref, slope_ref,
    dup_ref, ddown_ref, bias_ref, own_ref, other_ref, acc,
):
    step = pl.program_id(0)
    grads = g_ref[...]
    active = active_ref[...]
    grad = dims(active, grads, 0, 0).astype(BF16)
    for z in range(4):
        for s in range(2):
            at = (z * 2 + s) * 128
            ddown_ref[s ^ me_ref[SEQ], 0, 0, away(me_ref, Z, z)] = grad[:, at : at + 128]
    grad_pre = dims(grads, wide_down(wdown_ref, me_ref), 1, 1) * slope_ref[...].astype(F32)
    bias_ref[0] = jnp.sum(grad_pre, axis=0, keepdims=True)
    low = grad_pre.astype(BF16)
    grad = dims(low, n_ref[...], 0, 0).astype(BF16)
    for z in range(4):
        for s in range(2):
            at = (z * 2 + s) * 128
            dup_ref[away(me_ref, Z, z), s, 0, 0] = grad[:, at : at + 128]
    made = dims(low, wide_up(wup_ref, me_ref), 1, 0)

    @pl.when(step == 0)
    def _():
        acc[...] = made

    @pl.when(step > 0)
    def _():
        acc[...] += made

    @pl.when(step == pl.num_programs(0) - 1)
    def _():
        half = acc.shape[0] // 2
        own_ref[...] = acc[0:half]
        other_ref[...] = acc[half:].astype(BF16)


def out_back_kernel(me_ref, g_ref, ctx_ref, wo_ref, up_ref, dctx_ref, dwo_ref):
    core = me_ref[CORE]
    grads = g_ref[...]
    span = grads.shape[0] // 4
    weights = jnp.concatenate(
        [wide(wo_ref, up_at, me_ref, y, x, 0, HD) for y in range(4) for x in range(2)], axis=0
    )
    made = dims(grads, weights, 1, 1).astype(BF16)
    for y in range(4):
        for x in range(2):
            at = (y * 2 + x) * HD
            piece = made[:, at : at + HD]
            to = y * 2 + x
            for half in range(2):
                base = half * 2 * span
                dctx_ref[core ^ half, to] = jnp.concatenate(
                    [piece[base : base + span], piece[base + span : base + 2 * span]], axis=1
                )
    grad = dims(ctx_ref[...], grads, 0, 0)
    for y in range(4):
        for x in range(2):
            at = (y * 2 + x) * HD
            spread(dwo_ref, up_at, me_ref, y, x, 0, grad[at : at + HD])


def qkv_back_kernel(
    me_ref, recv_ref, x_ref, vec_ref, w0, w1, w2, w3, w4,
    d0, d1, d2, d3, d4, own_ref, other_ref, acc,
):
    core = me_ref[CORE]
    parts, grads = (w0, w1, w2, w3, w4), (d0, d1, d2, d3, d4)
    rows = [x_ref[:, features_of(me_ref, step)] for step in range(4)]
    span = x_ref.shape[0] // 4
    half = x_ref.shape[0] // 2

    def put(step, y, x, start, value):
        stop = start + value.shape[0]
        for s in range(2):
            if step == 2:
                ref, at = grads[3 + s], 0
            else:
                ref, at = grads[{0: 0, 1: 1, 3: 2}[step]], s
            ref[at, y, x, start:stop] = value[:, s * 128 : (s + 1) * 128].astype(BF16)

    sums = []
    totals = [None] * 4
    for y in range(4):
        for x in range(2):
            at = y * 2 + x
            top, low = recv_ref[core, at], recv_ref[1 - core, at]
            made = jnp.concatenate(
                [
                    unpack_rows(
                        top[i * span : (i + 1) * span], low[i * span : (i + 1) * span]
                    )
                    for i in range(3)
                ],
                axis=1,
            )
            sums.append(jnp.sum(made.astype(F32), axis=0, keepdims=True))
            for step in range(4):
                put(step, y, x, 0, dims(made, rows[step], 0, 0))
                part = dims(made, ring_rows(parts, step, y, x, 3 * HD), 1, 0)
                totals[step] = part if totals[step] is None else totals[step] + part
    for step in range(4):
        acc[:, features_of(me_ref, step)] = totals[step]
    own_ref[...] = acc[0:half]
    other_ref[...] = acc[half:].astype(BF16)
    zeros = jnp.zeros((14, 2 * HD), F32)
    twos = []
    for z in range(4):
        a, b = sums[2 * z], sums[2 * z + 1]
        bias_q = jnp.concatenate([a[:, 0:HD], b[:, 0:HD]], axis=1)
        bias_v = jnp.concatenate([a[:, 2 * HD :], b[:, 2 * HD :]], axis=1)
        twos.append(jnp.concatenate([bias_q, bias_v, zeros], axis=0))
    for step in range(4):
        z_abs = lax.rem(me_ref[Z] + step, 4)
        two = twos[3]
        for z in range(3):
            two = jnp.where(z_abs == z, twos[z], two)
        block = jnp.concatenate(
            [vec_ref[z_abs, s] + jnp.where(core == s, two, 0.0) for s in range(2)], axis=1
        )
        for y in range(4):
            for x in range(2):
                put(step, y, x, 3 * HD, block)


def norm_forward(hidden, gain, shift):
    centre = jnp.mean(hidden, axis=-1, keepdims=True)
    centered = hidden - centre
    inverse = lax.rsqrt(jnp.mean(centered * centered, axis=-1, keepdims=True) + EPS)
    normed = centered * inverse
    return (normed * gain + shift, normed, inverse)


def norm_backward(grad_in, normed, inverse, gain):
    scaled = grad_in * gain
    inner_term = (
        scaled
        - jnp.mean(scaled, axis=-1, keepdims=True)
        - normed * jnp.mean(scaled * normed, axis=-1, keepdims=True)
    )
    return (
        inverse * inner_term,
        jnp.sum(grad_in * normed, axis=0),
        jnp.sum(grad_in, axis=0),
    )


def sds(shape, dtype=BF16):
    return jax.ShapeDtypeStruct(shape, dtype)


def took(us):
    return pl.CostEstimate(flops=int(us * 1.15e9), bytes_accessed=1 << 20, transcendentals=0)


def local(
    tokens, w_query, w_key, w_value, w_out, w_up, w_down,
    b_query, b_value, b_out, b_up, b_down,
    gain_attn, shift_attn, gain_mlp, shift_mlp, cotangent,
):
    core = lax.axis_index("core")
    me_z, me_s = lax.axis_index("z"), lax.axis_index("seq")
    me_y, me_x = lax.axis_index("y"), lax.axis_index("xhi")
    first_core = core == 0
    me = jnp.stack([core, me_z, me_s, me_y, me_x]).astype(jnp.int32)
    seqs, span, width = tokens.shape
    rows = seqs * span
    hidden = w_up.shape[1] // 2

    at = jnp.arange(width, dtype=jnp.int32)
    z_of, c_of, s_of, i_of = at // 256, (at // 128) % 2, (at // 64) % 2, at % 64
    stored = z_of * 256 + s_of * 128 + c_of * 64 + i_of
    order = (stored[:, None] == at[None, :]).astype(BF16)

    small = jnp.stack(
        [b_query, b_value, b_out, b_down, gain_attn, shift_attn, gain_mlp, shift_mlp]
    )
    small = jnp.concatenate([small, b_up.reshape(4, HD), jnp.zeros((4, HD), BF16)], axis=0)
    shard_rows = 4 * HD + 2 * hidden + 16
    with jax.named_scope("split"):
        keep, give = pl.pallas_call(
            split_kernel,
            out_shape=(sds((shard_rows, HD)),) * 2,
            in_specs=[smem()] + [vmem()] * 7,
            out_specs=(vmem(), vmem()),
            compiler_params=params(),
            cost_estimate=took(2),
        )(me, w_query, w_key, w_value, w_out.T, w_up, w_down.T, small)
    got = other_core(give)
    shard = jnp.where(
        first_core,
        jnp.concatenate([keep, got], axis=1),
        jnp.concatenate([got, keep], axis=1),
    )
    at_o, at_up, at_down, at_vec = 3 * HD, 4 * HD, 4 * HD + hidden, 4 * HD + 2 * hidden
    qkv_shard = jnp.concatenate([shard[0:at_o], shard[at_vec:]], axis=0)
    up_shard = jnp.concatenate([shard[at_up:at_down], shard[at_o:at_up]])
    sixteen = lambda part: jnp.broadcast_to(part[None], (16,) + part.shape)
    qkv_block = plane_gather(sixteen(qkv_shard))
    qkv_block, up_shard, down_shard = tie(qkv_block, up_shard, shard[at_down:at_vec])
    *near, head, tail = ring_finish(qkv_block, *ring_begin(qkv_block, "z"), "z")
    up_block = plane_gather(sixteen(up_shard))
    down_block = ring_gather(direct_gather(down_shard, "z"), "y")
    head, tail, up_block, down_block = tie(head, tail, up_block, down_block)
    qkv_parts = (*near, head, tail)
    up_begun, down_begun = ring_begin(up_block, "z"), ring_begin(down_block, "x")

    both_in = jnp.concatenate([tokens.reshape(rows, width), cotangent.reshape(rows, width)], axis=0)
    both_in = dims(both_in, order, 1, 0)
    mine = both_in[0:rows]
    grad_final = both_in[rows:]
    mine_low = mine.astype(BF16)
    x_rows = jnp.concatenate([mine_low, other_core(mine_low)], axis=0)

    fours = jnp.arange(4, dtype=jnp.int32)
    turn = ((fours[:, None] - me_z) % 4 == fours[None, :]).astype(F32)
    ring = [p[:, 0, 0, 3 * HD :, :].reshape(-1) for p in qkv_parts]
    vec = jnp.concatenate([ring[0], ring[1], ring[3], ring[4], ring[2]])
    vec = vec.reshape(4, 4096).astype(F32)
    vec = jnp.dot(turn, vec, precision=HIGHEST).reshape(4, 2, 16, 2 * HD)
    feature = lambda i: vec[:, :, i, :].reshape(width)
    chosen = jnp.where(first_core, vec[:, 0], vec[:, 1])
    chosen = chosen.reshape(4, 16, 2, HD).transpose(0, 2, 1, 3).reshape(8, 16 * HD)
    zeros = jnp.zeros((8, HD), F32)
    bias_qkv = jnp.concatenate([chosen[:, 0:HD], zeros, chosen[:, HD : 2 * HD]], axis=1)
    bias_qkv = bias_qkv[:, None, :]
    bias_up = chosen[:, 8 * HD : 12 * HD][:, None, :]
    gain_one, gain_two = feature(4), feature(6)

    with jax.named_scope("project"):
        packed = pl.pallas_call(
            qkv_kernel,
            out_shape=sds((2, 8, 3 * span, 2 * HD)),
            in_specs=[smem()] + [vmem()] * 7,
            out_specs=vmem(),
            compiler_params=params(),
            cost_estimate=took(5),
        )(me, x_rows, bias_qkv, *qkv_parts)

    def exchange(block):
        flat = block.reshape((16,) + block.shape[2:])
        return lax.all_to_all(flat, PLANE, 0, 0, tiled=False)

    qkv = exchange(packed)
    per = Q_BLOCKS
    chunk = per * span
    steps = 16 // per
    length = 16 * span
    with jax.named_scope("attend"):
        ctx_heads, lse = pl.pallas_call(
            functools.partial(attend_kernel, rows=span),
            grid=(steps,),
            out_shape=(sds((16, span, 2 * HD)), sds((2, 8, length), F32)),
            in_specs=[
                pl.BlockSpec((per, 3 * span, 2 * HD), lambda i: (i, 0, 0)),
                pl.BlockSpec((16, 3 * span, 2 * HD), lambda i: (0, 0, 0)),
            ],
            out_specs=(
                pl.BlockSpec((per, span, 2 * HD), lambda i: (i, 0, 0)),
                pl.BlockSpec((2, 8, chunk), lambda i: (0, 0, i)),
            ),
            compiler_params=params("arbitrary"),
            cost_estimate=took(11),
        )(qkv, qkv)
    ctx_heads, *begun = tie(ctx_heads, *up_begun, *down_begun)
    w_upo = ring_joined(up_block, *begun[0:2], "z")
    wdown = ring_joined(down_block, *begun[2:4], "x")
    recv = lax.all_to_all(ctx_heads, PLANE, 0, 0, tiled=False)
    recv = recv.reshape(2, 8, span, 2 * HD)
    out_spec = pl.BlockSpec((4, 2, 4, 2, HD, 2 * HD), lambda i: (0, 0, 0, 0, hidden // HD, 0))
    with jax.named_scope("out_project"):
        ctx, own, other = pl.pallas_call(
            out_kernel,
            out_shape=(sds((2 * rows, 8 * HD)), sds((rows, width), F32), sds((rows, width))),
            grid=(1,),
            in_specs=[smem(), vmem(), out_spec],
            out_specs=(vmem(), vmem(), vmem()),
            compiler_params=params("arbitrary"),
            cost_estimate=took(3),
        )(me, recv, w_upo)
    attended = own + other_core(other).astype(F32)
    resid_one = mine + attended + feature(2)
    normed_one, norm_first, inverse_first = norm_forward(resid_one, gain_one, feature(5))
    normed_low = normed_one.astype(BF16)
    n_rows = jnp.concatenate([normed_low, other_core(normed_low)], axis=0)

    up_spec = pl.BlockSpec(
        (4, 2, 1, 1, hidden, 2 * HD),
        lambda t, at: (0, 0, t // 2, t % 2, 0, 0),
    )
    down_spec = pl.BlockSpec(
        (2, 1, 1, 4, hidden, 2 * HD),
        lambda t, at: (0, (t % 2) ^ at[XHI], away(at, Y, t // 2), 0, 0, 0),
    )
    whole_spec = pl.BlockSpec((2 * rows, width), lambda t, at: (0, 0))
    cols_spec = pl.BlockSpec((2 * rows, hidden), lambda t, at: (0, t))
    half_spec = pl.BlockSpec((rows, width), lambda t, at: (0, 0))
    bias_spec = pl.BlockSpec((1, 1, hidden), lambda t, at: (t, 0, 0))
    with jax.named_scope("feed_forward"):
        active, slope, own, other = pl.pallas_call(
            ffn_kernel,
            grid_spec=pltpu.PrefetchScalarGridSpec(
                num_scalar_prefetch=1,
                grid=(8,),
                in_specs=[whole_spec, up_spec, down_spec, bias_spec],
                out_specs=(cols_spec, cols_spec, half_spec, half_spec),
                scratch_shapes=[pltpu.VMEM((2 * rows, width), F32)],
            ),
            out_shape=(
                sds((2 * rows, 8 * hidden)),
                sds((2 * rows, 8 * hidden)),
                sds((rows, width), F32),
                sds((rows, width)),
            ),
            compiler_params=params("arbitrary"),
            cost_estimate=took(14),
        )(me, n_rows, w_upo, wdown, bias_up)
    mixed = own + other_core(other).astype(F32)
    resid_two = normed_one + mixed + feature(3)
    final, norm_second, inverse_second = norm_forward(resid_two, gain_two, feature(7))
    output = dims(final.astype(BF16), order, 1, 1).astype(BF16)
    grad_two, part_gain_mlp, part_shift_mlp = norm_backward(
        grad_final, norm_second, inverse_second, gain_two
    )
    grad_low = grad_two.astype(BF16)
    g_rows = jnp.concatenate([grad_low, other_core(grad_low)], axis=0)
    with jax.named_scope("feed_forward_back"):
        grad_up, grad_down, part_up, own, other = pl.pallas_call(
            ffn_back_kernel,
            grid_spec=pltpu.PrefetchScalarGridSpec(
                num_scalar_prefetch=1,
                grid=(8,),
                in_specs=[whole_spec, whole_spec, up_spec, down_spec, cols_spec, cols_spec],
                out_specs=(up_spec, down_spec, bias_spec, half_spec, half_spec),
                scratch_shapes=[pltpu.VMEM((2 * rows, width), F32)],
            ),
            out_shape=(
                sds(w_upo.shape),
                sds(wdown.shape),
                sds((8, 1, hidden), F32),
                sds((rows, width), F32),
                sds((rows, width)),
            ),
            compiler_params=params("arbitrary"),
            cost_estimate=took(20),
        )(me, n_rows, g_rows, w_upo, wdown, active, slope)
    grad_mid = grad_two + (own + other_core(other).astype(F32))
    grad_one, part_gain_attn, part_shift_attn = norm_backward(
        grad_mid, norm_first, inverse_first, gain_one
    )
    grad_low = grad_one.astype(BF16)
    g_rows = jnp.concatenate([grad_low, other_core(grad_low)], axis=0)
    with jax.named_scope("out_project_back"):
        dctx, grad_upo = pl.pallas_call(
            out_back_kernel,
            grid=(1,),
            out_shape=(sds((2, 8, span, 2 * HD)), sds(grad_up.shape)),
            in_specs=[smem(), vmem(), vmem(), out_spec, pl.BlockSpec(memory_space=pl.ANY)],
            out_specs=(vmem(), out_spec),
            input_output_aliases={4: 1},
            compiler_params=params("arbitrary"),
            cost_estimate=took(4),
        )(me, g_rows, ctx, w_upo, grad_up)
    dctx, grad_down, grad_upo = tie(exchange(dctx), grad_down, grad_upo)
    down_begun = reduce_start(reduce_parts(grad_down, "x"), "x")
    up_begun = reduce_start(reduce_parts(grad_upo, "z"), "z")
    down_sum = reduce_end(reduce_middle(down_begun, "x"), "x")
    up_sum = reduce_end(reduce_middle(up_begun, "z"), "z")
    with jax.named_scope("attend_back"):
        dq, dkv = pl.pallas_call(
            functools.partial(attend_back_kernel, rows=span),
            grid=(steps,),
            out_shape=(sds((16, span, 2 * HD)), sds((16, 2 * span, 2 * HD))),
            in_specs=[
                pl.BlockSpec((per, 3 * span, 2 * HD), lambda i: (i, 0, 0)),
                pl.BlockSpec((16, 3 * span, 2 * HD), lambda i: (0, 0, 0)),
                pl.BlockSpec((per, span, 2 * HD), lambda i: (i, 0, 0)),
                pl.BlockSpec((per, span, 2 * HD), lambda i: (i, 0, 0)),
                pl.BlockSpec((2, 8, chunk), lambda i: (0, 0, i)),
            ],
            out_specs=(
                pl.BlockSpec((per, span, 2 * HD), lambda i: (i, 0, 0)),
                pl.BlockSpec((16, 2 * span, 2 * HD), lambda i: (0, 0, 0)),
            ),
            scratch_shapes=[pltpu.VMEM((length, 2 * HD), F32)] * 2,
            compiler_params=params("arbitrary"),
            cost_estimate=took(18),
        )(qkv, qkv, ctx_heads, dctx, lse)
    dqkv = exchange(jnp.concatenate([dq, dkv], axis=1)[None])
    dqkv, up_sum, down_sum = tie(dqkv, up_sum, down_sum)
    dqkv = dqkv.reshape(2, 8, 3 * span, 2 * HD)
    down_begun = reduce_start(reduce_parts(down_sum, "y"), "y")
    ups = part_up.reshape(4, 2, 4, HD).transpose(0, 2, 1, 3).reshape(4, 1, 4, 2 * HD)
    nothing = jnp.zeros_like(ups)
    ups = jnp.concatenate(
        [jnp.where(first_core, ups, nothing), jnp.where(first_core, nothing, ups)], axis=1
    )
    six = jnp.stack(
        [
            jnp.sum(grad_one, axis=0), jnp.sum(grad_two, axis=0),
            part_gain_attn, part_shift_attn, part_gain_mlp, part_shift_mlp,
        ]
    ).reshape(6, 4, 2, 2 * HD).transpose(1, 2, 0, 3)
    vec_rows = jnp.concatenate(
        [jnp.zeros((4, 2, 2, 2 * HD), F32), six, ups, jnp.zeros((4, 2, 4, 2 * HD), F32)], axis=2
    )
    with jax.named_scope("project_back"):
        part, far = sds((2, 4, 2, 3 * HD + 16, 2 * HD)), sds((1, 4, 2, 3 * HD + 16, 2 * HD))
        *grad_qkv, own, other = pl.pallas_call(
            qkv_back_kernel,
            out_shape=(
                part, part, part, far, far, sds((rows, width), F32), sds((rows, width)),
            ),
            in_specs=[smem()] + [vmem()] * 8,
            out_specs=(vmem(),) * 7,
            scratch_shapes=[pltpu.VMEM((2 * rows, width), F32)],
            compiler_params=params(),
            cost_estimate=took(8),
        )(me, dqkv, x_rows, vec_rows, *qkv_parts)
    qkv_middle = reduce_middle(reduce_start(grad_qkv, "z"), "z")
    qkv_sum = reduce_end(qkv_middle, "z")
    down_sum = reduce_end(reduce_middle(down_begun, "y"), "y")
    got_up = plane_reduce(up_sum).astype(BF16)
    got_down = direct_reduce(down_sum, "z")
    input_sum = own + other_core(other).astype(F32)
    grad_tokens = lax.dot_general(
        grad_one + input_sum, order.astype(F32), (((1,), (1,)), ((), ())), precision=HIGHEST
    )

    qkv_sum, grad_tokens = tie(qkv_sum, grad_tokens)
    got_qkv = plane_reduce(qkv_sum)
    final_rows = jnp.concatenate([got_qkv.astype(BF16), got_up, got_down], axis=0)
    swapped = other_core(final_rows)
    with jax.named_scope("join"):
        square = sds((HD, 2 * HD), F32)
        *weights, g_out, g_up, g_down, vecs = pl.pallas_call(
            join_kernel,
            out_shape=(
                square, square, square, square,
                sds((HD, 2 * hidden), F32),
                sds((HD, 2 * hidden), F32),
                sds((16, HD), F32),
            ),
            in_specs=[smem(), vmem(), vmem()],
            out_specs=(vmem(),) * 7,
            compiler_params=params(),
            cost_estimate=took(2),
        )(me, final_rows, swapped)
    return (
        output.reshape(seqs, span, width),
        grad_tokens.reshape(seqs, span, width),
        *weights,
        g_out.T,
        g_up,
        g_down.T,
        vecs[0],
        vecs[1],
        vecs[2],
        vecs[8:12].reshape(4 * HD),
        vecs[3],
        vecs[4],
        vecs[5],
        vecs[6],
        vecs[7],
    )


def solution(mesh):
    fine = Mesh(mesh.devices.reshape(4, 2, 2, 4, 2), ("z", "core", "seq", "y", "xhi"))
    owners, tensor = ("z", "core", "seq"), ("y", "xhi")
    tokens = P(("z", "core"), ("seq", "y", "xhi"), None)
    columns, by_rows, vector = P(owners, tensor), P(tensor, owners), P(owners)
    weights = (columns, columns, columns, by_rows, columns, by_rows)
    return jax.shard_map(
        local,
        mesh=fine,
        in_specs=(tokens,) + weights + (vector,) * 9 + (tokens,),
        out_specs=(tokens, tokens) + weights + (vector,) * 9,
        check_vma=False,
    )
```

```python
import functools

import jax
import jax.numpy as jnp
from jax import lax
from jax.experimental import pallas as pl
from jax.experimental.pallas import tpu as pltpu
from jax.sharding import Mesh, PartitionSpec as P

HD = 64
EPS = 1e-05
F32 = jnp.float32
BF16 = jnp.bfloat16
HIGHEST = lax.Precision.HIGHEST
VMEM_LIMIT = 56 * 1024 * 1024
Q_BLOCKS = 4
PLANE = ("seq", "y", "xhi")


def dims(a, b, ca, cb):
    return lax.dot_general(a, b, (((ca,), (cb,)), ((), ())), preferred_element_type=F32)


def shift4(by):
    return [(i, (i + by) % 4) for i in range(4)]


def flip(seq_too, xhi_too):
    return [
        (seq * 2 + xhi, (seq ^ seq_too) * 2 + (xhi ^ xhi_too))
        for seq in range(2)
        for xhi in range(2)
    ]


def links(axis):
    if axis == "x":
        return ("seq", "xhi"), flip(1, 0), flip(1, 1)
    return axis, shift4(-1), shift4(1)


def halves(block):
    half = block.shape[0] // 2
    return block[0:half], block[half:]


def ring_begin(block, axis):
    names, one, two = links(axis)
    return lax.ppermute(block, names, one), lax.ppermute(block, names, two)


def ring_finish(block, first, second, axis):
    names, one, two = links(axis)
    if axis == "x":
        head, tail = halves(second)[0], halves(first)[1]
    else:
        head, tail = halves(first)[0], halves(second)[1]
    head = lax.ppermute(head, names, one)
    tail = lax.ppermute(tail, names, two)
    return block, first, second, head, tail


def ring_joined(block, first, second, axis):
    block, first, second, head, tail = ring_finish(block, first, second, axis)
    if axis == "x":
        whole = jnp.concatenate([block, head, tail, first, second], axis=0)
        return whole.reshape((2, 2) + block.shape)
    whole = jnp.concatenate([block, first, head, tail, second], axis=0)
    return whole.reshape((4,) + block.shape)


def ring_gather(block, axis):
    return ring_joined(block, *ring_begin(block, axis), axis)


def direct_gather(block, axis):
    parts = [block] + [lax.ppermute(block, axis, shift4(-i)) for i in (1, 2, 3)]
    return jnp.stack(parts)


def add(*terms):
    total = terms[0].astype(F32)
    for term in terms[1:]:
        total = total + term.astype(F32)
    return total.astype(BF16)


def ring_messages(block):
    first_head, first_tail = halves(block[1])
    far_head, far_tail = halves(block[2])
    second_head, second_tail = halves(block[3])
    return (
        block[0],
        jnp.concatenate([far_head, first_tail], axis=0),
        jnp.concatenate([second_head, far_tail], axis=0),
        first_head,
        second_tail,
    )


def cross_messages(block):
    first_head, first_tail = halves(block[1, 0])
    far_head, far_tail = halves(block[0, 1])
    second_head, second_tail = halves(block[1, 1])
    return (
        block[0, 0],
        jnp.concatenate([far_head, first_head], axis=0),
        jnp.concatenate([far_tail, second_tail], axis=0),
        first_tail,
        second_head,
    )


def reduce_ways(axis):
    names, one, two = links(axis)
    return (names, one, two) if axis == "x" else (names, two, one)


def reduce_start(messages, axis):
    names, to_first, to_second = reduce_ways(axis)
    own, a, b, first, second = messages
    return own, lax.ppermute(a, names, to_first), lax.ppermute(b, names, to_second), first, second


def reduce_middle(begun, axis):
    own, a, b, first, second = begun
    (a_head, a_tail), (b_head, b_tail) = halves(a), halves(b)
    if axis == "x":
        return own, a_tail, b_tail, add(first, b_head), add(second, a_head)
    return own, b_head, a_tail, add(first, a_head), add(second, b_tail)


def reduce_end(middle, axis):
    names, to_first, to_second = reduce_ways(axis)
    own, near_head, near_tail, first, second = middle
    first = lax.ppermute(first, names, to_first)
    second = lax.ppermute(second, names, to_second)
    if axis == "x":
        first, second = second, first
    head, tail = halves(own)
    return jnp.concatenate([add(head, near_head, first), add(tail, near_tail, second)], axis=0)


def tie(*values):
    return lax.optimization_barrier(values)


def direct_reduce(block, axis):
    parts = [block[0]] + [lax.ppermute(block[i], axis, shift4(i)) for i in (1, 2, 3)]
    return add(*parts)


def plane_gather(copies):
    got = lax.all_to_all(copies, PLANE, 0, 0, tiled=False)
    return got.reshape((2, 4, 2) + copies.shape[1:])


def plane_reduce(block):
    flat = block.reshape((16,) + block.shape[-2:])
    got = lax.all_to_all(flat, PLANE, 0, 0, tiled=False)
    return jnp.sum(got.astype(F32), axis=0)


def other_core(block):
    return lax.ppermute(block, "core", [(0, 1), (1, 0)])


def params(*semantics):
    return pltpu.CompilerParams(
        vmem_limit_bytes=VMEM_LIMIT,
        dimension_semantics=semantics if semantics else None,
    )


def vmem():
    return pl.BlockSpec(memory_space=pltpu.VMEM)


def smem():
    return pl.BlockSpec(memory_space=pltpu.SMEM)


CORE, Z, SEQ, Y, XHI = range(5)


def away(me, axis, at):
    return lax.rem(at + 4 - me[axis], 4)


def ring_rows(parts, step, y, x, size):
    if step == 2:
        a, b = parts[3][0, y, x, 0:size], parts[4][0, y, x, 0:size]
    else:
        ref = parts[{0: 0, 1: 1, 3: 2}[step]]
        a, b = ref[0, y, x, 0:size], ref[1, y, x, 0:size]
    return jnp.concatenate([a, b], axis=1)


def features_of(me, step):
    return pl.ds(pl.multiple_of(lax.rem(me[Z] + step, 4) * 256, 256), 256)


def put(messages, step, y, x, rows, value):
    for s in range(2):
        name, at = {
            (0, 0): (0, 0), (0, 1): (0, 1), (1, 0): (3, 0), (1, 1): (1, 1),
            (2, 0): (1, 0), (2, 1): (2, 1), (3, 0): (2, 0), (3, 1): (4, 0),
        }[step, s]
        messages[name][at, y, x, rows] = value[:, s * 128 : (s + 1) * 128].astype(BF16)


def split_kernel(me_ref, wq, wk, wv, wo, wup, wdown, small, keep_ref, give_ref):
    first = me_ref[CORE] == 0
    at = 0
    for ref in (wq, wk, wv, wo, wup, wdown):
        value = jnp.transpose(ref[...].astype(F32))
        half = value.shape[0] // 2
        a, b = value[0:half], value[half:]
        keep_ref[at : at + half] = jnp.where(first, a, b).astype(BF16)
        give_ref[at : at + half] = jnp.where(first, b, a).astype(BF16)
        at += half
    keep_ref[at:] = small[...]
    give_ref[at:] = small[...]


def join_kernel(me_ref, mine_ref, other_ref, dq, dk, dv, do, dup, ddown, vec_ref):
    first = me_ref[CORE] == 0
    hidden = ddown.shape[1] // 2

    def rows(start, size):
        a = mine_ref[start : start + size].astype(F32)
        b = other_ref[start : start + size].astype(F32)
        zero, one = jnp.where(first, a, b), jnp.where(first, b, a)
        zero = jnp.where(first, zero[:, 0:HD], zero[:, HD:])
        one = jnp.where(first, one[:, 0:HD], one[:, HD:])
        return zero, one

    at = 0
    plan = ((dq, HD), (dk, HD), (dv, HD), (vec_ref, 16), (dup, hidden), (do, HD), (ddown, hidden))
    for ref, size in plan:
        zero, one = rows(at, size)
        at += size
        if size == 16:
            ref[...] = zero + one
        else:
            ref[...] = jnp.transpose(jnp.concatenate([zero, one], axis=0))


def qkv_kernel(me_ref, x_ref, bias_ref, w0, w1, w2, w3, w4, out_ref):
    parts = (w0, w1, w2, w3, w4)
    core = me_ref[CORE]
    rows = [x_ref[:, features_of(me_ref, step)] for step in range(4)]
    span = x_ref.shape[0] // 4
    for y in range(4):
        for x in range(2):
            made = bias_ref[y * 2 + x]
            for step in range(4):
                made = made + dims(rows[step], ring_rows(parts, step, y, x, 3 * HD), 1, 1)
            made = made.astype(BF16)
            to = y * 2 + x
            for half in range(2):
                top = made[half * 2 * span : half * 2 * span + span]
                low = made[half * 2 * span + span : (half + 1) * 2 * span]
                packed = jnp.concatenate(
                    [
                        jnp.concatenate(
                            [top[:, i * HD : (i + 1) * HD], low[:, i * HD : (i + 1) * HD]],
                            axis=1,
                        )
                        for i in range(3)
                    ],
                    axis=0,
                )
                out_ref[core ^ half, to] = packed


def attend_kernel(q_ref, kv_ref, ctx_ref, lse_ref, *, rows):
    chunk = q_ref.shape[0] * rows
    length = kv_ref.shape[0] * rows
    queries = q_ref[:, 0:rows].reshape(chunk, 2 * HD) * jnp.bfloat16(0.125)
    keys = kv_ref[:, rows : 2 * rows].reshape(length, 2 * HD)
    values = kv_ref[:, 2 * rows : 3 * rows].reshape(length, 2 * HD)
    lane = lax.broadcasted_iota(jnp.int32, (chunk, 2 * HD), 1)
    parts = []
    for s in range(2):
        mine = (lane < HD) if s == 0 else (lane >= HD)
        picked = jnp.where(mine, queries, jnp.bfloat16(0))
        scores = dims(picked, keys, 1, 1)
        top = jnp.max(scores, axis=1, keepdims=True)
        weights = jnp.exp(scores - top)
        total = jnp.sum(weights, axis=1, keepdims=True)
        mixed = dims(weights.astype(BF16), values, 1, 0)
        parts.append(mixed / total)
        lse = jnp.broadcast_to(top + jnp.log(total), (chunk, 128))
        lse_ref[s] = jnp.transpose(lse)[0:8]
    ctx = jnp.where(lane < HD, parts[0], parts[1])
    ctx_ref[...] = ctx.astype(BF16).reshape(ctx_ref.shape)


def attend_back_kernel(
    q_ref, kv_ref, ctx_ref, dctx_ref, lse_ref, dq_ref, dkv_ref, dk_acc, dv_acc, *, rows
):
    step = pl.program_id(0)
    chunk = q_ref.shape[0] * rows
    length = kv_ref.shape[0] * rows
    queries = q_ref[:, 0:rows].reshape(chunk, 2 * HD) * jnp.bfloat16(0.125)
    grads = dctx_ref[...].reshape(chunk, 2 * HD)
    context = ctx_ref[...].reshape(chunk, 2 * HD)
    keys = kv_ref[:, rows : 2 * rows].reshape(length, 2 * HD)
    values = kv_ref[:, 2 * rows : 3 * rows].reshape(length, 2 * HD)
    lane = lax.broadcasted_iota(jnp.int32, (chunk, 2 * HD), 1)
    long_lane = lax.broadcasted_iota(jnp.int32, (length, 2 * HD), 1)
    both = grads.astype(F32) * context.astype(F32)

    @pl.when(step == 0)
    def _():
        dk_acc[...] = jnp.zeros_like(dk_acc)
        dv_acc[...] = jnp.zeros_like(dv_acc)

    dq_parts, dk_parts, dv_parts = [], [], []
    for s in range(2):
        mine = (lane < HD) if s == 0 else (lane >= HD)
        q_mine = jnp.where(mine, queries, jnp.bfloat16(0))
        g_mine = jnp.where(mine, grads, jnp.bfloat16(0))
        delta = jnp.sum(jnp.where(mine, both, 0.0), axis=1, keepdims=True)
        delta = jnp.transpose(jnp.broadcast_to(delta, (chunk, 128)))[0:1]
        scores = dims(keys, q_mine, 1, 1)
        exact = jnp.exp(scores - lse_ref[s, 0:1])
        grad_probs = dims(values, g_mine, 1, 1)
        grad_scores = (exact * (grad_probs - delta)).astype(BF16)
        dq_parts.append(dims(grad_scores, keys, 0, 0))
        dk_parts.append(dims(grad_scores, queries, 1, 0))
        dv_parts.append(dims(exact.astype(BF16), grads, 1, 0))
    dq = jnp.where(lane < HD, dq_parts[0], dq_parts[1]) * 0.125
    dq_ref[...] = dq.astype(BF16).reshape(dq_ref.shape)
    dk_acc[...] += jnp.where(long_lane < HD, dk_parts[0], dk_parts[1])
    dv_acc[...] += jnp.where(long_lane < HD, dv_parts[0], dv_parts[1])

    @pl.when(step == pl.num_programs(0) - 1)
    def _():
        shape = (kv_ref.shape[0], rows, 2 * HD)
        dkv_ref[:, 0:rows] = dk_acc[...].astype(BF16).reshape(shape)
        dkv_ref[:, rows : 2 * rows] = dv_acc[...].astype(BF16).reshape(shape)


def unpack_rows(top, low):
    return jnp.concatenate([top[:, 0:HD], top[:, HD:], low[:, 0:HD], low[:, HD:]], axis=0)


def out_rows(parts, step):
    return jnp.concatenate(
        [ring_rows(parts, step, y, x, HD) for y in range(4) for x in range(2)], axis=0
    )


def out_kernel(me_ref, recv_ref, w0, w1, w2, w3, w4, ctx_ref, own_ref, other_ref, acc):
    core = me_ref[CORE]
    parts = (w0, w1, w2, w3, w4)
    pieces = [unpack_rows(recv_ref[core, at], recv_ref[1 - core, at]) for at in range(8)]
    ctx = jnp.concatenate(pieces, axis=1)
    ctx_ref[...] = ctx
    for step in range(4):
        acc[:, features_of(me_ref, step)] = dims(ctx, out_rows(parts, step), 1, 0)
    half = ctx.shape[0] // 2
    own_ref[...] = acc[0:half]
    other_ref[...] = acc[half:].astype(BF16)


def wide_down(ref, me):
    return jnp.concatenate(
        [ref[s ^ me[SEQ], 0, 0, away(me, Z, z)] for z in range(4) for s in range(2)], axis=1
    )


def ffn_kernel(
    me_ref, n_ref, w0, w1, w2, w3, w4, wdown_ref, bias_ref,
    active_ref, slope_ref, own_ref, other_ref, acc,
):
    step = pl.program_id(0)
    parts = (w0, w1, w2, w3, w4)
    hidden = bias_ref.shape[2]
    pre = bias_ref[0]
    for turn in range(4):
        rows = n_ref[:, features_of(me_ref, turn)]
        pre = pre + dims(rows, ring_rows(parts, turn, 0, 0, hidden), 1, 1)
    cdf = 0.5 * (1.0 + lax.erf(pre * 0.7071067811865476))
    pdf = jnp.exp(-0.5 * pre * pre) * 0.3989422804014327
    active = (pre * cdf).astype(BF16)
    active_ref[...] = active
    slope_ref[...] = (cdf + pre * pdf).astype(BF16)
    made = dims(active, wide_down(wdown_ref, me_ref), 1, 0)

    @pl.when(step == 0)
    def _():
        acc[...] = made

    @pl.when(step > 0)
    def _():
        acc[...] += made

    @pl.when(step == pl.num_programs(0) - 1)
    def _():
        half = acc.shape[0] // 2
        own_ref[...] = acc[0:half]
        other_ref[...] = acc[half:].astype(BF16)


def ffn_back_kernel(
    me_ref, n_ref, g_ref, w0, w1, w2, w3, w4, wdown_ref, active_ref, slope_ref,
    d0, d1, d2, d3, d4, ddown_ref, bias_ref, own_ref, other_ref, acc,
):
    step = pl.program_id(0)
    parts, messages = (w0, w1, w2, w3, w4), (d0, d1, d2, d3, d4)
    grads = g_ref[...]
    active = active_ref[...]
    hidden = active.shape[1]
    grad = dims(active, grads, 0, 0).astype(BF16)
    for z in range(4):
        for s in range(2):
            at = (z * 2 + s) * 128
            ddown_ref[s ^ me_ref[SEQ], 0, 0, away(me_ref, Z, z)] = grad[:, at : at + 128]
    grad_pre = dims(grads, wide_down(wdown_ref, me_ref), 1, 1) * slope_ref[...].astype(F32)
    bias_ref[0] = jnp.sum(grad_pre, axis=0, keepdims=True)
    low = grad_pre.astype(BF16)

    @pl.when(step == 0)
    def _():
        acc[...] = jnp.zeros_like(acc)

    for turn in range(4):
        at = features_of(me_ref, turn)
        put(messages, turn, 0, 0, slice(0, hidden), dims(low, n_ref[:, at], 0, 0))
        acc[:, at] += dims(low, ring_rows(parts, turn, 0, 0, hidden), 1, 0)

    @pl.when(step == pl.num_programs(0) - 1)
    def _():
        half = acc.shape[0] // 2
        own_ref[...] = acc[0:half]
        other_ref[...] = acc[half:].astype(BF16)


def out_back_kernel(
    me_ref, g_ref, ctx_ref, w0, w1, w2, w3, w4, u0, u1, u2, u3, u4,
    dctx_ref, d0, d1, d2, d3, d4,
):
    core = me_ref[CORE]
    parts, messages = (w0, w1, w2, w3, w4), (d0, d1, d2, d3, d4)
    span = g_ref.shape[0] // 4
    ctx = ctx_ref[...]
    made = None
    for step in range(4):
        grads = g_ref[:, features_of(me_ref, step)]
        part = dims(grads, out_rows(parts, step), 1, 1)
        made = part if made is None else made + part
        grad = dims(ctx, grads, 0, 0)
        for y in range(4):
            for x in range(2):
                at = (y * 2 + x) * HD
                put(messages, step, y, x, slice(0, HD), grad[at : at + HD])
    made = made.astype(BF16)
    for to in range(8):
        piece = made[:, to * HD : (to + 1) * HD]
        for half in range(2):
            base = half * 2 * span
            dctx_ref[core ^ half, to] = jnp.concatenate(
                [piece[base : base + span], piece[base + span : base + 2 * span]], axis=1
            )


def qkv_back_kernel(
    me_ref, recv_ref, x_ref, vec_ref, w0, w1, w2, w3, w4,
    d0, d1, d2, d3, d4, own_ref, other_ref, acc,
):
    core = me_ref[CORE]
    parts, grads = (w0, w1, w2, w3, w4), (d0, d1, d2, d3, d4)
    rows = [x_ref[:, features_of(me_ref, step)] for step in range(4)]
    span = x_ref.shape[0] // 4
    half = x_ref.shape[0] // 2

    sums = []
    totals = [None] * 4
    for y in range(4):
        for x in range(2):
            at = y * 2 + x
            top, low = recv_ref[core, at], recv_ref[1 - core, at]
            made = jnp.concatenate(
                [
                    unpack_rows(
                        top[i * span : (i + 1) * span], low[i * span : (i + 1) * span]
                    )
                    for i in range(3)
                ],
                axis=1,
            )
            sums.append(jnp.sum(made.astype(F32), axis=0, keepdims=True))
            for step in range(4):
                put(grads, step, y, x, slice(0, 3 * HD), dims(made, rows[step], 0, 0))
                part = dims(made, ring_rows(parts, step, y, x, 3 * HD), 1, 0)
                totals[step] = part if totals[step] is None else totals[step] + part
    for step in range(4):
        acc[:, features_of(me_ref, step)] = totals[step]
    own_ref[...] = acc[0:half]
    other_ref[...] = acc[half:].astype(BF16)
    zeros = jnp.zeros((14, 2 * HD), F32)
    twos = []
    for z in range(4):
        a, b = sums[2 * z], sums[2 * z + 1]
        bias_q = jnp.concatenate([a[:, 0:HD], b[:, 0:HD]], axis=1)
        bias_v = jnp.concatenate([a[:, 2 * HD :], b[:, 2 * HD :]], axis=1)
        twos.append(jnp.concatenate([bias_q, bias_v, zeros], axis=0))
    for step in range(4):
        z_abs = lax.rem(me_ref[Z] + step, 4)
        two = twos[3]
        for z in range(3):
            two = jnp.where(z_abs == z, twos[z], two)
        block = jnp.concatenate(
            [vec_ref[z_abs, s] + jnp.where(core == s, two, 0.0) for s in range(2)], axis=1
        )
        for y in range(4):
            for x in range(2):
                put(grads, step, y, x, slice(3 * HD, 3 * HD + 16), block)


def norm_forward(hidden, gain, shift):
    centre = jnp.mean(hidden, axis=-1, keepdims=True)
    centered = hidden - centre
    inverse = lax.rsqrt(jnp.mean(centered * centered, axis=-1, keepdims=True) + EPS)
    normed = centered * inverse
    return (normed * gain + shift, normed, inverse)


def norm_backward(grad_in, normed, inverse, gain):
    scaled = grad_in * gain
    inner_term = (
        scaled
        - jnp.mean(scaled, axis=-1, keepdims=True)
        - normed * jnp.mean(scaled * normed, axis=-1, keepdims=True)
    )
    return (
        inverse * inner_term,
        jnp.sum(grad_in * normed, axis=0),
        jnp.sum(grad_in, axis=0),
    )


def sds(shape, dtype=BF16):
    return jax.ShapeDtypeStruct(shape, dtype)


def took(us):
    return pl.CostEstimate(flops=int(us * 1.15e9), bytes_accessed=1 << 20, transcendentals=0)


def local(
    tokens, w_query, w_key, w_value, w_out, w_up, w_down,
    b_query, b_value, b_out, b_up, b_down,
    gain_attn, shift_attn, gain_mlp, shift_mlp, cotangent,
):
    core = lax.axis_index("core")
    me_z, me_s = lax.axis_index("z"), lax.axis_index("seq")
    me_y, me_x = lax.axis_index("y"), lax.axis_index("xhi")
    first_core = core == 0
    me = jnp.stack([core, me_z, me_s, me_y, me_x]).astype(jnp.int32)
    seqs, span, width = tokens.shape
    rows = seqs * span
    hidden = w_up.shape[1] // 2

    at = jnp.arange(width, dtype=jnp.int32)
    z_of, c_of, s_of, i_of = at // 256, (at // 128) % 2, (at // 64) % 2, at % 64
    stored = z_of * 256 + s_of * 128 + c_of * 64 + i_of
    order = (stored[:, None] == at[None, :]).astype(BF16)

    small = jnp.stack(
        [b_query, b_value, b_out, b_down, gain_attn, shift_attn, gain_mlp, shift_mlp]
    )
    small = jnp.concatenate([small, b_up.reshape(4, HD), jnp.zeros((4, HD), BF16)], axis=0)
    shard_rows = 4 * HD + 2 * hidden + 16
    with jax.named_scope("split"):
        keep, give = pl.pallas_call(
            split_kernel,
            out_shape=(sds((shard_rows, HD)),) * 2,
            in_specs=[smem()] + [vmem()] * 7,
            out_specs=(vmem(), vmem()),
            compiler_params=params(),
            cost_estimate=took(2),
        )(me, w_query, w_key, w_value, w_out.T, w_up, w_down.T, small)
    got = other_core(give)
    shard = jnp.where(
        first_core,
        jnp.concatenate([keep, got], axis=1),
        jnp.concatenate([got, keep], axis=1),
    )
    at_o, at_up, at_down, at_vec = 3 * HD, 4 * HD, 4 * HD + hidden, 4 * HD + 2 * hidden
    qkv_shard = jnp.concatenate([shard[0:at_o], shard[at_vec:]], axis=0)
    up_shard = jnp.concatenate([shard[at_up:at_down], shard[at_o:at_up]])
    sixteen = lambda part: jnp.broadcast_to(part[None], (16,) + part.shape)
    qkv_block = plane_gather(sixteen(qkv_shard))
    qkv_block, up_shard = tie(qkv_block, up_shard)
    *near, head, tail = ring_finish(qkv_block, *ring_begin(qkv_block, "z"), "z")
    up_block = plane_gather(sixteen(up_shard))

    both_in = jnp.concatenate([tokens.reshape(rows, width), cotangent.reshape(rows, width)], axis=0)
    both_in = dims(both_in, order, 1, 0)
    mine = both_in[0:rows]
    grad_final = both_in[rows:]
    mine_low = mine.astype(BF16)
    x_rows = jnp.concatenate([mine_low, other_core(mine_low)], axis=0)

    x_rows, down_shard = tie(x_rows, shard[at_down:at_vec])
    down_block = ring_gather(direct_gather(down_shard, "z"), "y")
    head, tail, up_block, down_block = tie(head, tail, up_block, down_block)
    qkv_parts = (*near, head, tail)
    up_begun, down_begun = ring_begin(up_block, "z"), ring_begin(down_block, "x")

    fours = jnp.arange(4, dtype=jnp.int32)
    turn = ((fours[:, None] - me_z) % 4 == fours[None, :]).astype(F32)
    ring = [p[:, 0, 0, 3 * HD :, :].reshape(-1) for p in qkv_parts]
    vec = jnp.concatenate([ring[0], ring[1], ring[3], ring[4], ring[2]])
    vec = vec.reshape(4, 4096).astype(F32)
    vec = jnp.dot(turn, vec, precision=HIGHEST).reshape(4, 2, 16, 2 * HD)
    feature = lambda i: vec[:, :, i, :].reshape(width)
    chosen = jnp.where(first_core, vec[:, 0], vec[:, 1])
    chosen = chosen.reshape(4, 16, 2, HD).transpose(0, 2, 1, 3).reshape(8, 16 * HD)
    zeros = jnp.zeros((8, HD), F32)
    bias_qkv = jnp.concatenate([chosen[:, 0:HD], zeros, chosen[:, HD : 2 * HD]], axis=1)
    bias_qkv = bias_qkv[:, None, :]
    bias_up = chosen[:, 8 * HD : 12 * HD][:, None, :]
    gain_one, gain_two = feature(4), feature(6)

    with jax.named_scope("project"):
        packed = pl.pallas_call(
            qkv_kernel,
            out_shape=sds((2, 8, 3 * span, 2 * HD)),
            in_specs=[smem()] + [vmem()] * 7,
            out_specs=vmem(),
            compiler_params=params(),
            cost_estimate=took(5),
        )(me, x_rows, bias_qkv, *qkv_parts)

    def exchange(block):
        flat = block.reshape((16,) + block.shape[2:])
        return lax.all_to_all(flat, PLANE, 0, 0, tiled=False)

    qkv = exchange(packed)
    per = Q_BLOCKS
    chunk = per * span
    steps = 16 // per
    length = 16 * span
    with jax.named_scope("attend"):
        ctx_heads, lse = pl.pallas_call(
            functools.partial(attend_kernel, rows=span),
            grid=(steps,),
            out_shape=(sds((16, span, 2 * HD)), sds((2, 8, length), F32)),
            in_specs=[
                pl.BlockSpec((per, 3 * span, 2 * HD), lambda i: (i, 0, 0)),
                pl.BlockSpec((16, 3 * span, 2 * HD), lambda i: (0, 0, 0)),
            ],
            out_specs=(
                pl.BlockSpec((per, span, 2 * HD), lambda i: (i, 0, 0)),
                pl.BlockSpec((2, 8, chunk), lambda i: (0, 0, i)),
            ),
            compiler_params=params("arbitrary"),
            cost_estimate=took(11),
        )(qkv, qkv)
    ctx_heads, *begun = tie(ctx_heads, *up_begun, *down_begun)
    up_parts = ring_finish(up_block, *begun[0:2], "z")
    wdown = ring_joined(down_block, *begun[2:4], "x")
    recv = lax.all_to_all(ctx_heads, PLANE, 0, 0, tiled=False)
    recv = recv.reshape(2, 8, span, 2 * HD)
    out_block = hidden // HD
    out_specs = [
        pl.BlockSpec((p.shape[0], 4, 2, HD, 2 * HD), lambda i: (0, 0, 0, out_block, 0))
        for p in up_parts
    ]
    message_shapes = [sds(p.shape) for p in up_parts]
    with jax.named_scope("out_project"):
        ctx, own, other = pl.pallas_call(
            out_kernel,
            out_shape=(sds((2 * rows, 8 * HD)), sds((rows, width), F32), sds((rows, width))),
            grid=(1,),
            in_specs=[smem(), vmem()] + out_specs,
            out_specs=(vmem(), vmem(), vmem()),
            scratch_shapes=[pltpu.VMEM((2 * rows, width), F32)],
            compiler_params=params("arbitrary"),
            cost_estimate=took(3),
        )(me, recv, *up_parts)
    attended = own + other_core(other).astype(F32)
    resid_one = mine + attended + feature(2)
    normed_one, norm_first, inverse_first = norm_forward(resid_one, gain_one, feature(5))
    normed_low = normed_one.astype(BF16)
    n_rows = jnp.concatenate([normed_low, other_core(normed_low)], axis=0)

    up_specs = [
        pl.BlockSpec(
            (p.shape[0], 1, 1, hidden, 2 * HD), lambda t, at: (0, t // 2, t % 2, 0, 0)
        )
        for p in up_parts
    ]
    down_spec = pl.BlockSpec(
        (2, 1, 1, 4, hidden, 2 * HD),
        lambda t, at: (0, (t % 2) ^ at[XHI], away(at, Y, t // 2), 0, 0, 0),
    )
    whole_spec = pl.BlockSpec((2 * rows, width), lambda t, at: (0, 0))
    cols_spec = pl.BlockSpec((2 * rows, hidden), lambda t, at: (0, t))
    half_spec = pl.BlockSpec((rows, width), lambda t, at: (0, 0))
    bias_spec = pl.BlockSpec((1, 1, hidden), lambda t, at: (t, 0, 0))
    with jax.named_scope("feed_forward"):
        active, slope, own, other = pl.pallas_call(
            ffn_kernel,
            grid_spec=pltpu.PrefetchScalarGridSpec(
                num_scalar_prefetch=1,
                grid=(8,),
                in_specs=[whole_spec] + up_specs + [down_spec, bias_spec],
                out_specs=(cols_spec, cols_spec, half_spec, half_spec),
                scratch_shapes=[pltpu.VMEM((2 * rows, width), F32)],
            ),
            out_shape=(
                sds((2 * rows, 8 * hidden)),
                sds((2 * rows, 8 * hidden)),
                sds((rows, width), F32),
                sds((rows, width)),
            ),
            compiler_params=params("arbitrary"),
            cost_estimate=took(14),
        )(me, n_rows, *up_parts, wdown, bias_up)
    mixed = own + other_core(other).astype(F32)
    resid_two = normed_one + mixed + feature(3)
    final, norm_second, inverse_second = norm_forward(resid_two, gain_two, feature(7))
    output = dims(final.astype(BF16), order, 1, 1).astype(BF16)
    grad_two, part_gain_mlp, part_shift_mlp = norm_backward(
        grad_final, norm_second, inverse_second, gain_two
    )
    grad_low = grad_two.astype(BF16)
    g_rows = jnp.concatenate([grad_low, other_core(grad_low)], axis=0)
    with jax.named_scope("feed_forward_back"):
        *grad_up, grad_down, part_up, own, other = pl.pallas_call(
            ffn_back_kernel,
            grid_spec=pltpu.PrefetchScalarGridSpec(
                num_scalar_prefetch=1,
                grid=(8,),
                in_specs=[whole_spec] * 2 + up_specs + [down_spec, cols_spec, cols_spec],
                out_specs=(*up_specs, down_spec, bias_spec, half_spec, half_spec),
                scratch_shapes=[pltpu.VMEM((2 * rows, width), F32)],
            ),
            out_shape=(
                *message_shapes,
                sds(wdown.shape),
                sds((8, 1, hidden), F32),
                sds((rows, width), F32),
                sds((rows, width)),
            ),
            compiler_params=params("arbitrary"),
            cost_estimate=took(20),
        )(me, n_rows, g_rows, *up_parts, wdown, active, slope)
    grad_mid = grad_two + (own + other_core(other).astype(F32))
    grad_one, part_gain_attn, part_shift_attn = norm_backward(
        grad_mid, norm_first, inverse_first, gain_one
    )
    grad_low = grad_one.astype(BF16)
    g_rows = jnp.concatenate([grad_low, other_core(grad_low)], axis=0)
    with jax.named_scope("out_project_back"):
        dctx, *grad_up = pl.pallas_call(
            out_back_kernel,
            grid=(1,),
            out_shape=(sds((2, 8, span, 2 * HD)), *message_shapes),
            in_specs=[smem(), vmem(), vmem()]
            + out_specs
            + [pl.BlockSpec(memory_space=pl.ANY)] * 5,
            out_specs=(vmem(), *out_specs),
            input_output_aliases={8 + i: 1 + i for i in range(5)},
            compiler_params=params("arbitrary"),
            cost_estimate=took(4),
        )(me, g_rows, ctx, *up_parts, *grad_up)
    dctx, grad_down, *grad_up = tie(exchange(dctx), grad_down, *grad_up)
    down_begun = reduce_start(cross_messages(grad_down), "x")
    up_begun = reduce_start(grad_up, "z")
    with jax.named_scope("attend_back"):
        dq, dkv = pl.pallas_call(
            functools.partial(attend_back_kernel, rows=span),
            grid=(steps,),
            out_shape=(sds((16, span, 2 * HD)), sds((16, 2 * span, 2 * HD))),
            in_specs=[
                pl.BlockSpec((per, 3 * span, 2 * HD), lambda i: (i, 0, 0)),
                pl.BlockSpec((16, 3 * span, 2 * HD), lambda i: (0, 0, 0)),
                pl.BlockSpec((per, span, 2 * HD), lambda i: (i, 0, 0)),
                pl.BlockSpec((per, span, 2 * HD), lambda i: (i, 0, 0)),
                pl.BlockSpec((2, 8, chunk), lambda i: (0, 0, i)),
            ],
            out_specs=(
                pl.BlockSpec((per, span, 2 * HD), lambda i: (i, 0, 0)),
                pl.BlockSpec((16, 2 * span, 2 * HD), lambda i: (0, 0, 0)),
            ),
            scratch_shapes=[pltpu.VMEM((length, 2 * HD), F32)] * 2,
            compiler_params=params("arbitrary"),
            cost_estimate=took(18),
        )(qkv, qkv, ctx_heads, dctx, lse)
    dq, *begun = tie(dq, *down_begun, *up_begun)
    dqkv = exchange(jnp.concatenate([dq, dkv], axis=1)[None])
    down_sum = reduce_end(reduce_middle(begun[0:5], "x"), "x")
    up_sum = reduce_end(reduce_middle(begun[5:10], "z"), "z")
    dqkv, down_sum, up_sum = tie(dqkv, down_sum, up_sum)
    down_begun = reduce_start(ring_messages(down_sum), "y")
    dqkv = dqkv.reshape(2, 8, 3 * span, 2 * HD)
    ups = part_up.reshape(4, 2, 4, HD).transpose(0, 2, 1, 3).reshape(4, 1, 4, 2 * HD)
    nothing = jnp.zeros_like(ups)
    ups = jnp.concatenate(
        [jnp.where(first_core, ups, nothing), jnp.where(first_core, nothing, ups)], axis=1
    )
    six = jnp.stack(
        [
            jnp.sum(grad_one, axis=0), jnp.sum(grad_two, axis=0),
            part_gain_attn, part_shift_attn, part_gain_mlp, part_shift_mlp,
        ]
    ).reshape(6, 4, 2, 2 * HD).transpose(1, 2, 0, 3)
    vec_rows = jnp.concatenate(
        [jnp.zeros((4, 2, 2, 2 * HD), F32), six, ups, jnp.zeros((4, 2, 4, 2 * HD), F32)], axis=2
    )
    with jax.named_scope("project_back"):
        part, far = sds((2, 4, 2, 3 * HD + 16, 2 * HD)), sds((1, 4, 2, 3 * HD + 16, 2 * HD))
        *grad_qkv, own, other = pl.pallas_call(
            qkv_back_kernel,
            out_shape=(
                part, part, part, far, far, sds((rows, width), F32), sds((rows, width)),
            ),
            in_specs=[smem()] + [vmem()] * 8,
            out_specs=(vmem(),) * 7,
            scratch_shapes=[pltpu.VMEM((2 * rows, width), F32)],
            compiler_params=params(),
            cost_estimate=took(8),
        )(me, dqkv, x_rows, vec_rows, *qkv_parts)
    qkv_middle = reduce_middle(reduce_start(grad_qkv, "z"), "z")
    qkv_sum = reduce_end(qkv_middle, "z")
    down_sum = reduce_end(reduce_middle(down_begun, "y"), "y")
    got_up = plane_reduce(up_sum).astype(BF16)
    got_down = direct_reduce(down_sum, "z")
    input_sum = own + other_core(other).astype(F32)
    grad_tokens = lax.dot_general(
        grad_one + input_sum, order.astype(F32), (((1,), (1,)), ((), ())), precision=HIGHEST
    )

    qkv_sum, grad_tokens = tie(qkv_sum, grad_tokens)
    got_qkv = plane_reduce(qkv_sum)
    final_rows = jnp.concatenate([got_qkv.astype(BF16), got_up, got_down], axis=0)
    swapped = other_core(final_rows)
    with jax.named_scope("join"):
        square = sds((HD, 2 * HD), F32)
        *weights, g_out, g_up, g_down, vecs = pl.pallas_call(
            join_kernel,
            out_shape=(
                square, square, square, square,
                sds((HD, 2 * hidden), F32),
                sds((HD, 2 * hidden), F32),
                sds((16, HD), F32),
            ),
            in_specs=[smem(), vmem(), vmem()],
            out_specs=(vmem(),) * 7,
            compiler_params=params(),
            cost_estimate=took(2),
        )(me, final_rows, swapped)
    return (
        output.reshape(seqs, span, width),
        grad_tokens.reshape(seqs, span, width),
        *weights,
        g_out.T,
        g_up,
        g_down.T,
        vecs[0],
        vecs[1],
        vecs[2],
        vecs[8:12].reshape(4 * HD),
        vecs[3],
        vecs[4],
        vecs[5],
        vecs[6],
        vecs[7],
    )


def solution(mesh):
    fine = Mesh(mesh.devices.reshape(4, 2, 2, 4, 2), ("z", "core", "seq", "y", "xhi"))
    owners, tensor = ("z", "core", "seq"), ("y", "xhi")
    tokens = P(("z", "core"), ("seq", "y", "xhi"), None)
    columns, by_rows, vector = P(owners, tensor), P(tensor, owners), P(owners)
    weights = (columns, columns, columns, by_rows, columns, by_rows)
    return jax.shard_map(
        local,
        mesh=fine,
        in_specs=(tokens,) + weights + (vector,) * 9 + (tokens,),
        out_specs=(tokens, tokens) + weights + (vector,) * 9,
        check_vma=False,
    )
```

```python
import functools

import jax
import jax.numpy as jnp
from jax import lax
from jax.experimental import pallas as pl
from jax.experimental.pallas import tpu as pltpu
from jax.sharding import Mesh, PartitionSpec as P

HD = 64
EPS = 1e-05
F32 = jnp.float32
BF16 = jnp.bfloat16
HIGHEST = lax.Precision.HIGHEST
VMEM_LIMIT = 56 * 1024 * 1024
Q_BLOCKS = 4
PLANE = ("seq", "y", "xhi")


def dims(a, b, ca, cb):
    return lax.dot_general(a, b, (((ca,), (cb,)), ((), ())), preferred_element_type=F32)


def shift4(by):
    return [(i, (i + by) % 4) for i in range(4)]


def flip(seq_too, xhi_too):
    return [
        (seq * 2 + xhi, (seq ^ seq_too) * 2 + (xhi ^ xhi_too))
        for seq in range(2)
        for xhi in range(2)
    ]


def links(axis):
    if axis == "x":
        return ("seq", "xhi"), flip(1, 0), flip(1, 1)
    return axis, shift4(-1), shift4(1)


def halves(block):
    half = block.shape[0] // 2
    return block[0:half], block[half:]


def ring_begin(block, axis):
    names, one, two = links(axis)
    return lax.ppermute(block, names, one), lax.ppermute(block, names, two)


def ring_finish(block, first, second, axis):
    names, one, two = links(axis)
    if axis == "x":
        head, tail = halves(second)[0], halves(first)[1]
    else:
        head, tail = halves(first)[0], halves(second)[1]
    head = lax.ppermute(head, names, one)
    tail = lax.ppermute(tail, names, two)
    return block, first, second, head, tail


def ring_join(block, first, second, head, tail, axis):
    if axis == "x":
        whole = jnp.concatenate([block, head, tail, first, second], axis=0)
        return whole.reshape((2, 2) + block.shape)
    whole = jnp.concatenate([block, first, head, tail, second], axis=0)
    return whole.reshape((4,) + block.shape)


def ring_gather(block, axis):
    return ring_join(*ring_finish(block, *ring_begin(block, axis), axis), axis)


def direct_gather(block, axis):
    parts = [block] + [lax.ppermute(block, axis, shift4(-i)) for i in (1, 2, 3)]
    return jnp.stack(parts)


def add(*terms):
    total = terms[0].astype(F32)
    for term in terms[1:]:
        total = total + term.astype(F32)
    return total.astype(BF16)


def ring_messages(block):
    first_head, first_tail = halves(block[1])
    far_head, far_tail = halves(block[2])
    second_head, second_tail = halves(block[3])
    return (
        block[0],
        jnp.concatenate([far_head, first_tail], axis=0),
        jnp.concatenate([second_head, far_tail], axis=0),
        first_head,
        second_tail,
    )


def cross_messages(block):
    first_head, first_tail = halves(block[1, 0])
    far_head, far_tail = halves(block[0, 1])
    second_head, second_tail = halves(block[1, 1])
    return (
        block[0, 0],
        jnp.concatenate([far_head, first_head], axis=0),
        jnp.concatenate([far_tail, second_tail], axis=0),
        first_tail,
        second_head,
    )


def reduce_ways(axis):
    names, one, two = links(axis)
    return (names, one, two) if axis == "x" else (names, two, one)


def reduce_start(messages, axis):
    names, to_first, to_second = reduce_ways(axis)
    own, a, b, first, second = messages
    return own, lax.ppermute(a, names, to_first), lax.ppermute(b, names, to_second), first, second


def reduce_middle(begun, axis):
    own, a, b, first, second = begun
    (a_head, a_tail), (b_head, b_tail) = halves(a), halves(b)
    if axis == "x":
        return own, a_tail, b_tail, add(first, b_head), add(second, a_head)
    return own, b_head, a_tail, add(first, a_head), add(second, b_tail)


def reduce_end(middle, axis):
    names, to_first, to_second = reduce_ways(axis)
    own, near_head, near_tail, first, second = middle
    first = lax.ppermute(first, names, to_first)
    second = lax.ppermute(second, names, to_second)
    if axis == "x":
        first, second = second, first
    head, tail = halves(own)
    return jnp.concatenate([add(head, near_head, first), add(tail, near_tail, second)], axis=0)


def tie(*values):
    return lax.optimization_barrier(values)


def direct_reduce(block, axis):
    parts = [block[0]] + [lax.ppermute(block[i], axis, shift4(i)) for i in (1, 2, 3)]
    return add(*parts)


def plane_gather(copies):
    got = lax.all_to_all(copies, PLANE, 0, 0, tiled=False)
    return got.reshape((2, 4, 2) + copies.shape[1:])


def plane_reduce(block):
    flat = block.reshape((16,) + block.shape[-2:])
    got = lax.all_to_all(flat, PLANE, 0, 0, tiled=False)
    return jnp.sum(got.astype(F32), axis=0)


def other_core(block):
    return lax.ppermute(block, "core", [(0, 1), (1, 0)])


def params(*semantics):
    return pltpu.CompilerParams(
        vmem_limit_bytes=VMEM_LIMIT,
        dimension_semantics=semantics if semantics else None,
    )


def vmem():
    return pl.BlockSpec(memory_space=pltpu.VMEM)


def smem():
    return pl.BlockSpec(memory_space=pltpu.SMEM)


CORE, Z, SEQ, Y, XHI = range(5)


def away(me, axis, at):
    return lax.rem(at + 4 - me[axis], 4)


def ring_rows(parts, step, y, x, size):
    if step == 2:
        a, b = parts[3][0, y, x, 0:size], parts[4][0, y, x, 0:size]
    else:
        ref = parts[{0: 0, 1: 1, 3: 2}[step]]
        a, b = ref[0, y, x, 0:size], ref[1, y, x, 0:size]
    return jnp.concatenate([a, b], axis=1)


def features_of(me, step):
    return pl.ds(pl.multiple_of(lax.rem(me[Z] + step, 4) * 256, 256), 256)


def put(messages, step, y, x, rows, value):
    for s in range(2):
        name, at = {
            (0, 0): (0, 0), (0, 1): (0, 1), (1, 0): (3, 0), (1, 1): (1, 1),
            (2, 0): (1, 0), (2, 1): (2, 1), (3, 0): (2, 0), (3, 1): (4, 0),
        }[step, s]
        messages[name][at, y, x, rows] = value[:, s * 128 : (s + 1) * 128].astype(BF16)


def split_kernel(me_ref, wq, wk, wv, wo, wup, wdown, small, keep_ref, give_ref):
    first = me_ref[CORE] == 0
    at = 0
    for ref in (wq, wk, wv, wo, wup, wdown):
        value = jnp.transpose(ref[...].astype(F32))
        half = value.shape[0] // 2
        a, b = value[0:half], value[half:]
        keep_ref[at : at + half] = jnp.where(first, a, b).astype(BF16)
        give_ref[at : at + half] = jnp.where(first, b, a).astype(BF16)
        at += half
    keep_ref[at:] = small[...]
    give_ref[at:] = small[...]


def join_kernel(me_ref, mine_ref, other_ref, dq, dk, dv, do, dup, ddown, vec_ref):
    first = me_ref[CORE] == 0
    hidden = ddown.shape[1] // 2

    def rows(start, size):
        a = mine_ref[start : start + size].astype(F32)
        b = other_ref[start : start + size].astype(F32)
        zero, one = jnp.where(first, a, b), jnp.where(first, b, a)
        zero = jnp.where(first, zero[:, 0:HD], zero[:, HD:])
        one = jnp.where(first, one[:, 0:HD], one[:, HD:])
        return zero, one

    at = 0
    plan = ((dq, HD), (dk, HD), (dv, HD), (vec_ref, 16), (dup, hidden), (do, HD), (ddown, hidden))
    for ref, size in plan:
        zero, one = rows(at, size)
        at += size
        if size == 16:
            ref[...] = zero + one
        else:
            ref[...] = jnp.transpose(jnp.concatenate([zero, one], axis=0))


def qkv_kernel(me_ref, x_ref, bias_ref, w0, w1, w2, w3, w4, out_ref):
    parts = (w0, w1, w2, w3, w4)
    core = me_ref[CORE]
    rows = [x_ref[:, features_of(me_ref, step)] for step in range(4)]
    span = x_ref.shape[0] // 4
    for y in range(4):
        for x in range(2):
            made = bias_ref[y * 2 + x]
            for step in range(4):
                made = made + dims(rows[step], ring_rows(parts, step, y, x, 3 * HD), 1, 1)
            made = made.astype(BF16)
            to = y * 2 + x
            for half in range(2):
                top = made[half * 2 * span : half * 2 * span + span]
                low = made[half * 2 * span + span : (half + 1) * 2 * span]
                packed = jnp.concatenate(
                    [
                        jnp.concatenate(
                            [top[:, i * HD : (i + 1) * HD], low[:, i * HD : (i + 1) * HD]],
                            axis=1,
                        )
                        for i in range(3)
                    ],
                    axis=0,
                )
                out_ref[core ^ half, to] = packed


def attend_kernel(q_ref, kv_ref, ctx_ref, lse_ref, *, rows):
    chunk = q_ref.shape[0] * rows
    length = kv_ref.shape[0] * rows
    queries = q_ref[:, 0:rows].reshape(chunk, 2 * HD) * jnp.bfloat16(0.125)
    keys = kv_ref[:, rows : 2 * rows].reshape(length, 2 * HD)
    values = kv_ref[:, 2 * rows : 3 * rows].reshape(length, 2 * HD)
    lane = lax.broadcasted_iota(jnp.int32, (chunk, 2 * HD), 1)
    parts = []
    for s in range(2):
        mine = (lane < HD) if s == 0 else (lane >= HD)
        picked = jnp.where(mine, queries, jnp.bfloat16(0))
        scores = dims(picked, keys, 1, 1)
        top = jnp.max(scores, axis=1, keepdims=True)
        weights = jnp.exp(scores - top)
        total = jnp.sum(weights, axis=1, keepdims=True)
        mixed = dims(weights.astype(BF16), values, 1, 0)
        parts.append(mixed / total)
        lse = jnp.broadcast_to(top + jnp.log(total), (chunk, 128))
        lse_ref[s] = jnp.transpose(lse)[0:8]
    ctx = jnp.where(lane < HD, parts[0], parts[1])
    ctx_ref[...] = ctx.astype(BF16).reshape(ctx_ref.shape)


def attend_back_kernel(
    q_ref, kv_ref, ctx_ref, dctx_ref, lse_ref, dq_ref, dkv_ref, dk_acc, dv_acc, *, rows
):
    step = pl.program_id(0)
    chunk = q_ref.shape[0] * rows
    length = kv_ref.shape[0] * rows
    queries = q_ref[:, 0:rows].reshape(chunk, 2 * HD) * jnp.bfloat16(0.125)
    grads = dctx_ref[...].reshape(chunk, 2 * HD)
    context = ctx_ref[...].reshape(chunk, 2 * HD)
    keys = kv_ref[:, rows : 2 * rows].reshape(length, 2 * HD)
    values = kv_ref[:, 2 * rows : 3 * rows].reshape(length, 2 * HD)
    lane = lax.broadcasted_iota(jnp.int32, (chunk, 2 * HD), 1)
    long_lane = lax.broadcasted_iota(jnp.int32, (length, 2 * HD), 1)
    both = grads.astype(F32) * context.astype(F32)

    @pl.when(step == 0)
    def _():
        dk_acc[...] = jnp.zeros_like(dk_acc)
        dv_acc[...] = jnp.zeros_like(dv_acc)

    dq_parts, dk_parts, dv_parts = [], [], []
    for s in range(2):
        mine = (lane < HD) if s == 0 else (lane >= HD)
        q_mine = jnp.where(mine, queries, jnp.bfloat16(0))
        g_mine = jnp.where(mine, grads, jnp.bfloat16(0))
        delta = jnp.sum(jnp.where(mine, both, 0.0), axis=1, keepdims=True)
        delta = jnp.transpose(jnp.broadcast_to(delta, (chunk, 128)))[0:1]
        scores = dims(keys, q_mine, 1, 1)
        exact = jnp.exp(scores - lse_ref[s, 0:1])
        grad_probs = dims(values, g_mine, 1, 1)
        grad_scores = (exact * (grad_probs - delta)).astype(BF16)
        dq_parts.append(dims(grad_scores, keys, 0, 0))
        dk_parts.append(dims(grad_scores, queries, 1, 0))
        dv_parts.append(dims(exact.astype(BF16), grads, 1, 0))
    dq = jnp.where(lane < HD, dq_parts[0], dq_parts[1]) * 0.125
    dq_ref[...] = dq.astype(BF16).reshape(dq_ref.shape)
    dk_acc[...] += jnp.where(long_lane < HD, dk_parts[0], dk_parts[1])
    dv_acc[...] += jnp.where(long_lane < HD, dv_parts[0], dv_parts[1])

    @pl.when(step == pl.num_programs(0) - 1)
    def _():
        shape = (kv_ref.shape[0], rows, 2 * HD)
        dkv_ref[:, 0:rows] = dk_acc[...].astype(BF16).reshape(shape)
        dkv_ref[:, rows : 2 * rows] = dv_acc[...].astype(BF16).reshape(shape)


def unpack_rows(top, low):
    return jnp.concatenate([top[:, 0:HD], top[:, HD:], low[:, 0:HD], low[:, HD:]], axis=0)


def out_rows(parts, step):
    return jnp.concatenate(
        [ring_rows(parts, step, y, x, HD) for y in range(4) for x in range(2)], axis=0
    )


def out_kernel(me_ref, recv_ref, w0, w1, w2, w3, w4, ctx_ref, own_ref, other_ref, acc):
    core = me_ref[CORE]
    parts = (w0, w1, w2, w3, w4)
    pieces = [unpack_rows(recv_ref[core, at], recv_ref[1 - core, at]) for at in range(8)]
    ctx = jnp.concatenate(pieces, axis=1)
    ctx_ref[...] = ctx
    for step in range(4):
        acc[:, features_of(me_ref, step)] = dims(ctx, out_rows(parts, step), 1, 0)
    half = ctx.shape[0] // 2
    own_ref[...] = acc[0:half]
    other_ref[...] = acc[half:].astype(BF16)


def wide_down(ref, me):
    return jnp.concatenate(
        [ref[s ^ me[SEQ], 0, 0, away(me, Z, z)] for z in range(4) for s in range(2)], axis=1
    )


def ffn_kernel(
    me_ref, n_ref, w0, w1, w2, w3, w4, wdown_ref, bias_ref,
    active_ref, slope_ref, own_ref, other_ref, acc,
):
    step = pl.program_id(0)
    parts = (w0, w1, w2, w3, w4)
    hidden = bias_ref.shape[2]
    pre = bias_ref[0]
    for turn in range(4):
        rows = n_ref[:, features_of(me_ref, turn)]
        pre = pre + dims(rows, ring_rows(parts, turn, 0, 0, hidden), 1, 1)
    cdf = 0.5 * (1.0 + lax.erf(pre * 0.7071067811865476))
    pdf = jnp.exp(-0.5 * pre * pre) * 0.3989422804014327
    active = (pre * cdf).astype(BF16)
    active_ref[...] = active
    slope_ref[...] = (cdf + pre * pdf).astype(BF16)
    made = dims(active, wide_down(wdown_ref, me_ref), 1, 0)

    @pl.when(step == 0)
    def _():
        acc[...] = made

    @pl.when(step > 0)
    def _():
        acc[...] += made

    @pl.when(step == pl.num_programs(0) - 1)
    def _():
        half = acc.shape[0] // 2
        own_ref[...] = acc[0:half]
        other_ref[...] = acc[half:].astype(BF16)


def ffn_back_kernel(
    me_ref, n_ref, g_ref, w0, w1, w2, w3, w4, wdown_ref, active_ref, slope_ref,
    d0, d1, d2, d3, d4, ddown_ref, bias_ref, own_ref, other_ref, acc,
):
    step = pl.program_id(0)
    parts, messages = (w0, w1, w2, w3, w4), (d0, d1, d2, d3, d4)
    grads = g_ref[...]
    active = active_ref[...]
    hidden = active.shape[1]
    grad = dims(active, grads, 0, 0).astype(BF16)
    for z in range(4):
        for s in range(2):
            at = (z * 2 + s) * 128
            ddown_ref[s ^ me_ref[SEQ], 0, 0, away(me_ref, Z, z)] = grad[:, at : at + 128]
    grad_pre = dims(grads, wide_down(wdown_ref, me_ref), 1, 1) * slope_ref[...].astype(F32)
    bias_ref[0] = jnp.sum(grad_pre, axis=0, keepdims=True)
    low = grad_pre.astype(BF16)

    @pl.when(step == 0)
    def _():
        acc[...] = jnp.zeros_like(acc)

    for turn in range(4):
        at = features_of(me_ref, turn)
        put(messages, turn, 0, 0, slice(0, hidden), dims(low, n_ref[:, at], 0, 0))
        acc[:, at] += dims(low, ring_rows(parts, turn, 0, 0, hidden), 1, 0)

    @pl.when(step == pl.num_programs(0) - 1)
    def _():
        half = acc.shape[0] // 2
        own_ref[...] = acc[0:half]
        other_ref[...] = acc[half:].astype(BF16)


def out_back_kernel(
    me_ref, g_ref, ctx_ref, w0, w1, w2, w3, w4, u0, u1, u2, u3, u4,
    dctx_ref, d0, d1, d2, d3, d4,
):
    core = me_ref[CORE]
    parts, messages = (w0, w1, w2, w3, w4), (d0, d1, d2, d3, d4)
    span = g_ref.shape[0] // 4
    ctx = ctx_ref[...]
    made = None
    for step in range(4):
        grads = g_ref[:, features_of(me_ref, step)]
        part = dims(grads, out_rows(parts, step), 1, 1)
        made = part if made is None else made + part
        grad = dims(ctx, grads, 0, 0)
        for y in range(4):
            for x in range(2):
                at = (y * 2 + x) * HD
                put(messages, step, y, x, slice(0, HD), grad[at : at + HD])
    made = made.astype(BF16)
    for to in range(8):
        piece = made[:, to * HD : (to + 1) * HD]
        for half in range(2):
            base = half * 2 * span
            dctx_ref[core ^ half, to] = jnp.concatenate(
                [piece[base : base + span], piece[base + span : base + 2 * span]], axis=1
            )


def qkv_back_kernel(
    me_ref, recv_ref, x_ref, vec_ref, w0, w1, w2, w3, w4,
    d0, d1, d2, d3, d4, own_ref, other_ref, acc,
):
    core = me_ref[CORE]
    parts, grads = (w0, w1, w2, w3, w4), (d0, d1, d2, d3, d4)
    rows = [x_ref[:, features_of(me_ref, step)] for step in range(4)]
    span = x_ref.shape[0] // 4
    half = x_ref.shape[0] // 2

    sums = []
    totals = [None] * 4
    for y in range(4):
        for x in range(2):
            at = y * 2 + x
            top, low = recv_ref[core, at], recv_ref[1 - core, at]
            made = jnp.concatenate(
                [
                    unpack_rows(
                        top[i * span : (i + 1) * span], low[i * span : (i + 1) * span]
                    )
                    for i in range(3)
                ],
                axis=1,
            )
            sums.append(jnp.sum(made.astype(F32), axis=0, keepdims=True))
            for step in range(4):
                put(grads, step, y, x, slice(0, 3 * HD), dims(made, rows[step], 0, 0))
                part = dims(made, ring_rows(parts, step, y, x, 3 * HD), 1, 0)
                totals[step] = part if totals[step] is None else totals[step] + part
    for step in range(4):
        acc[:, features_of(me_ref, step)] = totals[step]
    own_ref[...] = acc[0:half]
    other_ref[...] = acc[half:].astype(BF16)
    zeros = jnp.zeros((14, 2 * HD), F32)
    twos = []
    for z in range(4):
        a, b = sums[2 * z], sums[2 * z + 1]
        bias_q = jnp.concatenate([a[:, 0:HD], b[:, 0:HD]], axis=1)
        bias_v = jnp.concatenate([a[:, 2 * HD :], b[:, 2 * HD :]], axis=1)
        twos.append(jnp.concatenate([bias_q, bias_v, zeros], axis=0))
    for step in range(4):
        z_abs = lax.rem(me_ref[Z] + step, 4)
        two = twos[3]
        for z in range(3):
            two = jnp.where(z_abs == z, twos[z], two)
        block = jnp.concatenate(
            [vec_ref[z_abs, s] + jnp.where(core == s, two, 0.0) for s in range(2)], axis=1
        )
        for y in range(4):
            for x in range(2):
                put(grads, step, y, x, slice(3 * HD, 3 * HD + 16), block)


def norm_forward(hidden, gain, shift):
    centre = jnp.mean(hidden, axis=-1, keepdims=True)
    centered = hidden - centre
    inverse = lax.rsqrt(jnp.mean(centered * centered, axis=-1, keepdims=True) + EPS)
    normed = centered * inverse
    return (normed * gain + shift, normed, inverse)


def norm_backward(grad_in, normed, inverse, gain):
    scaled = grad_in * gain
    inner_term = (
        scaled
        - jnp.mean(scaled, axis=-1, keepdims=True)
        - normed * jnp.mean(scaled * normed, axis=-1, keepdims=True)
    )
    return (
        inverse * inner_term,
        jnp.sum(grad_in * normed, axis=0),
        jnp.sum(grad_in, axis=0),
    )


def sds(shape, dtype=BF16):
    return jax.ShapeDtypeStruct(shape, dtype)


def took(us):
    return pl.CostEstimate(flops=int(us * 1.15e9), bytes_accessed=1 << 20, transcendentals=0)


def local(
    tokens, w_query, w_key, w_value, w_out, w_up, w_down,
    b_query, b_value, b_out, b_up, b_down,
    gain_attn, shift_attn, gain_mlp, shift_mlp, cotangent,
):
    core = lax.axis_index("core")
    me_z, me_s = lax.axis_index("z"), lax.axis_index("seq")
    me_y, me_x = lax.axis_index("y"), lax.axis_index("xhi")
    first_core = core == 0
    me = jnp.stack([core, me_z, me_s, me_y, me_x]).astype(jnp.int32)
    seqs, span, width = tokens.shape
    rows = seqs * span
    hidden = w_up.shape[1] // 2

    at = jnp.arange(width, dtype=jnp.int32)
    z_of, c_of, s_of, i_of = at // 256, (at // 128) % 2, (at // 64) % 2, at % 64
    stored = z_of * 256 + s_of * 128 + c_of * 64 + i_of
    order = (stored[:, None] == at[None, :]).astype(BF16)

    small = jnp.stack(
        [b_query, b_value, b_out, b_down, gain_attn, shift_attn, gain_mlp, shift_mlp]
    )
    small = jnp.concatenate([small, b_up.reshape(4, HD), jnp.zeros((4, HD), BF16)], axis=0)
    shard_rows = 4 * HD + 2 * hidden + 16
    with jax.named_scope("split"):
        keep, give = pl.pallas_call(
            split_kernel,
            out_shape=(sds((shard_rows, HD)),) * 2,
            in_specs=[smem()] + [vmem()] * 7,
            out_specs=(vmem(), vmem()),
            compiler_params=params(),
            cost_estimate=took(2),
        )(me, w_query, w_key, w_value, w_out.T, w_up, w_down.T, small)
    got = other_core(give)
    shard = jnp.where(
        first_core,
        jnp.concatenate([keep, got], axis=1),
        jnp.concatenate([got, keep], axis=1),
    )
    at_o, at_up, at_down, at_vec = 3 * HD, 4 * HD, 4 * HD + hidden, 4 * HD + 2 * hidden
    qkv_shard = jnp.concatenate([shard[0:at_o], shard[at_vec:]], axis=0)
    up_shard = jnp.concatenate([shard[at_up:at_down], shard[at_o:at_up]])
    sixteen = lambda part: jnp.broadcast_to(part[None], (16,) + part.shape)
    qkv_block = plane_gather(sixteen(qkv_shard))
    qkv_block, up_shard = tie(qkv_block, up_shard)
    *near, head, tail = ring_finish(qkv_block, *ring_begin(qkv_block, "z"), "z")
    up_block = plane_gather(sixteen(up_shard))

    both_in = jnp.concatenate([tokens.reshape(rows, width), cotangent.reshape(rows, width)], axis=0)
    both_in = dims(both_in, order, 1, 0)
    mine = both_in[0:rows]
    grad_final = both_in[rows:]
    mine_low = mine.astype(BF16)
    x_rows = jnp.concatenate([mine_low, other_core(mine_low)], axis=0)

    x_rows, down_shard = tie(x_rows, shard[at_down:at_vec])
    down_block = ring_gather(direct_gather(down_shard, "z"), "y")
    head, tail, up_block = tie(head, tail, up_block)
    qkv_parts = (*near, head, tail)
    up_begun, down_begun = ring_begin(up_block, "z"), ring_begin(down_block, "x")

    fours = jnp.arange(4, dtype=jnp.int32)
    turn = ((fours[:, None] - me_z) % 4 == fours[None, :]).astype(F32)
    ring = [p[:, 0, 0, 3 * HD :, :].reshape(-1) for p in qkv_parts]
    vec = jnp.concatenate([ring[0], ring[1], ring[3], ring[4], ring[2]])
    vec = vec.reshape(4, 4096).astype(F32)
    vec = jnp.dot(turn, vec, precision=HIGHEST).reshape(4, 2, 16, 2 * HD)
    feature = lambda i: vec[:, :, i, :].reshape(width)
    chosen = jnp.where(first_core, vec[:, 0], vec[:, 1])
    chosen = chosen.reshape(4, 16, 2, HD).transpose(0, 2, 1, 3).reshape(8, 16 * HD)
    zeros = jnp.zeros((8, HD), F32)
    bias_qkv = jnp.concatenate([chosen[:, 0:HD], zeros, chosen[:, HD : 2 * HD]], axis=1)
    bias_qkv = bias_qkv[:, None, :]
    bias_up = chosen[:, 8 * HD : 12 * HD][:, None, :]
    gain_one, gain_two = feature(4), feature(6)

    with jax.named_scope("project"):
        packed = pl.pallas_call(
            qkv_kernel,
            out_shape=sds((2, 8, 3 * span, 2 * HD)),
            in_specs=[smem()] + [vmem()] * 7,
            out_specs=vmem(),
            compiler_params=params(),
            cost_estimate=took(5),
        )(me, x_rows, bias_qkv, *qkv_parts)

    def exchange(block):
        flat = block.reshape((16,) + block.shape[2:])
        return lax.all_to_all(flat, PLANE, 0, 0, tiled=False)

    packed, *down_begun = tie(packed, *down_begun)
    *down_near, head, tail = ring_finish(down_block, *down_begun, "x")
    qkv, *up_begun = tie(exchange(packed), *up_begun)
    up_parts = ring_finish(up_block, *up_begun, "z")
    per = Q_BLOCKS
    chunk = per * span
    steps = 16 // per
    length = 16 * span
    with jax.named_scope("attend"):
        ctx_heads, lse = pl.pallas_call(
            functools.partial(attend_kernel, rows=span),
            grid=(steps,),
            out_shape=(sds((16, span, 2 * HD)), sds((2, 8, length), F32)),
            in_specs=[
                pl.BlockSpec((per, 3 * span, 2 * HD), lambda i: (i, 0, 0)),
                pl.BlockSpec((16, 3 * span, 2 * HD), lambda i: (0, 0, 0)),
            ],
            out_specs=(
                pl.BlockSpec((per, span, 2 * HD), lambda i: (i, 0, 0)),
                pl.BlockSpec((2, 8, chunk), lambda i: (0, 0, i)),
            ),
            compiler_params=params("arbitrary"),
            cost_estimate=took(11),
        )(qkv, qkv)
    ctx_heads, head, tail = tie(ctx_heads, head, tail)
    wdown = ring_join(*down_near, head, tail, "x")
    recv = lax.all_to_all(ctx_heads, PLANE, 0, 0, tiled=False)
    recv = recv.reshape(2, 8, span, 2 * HD)
    out_block = hidden // HD
    out_specs = [
        pl.BlockSpec((p.shape[0], 4, 2, HD, 2 * HD), lambda i: (0, 0, 0, out_block, 0))
        for p in up_parts
    ]
    message_shapes = [sds(p.shape) for p in up_parts]
    with jax.named_scope("out_project"):
        ctx, own, other = pl.pallas_call(
            out_kernel,
            out_shape=(sds((2 * rows, 8 * HD)), sds((rows, width), F32), sds((rows, width))),
            grid=(1,),
            in_specs=[smem(), vmem()] + out_specs,
            out_specs=(vmem(), vmem(), vmem()),
            scratch_shapes=[pltpu.VMEM((2 * rows, width), F32)],
            compiler_params=params("arbitrary"),
            cost_estimate=took(3),
        )(me, recv, *up_parts)
    attended = own + other_core(other).astype(F32)
    resid_one = mine + attended + feature(2)
    normed_one, norm_first, inverse_first = norm_forward(resid_one, gain_one, feature(5))
    normed_low = normed_one.astype(BF16)
    n_rows = jnp.concatenate([normed_low, other_core(normed_low)], axis=0)

    up_specs = [
        pl.BlockSpec(
            (p.shape[0], 1, 1, hidden, 2 * HD), lambda t, at: (0, t // 2, t % 2, 0, 0)
        )
        for p in up_parts
    ]
    down_spec = pl.BlockSpec(
        (2, 1, 1, 4, hidden, 2 * HD),
        lambda t, at: (0, (t % 2) ^ at[XHI], away(at, Y, t // 2), 0, 0, 0),
    )
    whole_spec = pl.BlockSpec((2 * rows, width), lambda t, at: (0, 0))
    cols_spec = pl.BlockSpec((2 * rows, hidden), lambda t, at: (0, t))
    half_spec = pl.BlockSpec((rows, width), lambda t, at: (0, 0))
    bias_spec = pl.BlockSpec((1, 1, hidden), lambda t, at: (t, 0, 0))
    with jax.named_scope("feed_forward"):
        active, slope, own, other = pl.pallas_call(
            ffn_kernel,
            grid_spec=pltpu.PrefetchScalarGridSpec(
                num_scalar_prefetch=1,
                grid=(8,),
                in_specs=[whole_spec] + up_specs + [down_spec, bias_spec],
                out_specs=(cols_spec, cols_spec, half_spec, half_spec),
                scratch_shapes=[pltpu.VMEM((2 * rows, width), F32)],
            ),
            out_shape=(
                sds((2 * rows, 8 * hidden)),
                sds((2 * rows, 8 * hidden)),
                sds((rows, width), F32),
                sds((rows, width)),
            ),
            compiler_params=params("arbitrary"),
            cost_estimate=took(14),
        )(me, n_rows, *up_parts, wdown, bias_up)
    mixed = own + other_core(other).astype(F32)
    resid_two = normed_one + mixed + feature(3)
    final, norm_second, inverse_second = norm_forward(resid_two, gain_two, feature(7))
    output = dims(final.astype(BF16), order, 1, 1).astype(BF16)
    grad_two, part_gain_mlp, part_shift_mlp = norm_backward(
        grad_final, norm_second, inverse_second, gain_two
    )
    grad_low = grad_two.astype(BF16)
    g_rows = jnp.concatenate([grad_low, other_core(grad_low)], axis=0)
    with jax.named_scope("feed_forward_back"):
        *grad_up, grad_down, part_up, own, other = pl.pallas_call(
            ffn_back_kernel,
            grid_spec=pltpu.PrefetchScalarGridSpec(
                num_scalar_prefetch=1,
                grid=(8,),
                in_specs=[whole_spec] * 2 + up_specs + [down_spec, cols_spec, cols_spec],
                out_specs=(*up_specs, down_spec, bias_spec, half_spec, half_spec),
                scratch_shapes=[pltpu.VMEM((2 * rows, width), F32)],
            ),
            out_shape=(
                *message_shapes,
                sds(wdown.shape),
                sds((8, 1, hidden), F32),
                sds((rows, width), F32),
                sds((rows, width)),
            ),
            compiler_params=params("arbitrary"),
            cost_estimate=took(20),
        )(me, n_rows, g_rows, *up_parts, wdown, active, slope)
    grad_mid = grad_two + (own + other_core(other).astype(F32))
    grad_one, part_gain_attn, part_shift_attn = norm_backward(
        grad_mid, norm_first, inverse_first, gain_one
    )
    grad_low = grad_one.astype(BF16)
    g_rows = jnp.concatenate([grad_low, other_core(grad_low)], axis=0)
    with jax.named_scope("out_project_back"):
        dctx, *grad_up = pl.pallas_call(
            out_back_kernel,
            grid=(1,),
            out_shape=(sds((2, 8, span, 2 * HD)), *message_shapes),
            in_specs=[smem(), vmem(), vmem()]
            + out_specs
            + [pl.BlockSpec(memory_space=pl.ANY)] * 5,
            out_specs=(vmem(), *out_specs),
            input_output_aliases={8 + i: 1 + i for i in range(5)},
            compiler_params=params("arbitrary"),
            cost_estimate=took(4),
        )(me, g_rows, ctx, *up_parts, *grad_up)
    dctx, grad_down = tie(exchange(dctx), grad_down)
    down_begun = reduce_start(cross_messages(grad_down), "x")
    up_begun = reduce_start(grad_up, "z")
    with jax.named_scope("attend_back"):
        dq, dkv = pl.pallas_call(
            functools.partial(attend_back_kernel, rows=span),
            grid=(steps,),
            out_shape=(sds((16, span, 2 * HD)), sds((16, 2 * span, 2 * HD))),
            in_specs=[
                pl.BlockSpec((per, 3 * span, 2 * HD), lambda i: (i, 0, 0)),
                pl.BlockSpec((16, 3 * span, 2 * HD), lambda i: (0, 0, 0)),
                pl.BlockSpec((per, span, 2 * HD), lambda i: (i, 0, 0)),
                pl.BlockSpec((per, span, 2 * HD), lambda i: (i, 0, 0)),
                pl.BlockSpec((2, 8, chunk), lambda i: (0, 0, i)),
            ],
            out_specs=(
                pl.BlockSpec((per, span, 2 * HD), lambda i: (i, 0, 0)),
                pl.BlockSpec((16, 2 * span, 2 * HD), lambda i: (0, 0, 0)),
            ),
            scratch_shapes=[pltpu.VMEM((length, 2 * HD), F32)] * 2,
            compiler_params=params("arbitrary"),
            cost_estimate=took(18),
        )(qkv, qkv, ctx_heads, dctx, lse)
    dq, *begun = tie(dq, *down_begun, *up_begun)
    dqkv = exchange(jnp.concatenate([dq, dkv], axis=1)[None])
    down_sum = reduce_end(reduce_middle(begun[0:5], "x"), "x")
    up_sum = reduce_end(reduce_middle(begun[5:10], "z"), "z")
    dqkv, down_sum, up_sum = tie(dqkv, down_sum, up_sum)
    down_begun = reduce_start(ring_messages(down_sum), "y")
    dqkv = dqkv.reshape(2, 8, 3 * span, 2 * HD)
    ups = part_up.reshape(4, 2, 4, HD).transpose(0, 2, 1, 3).reshape(4, 1, 4, 2 * HD)
    nothing = jnp.zeros_like(ups)
    ups = jnp.concatenate(
        [jnp.where(first_core, ups, nothing), jnp.where(first_core, nothing, ups)], axis=1
    )
    six = jnp.stack(
        [
            jnp.sum(grad_one, axis=0), jnp.sum(grad_two, axis=0),
            part_gain_attn, part_shift_attn, part_gain_mlp, part_shift_mlp,
        ]
    ).reshape(6, 4, 2, 2 * HD).transpose(1, 2, 0, 3)
    vec_rows = jnp.concatenate(
        [jnp.zeros((4, 2, 2, 2 * HD), F32), six, ups, jnp.zeros((4, 2, 4, 2 * HD), F32)], axis=2
    )
    with jax.named_scope("project_back"):
        part, far = sds((2, 4, 2, 3 * HD + 16, 2 * HD)), sds((1, 4, 2, 3 * HD + 16, 2 * HD))
        *grad_qkv, own, other = pl.pallas_call(
            qkv_back_kernel,
            out_shape=(
                part, part, part, far, far, sds((rows, width), F32), sds((rows, width)),
            ),
            in_specs=[smem()] + [vmem()] * 8,
            out_specs=(vmem(),) * 7,
            scratch_shapes=[pltpu.VMEM((2 * rows, width), F32)],
            compiler_params=params(),
            cost_estimate=took(8),
        )(me, dqkv, x_rows, vec_rows, *qkv_parts)
    input_sum = own + other_core(other).astype(F32)
    grad_tokens = lax.dot_general(
        grad_one + input_sum, order.astype(F32), (((1,), (1,)), ((), ())),
        precision=lax.Precision.HIGH,
    )
    begun = tie(*reduce_start(grad_qkv, "z"), *down_begun, grad_tokens)
    qkv_sum = reduce_end(reduce_middle(begun[0:5], "z"), "z")
    down_begun, grad_tokens = begun[5:10], begun[10]
    down_sum = reduce_end(reduce_middle(down_begun, "y"), "y")
    got_up = plane_reduce(up_sum).astype(BF16)
    got_down = direct_reduce(down_sum, "z")
    got_qkv = plane_reduce(qkv_sum)
    final_rows = jnp.concatenate([got_qkv.astype(BF16), got_up, got_down], axis=0)
    swapped = other_core(final_rows)
    with jax.named_scope("join"):
        square = sds((HD, 2 * HD), F32)
        *weights, g_out, g_up, g_down, vecs = pl.pallas_call(
            join_kernel,
            out_shape=(
                square, square, square, square,
                sds((HD, 2 * hidden), F32),
                sds((HD, 2 * hidden), F32),
                sds((16, HD), F32),
            ),
            in_specs=[smem(), vmem(), vmem()],
            out_specs=(vmem(),) * 7,
            compiler_params=params(),
            cost_estimate=took(2),
        )(me, final_rows, swapped)
    return (
        output.reshape(seqs, span, width),
        grad_tokens.reshape(seqs, span, width),
        *weights,
        g_out.T,
        g_up,
        g_down.T,
        vecs[0],
        vecs[1],
        vecs[2],
        vecs[8:12].reshape(4 * HD),
        vecs[3],
        vecs[4],
        vecs[5],
        vecs[6],
        vecs[7],
    )


def solution(mesh):
    fine = Mesh(mesh.devices.reshape(4, 2, 2, 4, 2), ("z", "core", "seq", "y", "xhi"))
    owners, tensor = ("z", "core", "seq"), ("y", "xhi")
    tokens = P(("z", "core"), ("seq", "y", "xhi"), None)
    columns, by_rows, vector = P(owners, tensor), P(tensor, owners), P(owners)
    weights = (columns, columns, columns, by_rows, columns, by_rows)
    return jax.shard_map(
        local,
        mesh=fine,
        in_specs=(tokens,) + weights + (vector,) * 9 + (tokens,),
        out_specs=(tokens, tokens) + weights + (vector,) * 9,
        check_vma=False,
    )
```

```python
import functools

import jax
import jax.numpy as jnp
from jax import lax
from jax.experimental import pallas as pl
from jax.experimental.pallas import tpu as pltpu
from jax.sharding import Mesh, PartitionSpec as P

HD = 64
EPS = 1e-05
F32 = jnp.float32
BF16 = jnp.bfloat16
HIGHEST = lax.Precision.HIGHEST
VMEM_LIMIT = 56 * 1024 * 1024
Q_BLOCKS = 4
PLANE = ("seq", "y", "xhi")


def dims(a, b, ca, cb):
    return lax.dot_general(a, b, (((ca,), (cb,)), ((), ())), preferred_element_type=F32)


def shift4(by):
    return [(i, (i + by) % 4) for i in range(4)]


def flip(seq_too, xhi_too):
    return [
        (seq * 2 + xhi, (seq ^ seq_too) * 2 + (xhi ^ xhi_too))
        for seq in range(2)
        for xhi in range(2)
    ]


def links(axis):
    if axis == "x":
        return ("seq", "xhi"), flip(1, 0), flip(1, 1)
    return axis, shift4(-1), shift4(1)


def halves(block):
    half = block.shape[0] // 2
    return block[0:half], block[half:]


def ring_begin(block, axis):
    names, one, two = links(axis)
    return lax.ppermute(block, names, one), lax.ppermute(block, names, two)


def ring_halves(first, second, axis):
    if axis == "x":
        return halves(second)[0], halves(first)[1]
    return halves(first)[0], halves(second)[1]


def ring_forward(head, tail, axis):
    names, one, two = links(axis)
    return lax.ppermute(head, names, one), lax.ppermute(tail, names, two)


def ring_finish(block, first, second, axis):
    head, tail = ring_forward(*ring_halves(first, second, axis), axis)
    return block, first, second, head, tail


def ring_join(block, first, second, head, tail, axis):
    if axis == "x":
        whole = jnp.concatenate([block, head, tail, first, second], axis=0)
        return whole.reshape((2, 2) + block.shape)
    whole = jnp.concatenate([block, first, head, tail, second], axis=0)
    return whole.reshape((4,) + block.shape)


def ring_gather(block, axis):
    return ring_join(*ring_finish(block, *ring_begin(block, axis), axis), axis)


def direct_gather(block, axis):
    parts = [block] + [lax.ppermute(block, axis, shift4(-i)) for i in (1, 2, 3)]
    return jnp.stack(parts)


def add(*terms):
    total = terms[0].astype(F32)
    for term in terms[1:]:
        total = total + term.astype(F32)
    return total.astype(BF16)


def ring_messages(block):
    first_head, first_tail = halves(block[1])
    far_head, far_tail = halves(block[2])
    second_head, second_tail = halves(block[3])
    return (
        block[0],
        jnp.concatenate([far_head, first_tail], axis=0),
        jnp.concatenate([second_head, far_tail], axis=0),
        first_head,
        second_tail,
    )


def cross_messages(block):
    first_head, first_tail = halves(block[1, 0])
    far_head, far_tail = halves(block[0, 1])
    second_head, second_tail = halves(block[1, 1])
    return (
        block[0, 0],
        jnp.concatenate([far_head, first_head], axis=0),
        jnp.concatenate([far_tail, second_tail], axis=0),
        first_tail,
        second_head,
    )


def reduce_ways(axis):
    names, one, two = links(axis)
    return (names, one, two) if axis == "x" else (names, two, one)


def reduce_start(messages, axis):
    names, to_first, to_second = reduce_ways(axis)
    own, a, b, first, second = messages
    return own, lax.ppermute(a, names, to_first), lax.ppermute(b, names, to_second), first, second


def reduce_middle(begun, axis):
    own, a, b, first, second = begun
    (a_head, a_tail), (b_head, b_tail) = halves(a), halves(b)
    if axis == "x":
        return own, a_tail, b_tail, add(first, b_head), add(second, a_head)
    return own, b_head, a_tail, add(first, a_head), add(second, b_tail)


def reduce_end(middle, axis):
    names, to_first, to_second = reduce_ways(axis)
    own, near_head, near_tail, first, second = middle
    first = lax.ppermute(first, names, to_first)
    second = lax.ppermute(second, names, to_second)
    if axis == "x":
        first, second = second, first
    head, tail = halves(own)
    return jnp.concatenate([add(head, near_head, first), add(tail, near_tail, second)], axis=0)


def tie(*values):
    return lax.optimization_barrier(values)


def direct_reduce(block, axis):
    parts = [block[0]] + [lax.ppermute(block[i], axis, shift4(i)) for i in (1, 2, 3)]
    return add(*parts)


def plane_gather(copies):
    got = lax.all_to_all(copies, PLANE, 0, 0, tiled=False)
    return got.reshape((2, 4, 2) + copies.shape[1:])


def plane_reduce(block):
    flat = block.reshape((16,) + block.shape[-2:])
    got = lax.all_to_all(flat, PLANE, 0, 0, tiled=False)
    return jnp.sum(got.astype(F32), axis=0)


def other_core(block):
    return lax.ppermute(block, "core", [(0, 1), (1, 0)])


def params(*semantics):
    return pltpu.CompilerParams(
        vmem_limit_bytes=VMEM_LIMIT,
        dimension_semantics=semantics if semantics else None,
    )


def vmem():
    return pl.BlockSpec(memory_space=pltpu.VMEM)


def smem():
    return pl.BlockSpec(memory_space=pltpu.SMEM)


CORE, Z, SEQ, Y, XHI = range(5)


def away(me, axis, at):
    return lax.rem(at + 4 - me[axis], 4)


def ring_rows(parts, step, y, x, size):
    if step == 2:
        a, b = parts[3][0, y, x, 0:size], parts[4][0, y, x, 0:size]
    else:
        ref = parts[{0: 0, 1: 1, 3: 2}[step]]
        a, b = ref[0, y, x, 0:size], ref[1, y, x, 0:size]
    return jnp.concatenate([a, b], axis=1)


def features_of(me, step):
    return pl.ds(pl.multiple_of(lax.rem(me[Z] + step, 4) * 256, 256), 256)


def put(messages, step, y, x, rows, value):
    for s in range(2):
        name, at = {
            (0, 0): (0, 0), (0, 1): (0, 1), (1, 0): (3, 0), (1, 1): (1, 1),
            (2, 0): (1, 0), (2, 1): (2, 1), (3, 0): (2, 0), (3, 1): (4, 0),
        }[step, s]
        messages[name][at, y, x, rows] = value[:, s * 128 : (s + 1) * 128].astype(BF16)


def split_kernel(me_ref, wq, wk, wv, wo, wup, wdown, small, keep_ref, give_ref):
    first = me_ref[CORE] == 0
    at = 0
    for ref in (wq, wk, wv, wo, wup, wdown):
        value = jnp.transpose(ref[...].astype(F32))
        half = value.shape[0] // 2
        a, b = value[0:half], value[half:]
        keep_ref[at : at + half] = jnp.where(first, a, b).astype(BF16)
        give_ref[at : at + half] = jnp.where(first, b, a).astype(BF16)
        at += half
    keep_ref[at:] = small[...]
    give_ref[at:] = small[...]


def join_kernel(me_ref, mine_ref, other_ref, dq, dk, dv, do, dup, ddown, vec_ref):
    first = me_ref[CORE] == 0
    hidden = ddown.shape[1] // 2

    def rows(start, size):
        a = mine_ref[start : start + size].astype(F32)
        b = other_ref[start : start + size].astype(F32)
        zero, one = jnp.where(first, a, b), jnp.where(first, b, a)
        zero = jnp.where(first, zero[:, 0:HD], zero[:, HD:])
        one = jnp.where(first, one[:, 0:HD], one[:, HD:])
        return zero, one

    at = 0
    plan = ((dq, HD), (dk, HD), (dv, HD), (vec_ref, 16), (dup, hidden), (do, HD), (ddown, hidden))
    for ref, size in plan:
        zero, one = rows(at, size)
        at += size
        if size == 16:
            ref[...] = zero + one
        else:
            ref[...] = jnp.transpose(jnp.concatenate([zero, one], axis=0))


def qkv_kernel(me_ref, x_ref, bias_ref, w0, w1, w2, w3, w4, out_ref):
    parts = (w0, w1, w2, w3, w4)
    core = me_ref[CORE]
    rows = [x_ref[:, features_of(me_ref, step)] for step in range(4)]
    span = x_ref.shape[0] // 4
    for y in range(4):
        for x in range(2):
            made = bias_ref[y * 2 + x]
            for step in range(4):
                made = made + dims(rows[step], ring_rows(parts, step, y, x, 3 * HD), 1, 1)
            made = made.astype(BF16)
            to = y * 2 + x
            for half in range(2):
                top = made[half * 2 * span : half * 2 * span + span]
                low = made[half * 2 * span + span : (half + 1) * 2 * span]
                packed = jnp.concatenate(
                    [
                        jnp.concatenate(
                            [top[:, i * HD : (i + 1) * HD], low[:, i * HD : (i + 1) * HD]],
                            axis=1,
                        )
                        for i in range(3)
                    ],
                    axis=0,
                )
                out_ref[core ^ half, to] = packed


def attend_kernel(q_ref, kv_ref, ctx_ref, lse_ref, *, rows):
    chunk = q_ref.shape[0] * rows
    length = kv_ref.shape[0] * rows
    queries = q_ref[:, 0:rows].reshape(chunk, 2 * HD) * jnp.bfloat16(0.125)
    keys = kv_ref[:, rows : 2 * rows].reshape(length, 2 * HD)
    values = kv_ref[:, 2 * rows : 3 * rows].reshape(length, 2 * HD)
    lane = lax.broadcasted_iota(jnp.int32, (chunk, 2 * HD), 1)
    parts = []
    for s in range(2):
        mine = (lane < HD) if s == 0 else (lane >= HD)
        picked = jnp.where(mine, queries, jnp.bfloat16(0))
        scores = dims(picked, keys, 1, 1)
        top = jnp.max(scores, axis=1, keepdims=True)
        weights = jnp.exp(scores - top)
        total = jnp.sum(weights, axis=1, keepdims=True)
        mixed = dims(weights.astype(BF16), values, 1, 0)
        parts.append(mixed / total)
        lse = jnp.broadcast_to(top + jnp.log(total), (chunk, 128))
        lse_ref[s] = jnp.transpose(lse)[0:8]
    ctx = jnp.where(lane < HD, parts[0], parts[1])
    ctx_ref[...] = ctx.astype(BF16).reshape(ctx_ref.shape)


def attend_back_kernel(
    q_ref, kv_ref, ctx_ref, dctx_ref, lse_ref, dq_ref, dkv_ref, dk_acc, dv_acc, *, rows
):
    step = pl.program_id(0)
    chunk = q_ref.shape[0] * rows
    length = kv_ref.shape[0] * rows
    queries = q_ref[:, 0:rows].reshape(chunk, 2 * HD) * jnp.bfloat16(0.125)
    grads = dctx_ref[...].reshape(chunk, 2 * HD)
    context = ctx_ref[...].reshape(chunk, 2 * HD)
    keys = kv_ref[:, rows : 2 * rows].reshape(length, 2 * HD)
    values = kv_ref[:, 2 * rows : 3 * rows].reshape(length, 2 * HD)
    lane = lax.broadcasted_iota(jnp.int32, (chunk, 2 * HD), 1)
    long_lane = lax.broadcasted_iota(jnp.int32, (length, 2 * HD), 1)
    both = grads.astype(F32) * context.astype(F32)

    @pl.when(step == 0)
    def _():
        dk_acc[...] = jnp.zeros_like(dk_acc)
        dv_acc[...] = jnp.zeros_like(dv_acc)

    dq_parts, dk_parts, dv_parts = [], [], []
    for s in range(2):
        mine = (lane < HD) if s == 0 else (lane >= HD)
        q_mine = jnp.where(mine, queries, jnp.bfloat16(0))
        g_mine = jnp.where(mine, grads, jnp.bfloat16(0))
        delta = jnp.sum(jnp.where(mine, both, 0.0), axis=1, keepdims=True)
        delta = jnp.transpose(jnp.broadcast_to(delta, (chunk, 128)))[0:1]
        scores = dims(keys, q_mine, 1, 1)
        exact = jnp.exp(scores - lse_ref[s, 0:1])
        grad_probs = dims(values, g_mine, 1, 1)
        grad_scores = (exact * (grad_probs - delta)).astype(BF16)
        dq_parts.append(dims(grad_scores, keys, 0, 0))
        dk_parts.append(dims(grad_scores, queries, 1, 0))
        dv_parts.append(dims(exact.astype(BF16), grads, 1, 0))
    dq = jnp.where(lane < HD, dq_parts[0], dq_parts[1]) * 0.125
    dq_ref[...] = dq.astype(BF16).reshape(dq_ref.shape)
    dk_acc[...] += jnp.where(long_lane < HD, dk_parts[0], dk_parts[1])
    dv_acc[...] += jnp.where(long_lane < HD, dv_parts[0], dv_parts[1])

    @pl.when(step == pl.num_programs(0) - 1)
    def _():
        shape = (kv_ref.shape[0], rows, 2 * HD)
        dkv_ref[:, 0:rows] = dk_acc[...].astype(BF16).reshape(shape)
        dkv_ref[:, rows : 2 * rows] = dv_acc[...].astype(BF16).reshape(shape)


def unpack_rows(top, low):
    return jnp.concatenate([top[:, 0:HD], top[:, HD:], low[:, 0:HD], low[:, HD:]], axis=0)


def out_rows(parts, step):
    return jnp.concatenate(
        [ring_rows(parts, step, y, x, HD) for y in range(4) for x in range(2)], axis=0
    )


def out_kernel(me_ref, recv_ref, w0, w1, w2, w3, w4, ctx_ref, own_ref, other_ref, acc):
    core = me_ref[CORE]
    parts = (w0, w1, w2, w3, w4)
    pieces = [unpack_rows(recv_ref[core, at], recv_ref[1 - core, at]) for at in range(8)]
    ctx = jnp.concatenate(pieces, axis=1)
    ctx_ref[...] = ctx
    for step in range(4):
        acc[:, features_of(me_ref, step)] = dims(ctx, out_rows(parts, step), 1, 0)
    half = ctx.shape[0] // 2
    own_ref[...] = acc[0:half]
    other_ref[...] = acc[half:].astype(BF16)


def wide_down(ref, me):
    return jnp.concatenate(
        [ref[s ^ me[SEQ], 0, 0, away(me, Z, z)] for z in range(4) for s in range(2)], axis=1
    )


def ffn_kernel(
    me_ref, n_ref, w0, w1, w2, w3, w4, wdown_ref, bias_ref,
    active_ref, slope_ref, own_ref, other_ref, acc,
):
    step = pl.program_id(0)
    parts = (w0, w1, w2, w3, w4)
    hidden = bias_ref.shape[2]
    pre = bias_ref[0]
    for turn in range(4):
        rows = n_ref[:, features_of(me_ref, turn)]
        pre = pre + dims(rows, ring_rows(parts, turn, 0, 0, hidden), 1, 1)
    cdf = 0.5 * (1.0 + lax.erf(pre * 0.7071067811865476))
    pdf = jnp.exp(-0.5 * pre * pre) * 0.3989422804014327
    active = (pre * cdf).astype(BF16)
    active_ref[...] = active
    slope_ref[...] = (cdf + pre * pdf).astype(BF16)
    made = dims(active, wide_down(wdown_ref, me_ref), 1, 0)

    @pl.when(step == 0)
    def _():
        acc[...] = made

    @pl.when(step > 0)
    def _():
        acc[...] += made

    @pl.when(step == pl.num_programs(0) - 1)
    def _():
        half = acc.shape[0] // 2
        own_ref[...] = acc[0:half]
        other_ref[...] = acc[half:].astype(BF16)


def ffn_back_kernel(
    me_ref, n_ref, g_ref, w0, w1, w2, w3, w4, wdown_ref, active_ref, slope_ref,
    d0, d1, d2, d3, d4, ddown_ref, bias_ref, own_ref, other_ref, acc,
):
    step = pl.program_id(0)
    parts, messages = (w0, w1, w2, w3, w4), (d0, d1, d2, d3, d4)
    grads = g_ref[...]
    active = active_ref[...]
    hidden = active.shape[1]
    grad = dims(active, grads, 0, 0).astype(BF16)
    for z in range(4):
        for s in range(2):
            at = (z * 2 + s) * 128
            ddown_ref[s ^ me_ref[SEQ], 0, 0, away(me_ref, Z, z)] = grad[:, at : at + 128]
    grad_pre = dims(grads, wide_down(wdown_ref, me_ref), 1, 1) * slope_ref[...].astype(F32)
    bias_ref[0] = jnp.sum(grad_pre, axis=0, keepdims=True)
    low = grad_pre.astype(BF16)

    @pl.when(step == 0)
    def _():
        acc[...] = jnp.zeros_like(acc)

    for turn in range(4):
        at = features_of(me_ref, turn)
        put(messages, turn, 0, 0, slice(0, hidden), dims(low, n_ref[:, at], 0, 0))
        acc[:, at] += dims(low, ring_rows(parts, turn, 0, 0, hidden), 1, 0)

    @pl.when(step == pl.num_programs(0) - 1)
    def _():
        half = acc.shape[0] // 2
        own_ref[...] = acc[0:half]
        other_ref[...] = acc[half:].astype(BF16)


def out_back_kernel(
    me_ref, g_ref, ctx_ref, w0, w1, w2, w3, w4, u0, u1, u2, u3, u4,
    dctx_ref, d0, d1, d2, d3, d4,
):
    core = me_ref[CORE]
    parts, messages = (w0, w1, w2, w3, w4), (d0, d1, d2, d3, d4)
    span = g_ref.shape[0] // 4
    ctx = ctx_ref[...]
    made = None
    for step in range(4):
        grads = g_ref[:, features_of(me_ref, step)]
        part = dims(grads, out_rows(parts, step), 1, 1)
        made = part if made is None else made + part
        grad = dims(ctx, grads, 0, 0)
        for y in range(4):
            for x in range(2):
                at = (y * 2 + x) * HD
                put(messages, step, y, x, slice(0, HD), grad[at : at + HD])
    made = made.astype(BF16)
    for to in range(8):
        piece = made[:, to * HD : (to + 1) * HD]
        for half in range(2):
            base = half * 2 * span
            dctx_ref[core ^ half, to] = jnp.concatenate(
                [piece[base : base + span], piece[base + span : base + 2 * span]], axis=1
            )


def qkv_back_kernel(
    me_ref, recv_ref, x_ref, vec_ref, w0, w1, w2, w3, w4,
    d0, d1, d2, d3, d4, own_ref, other_ref, acc,
):
    core = me_ref[CORE]
    parts, grads = (w0, w1, w2, w3, w4), (d0, d1, d2, d3, d4)
    rows = [x_ref[:, features_of(me_ref, step)] for step in range(4)]
    span = x_ref.shape[0] // 4
    half = x_ref.shape[0] // 2

    sums = []
    totals = [None] * 4
    for y in range(4):
        for x in range(2):
            at = y * 2 + x
            top, low = recv_ref[core, at], recv_ref[1 - core, at]
            made = jnp.concatenate(
                [
                    unpack_rows(
                        top[i * span : (i + 1) * span], low[i * span : (i + 1) * span]
                    )
                    for i in range(3)
                ],
                axis=1,
            )
            sums.append(jnp.sum(made.astype(F32), axis=0, keepdims=True))
            for step in range(4):
                put(grads, step, y, x, slice(0, 3 * HD), dims(made, rows[step], 0, 0))
                part = dims(made, ring_rows(parts, step, y, x, 3 * HD), 1, 0)
                totals[step] = part if totals[step] is None else totals[step] + part
    for step in range(4):
        acc[:, features_of(me_ref, step)] = totals[step]
    own_ref[...] = acc[0:half]
    other_ref[...] = acc[half:].astype(BF16)
    zeros = jnp.zeros((14, 2 * HD), F32)
    twos = []
    for z in range(4):
        a, b = sums[2 * z], sums[2 * z + 1]
        bias_q = jnp.concatenate([a[:, 0:HD], b[:, 0:HD]], axis=1)
        bias_v = jnp.concatenate([a[:, 2 * HD :], b[:, 2 * HD :]], axis=1)
        twos.append(jnp.concatenate([bias_q, bias_v, zeros], axis=0))
    for step in range(4):
        z_abs = lax.rem(me_ref[Z] + step, 4)
        two = twos[3]
        for z in range(3):
            two = jnp.where(z_abs == z, twos[z], two)
        block = jnp.concatenate(
            [vec_ref[z_abs, s] + jnp.where(core == s, two, 0.0) for s in range(2)], axis=1
        )
        for y in range(4):
            for x in range(2):
                put(grads, step, y, x, slice(3 * HD, 3 * HD + 16), block)


def norm_forward(hidden, gain, shift):
    centre = jnp.mean(hidden, axis=-1, keepdims=True)
    centered = hidden - centre
    inverse = lax.rsqrt(jnp.mean(centered * centered, axis=-1, keepdims=True) + EPS)
    normed = centered * inverse
    return (normed * gain + shift, normed, inverse)


def norm_backward(grad_in, normed, inverse, gain):
    scaled = grad_in * gain
    inner_term = (
        scaled
        - jnp.mean(scaled, axis=-1, keepdims=True)
        - normed * jnp.mean(scaled * normed, axis=-1, keepdims=True)
    )
    return (
        inverse * inner_term,
        jnp.sum(grad_in * normed, axis=0),
        jnp.sum(grad_in, axis=0),
    )


def sds(shape, dtype=BF16):
    return jax.ShapeDtypeStruct(shape, dtype)


def took(us):
    return pl.CostEstimate(flops=int(us * 1.15e9), bytes_accessed=1 << 20, transcendentals=0)


def local(
    tokens, w_query, w_key, w_value, w_out, w_up, w_down,
    b_query, b_value, b_out, b_up, b_down,
    gain_attn, shift_attn, gain_mlp, shift_mlp, cotangent,
):
    core = lax.axis_index("core")
    me_z, me_s = lax.axis_index("z"), lax.axis_index("seq")
    me_y, me_x = lax.axis_index("y"), lax.axis_index("xhi")
    first_core = core == 0
    me = jnp.stack([core, me_z, me_s, me_y, me_x]).astype(jnp.int32)
    seqs, span, width = tokens.shape
    rows = seqs * span
    hidden = w_up.shape[1] // 2

    at = jnp.arange(width, dtype=jnp.int32)
    z_of, c_of, s_of, i_of = at // 256, (at // 128) % 2, (at // 64) % 2, at % 64
    stored = z_of * 256 + s_of * 128 + c_of * 64 + i_of
    order = (stored[:, None] == at[None, :]).astype(BF16)

    small = jnp.stack(
        [b_query, b_value, b_out, b_down, gain_attn, shift_attn, gain_mlp, shift_mlp]
    )
    small = jnp.concatenate([small, b_up.reshape(4, HD), jnp.zeros((4, HD), BF16)], axis=0)
    shard_rows = 4 * HD + 2 * hidden + 16
    with jax.named_scope("split"):
        keep, give = pl.pallas_call(
            split_kernel,
            out_shape=(sds((shard_rows, HD)),) * 2,
            in_specs=[smem()] + [vmem()] * 7,
            out_specs=(vmem(), vmem()),
            compiler_params=params(),
            cost_estimate=took(2),
        )(me, w_query, w_key, w_value, w_out.T, w_up, w_down.T, small)
    got = other_core(give)
    shard = jnp.where(
        first_core,
        jnp.concatenate([keep, got], axis=1),
        jnp.concatenate([got, keep], axis=1),
    )
    at_o, at_up, at_down, at_vec = 3 * HD, 4 * HD, 4 * HD + hidden, 4 * HD + 2 * hidden
    qkv_shard = jnp.concatenate([shard[0:at_o], shard[at_vec:]], axis=0)
    up_shard = jnp.concatenate([shard[at_up:at_down], shard[at_o:at_up]])
    sixteen = lambda part: jnp.broadcast_to(part[None], (16,) + part.shape)
    qkv_block = plane_gather(sixteen(qkv_shard))
    *near, head, tail = ring_finish(qkv_block, *ring_begin(qkv_block, "z"), "z")

    both_in = jnp.concatenate([tokens.reshape(rows, width), cotangent.reshape(rows, width)], axis=0)
    both_in = dims(both_in, order, 1, 0)
    mine = both_in[0:rows]
    grad_final = both_in[rows:]
    mine_low = mine.astype(BF16)
    x_rows = jnp.concatenate([mine_low, other_core(mine_low)], axis=0)

    x_rows, down_shard = tie(x_rows, shard[at_down:at_vec])
    down_line = direct_gather(down_shard, "z")
    *down_begun, up_shard = tie(*ring_begin(down_line, "y"), up_shard)
    up_block = plane_gather(sixteen(up_shard))
    down_block = ring_join(*ring_finish(down_line, *down_begun, "y"), "y")
    head, tail, up_block = tie(head, tail, up_block)
    qkv_parts = (*near, head, tail)
    up_begun, down_begun = ring_begin(up_block, "z"), ring_begin(down_block, "x")

    fours = jnp.arange(4, dtype=jnp.int32)
    turn = ((fours[:, None] - me_z) % 4 == fours[None, :]).astype(F32)
    ring = [p[:, 0, 0, 3 * HD :, :].reshape(-1) for p in qkv_parts]
    vec = jnp.concatenate([ring[0], ring[1], ring[3], ring[4], ring[2]])
    vec = vec.reshape(4, 4096).astype(F32)
    vec = jnp.dot(turn, vec, precision=HIGHEST).reshape(4, 2, 16, 2 * HD)
    feature = lambda i: vec[:, :, i, :].reshape(width)
    chosen = jnp.where(first_core, vec[:, 0], vec[:, 1])
    chosen = chosen.reshape(4, 16, 2, HD).transpose(0, 2, 1, 3).reshape(8, 16 * HD)
    zeros = jnp.zeros((8, HD), F32)
    bias_qkv = jnp.concatenate([chosen[:, 0:HD], zeros, chosen[:, HD : 2 * HD]], axis=1)
    bias_qkv = bias_qkv[:, None, :]
    bias_up = chosen[:, 8 * HD : 12 * HD][:, None, :]
    gain_one, gain_two = feature(4), feature(6)

    with jax.named_scope("project"):
        packed = pl.pallas_call(
            qkv_kernel,
            out_shape=sds((2, 8, 3 * span, 2 * HD)),
            in_specs=[smem()] + [vmem()] * 7,
            out_specs=vmem(),
            compiler_params=params(),
            cost_estimate=took(5),
        )(me, x_rows, bias_qkv, *qkv_parts)

    def exchange(block):
        flat = block.reshape((16,) + block.shape[2:])
        return lax.all_to_all(flat, PLANE, 0, 0, tiled=False)

    packed, *down_begun = tie(packed, *down_begun)
    *down_near, head, tail = ring_finish(down_block, *down_begun, "x")
    qkv, *up_halves = tie(exchange(packed), *ring_halves(*up_begun, "z"))
    up_parts = (up_block, *up_begun, *ring_forward(*up_halves, "z"))
    per = Q_BLOCKS
    chunk = per * span
    steps = 16 // per
    length = 16 * span
    with jax.named_scope("attend"):
        ctx_heads, lse = pl.pallas_call(
            functools.partial(attend_kernel, rows=span),
            grid=(steps,),
            out_shape=(sds((16, span, 2 * HD)), sds((2, 8, length), F32)),
            in_specs=[
                pl.BlockSpec((per, 3 * span, 2 * HD), lambda i: (i, 0, 0)),
                pl.BlockSpec((16, 3 * span, 2 * HD), lambda i: (0, 0, 0)),
            ],
            out_specs=(
                pl.BlockSpec((per, span, 2 * HD), lambda i: (i, 0, 0)),
                pl.BlockSpec((2, 8, chunk), lambda i: (0, 0, i)),
            ),
            compiler_params=params("arbitrary"),
            cost_estimate=took(11),
        )(qkv, qkv)
    ctx_heads, head, tail = tie(ctx_heads, head, tail)
    wdown = ring_join(*down_near, head, tail, "x")
    recv = lax.all_to_all(ctx_heads, PLANE, 0, 0, tiled=False)
    recv = recv.reshape(2, 8, span, 2 * HD)
    out_block = hidden // HD
    out_specs = [
        pl.BlockSpec((p.shape[0], 4, 2, HD, 2 * HD), lambda i: (0, 0, 0, out_block, 0))
        for p in up_parts
    ]
    message_shapes = [sds(p.shape) for p in up_parts]
    with jax.named_scope("out_project"):
        ctx, own, other = pl.pallas_call(
            out_kernel,
            out_shape=(sds((2 * rows, 8 * HD)), sds((rows, width), F32), sds((rows, width))),
            grid=(1,),
            in_specs=[smem(), vmem()] + out_specs,
            out_specs=(vmem(), vmem(), vmem()),
            scratch_shapes=[pltpu.VMEM((2 * rows, width), F32)],
            compiler_params=params("arbitrary"),
            cost_estimate=took(3),
        )(me, recv, *up_parts)
    attended = own + other_core(other).astype(F32)
    resid_one = mine + attended + feature(2)
    normed_one, norm_first, inverse_first = norm_forward(resid_one, gain_one, feature(5))
    normed_low = normed_one.astype(BF16)
    n_rows = jnp.concatenate([normed_low, other_core(normed_low)], axis=0)

    up_specs = [
        pl.BlockSpec(
            (p.shape[0], 1, 1, hidden, 2 * HD), lambda t, at: (0, t // 2, t % 2, 0, 0)
        )
        for p in up_parts
    ]
    down_spec = pl.BlockSpec(
        (2, 1, 1, 4, hidden, 2 * HD),
        lambda t, at: (0, (t % 2) ^ at[XHI], away(at, Y, t // 2), 0, 0, 0),
    )
    whole_spec = pl.BlockSpec((2 * rows, width), lambda t, at: (0, 0))
    cols_spec = pl.BlockSpec((2 * rows, hidden), lambda t, at: (0, t))
    half_spec = pl.BlockSpec((rows, width), lambda t, at: (0, 0))
    bias_spec = pl.BlockSpec((1, 1, hidden), lambda t, at: (t, 0, 0))
    with jax.named_scope("feed_forward"):
        active, slope, own, other = pl.pallas_call(
            ffn_kernel,
            grid_spec=pltpu.PrefetchScalarGridSpec(
                num_scalar_prefetch=1,
                grid=(8,),
                in_specs=[whole_spec] + up_specs + [down_spec, bias_spec],
                out_specs=(cols_spec, cols_spec, half_spec, half_spec),
                scratch_shapes=[pltpu.VMEM((2 * rows, width), F32)],
            ),
            out_shape=(
                sds((2 * rows, 8 * hidden)),
                sds((2 * rows, 8 * hidden)),
                sds((rows, width), F32),
                sds((rows, width)),
            ),
            compiler_params=params("arbitrary"),
            cost_estimate=took(14),
        )(me, n_rows, *up_parts, wdown, bias_up)
    mixed = own + other_core(other).astype(F32)
    resid_two = normed_one + mixed + feature(3)
    final, norm_second, inverse_second = norm_forward(resid_two, gain_two, feature(7))
    output = dims(final.astype(BF16), order, 1, 1).astype(BF16)
    grad_two, part_gain_mlp, part_shift_mlp = norm_backward(
        grad_final, norm_second, inverse_second, gain_two
    )
    grad_low = grad_two.astype(BF16)
    g_rows = jnp.concatenate([grad_low, other_core(grad_low)], axis=0)
    with jax.named_scope("feed_forward_back"):
        *grad_up, grad_down, part_up, own, other = pl.pallas_call(
            ffn_back_kernel,
            grid_spec=pltpu.PrefetchScalarGridSpec(
                num_scalar_prefetch=1,
                grid=(8,),
                in_specs=[whole_spec] * 2 + up_specs + [down_spec, cols_spec, cols_spec],
                out_specs=(*up_specs, down_spec, bias_spec, half_spec, half_spec),
                scratch_shapes=[pltpu.VMEM((2 * rows, width), F32)],
            ),
            out_shape=(
                *message_shapes,
                sds(wdown.shape),
                sds((8, 1, hidden), F32),
                sds((rows, width), F32),
                sds((rows, width)),
            ),
            compiler_params=params("arbitrary"),
            cost_estimate=took(20),
        )(me, n_rows, g_rows, *up_parts, wdown, active, slope)
    grad_mid = grad_two + (own + other_core(other).astype(F32))
    grad_one, part_gain_attn, part_shift_attn = norm_backward(
        grad_mid, norm_first, inverse_first, gain_one
    )
    grad_low = grad_one.astype(BF16)
    g_rows = jnp.concatenate([grad_low, other_core(grad_low)], axis=0)
    with jax.named_scope("out_project_back"):
        dctx, *grad_up = pl.pallas_call(
            out_back_kernel,
            grid=(1,),
            out_shape=(sds((2, 8, span, 2 * HD)), *message_shapes),
            in_specs=[smem(), vmem(), vmem()]
            + out_specs
            + [pl.BlockSpec(memory_space=pl.ANY)] * 5,
            out_specs=(vmem(), *out_specs),
            input_output_aliases={8 + i: 1 + i for i in range(5)},
            compiler_params=params("arbitrary"),
            cost_estimate=took(4),
        )(me, g_rows, ctx, *up_parts, *grad_up)
    dctx, grad_down = tie(exchange(dctx), grad_down)
    down_begun = reduce_start(cross_messages(grad_down), "x")
    up_begun = reduce_start(grad_up, "z")
    with jax.named_scope("attend_back"):
        dq, dkv = pl.pallas_call(
            functools.partial(attend_back_kernel, rows=span),
            grid=(steps,),
            out_shape=(sds((16, span, 2 * HD)), sds((16, 2 * span, 2 * HD))),
            in_specs=[
                pl.BlockSpec((per, 3 * span, 2 * HD), lambda i: (i, 0, 0)),
                pl.BlockSpec((16, 3 * span, 2 * HD), lambda i: (0, 0, 0)),
                pl.BlockSpec((per, span, 2 * HD), lambda i: (i, 0, 0)),
                pl.BlockSpec((per, span, 2 * HD), lambda i: (i, 0, 0)),
                pl.BlockSpec((2, 8, chunk), lambda i: (0, 0, i)),
            ],
            out_specs=(
                pl.BlockSpec((per, span, 2 * HD), lambda i: (i, 0, 0)),
                pl.BlockSpec((16, 2 * span, 2 * HD), lambda i: (0, 0, 0)),
            ),
            scratch_shapes=[pltpu.VMEM((length, 2 * HD), F32)] * 2,
            compiler_params=params("arbitrary"),
            cost_estimate=took(18),
        )(qkv, qkv, ctx_heads, dctx, lse)
    dq, *begun = tie(dq, *down_begun, *up_begun)
    dqkv = exchange(jnp.concatenate([dq, dkv], axis=1)[None])
    down_sum = reduce_end(reduce_middle(begun[0:5], "x"), "x")
    up_sum = reduce_end(reduce_middle(begun[5:10], "z"), "z")
    dqkv = dqkv.reshape(2, 8, 3 * span, 2 * HD)
    ups = part_up.reshape(4, 2, 4, HD).transpose(0, 2, 1, 3).reshape(4, 1, 4, 2 * HD)
    nothing = jnp.zeros_like(ups)
    ups = jnp.concatenate(
        [jnp.where(first_core, ups, nothing), jnp.where(first_core, nothing, ups)], axis=1
    )
    six = jnp.stack(
        [
            jnp.sum(grad_one, axis=0), jnp.sum(grad_two, axis=0),
            part_gain_attn, part_shift_attn, part_gain_mlp, part_shift_mlp,
        ]
    ).reshape(6, 4, 2, 2 * HD).transpose(1, 2, 0, 3)
    vec_rows = jnp.concatenate(
        [jnp.zeros((4, 2, 2, 2 * HD), F32), six, ups, jnp.zeros((4, 2, 4, 2 * HD), F32)], axis=2
    )
    with jax.named_scope("project_back"):
        part, far = sds((2, 4, 2, 3 * HD + 16, 2 * HD)), sds((1, 4, 2, 3 * HD + 16, 2 * HD))
        *grad_qkv, own, other = pl.pallas_call(
            qkv_back_kernel,
            out_shape=(
                part, part, part, far, far, sds((rows, width), F32), sds((rows, width)),
            ),
            in_specs=[smem()] + [vmem()] * 8,
            out_specs=(vmem(),) * 7,
            scratch_shapes=[pltpu.VMEM((2 * rows, width), F32)],
            compiler_params=params(),
            cost_estimate=took(8),
        )(me, dqkv, x_rows, vec_rows, *qkv_parts)
    own, other, down_sum, up_sum = tie(own, other, down_sum, up_sum)
    input_sum = own + other_core(other).astype(F32)
    grad_tokens = lax.dot_general(
        grad_one + input_sum, order.astype(F32), (((1,), (1,)), ((), ())),
        precision=lax.Precision.HIGH,
    )
    down_begun = reduce_start(ring_messages(down_sum), "y")
    begun = tie(*reduce_start(grad_qkv, "z"), *down_begun, grad_tokens)
    qkv_sum = reduce_end(reduce_middle(begun[0:5], "z"), "z")
    down_begun, grad_tokens = begun[5:10], begun[10]
    down_sum = reduce_end(reduce_middle(down_begun, "y"), "y")
    got_up = plane_reduce(up_sum).astype(BF16)
    got_down = direct_reduce(down_sum, "z")
    got_qkv = plane_reduce(qkv_sum)
    final_rows = jnp.concatenate([got_qkv.astype(BF16), got_up, got_down], axis=0)
    swapped = other_core(final_rows)
    with jax.named_scope("join"):
        square = sds((HD, 2 * HD), F32)
        *weights, g_out, g_up, g_down, vecs = pl.pallas_call(
            join_kernel,
            out_shape=(
                square, square, square, square,
                sds((HD, 2 * hidden), F32),
                sds((HD, 2 * hidden), F32),
                sds((16, HD), F32),
            ),
            in_specs=[smem(), vmem(), vmem()],
            out_specs=(vmem(),) * 7,
            compiler_params=params(),
            cost_estimate=took(2),
        )(me, final_rows, swapped)
    return (
        output.reshape(seqs, span, width),
        grad_tokens.reshape(seqs, span, width),
        *weights,
        g_out.T,
        g_up,
        g_down.T,
        vecs[0],
        vecs[1],
        vecs[2],
        vecs[8:12].reshape(4 * HD),
        vecs[3],
        vecs[4],
        vecs[5],
        vecs[6],
        vecs[7],
    )


def solution(mesh):
    fine = Mesh(mesh.devices.reshape(4, 2, 2, 4, 2), ("z", "core", "seq", "y", "xhi"))
    owners, tensor = ("z", "core", "seq"), ("y", "xhi")
    tokens = P(("z", "core"), ("seq", "y", "xhi"), None)
    columns, by_rows, vector = P(owners, tensor), P(tensor, owners), P(owners)
    weights = (columns, columns, columns, by_rows, columns, by_rows)
    return jax.shard_map(
        local,
        mesh=fine,
        in_specs=(tokens,) + weights + (vector,) * 9 + (tokens,),
        out_specs=(tokens, tokens) + weights + (vector,) * 9,
        check_vma=False,
    )
```

```python
import functools

import jax
import jax.numpy as jnp
from jax import lax
from jax.experimental import pallas as pl
from jax.experimental.pallas import tpu as pltpu
from jax.sharding import Mesh, PartitionSpec as P

HD = 64
EPS = 1e-05
F32 = jnp.float32
BF16 = jnp.bfloat16
HIGHEST = lax.Precision.HIGHEST
VMEM_LIMIT = 56 * 1024 * 1024
Q_BLOCKS = 4
PLANE = ("seq", "y", "xhi")


def dims(a, b, ca, cb):
    return lax.dot_general(a, b, (((ca,), (cb,)), ((), ())), preferred_element_type=F32)


def shift4(by):
    return [(i, (i + by) % 4) for i in range(4)]


def flip(seq_too, xhi_too):
    return [
        (seq * 2 + xhi, (seq ^ seq_too) * 2 + (xhi ^ xhi_too))
        for seq in range(2)
        for xhi in range(2)
    ]


def links(axis):
    if axis == "x":
        return ("seq", "xhi"), flip(1, 0), flip(1, 1)
    return axis, shift4(-1), shift4(1)


def halves(block):
    half = block.shape[0] // 2
    return block[0:half], block[half:]


def ring_begin(block, axis):
    names, one, two = links(axis)
    return lax.ppermute(block, names, one), lax.ppermute(block, names, two)


def ring_halves(first, second, axis):
    if axis == "x":
        return halves(second)[0], halves(first)[1]
    return halves(first)[0], halves(second)[1]


def ring_forward(head, tail, axis):
    names, one, two = links(axis)
    return lax.ppermute(head, names, one), lax.ppermute(tail, names, two)


def ring_finish(block, first, second, axis):
    head, tail = ring_forward(*ring_halves(first, second, axis), axis)
    return block, first, second, head, tail


def ring_join(block, first, second, head, tail, axis):
    if axis == "x":
        whole = jnp.concatenate([block, head, tail, first, second], axis=0)
        return whole.reshape((2, 2) + block.shape)
    whole = jnp.concatenate([block, first, head, tail, second], axis=0)
    return whole.reshape((4,) + block.shape)


def ring_gather(block, axis):
    return ring_join(*ring_finish(block, *ring_begin(block, axis), axis), axis)


def direct_gather(block, axis):
    parts = [block] + [lax.ppermute(block, axis, shift4(-i)) for i in (1, 2, 3)]
    return jnp.stack(parts)


def add(*terms):
    total = terms[0].astype(F32)
    for term in terms[1:]:
        total = total + term.astype(F32)
    return total.astype(BF16)


def ring_messages(block):
    first_head, first_tail = halves(block[1])
    far_head, far_tail = halves(block[2])
    second_head, second_tail = halves(block[3])
    return (
        block[0],
        jnp.concatenate([far_head, first_tail], axis=0),
        jnp.concatenate([second_head, far_tail], axis=0),
        first_head,
        second_tail,
    )


def cross_messages(block):
    first_head, first_tail = halves(block[1, 0])
    far_head, far_tail = halves(block[0, 1])
    second_head, second_tail = halves(block[1, 1])
    return (
        block[0, 0],
        jnp.concatenate([far_head, first_head], axis=0),
        jnp.concatenate([far_tail, second_tail], axis=0),
        first_tail,
        second_head,
    )


def reduce_ways(axis):
    names, one, two = links(axis)
    return (names, one, two) if axis == "x" else (names, two, one)


def reduce_start(messages, axis):
    names, to_first, to_second = reduce_ways(axis)
    own, a, b, first, second = messages
    return own, lax.ppermute(a, names, to_first), lax.ppermute(b, names, to_second), first, second


def reduce_middle(begun, axis):
    own, a, b, first, second = begun
    (a_head, a_tail), (b_head, b_tail) = halves(a), halves(b)
    if axis == "x":
        return own, a_tail, b_tail, add(first, b_head), add(second, a_head)
    return own, b_head, a_tail, add(first, a_head), add(second, b_tail)


def reduce_send(middle, axis):
    names, to_first, to_second = reduce_ways(axis)
    own, near_head, near_tail, first, second = middle
    first = lax.ppermute(first, names, to_first)
    second = lax.ppermute(second, names, to_second)
    if axis == "x":
        first, second = second, first
    return own, near_head, near_tail, first, second


def reduce_join(sent):
    own, near_head, near_tail, far_head, far_tail = sent
    head, tail = halves(own)
    return jnp.concatenate([add(head, near_head, far_head), add(tail, near_tail, far_tail)], axis=0)


def reduce_end(middle, axis):
    return reduce_join(reduce_send(middle, axis))


def tie(*values):
    return lax.optimization_barrier(values)


def direct_reduce(block, axis):
    parts = [block[0]] + [lax.ppermute(block[i], axis, shift4(i)) for i in (1, 2, 3)]
    return add(*parts)


def plane_gather(copies):
    got = lax.all_to_all(copies, PLANE, 0, 0, tiled=False)
    return got.reshape((2, 4, 2) + copies.shape[1:])


def plane_reduce(block):
    flat = block.reshape((16,) + block.shape[-2:])
    got = lax.all_to_all(flat, PLANE, 0, 0, tiled=False)
    return jnp.sum(got.astype(F32), axis=0)


def other_core(block):
    return lax.ppermute(block, "core", [(0, 1), (1, 0)])


def params(*semantics):
    return pltpu.CompilerParams(
        vmem_limit_bytes=VMEM_LIMIT,
        dimension_semantics=semantics if semantics else None,
    )


def vmem():
    return pl.BlockSpec(memory_space=pltpu.VMEM)


def smem():
    return pl.BlockSpec(memory_space=pltpu.SMEM)


CORE, Z, SEQ, Y, XHI = range(5)


def away(me, axis, at):
    return lax.rem(at + 4 - me[axis], 4)


def ring_rows(parts, step, y, x, size):
    if step == 2:
        a, b = parts[3][0, y, x, 0:size], parts[4][0, y, x, 0:size]
    else:
        ref = parts[{0: 0, 1: 1, 3: 2}[step]]
        a, b = ref[0, y, x, 0:size], ref[1, y, x, 0:size]
    return jnp.concatenate([a, b], axis=1)


def features_of(me, step):
    return pl.ds(pl.multiple_of(lax.rem(me[Z] + step, 4) * 256, 256), 256)


def put(messages, step, y, x, rows, value):
    for s in range(2):
        name, at = {
            (0, 0): (0, 0), (0, 1): (0, 1), (1, 0): (3, 0), (1, 1): (1, 1),
            (2, 0): (1, 0), (2, 1): (2, 1), (3, 0): (2, 0), (3, 1): (4, 0),
        }[step, s]
        messages[name][at, y, x, rows] = value[:, s * 128 : (s + 1) * 128].astype(BF16)


def split_kernel(me_ref, wq, wk, wv, wo, wup, wdown, small, keep_ref, give_ref):
    first = me_ref[CORE] == 0
    at = 0
    for ref in (wq, wk, wv, wo, wup, wdown):
        value = jnp.transpose(ref[...].astype(F32))
        half = value.shape[0] // 2
        a, b = value[0:half], value[half:]
        keep_ref[at : at + half] = jnp.where(first, a, b).astype(BF16)
        give_ref[at : at + half] = jnp.where(first, b, a).astype(BF16)
        at += half
    keep_ref[at:] = small[...]
    give_ref[at:] = small[...]


def join_kernel(me_ref, mine_ref, other_ref, dq, dk, dv, do, dup, ddown, vec_ref):
    first = me_ref[CORE] == 0
    hidden = ddown.shape[1] // 2

    def rows(start, size):
        a = mine_ref[start : start + size].astype(F32)
        b = other_ref[start : start + size].astype(F32)
        zero, one = jnp.where(first, a, b), jnp.where(first, b, a)
        zero = jnp.where(first, zero[:, 0:HD], zero[:, HD:])
        one = jnp.where(first, one[:, 0:HD], one[:, HD:])
        return zero, one

    at = 0
    plan = ((dq, HD), (dk, HD), (dv, HD), (vec_ref, 16), (dup, hidden), (do, HD), (ddown, hidden))
    for ref, size in plan:
        zero, one = rows(at, size)
        at += size
        if size == 16:
            ref[...] = zero + one
        else:
            ref[...] = jnp.transpose(jnp.concatenate([zero, one], axis=0))


def qkv_kernel(me_ref, x_ref, bias_ref, w0, w1, w2, w3, w4, out_ref):
    parts = (w0, w1, w2, w3, w4)
    core = me_ref[CORE]
    rows = [x_ref[:, features_of(me_ref, step)] for step in range(4)]
    span = x_ref.shape[0] // 4
    for y in range(4):
        for x in range(2):
            made = bias_ref[y * 2 + x]
            for step in range(4):
                made = made + dims(rows[step], ring_rows(parts, step, y, x, 3 * HD), 1, 1)
            made = made.astype(BF16)
            to = y * 2 + x
            for half in range(2):
                top = made[half * 2 * span : half * 2 * span + span]
                low = made[half * 2 * span + span : (half + 1) * 2 * span]
                packed = jnp.concatenate(
                    [
                        jnp.concatenate(
                            [top[:, i * HD : (i + 1) * HD], low[:, i * HD : (i + 1) * HD]],
                            axis=1,
                        )
                        for i in range(3)
                    ],
                    axis=0,
                )
                out_ref[core ^ half, to] = packed


def attend_kernel(q_ref, kv_ref, ctx_ref, lse_ref, *, rows):
    chunk = q_ref.shape[0] * rows
    length = kv_ref.shape[0] * rows
    queries = q_ref[:, 0:rows].reshape(chunk, 2 * HD) * jnp.bfloat16(0.125)
    keys = kv_ref[:, rows : 2 * rows].reshape(length, 2 * HD)
    values = kv_ref[:, 2 * rows : 3 * rows].reshape(length, 2 * HD)
    lane = lax.broadcasted_iota(jnp.int32, (chunk, 2 * HD), 1)
    parts = []
    for s in range(2):
        mine = (lane < HD) if s == 0 else (lane >= HD)
        picked = jnp.where(mine, queries, jnp.bfloat16(0))
        scores = dims(picked, keys, 1, 1)
        top = jnp.max(scores, axis=1, keepdims=True)
        weights = jnp.exp(scores - top)
        total = jnp.sum(weights, axis=1, keepdims=True)
        mixed = dims(weights.astype(BF16), values, 1, 0)
        parts.append(mixed / total)
        lse = jnp.broadcast_to(top + jnp.log(total), (chunk, 128))
        lse_ref[s] = jnp.transpose(lse)[0:8]
    ctx = jnp.where(lane < HD, parts[0], parts[1])
    ctx_ref[...] = ctx.astype(BF16).reshape(ctx_ref.shape)


def attend_back_kernel(
    q_ref, kv_ref, ctx_ref, dctx_ref, lse_ref, dq_ref, dkv_ref, dk_acc, dv_acc, *, rows
):
    step = pl.program_id(0)
    chunk = q_ref.shape[0] * rows
    length = kv_ref.shape[0] * rows
    queries = q_ref[:, 0:rows].reshape(chunk, 2 * HD) * jnp.bfloat16(0.125)
    grads = dctx_ref[...].reshape(chunk, 2 * HD)
    context = ctx_ref[...].reshape(chunk, 2 * HD)
    keys = kv_ref[:, rows : 2 * rows].reshape(length, 2 * HD)
    values = kv_ref[:, 2 * rows : 3 * rows].reshape(length, 2 * HD)
    lane = lax.broadcasted_iota(jnp.int32, (chunk, 2 * HD), 1)
    long_lane = lax.broadcasted_iota(jnp.int32, (length, 2 * HD), 1)
    both = grads.astype(F32) * context.astype(F32)

    @pl.when(step == 0)
    def _():
        dk_acc[...] = jnp.zeros_like(dk_acc)
        dv_acc[...] = jnp.zeros_like(dv_acc)

    dq_parts, dk_parts, dv_parts = [], [], []
    for s in range(2):
        mine = (lane < HD) if s == 0 else (lane >= HD)
        q_mine = jnp.where(mine, queries, jnp.bfloat16(0))
        g_mine = jnp.where(mine, grads, jnp.bfloat16(0))
        delta = jnp.sum(jnp.where(mine, both, 0.0), axis=1, keepdims=True)
        delta = jnp.transpose(jnp.broadcast_to(delta, (chunk, 128)))[0:1]
        scores = dims(keys, q_mine, 1, 1)
        exact = jnp.exp(scores - lse_ref[s, 0:1])
        grad_probs = dims(values, g_mine, 1, 1)
        grad_scores = (exact * (grad_probs - delta)).astype(BF16)
        dq_parts.append(dims(grad_scores, keys, 0, 0))
        dk_parts.append(dims(grad_scores, queries, 1, 0))
        dv_parts.append(dims(exact.astype(BF16), grads, 1, 0))
    dq = jnp.where(lane < HD, dq_parts[0], dq_parts[1]) * 0.125
    dq_ref[...] = dq.astype(BF16).reshape(dq_ref.shape)
    dk_acc[...] += jnp.where(long_lane < HD, dk_parts[0], dk_parts[1])
    dv_acc[...] += jnp.where(long_lane < HD, dv_parts[0], dv_parts[1])

    @pl.when(step == pl.num_programs(0) - 1)
    def _():
        shape = (kv_ref.shape[0], rows, 2 * HD)
        dkv_ref[:, 0:rows] = dk_acc[...].astype(BF16).reshape(shape)
        dkv_ref[:, rows : 2 * rows] = dv_acc[...].astype(BF16).reshape(shape)


def unpack_rows(top, low):
    return jnp.concatenate([top[:, 0:HD], top[:, HD:], low[:, 0:HD], low[:, HD:]], axis=0)


def out_rows(parts, step):
    return jnp.concatenate(
        [ring_rows(parts, step, y, x, HD) for y in range(4) for x in range(2)], axis=0
    )


def out_kernel(me_ref, recv_ref, w0, w1, w2, w3, w4, ctx_ref, own_ref, other_ref, acc):
    core = me_ref[CORE]
    parts = (w0, w1, w2, w3, w4)
    pieces = [unpack_rows(recv_ref[core, at], recv_ref[1 - core, at]) for at in range(8)]
    ctx = jnp.concatenate(pieces, axis=1)
    ctx_ref[...] = ctx
    for step in range(4):
        acc[:, features_of(me_ref, step)] = dims(ctx, out_rows(parts, step), 1, 0)
    half = ctx.shape[0] // 2
    own_ref[...] = acc[0:half]
    other_ref[...] = acc[half:].astype(BF16)


def wide_down(ref, me):
    return jnp.concatenate(
        [ref[s ^ me[SEQ], 0, 0, away(me, Z, z)] for z in range(4) for s in range(2)], axis=1
    )


def ffn_kernel(
    me_ref, n_ref, w0, w1, w2, w3, w4, wdown_ref, bias_ref,
    active_ref, slope_ref, own_ref, other_ref, acc,
):
    step = pl.program_id(0)
    parts = (w0, w1, w2, w3, w4)
    hidden = bias_ref.shape[2]
    pre = bias_ref[0]
    for turn in range(4):
        rows = n_ref[:, features_of(me_ref, turn)]
        pre = pre + dims(rows, ring_rows(parts, turn, 0, 0, hidden), 1, 1)
    cdf = 0.5 * (1.0 + lax.erf(pre * 0.7071067811865476))
    pdf = jnp.exp(-0.5 * pre * pre) * 0.3989422804014327
    active = (pre * cdf).astype(BF16)
    active_ref[...] = active
    slope_ref[...] = (cdf + pre * pdf).astype(BF16)
    made = dims(active, wide_down(wdown_ref, me_ref), 1, 0)

    @pl.when(step == 0)
    def _():
        acc[...] = made

    @pl.when(step > 0)
    def _():
        acc[...] += made

    @pl.when(step == pl.num_programs(0) - 1)
    def _():
        half = acc.shape[0] // 2
        own_ref[...] = acc[0:half]
        other_ref[...] = acc[half:].astype(BF16)


def ffn_back_kernel(
    me_ref, n_ref, g_ref, w0, w1, w2, w3, w4, wdown_ref, active_ref, slope_ref,
    d0, d1, d2, d3, d4, ddown_ref, bias_ref, own_ref, other_ref, acc,
):
    step = pl.program_id(0)
    parts, messages = (w0, w1, w2, w3, w4), (d0, d1, d2, d3, d4)
    grads = g_ref[...]
    active = active_ref[...]
    hidden = active.shape[1]
    grad = dims(active, grads, 0, 0).astype(BF16)
    for z in range(4):
        for s in range(2):
            at = (z * 2 + s) * 128
            ddown_ref[s ^ me_ref[SEQ], 0, 0, away(me_ref, Z, z)] = grad[:, at : at + 128]
    grad_pre = dims(grads, wide_down(wdown_ref, me_ref), 1, 1) * slope_ref[...].astype(F32)
    bias_ref[0] = jnp.sum(grad_pre, axis=0, keepdims=True)
    low = grad_pre.astype(BF16)

    @pl.when(step == 0)
    def _():
        acc[...] = jnp.zeros_like(acc)

    for turn in range(4):
        at = features_of(me_ref, turn)
        put(messages, turn, 0, 0, slice(0, hidden), dims(low, n_ref[:, at], 0, 0))
        acc[:, at] += dims(low, ring_rows(parts, turn, 0, 0, hidden), 1, 0)

    @pl.when(step == pl.num_programs(0) - 1)
    def _():
        half = acc.shape[0] // 2
        own_ref[...] = acc[0:half]
        other_ref[...] = acc[half:].astype(BF16)


def out_back_kernel(
    me_ref, g_ref, ctx_ref, w0, w1, w2, w3, w4, u0, u1, u2, u3, u4,
    dctx_ref, d0, d1, d2, d3, d4,
):
    core = me_ref[CORE]
    parts, messages = (w0, w1, w2, w3, w4), (d0, d1, d2, d3, d4)
    span = g_ref.shape[0] // 4
    ctx = ctx_ref[...]
    made = None
    for step in range(4):
        grads = g_ref[:, features_of(me_ref, step)]
        part = dims(grads, out_rows(parts, step), 1, 1)
        made = part if made is None else made + part
        grad = dims(ctx, grads, 0, 0)
        for y in range(4):
            for x in range(2):
                at = (y * 2 + x) * HD
                put(messages, step, y, x, slice(0, HD), grad[at : at + HD])
    made = made.astype(BF16)
    for to in range(8):
        piece = made[:, to * HD : (to + 1) * HD]
        for half in range(2):
            base = half * 2 * span
            dctx_ref[core ^ half, to] = jnp.concatenate(
                [piece[base : base + span], piece[base + span : base + 2 * span]], axis=1
            )


def qkv_back_kernel(
    me_ref, recv_ref, x_ref, vec_ref, w0, w1, w2, w3, w4,
    d0, d1, d2, d3, d4, own_ref, other_ref, acc,
):
    core = me_ref[CORE]
    parts, grads = (w0, w1, w2, w3, w4), (d0, d1, d2, d3, d4)
    rows = [x_ref[:, features_of(me_ref, step)] for step in range(4)]
    span = x_ref.shape[0] // 4
    half = x_ref.shape[0] // 2

    sums = []
    totals = [None] * 4
    for y in range(4):
        for x in range(2):
            at = y * 2 + x
            top, low = recv_ref[core, at], recv_ref[1 - core, at]
            made = jnp.concatenate(
                [
                    unpack_rows(
                        top[i * span : (i + 1) * span], low[i * span : (i + 1) * span]
                    )
                    for i in range(3)
                ],
                axis=1,
            )
            sums.append(jnp.sum(made.astype(F32), axis=0, keepdims=True))
            for step in range(4):
                put(grads, step, y, x, slice(0, 3 * HD), dims(made, rows[step], 0, 0))
                part = dims(made, ring_rows(parts, step, y, x, 3 * HD), 1, 0)
                totals[step] = part if totals[step] is None else totals[step] + part
    for step in range(4):
        acc[:, features_of(me_ref, step)] = totals[step]
    own_ref[...] = acc[0:half]
    other_ref[...] = acc[half:].astype(BF16)
    zeros = jnp.zeros((14, 2 * HD), F32)
    twos = []
    for z in range(4):
        a, b = sums[2 * z], sums[2 * z + 1]
        bias_q = jnp.concatenate([a[:, 0:HD], b[:, 0:HD]], axis=1)
        bias_v = jnp.concatenate([a[:, 2 * HD :], b[:, 2 * HD :]], axis=1)
        twos.append(jnp.concatenate([bias_q, bias_v, zeros], axis=0))
    for step in range(4):
        z_abs = lax.rem(me_ref[Z] + step, 4)
        two = twos[3]
        for z in range(3):
            two = jnp.where(z_abs == z, twos[z], two)
        block = jnp.concatenate(
            [vec_ref[z_abs, s] + jnp.where(core == s, two, 0.0) for s in range(2)], axis=1
        )
        for y in range(4):
            for x in range(2):
                put(grads, step, y, x, slice(3 * HD, 3 * HD + 16), block)


def norm_forward(hidden, gain, shift):
    centre = jnp.mean(hidden, axis=-1, keepdims=True)
    centered = hidden - centre
    inverse = lax.rsqrt(jnp.mean(centered * centered, axis=-1, keepdims=True) + EPS)
    normed = centered * inverse
    return (normed * gain + shift, normed, inverse)


def norm_backward(grad_in, normed, inverse, gain):
    scaled = grad_in * gain
    inner_term = (
        scaled
        - jnp.mean(scaled, axis=-1, keepdims=True)
        - normed * jnp.mean(scaled * normed, axis=-1, keepdims=True)
    )
    return (
        inverse * inner_term,
        jnp.sum(grad_in * normed, axis=0),
        jnp.sum(grad_in, axis=0),
    )


def sds(shape, dtype=BF16):
    return jax.ShapeDtypeStruct(shape, dtype)


def took(us):
    return pl.CostEstimate(flops=int(us * 1.15e9), bytes_accessed=1 << 20, transcendentals=0)


def local(
    tokens, w_query, w_key, w_value, w_out, w_up, w_down,
    b_query, b_value, b_out, b_up, b_down,
    gain_attn, shift_attn, gain_mlp, shift_mlp, cotangent,
):
    core = lax.axis_index("core")
    me_z, me_s = lax.axis_index("z"), lax.axis_index("seq")
    me_y, me_x = lax.axis_index("y"), lax.axis_index("xhi")
    first_core = core == 0
    me = jnp.stack([core, me_z, me_s, me_y, me_x]).astype(jnp.int32)
    seqs, span, width = tokens.shape
    rows = seqs * span
    hidden = w_up.shape[1] // 2

    at = jnp.arange(width, dtype=jnp.int32)
    z_of, c_of, s_of, i_of = at // 256, (at // 128) % 2, (at // 64) % 2, at % 64
    stored = z_of * 256 + s_of * 128 + c_of * 64 + i_of
    order = (stored[:, None] == at[None, :]).astype(BF16)

    small = jnp.stack(
        [b_query, b_value, b_out, b_down, gain_attn, shift_attn, gain_mlp, shift_mlp]
    )
    small = jnp.concatenate([small, b_up.reshape(4, HD), jnp.zeros((4, HD), BF16)], axis=0)
    shard_rows = 4 * HD + 2 * hidden + 16
    with jax.named_scope("split"):
        keep, give = pl.pallas_call(
            split_kernel,
            out_shape=(sds((shard_rows, HD)),) * 2,
            in_specs=[smem()] + [vmem()] * 7,
            out_specs=(vmem(), vmem()),
            compiler_params=params(),
            cost_estimate=took(2),
        )(me, w_query, w_key, w_value, w_out.T, w_up, w_down.T, small)
    got = other_core(give)
    shard = jnp.where(
        first_core,
        jnp.concatenate([keep, got], axis=1),
        jnp.concatenate([got, keep], axis=1),
    )
    at_o, at_up, at_down, at_vec = 3 * HD, 4 * HD, 4 * HD + hidden, 4 * HD + 2 * hidden
    qkv_shard = jnp.concatenate([shard[0:at_o], shard[at_vec:]], axis=0)
    up_shard = jnp.concatenate([shard[at_up:at_down], shard[at_o:at_up]])
    sixteen = lambda part: jnp.broadcast_to(part[None], (16,) + part.shape)
    qkv_block = plane_gather(sixteen(qkv_shard))

    both_in = jnp.concatenate([tokens.reshape(rows, width), cotangent.reshape(rows, width)], axis=0)
    both_in = dims(both_in, order, 1, 0)
    mine = both_in[0:rows]
    grad_final = both_in[rows:]
    mine_low = mine.astype(BF16)
    x_rows = jnp.concatenate([mine_low, other_core(mine_low)], axis=0)

    x_rows, down_shard = tie(x_rows, shard[at_down:at_vec])
    down_line = direct_gather(down_shard, "z")
    qkv_block, down_line, up_shard = tie(qkv_block, down_line, up_shard)
    qkv_begun, down_begun = ring_begin(qkv_block, "z"), ring_begin(down_line, "y")
    up_block = plane_gather(sixteen(up_shard))
    begun = tie(*qkv_begun, *down_begun)
    *near, head, tail = ring_finish(qkv_block, *begun[0:2], "z")
    down_block = ring_join(*ring_finish(down_line, *begun[2:4], "y"), "y")
    head, tail, up_block = tie(head, tail, up_block)
    qkv_parts = (*near, head, tail)
    up_begun, down_begun = ring_begin(up_block, "z"), ring_begin(down_block, "x")

    fours = jnp.arange(4, dtype=jnp.int32)
    turn = ((fours[:, None] - me_z) % 4 == fours[None, :]).astype(F32)
    ring = [p[:, 0, 0, 3 * HD :, :].reshape(-1) for p in qkv_parts]
    vec = jnp.concatenate([ring[0], ring[1], ring[3], ring[4], ring[2]])
    vec = vec.reshape(4, 4096).astype(F32)
    vec = jnp.dot(turn, vec, precision=HIGHEST).reshape(4, 2, 16, 2 * HD)
    feature = lambda i: vec[:, :, i, :].reshape(width)
    chosen = jnp.where(first_core, vec[:, 0], vec[:, 1])
    chosen = chosen.reshape(4, 16, 2, HD).transpose(0, 2, 1, 3).reshape(8, 16 * HD)
    zeros = jnp.zeros((8, HD), F32)
    bias_qkv = jnp.concatenate([chosen[:, 0:HD], zeros, chosen[:, HD : 2 * HD]], axis=1)
    bias_qkv = bias_qkv[:, None, :]
    bias_up = chosen[:, 8 * HD : 12 * HD][:, None, :]
    gain_one, gain_two = feature(4), feature(6)

    with jax.named_scope("project"):
        packed = pl.pallas_call(
            qkv_kernel,
            out_shape=sds((2, 8, 3 * span, 2 * HD)),
            in_specs=[smem()] + [vmem()] * 7,
            out_specs=vmem(),
            compiler_params=params(),
            cost_estimate=took(5),
        )(me, x_rows, bias_qkv, *qkv_parts)

    def exchange(block):
        flat = block.reshape((16,) + block.shape[2:])
        return lax.all_to_all(flat, PLANE, 0, 0, tiled=False)

    qkv, *parts = tie(
        exchange(packed), *ring_halves(*up_begun, "z"), *ring_halves(*down_begun, "x")
    )
    up_parts = (up_block, *up_begun, *ring_forward(*parts[0:2], "z"))
    down_parts = (down_block, *down_begun, *ring_forward(*parts[2:4], "x"))
    per = Q_BLOCKS
    chunk = per * span
    steps = 16 // per
    length = 16 * span
    with jax.named_scope("attend"):
        ctx_heads, lse = pl.pallas_call(
            functools.partial(attend_kernel, rows=span),
            grid=(steps,),
            out_shape=(sds((16, span, 2 * HD)), sds((2, 8, length), F32)),
            in_specs=[
                pl.BlockSpec((per, 3 * span, 2 * HD), lambda i: (i, 0, 0)),
                pl.BlockSpec((16, 3 * span, 2 * HD), lambda i: (0, 0, 0)),
            ],
            out_specs=(
                pl.BlockSpec((per, span, 2 * HD), lambda i: (i, 0, 0)),
                pl.BlockSpec((2, 8, chunk), lambda i: (0, 0, i)),
            ),
            compiler_params=params("arbitrary"),
            cost_estimate=took(11),
        )(qkv, qkv)
    ctx_heads, head, tail = tie(ctx_heads, *down_parts[3:5])
    wdown = ring_join(*down_parts[0:3], head, tail, "x")
    recv = lax.all_to_all(ctx_heads, PLANE, 0, 0, tiled=False)
    recv = recv.reshape(2, 8, span, 2 * HD)
    out_block = hidden // HD
    out_specs = [
        pl.BlockSpec((p.shape[0], 4, 2, HD, 2 * HD), lambda i: (0, 0, 0, out_block, 0))
        for p in up_parts
    ]
    message_shapes = [sds(p.shape) for p in up_parts]
    with jax.named_scope("out_project"):
        ctx, own, other = pl.pallas_call(
            out_kernel,
            out_shape=(sds((2 * rows, 8 * HD)), sds((rows, width), F32), sds((rows, width))),
            grid=(1,),
            in_specs=[smem(), vmem()] + out_specs,
            out_specs=(vmem(), vmem(), vmem()),
            scratch_shapes=[pltpu.VMEM((2 * rows, width), F32)],
            compiler_params=params("arbitrary"),
            cost_estimate=took(3),
        )(me, recv, *up_parts)
    attended = own + other_core(other).astype(F32)
    resid_one = mine + attended + feature(2)
    normed_one, norm_first, inverse_first = norm_forward(resid_one, gain_one, feature(5))
    normed_low = normed_one.astype(BF16)
    n_rows = jnp.concatenate([normed_low, other_core(normed_low)], axis=0)

    up_specs = [
        pl.BlockSpec(
            (p.shape[0], 1, 1, hidden, 2 * HD), lambda t, at: (0, t // 2, t % 2, 0, 0)
        )
        for p in up_parts
    ]
    down_spec = pl.BlockSpec(
        (2, 1, 1, 4, hidden, 2 * HD),
        lambda t, at: (0, (t % 2) ^ at[XHI], away(at, Y, t // 2), 0, 0, 0),
    )
    whole_spec = pl.BlockSpec((2 * rows, width), lambda t, at: (0, 0))
    cols_spec = pl.BlockSpec((2 * rows, hidden), lambda t, at: (0, t))
    half_spec = pl.BlockSpec((rows, width), lambda t, at: (0, 0))
    bias_spec = pl.BlockSpec((1, 1, hidden), lambda t, at: (t, 0, 0))
    with jax.named_scope("feed_forward"):
        active, slope, own, other = pl.pallas_call(
            ffn_kernel,
            grid_spec=pltpu.PrefetchScalarGridSpec(
                num_scalar_prefetch=1,
                grid=(8,),
                in_specs=[whole_spec] + up_specs + [down_spec, bias_spec],
                out_specs=(cols_spec, cols_spec, half_spec, half_spec),
                scratch_shapes=[pltpu.VMEM((2 * rows, width), F32)],
            ),
            out_shape=(
                sds((2 * rows, 8 * hidden)),
                sds((2 * rows, 8 * hidden)),
                sds((rows, width), F32),
                sds((rows, width)),
            ),
            compiler_params=params("arbitrary"),
            cost_estimate=took(14),
        )(me, n_rows, *up_parts, wdown, bias_up)
    mixed = own + other_core(other).astype(F32)
    resid_two = normed_one + mixed + feature(3)
    final, norm_second, inverse_second = norm_forward(resid_two, gain_two, feature(7))
    output = dims(final.astype(BF16), order, 1, 1).astype(BF16)
    grad_two, part_gain_mlp, part_shift_mlp = norm_backward(
        grad_final, norm_second, inverse_second, gain_two
    )
    grad_low = grad_two.astype(BF16)
    g_rows = jnp.concatenate([grad_low, other_core(grad_low)], axis=0)
    with jax.named_scope("feed_forward_back"):
        *grad_up, grad_down, part_up, own, other = pl.pallas_call(
            ffn_back_kernel,
            grid_spec=pltpu.PrefetchScalarGridSpec(
                num_scalar_prefetch=1,
                grid=(8,),
                in_specs=[whole_spec] * 2 + up_specs + [down_spec, cols_spec, cols_spec],
                out_specs=(*up_specs, down_spec, bias_spec, half_spec, half_spec),
                scratch_shapes=[pltpu.VMEM((2 * rows, width), F32)],
            ),
            out_shape=(
                *message_shapes,
                sds(wdown.shape),
                sds((8, 1, hidden), F32),
                sds((rows, width), F32),
                sds((rows, width)),
            ),
            compiler_params=params("arbitrary"),
            cost_estimate=took(20),
        )(me, n_rows, g_rows, *up_parts, wdown, active, slope)
    grad_mid = grad_two + (own + other_core(other).astype(F32))
    grad_one, part_gain_attn, part_shift_attn = norm_backward(
        grad_mid, norm_first, inverse_first, gain_one
    )
    grad_low = grad_one.astype(BF16)
    g_rows = jnp.concatenate([grad_low, other_core(grad_low)], axis=0)
    with jax.named_scope("out_project_back"):
        dctx, *grad_up = pl.pallas_call(
            out_back_kernel,
            grid=(1,),
            out_shape=(sds((2, 8, span, 2 * HD)), *message_shapes),
            in_specs=[smem(), vmem(), vmem()]
            + out_specs
            + [pl.BlockSpec(memory_space=pl.ANY)] * 5,
            out_specs=(vmem(), *out_specs),
            input_output_aliases={8 + i: 1 + i for i in range(5)},
            compiler_params=params("arbitrary"),
            cost_estimate=took(4),
        )(me, g_rows, ctx, *up_parts, *grad_up)
    dctx, *messages = tie(exchange(dctx), *cross_messages(grad_down))
    down_begun = reduce_start(messages, "x")
    up_begun = reduce_start(grad_up, "z")
    with jax.named_scope("attend_back"):
        dq, dkv = pl.pallas_call(
            functools.partial(attend_back_kernel, rows=span),
            grid=(steps,),
            out_shape=(sds((16, span, 2 * HD)), sds((16, 2 * span, 2 * HD))),
            in_specs=[
                pl.BlockSpec((per, 3 * span, 2 * HD), lambda i: (i, 0, 0)),
                pl.BlockSpec((16, 3 * span, 2 * HD), lambda i: (0, 0, 0)),
                pl.BlockSpec((per, span, 2 * HD), lambda i: (i, 0, 0)),
                pl.BlockSpec((per, span, 2 * HD), lambda i: (i, 0, 0)),
                pl.BlockSpec((2, 8, chunk), lambda i: (0, 0, i)),
            ],
            out_specs=(
                pl.BlockSpec((per, span, 2 * HD), lambda i: (i, 0, 0)),
                pl.BlockSpec((16, 2 * span, 2 * HD), lambda i: (0, 0, 0)),
            ),
            scratch_shapes=[pltpu.VMEM((length, 2 * HD), F32)] * 2,
            compiler_params=params("arbitrary"),
            cost_estimate=took(18),
        )(qkv, qkv, ctx_heads, dctx, lse)
    dq, *up_begun = tie(dq, *up_begun)
    dqkv = exchange(jnp.concatenate([dq, dkv], axis=1)[None])
    begun = tie(*reduce_middle(up_begun, "z"), *down_begun)
    up_sent = reduce_send(begun[0:5], "z")
    down_sent = reduce_send(reduce_middle(begun[5:10], "x"), "x")
    dqkv = dqkv.reshape(2, 8, 3 * span, 2 * HD)
    ups = part_up.reshape(4, 2, 4, HD).transpose(0, 2, 1, 3).reshape(4, 1, 4, 2 * HD)
    nothing = jnp.zeros_like(ups)
    ups = jnp.concatenate(
        [jnp.where(first_core, ups, nothing), jnp.where(first_core, nothing, ups)], axis=1
    )
    six = jnp.stack(
        [
            jnp.sum(grad_one, axis=0), jnp.sum(grad_two, axis=0),
            part_gain_attn, part_shift_attn, part_gain_mlp, part_shift_mlp,
        ]
    ).reshape(6, 4, 2, 2 * HD).transpose(1, 2, 0, 3)
    vec_rows = jnp.concatenate(
        [jnp.zeros((4, 2, 2, 2 * HD), F32), six, ups, jnp.zeros((4, 2, 4, 2 * HD), F32)], axis=2
    )
    with jax.named_scope("project_back"):
        part, far = sds((2, 4, 2, 3 * HD + 16, 2 * HD)), sds((1, 4, 2, 3 * HD + 16, 2 * HD))
        *grad_qkv, own, other = pl.pallas_call(
            qkv_back_kernel,
            out_shape=(
                part, part, part, far, far, sds((rows, width), F32), sds((rows, width)),
            ),
            in_specs=[smem()] + [vmem()] * 8,
            out_specs=(vmem(),) * 7,
            scratch_shapes=[pltpu.VMEM((2 * rows, width), F32)],
            compiler_params=params(),
            cost_estimate=took(8),
        )(me, dqkv, x_rows, vec_rows, *qkv_parts)
    own, other, *sent = tie(own, other, *up_sent, *down_sent)
    up_sum, down_sum = reduce_join(sent[0:5]), reduce_join(sent[5:10])
    input_sum = own + other_core(other).astype(F32)
    grad_tokens = lax.dot_general(
        grad_one + input_sum, order.astype(F32), (((1,), (1,)), ((), ())),
        precision=lax.Precision.HIGH,
    )
    down_begun = reduce_start(ring_messages(down_sum), "y")
    begun = tie(*reduce_start(grad_qkv, "z"), *down_begun, grad_tokens)
    qkv_sum = reduce_end(reduce_middle(begun[0:5], "z"), "z")
    down_begun, grad_tokens = begun[5:10], begun[10]
    down_sum = reduce_end(reduce_middle(down_begun, "y"), "y")
    got_up = plane_reduce(up_sum).astype(BF16)
    got_down = direct_reduce(down_sum, "z")
    got_qkv = plane_reduce(qkv_sum)
    final_rows = jnp.concatenate([got_qkv.astype(BF16), got_up, got_down], axis=0)
    swapped = other_core(final_rows)
    with jax.named_scope("join"):
        square = sds((HD, 2 * HD), F32)
        *weights, g_out, g_up, g_down, vecs = pl.pallas_call(
            join_kernel,
            out_shape=(
                square, square, square, square,
                sds((HD, 2 * hidden), F32),
                sds((HD, 2 * hidden), F32),
                sds((16, HD), F32),
            ),
            in_specs=[smem(), vmem(), vmem()],
            out_specs=(vmem(),) * 7,
            compiler_params=params(),
            cost_estimate=took(2),
        )(me, final_rows, swapped)
    return (
        output.reshape(seqs, span, width),
        grad_tokens.reshape(seqs, span, width),
        *weights,
        g_out.T,
        g_up,
        g_down.T,
        vecs[0],
        vecs[1],
        vecs[2],
        vecs[8:12].reshape(4 * HD),
        vecs[3],
        vecs[4],
        vecs[5],
        vecs[6],
        vecs[7],
    )


def solution(mesh):
    fine = Mesh(mesh.devices.reshape(4, 2, 2, 4, 2), ("z", "core", "seq", "y", "xhi"))
    owners, tensor = ("z", "core", "seq"), ("y", "xhi")
    tokens = P(("z", "core"), ("seq", "y", "xhi"), None)
    columns, by_rows, vector = P(owners, tensor), P(tensor, owners), P(owners)
    weights = (columns, columns, columns, by_rows, columns, by_rows)
    return jax.shard_map(
        local,
        mesh=fine,
        in_specs=(tokens,) + weights + (vector,) * 9 + (tokens,),
        out_specs=(tokens, tokens) + weights + (vector,) * 9,
        check_vma=False,
    )
```

```python
import functools

import jax
import jax.numpy as jnp
from jax import lax
from jax.experimental import pallas as pl
from jax.experimental.pallas import tpu as pltpu
from jax.sharding import Mesh, PartitionSpec as P

HD = 64
EPS = 1e-05
F32 = jnp.float32
BF16 = jnp.bfloat16
HIGHEST = lax.Precision.HIGHEST
VMEM_LIMIT = 56 * 1024 * 1024
Q_BLOCKS = 4
PLANE = ("seq", "y", "xhi")


def dims(a, b, ca, cb):
    return lax.dot_general(a, b, (((ca,), (cb,)), ((), ())), preferred_element_type=F32)


def shift4(by):
    return [(i, (i + by) % 4) for i in range(4)]


def flip(seq_too, xhi_too):
    return [
        (seq * 2 + xhi, (seq ^ seq_too) * 2 + (xhi ^ xhi_too))
        for seq in range(2)
        for xhi in range(2)
    ]


def links(axis):
    if axis == "x":
        return ("seq", "xhi"), flip(1, 0), flip(1, 1)
    return axis, shift4(-1), shift4(1)


def halves(block):
    half = block.shape[0] // 2
    return block[0:half], block[half:]


def ring_begin(block, axis):
    names, one, two = links(axis)
    return lax.ppermute(block, names, one), lax.ppermute(block, names, two)


def ring_halves(first, second, axis):
    if axis == "x":
        return halves(second)[0], halves(first)[1]
    return halves(first)[0], halves(second)[1]


def ring_forward(head, tail, axis):
    names, one, two = links(axis)
    return lax.ppermute(head, names, one), lax.ppermute(tail, names, two)


def ring_finish(block, first, second, axis):
    head, tail = ring_forward(*ring_halves(first, second, axis), axis)
    return block, first, second, head, tail


def ring_join(block, first, second, head, tail, axis):
    if axis == "x":
        whole = jnp.concatenate([block, head, tail, first, second], axis=0)
        return whole.reshape((2, 2) + block.shape)
    whole = jnp.concatenate([block, first, head, tail, second], axis=0)
    return whole.reshape((4,) + block.shape)


def ring_gather(block, axis):
    return ring_join(*ring_finish(block, *ring_begin(block, axis), axis), axis)


def direct_gather(block, axis):
    parts = [block] + [lax.ppermute(block, axis, shift4(-i)) for i in (1, 2, 3)]
    return jnp.stack(parts)


def add(*terms):
    total = terms[0].astype(F32)
    for term in terms[1:]:
        total = total + term.astype(F32)
    return total.astype(BF16)


def ring_messages(block):
    first_head, first_tail = halves(block[1])
    far_head, far_tail = halves(block[2])
    second_head, second_tail = halves(block[3])
    return (
        block[0],
        jnp.concatenate([far_head, first_tail], axis=0),
        jnp.concatenate([second_head, far_tail], axis=0),
        first_head,
        second_tail,
    )


def cross_messages(block):
    first_head, first_tail = halves(block[1, 0])
    far_head, far_tail = halves(block[0, 1])
    second_head, second_tail = halves(block[1, 1])
    return (
        block[0, 0],
        jnp.concatenate([far_head, first_head], axis=0),
        jnp.concatenate([far_tail, second_tail], axis=0),
        first_tail,
        second_head,
    )


def reduce_ways(axis):
    names, one, two = links(axis)
    return (names, one, two) if axis == "x" else (names, two, one)


def reduce_start(messages, axis):
    names, to_first, to_second = reduce_ways(axis)
    own, a, b, first, second = messages
    return own, lax.ppermute(a, names, to_first), lax.ppermute(b, names, to_second), first, second


def reduce_middle(begun, axis):
    own, a, b, first, second = begun
    (a_head, a_tail), (b_head, b_tail) = halves(a), halves(b)
    if axis == "x":
        return own, a_tail, b_tail, add(first, b_head), add(second, a_head)
    return own, b_head, a_tail, add(first, a_head), add(second, b_tail)


def reduce_send(middle, axis):
    names, to_first, to_second = reduce_ways(axis)
    own, near_head, near_tail, first, second = middle
    first = lax.ppermute(first, names, to_first)
    second = lax.ppermute(second, names, to_second)
    if axis == "x":
        first, second = second, first
    return own, near_head, near_tail, first, second


def reduce_join(sent):
    own, near_head, near_tail, far_head, far_tail = sent
    head, tail = halves(own)
    return jnp.concatenate([add(head, near_head, far_head), add(tail, near_tail, far_tail)], axis=0)


def reduce_end(middle, axis):
    return reduce_join(reduce_send(middle, axis))


def tie(*values):
    return lax.optimization_barrier(values)


def direct_reduce(block, axis):
    parts = [block[0]] + [lax.ppermute(block[i], axis, shift4(i)) for i in (1, 2, 3)]
    return add(*parts)


def plane_gather(copies):
    got = lax.all_to_all(copies, PLANE, 0, 0, tiled=False)
    return got.reshape((2, 4, 2) + copies.shape[1:])


def plane_reduce(block):
    flat = block.reshape((16,) + block.shape[-2:])
    got = lax.all_to_all(flat, PLANE, 0, 0, tiled=False)
    return jnp.sum(got.astype(F32), axis=0)


def other_core(block):
    return lax.ppermute(block, "core", [(0, 1), (1, 0)])


def params(*semantics):
    return pltpu.CompilerParams(
        vmem_limit_bytes=VMEM_LIMIT,
        dimension_semantics=semantics if semantics else None,
    )


def vmem():
    return pl.BlockSpec(memory_space=pltpu.VMEM)


def smem():
    return pl.BlockSpec(memory_space=pltpu.SMEM)


CORE, Z, SEQ, Y, XHI = range(5)


def away(me, axis, at):
    return lax.rem(at + 4 - me[axis], 4)


def ring_rows(parts, step, y, x, size):
    if step == 2:
        a, b = parts[3][0, y, x, 0:size], parts[4][0, y, x, 0:size]
    else:
        ref = parts[{0: 0, 1: 1, 3: 2}[step]]
        a, b = ref[0, y, x, 0:size], ref[1, y, x, 0:size]
    return jnp.concatenate([a, b], axis=1)


def features_of(me, step):
    return pl.ds(pl.multiple_of(lax.rem(me[Z] + step, 4) * 256, 256), 256)


def put(messages, step, y, x, rows, value):
    for s in range(2):
        name, at = {
            (0, 0): (0, 0), (0, 1): (0, 1), (1, 0): (3, 0), (1, 1): (1, 1),
            (2, 0): (1, 0), (2, 1): (2, 1), (3, 0): (2, 0), (3, 1): (4, 0),
        }[step, s]
        messages[name][at, y, x, rows] = value[:, s * 128 : (s + 1) * 128].astype(BF16)


def split_kernel(me_ref, wq, wk, wv, wo, wup, wdown, small, keep_ref, give_ref):
    first = me_ref[CORE] == 0
    at = 0
    for ref in (wq, wk, wv, wo, wup, wdown):
        value = jnp.transpose(ref[...].astype(F32))
        half = value.shape[0] // 2
        a, b = value[0:half], value[half:]
        keep_ref[at : at + half] = jnp.where(first, a, b).astype(BF16)
        give_ref[at : at + half] = jnp.where(first, b, a).astype(BF16)
        at += half
    keep_ref[at:] = small[...]
    give_ref[at:] = small[...]


def join_kernel(me_ref, mine_ref, other_ref, dq, dk, dv, do, dup, ddown, vec_ref):
    first = me_ref[CORE] == 0
    hidden = ddown.shape[1] // 2

    def rows(start, size):
        a = mine_ref[start : start + size].astype(F32)
        b = other_ref[start : start + size].astype(F32)
        zero, one = jnp.where(first, a, b), jnp.where(first, b, a)
        zero = jnp.where(first, zero[:, 0:HD], zero[:, HD:])
        one = jnp.where(first, one[:, 0:HD], one[:, HD:])
        return zero, one

    at = 0
    plan = ((dq, HD), (dk, HD), (dv, HD), (vec_ref, 16), (dup, hidden), (do, HD), (ddown, hidden))
    for ref, size in plan:
        zero, one = rows(at, size)
        at += size
        if size == 16:
            ref[...] = zero + one
        else:
            ref[...] = jnp.transpose(jnp.concatenate([zero, one], axis=0))


def qkv_kernel(me_ref, x_ref, bias_ref, w0, w1, w2, w3, w4, out_ref):
    parts = (w0, w1, w2, w3, w4)
    core = me_ref[CORE]
    rows = [x_ref[:, features_of(me_ref, step)] for step in range(4)]
    span = x_ref.shape[0] // 4
    for y in range(4):
        for x in range(2):
            made = bias_ref[y * 2 + x]
            for step in range(4):
                made = made + dims(rows[step], ring_rows(parts, step, y, x, 3 * HD), 1, 1)
            made = made.astype(BF16)
            to = y * 2 + x
            for half in range(2):
                top = made[half * 2 * span : half * 2 * span + span]
                low = made[half * 2 * span + span : (half + 1) * 2 * span]
                packed = jnp.concatenate(
                    [
                        jnp.concatenate(
                            [top[:, i * HD : (i + 1) * HD], low[:, i * HD : (i + 1) * HD]],
                            axis=1,
                        )
                        for i in range(3)
                    ],
                    axis=0,
                )
                out_ref[core ^ half, to] = packed


def attend_kernel(q_ref, kv_ref, ctx_ref, lse_ref, *, rows):
    chunk = q_ref.shape[0] * rows
    length = kv_ref.shape[0] * rows
    queries = q_ref[:, 0:rows].reshape(chunk, 2 * HD) * jnp.bfloat16(0.125)
    keys = kv_ref[:, rows : 2 * rows].reshape(length, 2 * HD)
    values = kv_ref[:, 2 * rows : 3 * rows].reshape(length, 2 * HD)
    lane = lax.broadcasted_iota(jnp.int32, (chunk, 2 * HD), 1)
    parts = []
    for s in range(2):
        mine = (lane < HD) if s == 0 else (lane >= HD)
        picked = jnp.where(mine, queries, jnp.bfloat16(0))
        scores = dims(picked, keys, 1, 1)
        top = jnp.max(scores, axis=1, keepdims=True)
        weights = jnp.exp(scores - top)
        total = jnp.sum(weights, axis=1, keepdims=True)
        mixed = dims(weights.astype(BF16), values, 1, 0)
        parts.append(mixed / total)
        lse = jnp.broadcast_to(top + jnp.log(total), (chunk, 128))
        lse_ref[s] = jnp.transpose(lse)[0:8]
    ctx = jnp.where(lane < HD, parts[0], parts[1])
    ctx_ref[...] = ctx.astype(BF16).reshape(ctx_ref.shape)


def attend_back_kernel(
    q_ref, kv_ref, ctx_ref, dctx_ref, lse_ref, dq_ref, dkv_ref, dk_acc, dv_acc, *, rows
):
    step = pl.program_id(0)
    chunk = q_ref.shape[0] * rows
    length = kv_ref.shape[0] * rows
    queries = q_ref[:, 0:rows].reshape(chunk, 2 * HD) * jnp.bfloat16(0.125)
    grads = dctx_ref[...].reshape(chunk, 2 * HD)
    context = ctx_ref[...].reshape(chunk, 2 * HD)
    keys = kv_ref[:, rows : 2 * rows].reshape(length, 2 * HD)
    values = kv_ref[:, 2 * rows : 3 * rows].reshape(length, 2 * HD)
    lane = lax.broadcasted_iota(jnp.int32, (chunk, 2 * HD), 1)
    long_lane = lax.broadcasted_iota(jnp.int32, (length, 2 * HD), 1)
    both = grads.astype(F32) * context.astype(F32)

    @pl.when(step == 0)
    def _():
        dk_acc[...] = jnp.zeros_like(dk_acc)
        dv_acc[...] = jnp.zeros_like(dv_acc)

    dq_parts, dk_parts, dv_parts = [], [], []
    for s in range(2):
        mine = (lane < HD) if s == 0 else (lane >= HD)
        q_mine = jnp.where(mine, queries, jnp.bfloat16(0))
        g_mine = jnp.where(mine, grads, jnp.bfloat16(0))
        delta = jnp.sum(jnp.where(mine, both, 0.0), axis=1, keepdims=True)
        delta = jnp.transpose(jnp.broadcast_to(delta, (chunk, 128)))[0:1]
        scores = dims(keys, q_mine, 1, 1)
        exact = jnp.exp(scores - lse_ref[s, 0:1])
        grad_probs = dims(values, g_mine, 1, 1)
        grad_scores = (exact * (grad_probs - delta)).astype(BF16)
        dq_parts.append(dims(grad_scores, keys, 0, 0))
        dk_parts.append(dims(grad_scores, queries, 1, 0))
        dv_parts.append(dims(exact.astype(BF16), grads, 1, 0))
    dq = jnp.where(lane < HD, dq_parts[0], dq_parts[1]) * 0.125
    dq_ref[...] = dq.astype(BF16).reshape(dq_ref.shape)
    dk_acc[...] += jnp.where(long_lane < HD, dk_parts[0], dk_parts[1])
    dv_acc[...] += jnp.where(long_lane < HD, dv_parts[0], dv_parts[1])

    @pl.when(step == pl.num_programs(0) - 1)
    def _():
        shape = (kv_ref.shape[0], rows, 2 * HD)
        dkv_ref[:, 0:rows] = dk_acc[...].astype(BF16).reshape(shape)
        dkv_ref[:, rows : 2 * rows] = dv_acc[...].astype(BF16).reshape(shape)


def unpack_rows(top, low):
    return jnp.concatenate([top[:, 0:HD], top[:, HD:], low[:, 0:HD], low[:, HD:]], axis=0)


def out_rows(parts, step):
    return jnp.concatenate(
        [ring_rows(parts, step, y, x, HD) for y in range(4) for x in range(2)], axis=0
    )


def out_kernel(me_ref, recv_ref, w0, w1, w2, w3, w4, ctx_ref, own_ref, other_ref, acc):
    core = me_ref[CORE]
    parts = (w0, w1, w2, w3, w4)
    pieces = [unpack_rows(recv_ref[core, at], recv_ref[1 - core, at]) for at in range(8)]
    ctx = jnp.concatenate(pieces, axis=1)
    ctx_ref[...] = ctx
    for step in range(4):
        acc[:, features_of(me_ref, step)] = dims(ctx, out_rows(parts, step), 1, 0)
    half = ctx.shape[0] // 2
    own_ref[...] = acc[0:half]
    other_ref[...] = acc[half:].astype(BF16)


def wide_down(ref, me):
    return jnp.concatenate(
        [ref[s ^ me[SEQ], 0, 0, away(me, Z, z)] for z in range(4) for s in range(2)], axis=1
    )


def ffn_kernel(
    me_ref, n_ref, w0, w1, w2, w3, w4, wdown_ref, bias_ref,
    active_ref, slope_ref, own_ref, other_ref, acc,
):
    step = pl.program_id(0)
    parts = (w0, w1, w2, w3, w4)
    hidden = bias_ref.shape[2]
    pre = bias_ref[0]
    for turn in range(4):
        rows = n_ref[:, features_of(me_ref, turn)]
        pre = pre + dims(rows, ring_rows(parts, turn, 0, 0, hidden), 1, 1)
    cdf = 0.5 * (1.0 + lax.erf(pre * 0.7071067811865476))
    pdf = jnp.exp(-0.5 * pre * pre) * 0.3989422804014327
    active = (pre * cdf).astype(BF16)
    active_ref[...] = active
    slope_ref[...] = (cdf + pre * pdf).astype(BF16)
    made = dims(active, wide_down(wdown_ref, me_ref), 1, 0)

    @pl.when(step == 0)
    def _():
        acc[...] = made

    @pl.when(step > 0)
    def _():
        acc[...] += made

    @pl.when(step == pl.num_programs(0) - 1)
    def _():
        half = acc.shape[0] // 2
        own_ref[...] = acc[0:half]
        other_ref[...] = acc[half:].astype(BF16)


def ffn_back_kernel(
    me_ref, n_ref, g_ref, w0, w1, w2, w3, w4, wdown_ref, active_ref, slope_ref,
    d0, d1, d2, d3, d4, ddown_ref, bias_ref, own_ref, other_ref, acc,
):
    step = pl.program_id(0)
    parts, messages = (w0, w1, w2, w3, w4), (d0, d1, d2, d3, d4)
    grads = g_ref[...]
    active = active_ref[...]
    hidden = active.shape[1]
    grad = dims(active, grads, 0, 0).astype(BF16)
    for z in range(4):
        for s in range(2):
            at = (z * 2 + s) * 128
            ddown_ref[s ^ me_ref[SEQ], 0, 0, away(me_ref, Z, z)] = grad[:, at : at + 128]
    grad_pre = dims(grads, wide_down(wdown_ref, me_ref), 1, 1) * slope_ref[...].astype(F32)
    bias_ref[0] = jnp.sum(grad_pre, axis=0, keepdims=True)
    low = grad_pre.astype(BF16)

    @pl.when(step == 0)
    def _():
        acc[...] = jnp.zeros_like(acc)

    for turn in range(4):
        at = features_of(me_ref, turn)
        put(messages, turn, 0, 0, slice(0, hidden), dims(low, n_ref[:, at], 0, 0))
        acc[:, at] += dims(low, ring_rows(parts, turn, 0, 0, hidden), 1, 0)

    @pl.when(step == pl.num_programs(0) - 1)
    def _():
        half = acc.shape[0] // 2
        own_ref[...] = acc[0:half]
        other_ref[...] = acc[half:].astype(BF16)


def out_back_kernel(
    me_ref, g_ref, ctx_ref, w0, w1, w2, w3, w4, u0, u1, u2, u3, u4,
    dctx_ref, d0, d1, d2, d3, d4,
):
    core = me_ref[CORE]
    parts, messages = (w0, w1, w2, w3, w4), (d0, d1, d2, d3, d4)
    span = g_ref.shape[0] // 4
    ctx = ctx_ref[...]
    made = None
    for step in range(4):
        grads = g_ref[:, features_of(me_ref, step)]
        part = dims(grads, out_rows(parts, step), 1, 1)
        made = part if made is None else made + part
        grad = dims(ctx, grads, 0, 0)
        for y in range(4):
            for x in range(2):
                at = (y * 2 + x) * HD
                put(messages, step, y, x, slice(0, HD), grad[at : at + HD])
    made = made.astype(BF16)
    for to in range(8):
        piece = made[:, to * HD : (to + 1) * HD]
        for half in range(2):
            base = half * 2 * span
            dctx_ref[core ^ half, to] = jnp.concatenate(
                [piece[base : base + span], piece[base + span : base + 2 * span]], axis=1
            )


def qkv_back_kernel(
    me_ref, recv_ref, x_ref, vec_ref, w0, w1, w2, w3, w4,
    d0, d1, d2, d3, d4, own_ref, other_ref, acc,
):
    core = me_ref[CORE]
    parts, grads = (w0, w1, w2, w3, w4), (d0, d1, d2, d3, d4)
    rows = [x_ref[:, features_of(me_ref, step)] for step in range(4)]
    span = x_ref.shape[0] // 4
    half = x_ref.shape[0] // 2

    sums = []
    totals = [None] * 4
    for y in range(4):
        for x in range(2):
            at = y * 2 + x
            top, low = recv_ref[core, at], recv_ref[1 - core, at]
            made = jnp.concatenate(
                [
                    unpack_rows(
                        top[i * span : (i + 1) * span], low[i * span : (i + 1) * span]
                    )
                    for i in range(3)
                ],
                axis=1,
            )
            sums.append(jnp.sum(made.astype(F32), axis=0, keepdims=True))
            for step in range(4):
                put(grads, step, y, x, slice(0, 3 * HD), dims(made, rows[step], 0, 0))
                part = dims(made, ring_rows(parts, step, y, x, 3 * HD), 1, 0)
                totals[step] = part if totals[step] is None else totals[step] + part
    for step in range(4):
        acc[:, features_of(me_ref, step)] = totals[step]
    own_ref[...] = acc[0:half]
    other_ref[...] = acc[half:].astype(BF16)
    zeros = jnp.zeros((14, 2 * HD), F32)
    twos = []
    for z in range(4):
        a, b = sums[2 * z], sums[2 * z + 1]
        bias_q = jnp.concatenate([a[:, 0:HD], b[:, 0:HD]], axis=1)
        bias_v = jnp.concatenate([a[:, 2 * HD :], b[:, 2 * HD :]], axis=1)
        twos.append(jnp.concatenate([bias_q, bias_v, zeros], axis=0))
    for step in range(4):
        z_abs = lax.rem(me_ref[Z] + step, 4)
        two = twos[3]
        for z in range(3):
            two = jnp.where(z_abs == z, twos[z], two)
        block = jnp.concatenate(
            [vec_ref[z_abs, s] + jnp.where(core == s, two, 0.0) for s in range(2)], axis=1
        )
        for y in range(4):
            for x in range(2):
                put(grads, step, y, x, slice(3 * HD, 3 * HD + 16), block)


def norm_forward(hidden, gain, shift):
    centre = jnp.mean(hidden, axis=-1, keepdims=True)
    centered = hidden - centre
    inverse = lax.rsqrt(jnp.mean(centered * centered, axis=-1, keepdims=True) + EPS)
    normed = centered * inverse
    return (normed * gain + shift, normed, inverse)


def norm_backward(grad_in, normed, inverse, gain):
    scaled = grad_in * gain
    inner_term = (
        scaled
        - jnp.mean(scaled, axis=-1, keepdims=True)
        - normed * jnp.mean(scaled * normed, axis=-1, keepdims=True)
    )
    return (
        inverse * inner_term,
        jnp.sum(grad_in * normed, axis=0),
        jnp.sum(grad_in, axis=0),
    )


def sds(shape, dtype=BF16):
    return jax.ShapeDtypeStruct(shape, dtype)


def took(us):
    return pl.CostEstimate(flops=int(us * 1.15e9), bytes_accessed=1 << 20, transcendentals=0)


def local(
    tokens, w_query, w_key, w_value, w_out, w_up, w_down,
    b_query, b_value, b_out, b_up, b_down,
    gain_attn, shift_attn, gain_mlp, shift_mlp, cotangent,
):
    core = lax.axis_index("core")
    me_z, me_s = lax.axis_index("z"), lax.axis_index("seq")
    me_y, me_x = lax.axis_index("y"), lax.axis_index("xhi")
    first_core = core == 0
    me = jnp.stack([core, me_z, me_s, me_y, me_x]).astype(jnp.int32)
    seqs, span, width = tokens.shape
    rows = seqs * span
    hidden = w_up.shape[1] // 2

    at = jnp.arange(width, dtype=jnp.int32)
    z_of, c_of, s_of, i_of = at // 256, (at // 128) % 2, (at // 64) % 2, at % 64
    stored = z_of * 256 + s_of * 128 + c_of * 64 + i_of
    order = (stored[:, None] == at[None, :]).astype(BF16)

    small = jnp.stack(
        [b_query, b_value, b_out, b_down, gain_attn, shift_attn, gain_mlp, shift_mlp]
    )
    small = jnp.concatenate([small, b_up.reshape(4, HD), jnp.zeros((4, HD), BF16)], axis=0)
    shard_rows = 4 * HD + 2 * hidden + 16
    with jax.named_scope("split"):
        keep, give = pl.pallas_call(
            split_kernel,
            out_shape=(sds((shard_rows, HD)),) * 2,
            in_specs=[smem()] + [vmem()] * 7,
            out_specs=(vmem(), vmem()),
            compiler_params=params(),
            cost_estimate=took(2),
        )(me, w_query, w_key, w_value, w_out.T, w_up, w_down.T, small)
    got = other_core(give)
    shard = jnp.where(
        first_core,
        jnp.concatenate([keep, got], axis=1),
        jnp.concatenate([got, keep], axis=1),
    )
    at_o, at_up, at_down, at_vec = 3 * HD, 4 * HD, 4 * HD + hidden, 4 * HD + 2 * hidden
    qkv_shard = jnp.concatenate([shard[0:at_o], shard[at_vec:]], axis=0)
    up_shard = jnp.concatenate([shard[at_up:at_down], shard[at_o:at_up]])
    sixteen = lambda part: jnp.broadcast_to(part[None], (16,) + part.shape)
    qkv_block = plane_gather(sixteen(qkv_shard))
    *near, head, tail = ring_finish(qkv_block, *ring_begin(qkv_block, "z"), "z")

    both_in = jnp.concatenate([tokens.reshape(rows, width), cotangent.reshape(rows, width)], axis=0)
    both_in = dims(both_in, order, 1, 0)
    mine = both_in[0:rows]
    grad_final = both_in[rows:]
    mine_low = mine.astype(BF16)
    x_rows = jnp.concatenate([mine_low, other_core(mine_low)], axis=0)

    x_rows, down_shard = tie(x_rows, shard[at_down:at_vec])
    down_line = direct_gather(down_shard, "z")
    *down_begun, up_shard = tie(*ring_begin(down_line, "y"), up_shard)
    up_block = plane_gather(sixteen(up_shard))
    down_block = ring_join(*ring_finish(down_line, *down_begun, "y"), "y")
    head, tail, up_block = tie(head, tail, up_block)
    qkv_parts = (*near, head, tail)
    up_begun, down_begun = ring_begin(up_block, "z"), ring_begin(down_block, "x")

    fours = jnp.arange(4, dtype=jnp.int32)
    turn = ((fours[:, None] - me_z) % 4 == fours[None, :]).astype(F32)
    ring = [p[:, 0, 0, 3 * HD :, :].reshape(-1) for p in qkv_parts]
    vec = jnp.concatenate([ring[0], ring[1], ring[3], ring[4], ring[2]])
    vec = vec.reshape(4, 4096).astype(F32)
    vec = jnp.dot(turn, vec, precision=HIGHEST).reshape(4, 2, 16, 2 * HD)
    feature = lambda i: vec[:, :, i, :].reshape(width)
    chosen = jnp.where(first_core, vec[:, 0], vec[:, 1])
    chosen = chosen.reshape(4, 16, 2, HD).transpose(0, 2, 1, 3).reshape(8, 16 * HD)
    zeros = jnp.zeros((8, HD), F32)
    bias_qkv = jnp.concatenate([chosen[:, 0:HD], zeros, chosen[:, HD : 2 * HD]], axis=1)
    bias_qkv = bias_qkv[:, None, :]
    bias_up = chosen[:, 8 * HD : 12 * HD][:, None, :]
    gain_one, gain_two = feature(4), feature(6)

    with jax.named_scope("project"):
        packed = pl.pallas_call(
            qkv_kernel,
            out_shape=sds((2, 8, 3 * span, 2 * HD)),
            in_specs=[smem()] + [vmem()] * 7,
            out_specs=vmem(),
            compiler_params=params(),
            cost_estimate=took(5),
        )(me, x_rows, bias_qkv, *qkv_parts)

    def exchange(block):
        flat = block.reshape((16,) + block.shape[2:])
        return lax.all_to_all(flat, PLANE, 0, 0, tiled=False)

    packed, *down_begun = tie(packed, *down_begun)
    *down_near, head, tail = ring_finish(down_block, *down_begun, "x")
    qkv, *up_halves = tie(exchange(packed), *ring_halves(*up_begun, "z"))
    up_parts = (up_block, *up_begun, *ring_forward(*up_halves, "z"))
    per = Q_BLOCKS
    chunk = per * span
    steps = 16 // per
    length = 16 * span
    with jax.named_scope("attend"):
        ctx_heads, lse = pl.pallas_call(
            functools.partial(attend_kernel, rows=span),
            grid=(steps,),
            out_shape=(sds((16, span, 2 * HD)), sds((2, 8, length), F32)),
            in_specs=[
                pl.BlockSpec((per, 3 * span, 2 * HD), lambda i: (i, 0, 0)),
                pl.BlockSpec((16, 3 * span, 2 * HD), lambda i: (0, 0, 0)),
            ],
            out_specs=(
                pl.BlockSpec((per, span, 2 * HD), lambda i: (i, 0, 0)),
                pl.BlockSpec((2, 8, chunk), lambda i: (0, 0, i)),
            ),
            compiler_params=params("arbitrary"),
            cost_estimate=took(11),
        )(qkv, qkv)
    ctx_heads, head, tail = tie(ctx_heads, head, tail)
    wdown = ring_join(*down_near, head, tail, "x")
    recv = lax.all_to_all(ctx_heads, PLANE, 0, 0, tiled=False)
    recv = recv.reshape(2, 8, span, 2 * HD)
    out_block = hidden // HD
    out_specs = [
        pl.BlockSpec((p.shape[0], 4, 2, HD, 2 * HD), lambda i: (0, 0, 0, out_block, 0))
        for p in up_parts
    ]
    message_shapes = [sds(p.shape) for p in up_parts]
    with jax.named_scope("out_project"):
        ctx, own, other = pl.pallas_call(
            out_kernel,
            out_shape=(sds((2 * rows, 8 * HD)), sds((rows, width), F32), sds((rows, width))),
            grid=(1,),
            in_specs=[smem(), vmem()] + out_specs,
            out_specs=(vmem(), vmem(), vmem()),
            scratch_shapes=[pltpu.VMEM((2 * rows, width), F32)],
            compiler_params=params("arbitrary"),
            cost_estimate=took(3),
        )(me, recv, *up_parts)
    attended = own + other_core(other).astype(F32)
    resid_one = mine + attended + feature(2)
    normed_one, norm_first, inverse_first = norm_forward(resid_one, gain_one, feature(5))
    normed_low = normed_one.astype(BF16)
    n_rows = jnp.concatenate([normed_low, other_core(normed_low)], axis=0)

    up_specs = [
        pl.BlockSpec(
            (p.shape[0], 1, 1, hidden, 2 * HD), lambda t, at: (0, t // 2, t % 2, 0, 0)
        )
        for p in up_parts
    ]
    down_spec = pl.BlockSpec(
        (2, 1, 1, 4, hidden, 2 * HD),
        lambda t, at: (0, (t % 2) ^ at[XHI], away(at, Y, t // 2), 0, 0, 0),
    )
    whole_spec = pl.BlockSpec((2 * rows, width), lambda t, at: (0, 0))
    cols_spec = pl.BlockSpec((2 * rows, hidden), lambda t, at: (0, t))
    half_spec = pl.BlockSpec((rows, width), lambda t, at: (0, 0))
    bias_spec = pl.BlockSpec((1, 1, hidden), lambda t, at: (t, 0, 0))
    with jax.named_scope("feed_forward"):
        active, slope, own, other = pl.pallas_call(
            ffn_kernel,
            grid_spec=pltpu.PrefetchScalarGridSpec(
                num_scalar_prefetch=1,
                grid=(8,),
                in_specs=[whole_spec] + up_specs + [down_spec, bias_spec],
                out_specs=(cols_spec, cols_spec, half_spec, half_spec),
                scratch_shapes=[pltpu.VMEM((2 * rows, width), F32)],
            ),
            out_shape=(
                sds((2 * rows, 8 * hidden)),
                sds((2 * rows, 8 * hidden)),
                sds((rows, width), F32),
                sds((rows, width)),
            ),
            compiler_params=params("arbitrary"),
            cost_estimate=took(14),
        )(me, n_rows, *up_parts, wdown, bias_up)
    mixed = own + other_core(other).astype(F32)
    resid_two = normed_one + mixed + feature(3)
    final, norm_second, inverse_second = norm_forward(resid_two, gain_two, feature(7))
    output = dims(final.astype(BF16), order, 1, 1).astype(BF16)
    grad_two, part_gain_mlp, part_shift_mlp = norm_backward(
        grad_final, norm_second, inverse_second, gain_two
    )
    grad_low = grad_two.astype(BF16)
    g_rows = jnp.concatenate([grad_low, other_core(grad_low)], axis=0)
    with jax.named_scope("feed_forward_back"):
        *grad_up, grad_down, part_up, own, other = pl.pallas_call(
            ffn_back_kernel,
            grid_spec=pltpu.PrefetchScalarGridSpec(
                num_scalar_prefetch=1,
                grid=(8,),
                in_specs=[whole_spec] * 2 + up_specs + [down_spec, cols_spec, cols_spec],
                out_specs=(*up_specs, down_spec, bias_spec, half_spec, half_spec),
                scratch_shapes=[pltpu.VMEM((2 * rows, width), F32)],
            ),
            out_shape=(
                *message_shapes,
                sds(wdown.shape),
                sds((8, 1, hidden), F32),
                sds((rows, width), F32),
                sds((rows, width)),
            ),
            compiler_params=params("arbitrary"),
            cost_estimate=took(20),
        )(me, n_rows, g_rows, *up_parts, wdown, active, slope)
    grad_mid = grad_two + (own + other_core(other).astype(F32))
    grad_one, part_gain_attn, part_shift_attn = norm_backward(
        grad_mid, norm_first, inverse_first, gain_one
    )
    grad_low = grad_one.astype(BF16)
    g_rows = jnp.concatenate([grad_low, other_core(grad_low)], axis=0)
    with jax.named_scope("out_project_back"):
        dctx, *grad_up = pl.pallas_call(
            out_back_kernel,
            grid=(1,),
            out_shape=(sds((2, 8, span, 2 * HD)), *message_shapes),
            in_specs=[smem(), vmem(), vmem()]
            + out_specs
            + [pl.BlockSpec(memory_space=pl.ANY)] * 5,
            out_specs=(vmem(), *out_specs),
            input_output_aliases={8 + i: 1 + i for i in range(5)},
            compiler_params=params("arbitrary"),
            cost_estimate=took(4),
        )(me, g_rows, ctx, *up_parts, *grad_up)
    dctx, grad_down = tie(exchange(dctx), grad_down)
    down_begun = reduce_start(cross_messages(grad_down), "x")
    up_begun = reduce_start(grad_up, "z")
    with jax.named_scope("attend_back"):
        dq, dkv = pl.pallas_call(
            functools.partial(attend_back_kernel, rows=span),
            grid=(steps,),
            out_shape=(sds((16, span, 2 * HD)), sds((16, 2 * span, 2 * HD))),
            in_specs=[
                pl.BlockSpec((per, 3 * span, 2 * HD), lambda i: (i, 0, 0)),
                pl.BlockSpec((16, 3 * span, 2 * HD), lambda i: (0, 0, 0)),
                pl.BlockSpec((per, span, 2 * HD), lambda i: (i, 0, 0)),
                pl.BlockSpec((per, span, 2 * HD), lambda i: (i, 0, 0)),
                pl.BlockSpec((2, 8, chunk), lambda i: (0, 0, i)),
            ],
            out_specs=(
                pl.BlockSpec((per, span, 2 * HD), lambda i: (i, 0, 0)),
                pl.BlockSpec((16, 2 * span, 2 * HD), lambda i: (0, 0, 0)),
            ),
            scratch_shapes=[pltpu.VMEM((length, 2 * HD), F32)] * 2,
            compiler_params=params("arbitrary"),
            cost_estimate=took(18),
        )(qkv, qkv, ctx_heads, dctx, lse)
    dq, *up_begun = tie(dq, *up_begun)
    dqkv = exchange(jnp.concatenate([dq, dkv], axis=1)[None])
    *up_middle, down_first, down_second = tie(*reduce_middle(up_begun, "z"), *down_begun[1:3])
    up_sent = reduce_send(up_middle, "z")
    down_begun = (down_begun[0], down_first, down_second) + down_begun[3:5]
    down_sent = reduce_send(reduce_middle(down_begun, "x"), "x")
    up_sum = reduce_join(up_sent)
    dqkv, up_sum = tie(dqkv, up_sum)
    dqkv = dqkv.reshape(2, 8, 3 * span, 2 * HD)
    ups = part_up.reshape(4, 2, 4, HD).transpose(0, 2, 1, 3).reshape(4, 1, 4, 2 * HD)
    nothing = jnp.zeros_like(ups)
    ups = jnp.concatenate(
        [jnp.where(first_core, ups, nothing), jnp.where(first_core, nothing, ups)], axis=1
    )
    six = jnp.stack(
        [
            jnp.sum(grad_one, axis=0), jnp.sum(grad_two, axis=0),
            part_gain_attn, part_shift_attn, part_gain_mlp, part_shift_mlp,
        ]
    ).reshape(6, 4, 2, 2 * HD).transpose(1, 2, 0, 3)
    vec_rows = jnp.concatenate(
        [jnp.zeros((4, 2, 2, 2 * HD), F32), six, ups, jnp.zeros((4, 2, 4, 2 * HD), F32)], axis=2
    )
    with jax.named_scope("project_back"):
        part, far = sds((2, 4, 2, 3 * HD + 16, 2 * HD)), sds((1, 4, 2, 3 * HD + 16, 2 * HD))
        *grad_qkv, own, other = pl.pallas_call(
            qkv_back_kernel,
            out_shape=(
                part, part, part, far, far, sds((rows, width), F32), sds((rows, width)),
            ),
            in_specs=[smem()] + [vmem()] * 8,
            out_specs=(vmem(),) * 7,
            scratch_shapes=[pltpu.VMEM((2 * rows, width), F32)],
            compiler_params=params(),
            cost_estimate=took(8),
        )(me, dqkv, x_rows, vec_rows, *qkv_parts)
    own, other, *sent = tie(own, other, *down_sent)
    down_sum = reduce_join(sent)
    input_sum = own + other_core(other).astype(F32)
    grad_tokens = lax.dot_general(
        grad_one + input_sum, order.astype(F32), (((1,), (1,)), ((), ())),
        precision=lax.Precision.HIGH,
    )
    down_begun = reduce_start(ring_messages(down_sum), "y")
    begun = tie(*reduce_start(grad_qkv, "z"), *down_begun, grad_tokens)
    qkv_sum = reduce_end(reduce_middle(begun[0:5], "z"), "z")
    down_begun, grad_tokens = begun[5:10], begun[10]
    down_sum = reduce_end(reduce_middle(down_begun, "y"), "y")
    got_up = plane_reduce(up_sum).astype(BF16)
    got_down = direct_reduce(down_sum, "z")
    got_qkv = plane_reduce(qkv_sum)
    final_rows = jnp.concatenate([got_qkv.astype(BF16), got_up, got_down], axis=0)
    swapped = other_core(final_rows)
    with jax.named_scope("join"):
        square = sds((HD, 2 * HD), F32)
        *weights, g_out, g_up, g_down, vecs = pl.pallas_call(
            join_kernel,
            out_shape=(
                square, square, square, square,
                sds((HD, 2 * hidden), F32),
                sds((HD, 2 * hidden), F32),
                sds((16, HD), F32),
            ),
            in_specs=[smem(), vmem(), vmem()],
            out_specs=(vmem(),) * 7,
            compiler_params=params(),
            cost_estimate=took(2),
        )(me, final_rows, swapped)
    return (
        output.reshape(seqs, span, width),
        grad_tokens.reshape(seqs, span, width),
        *weights,
        g_out.T,
        g_up,
        g_down.T,
        vecs[0],
        vecs[1],
        vecs[2],
        vecs[8:12].reshape(4 * HD),
        vecs[3],
        vecs[4],
        vecs[5],
        vecs[6],
        vecs[7],
    )


def solution(mesh):
    fine = Mesh(mesh.devices.reshape(4, 2, 2, 4, 2), ("z", "core", "seq", "y", "xhi"))
    owners, tensor = ("z", "core", "seq"), ("y", "xhi")
    tokens = P(("z", "core"), ("seq", "y", "xhi"), None)
    columns, by_rows, vector = P(owners, tensor), P(tensor, owners), P(owners)
    weights = (columns, columns, columns, by_rows, columns, by_rows)
    return jax.shard_map(
        local,
        mesh=fine,
        in_specs=(tokens,) + weights + (vector,) * 9 + (tokens,),
        out_specs=(tokens, tokens) + weights + (vector,) * 9,
        check_vma=False,
    )
```

```python
import functools

import jax
import jax.numpy as jnp
from jax import lax
from jax.experimental import pallas as pl
from jax.experimental.pallas import tpu as pltpu
from jax.sharding import Mesh, PartitionSpec as P

HD = 64
EPS = 1e-05
F32 = jnp.float32
BF16 = jnp.bfloat16
HIGHEST = lax.Precision.HIGHEST
VMEM_LIMIT = 56 * 1024 * 1024
Q_BLOCKS = 4
PLANE = ("seq", "y", "xhi")


def dims(a, b, ca, cb):
    return lax.dot_general(a, b, (((ca,), (cb,)), ((), ())), preferred_element_type=F32)


def shift4(by):
    return [(i, (i + by) % 4) for i in range(4)]


def flip(seq_too, xhi_too):
    return [
        (seq * 2 + xhi, (seq ^ seq_too) * 2 + (xhi ^ xhi_too))
        for seq in range(2)
        for xhi in range(2)
    ]


def links(axis):
    if axis == "x":
        return ("seq", "xhi"), flip(1, 0), flip(1, 1)
    return axis, shift4(-1), shift4(1)


def halves(block):
    half = block.shape[0] // 2
    return block[0:half], block[half:]


def ring_begin(block, axis):
    names, one, two = links(axis)
    return lax.ppermute(block, names, one), lax.ppermute(block, names, two)


def ring_halves(first, second, axis):
    if axis == "x":
        return halves(second)[0], halves(first)[1]
    return halves(first)[0], halves(second)[1]


def ring_forward(head, tail, axis):
    names, one, two = links(axis)
    return lax.ppermute(head, names, one), lax.ppermute(tail, names, two)


def ring_finish(block, first, second, axis):
    head, tail = ring_forward(*ring_halves(first, second, axis), axis)
    return block, first, second, head, tail


def ring_join(block, first, second, head, tail, axis):
    if axis == "x":
        whole = jnp.concatenate([block, head, tail, first, second], axis=0)
        return whole.reshape((2, 2) + block.shape)
    whole = jnp.concatenate([block, first, head, tail, second], axis=0)
    return whole.reshape((4,) + block.shape)


def ring_gather(block, axis):
    return ring_join(*ring_finish(block, *ring_begin(block, axis), axis), axis)


def direct_gather(block, axis):
    parts = [block] + [lax.ppermute(block, axis, shift4(-i)) for i in (1, 2, 3)]
    return jnp.stack(parts)


def add(*terms):
    total = terms[0].astype(F32)
    for term in terms[1:]:
        total = total + term.astype(F32)
    return total.astype(BF16)


def ring_messages(block):
    first_head, first_tail = halves(block[1])
    far_head, far_tail = halves(block[2])
    second_head, second_tail = halves(block[3])
    return (
        block[0],
        jnp.concatenate([far_head, first_tail], axis=0),
        jnp.concatenate([second_head, far_tail], axis=0),
        first_head,
        second_tail,
    )


def cross_messages(block):
    first_head, first_tail = halves(block[1, 0])
    far_head, far_tail = halves(block[0, 1])
    second_head, second_tail = halves(block[1, 1])
    return (
        block[0, 0],
        jnp.concatenate([far_head, first_head], axis=0),
        jnp.concatenate([far_tail, second_tail], axis=0),
        first_tail,
        second_head,
    )


def reduce_ways(axis):
    names, one, two = links(axis)
    return (names, one, two) if axis == "x" else (names, two, one)


def reduce_start(messages, axis):
    names, to_first, to_second = reduce_ways(axis)
    own, a, b, first, second = messages
    return own, lax.ppermute(a, names, to_first), lax.ppermute(b, names, to_second), first, second


def reduce_middle(begun, axis):
    own, a, b, first, second = begun
    (a_head, a_tail), (b_head, b_tail) = halves(a), halves(b)
    if axis == "x":
        return own, a_tail, b_tail, add(first, b_head), add(second, a_head)
    return own, b_head, a_tail, add(first, a_head), add(second, b_tail)


def reduce_send(middle, axis):
    names, to_first, to_second = reduce_ways(axis)
    own, near_head, near_tail, first, second = middle
    first = lax.ppermute(first, names, to_first)
    second = lax.ppermute(second, names, to_second)
    if axis == "x":
        first, second = second, first
    return own, near_head, near_tail, first, second


def reduce_join(sent):
    own, near_head, near_tail, far_head, far_tail = sent
    head, tail = halves(own)
    return jnp.concatenate([add(head, near_head, far_head), add(tail, near_tail, far_tail)], axis=0)


def reduce_end(middle, axis):
    return reduce_join(reduce_send(middle, axis))


def tie(*values):
    return lax.optimization_barrier(values)


def direct_reduce(block, axis):
    parts = [block[0]] + [lax.ppermute(block[i], axis, shift4(i)) for i in (1, 2, 3)]
    return add(*parts)


def plane_gather(copies):
    got = lax.all_to_all(copies, PLANE, 0, 0, tiled=False)
    return got.reshape((2, 4, 2) + copies.shape[1:])


def plane_reduce(block):
    flat = block.reshape((16,) + block.shape[-2:])
    got = lax.all_to_all(flat, PLANE, 0, 0, tiled=False)
    return jnp.sum(got.astype(F32), axis=0)


def other_core(block):
    return lax.ppermute(block, "core", [(0, 1), (1, 0)])


def params(*semantics):
    return pltpu.CompilerParams(
        vmem_limit_bytes=VMEM_LIMIT,
        dimension_semantics=semantics if semantics else None,
    )


def vmem():
    return pl.BlockSpec(memory_space=pltpu.VMEM)


def smem():
    return pl.BlockSpec(memory_space=pltpu.SMEM)


CORE, Z, SEQ, Y, XHI = range(5)


def away(me, axis, at):
    return lax.rem(at + 4 - me[axis], 4)


def ring_rows(parts, step, y, x, size):
    if step == 2:
        a, b = parts[3][0, y, x, 0:size], parts[4][0, y, x, 0:size]
    else:
        ref = parts[{0: 0, 1: 1, 3: 2}[step]]
        a, b = ref[0, y, x, 0:size], ref[1, y, x, 0:size]
    return jnp.concatenate([a, b], axis=1)


def features_of(me, step):
    return pl.ds(pl.multiple_of(lax.rem(me[Z] + step, 4) * 256, 256), 256)


def put(messages, step, y, x, rows, value):
    for s in range(2):
        name, at = {
            (0, 0): (0, 0), (0, 1): (0, 1), (1, 0): (3, 0), (1, 1): (1, 1),
            (2, 0): (1, 0), (2, 1): (2, 1), (3, 0): (2, 0), (3, 1): (4, 0),
        }[step, s]
        messages[name][at, y, x, rows] = value[:, s * 128 : (s + 1) * 128].astype(BF16)


def split_kernel(me_ref, wq, wk, wv, wo, wup, wdown, small, keep_ref, give_ref):
    first = me_ref[CORE] == 0
    at = 0
    for ref in (wq, wk, wv, wo, wup, wdown):
        value = jnp.transpose(ref[...].astype(F32))
        half = value.shape[0] // 2
        a, b = value[0:half], value[half:]
        keep_ref[at : at + half] = jnp.where(first, a, b).astype(BF16)
        give_ref[at : at + half] = jnp.where(first, b, a).astype(BF16)
        at += half
    keep_ref[at:] = small[...]
    give_ref[at:] = small[...]


def join_kernel(me_ref, mine_ref, other_ref, dq, dk, dv, do, dup, ddown, vec_ref):
    first = me_ref[CORE] == 0
    hidden = ddown.shape[1] // 2

    def rows(start, size):
        a = mine_ref[start : start + size].astype(F32)
        b = other_ref[start : start + size].astype(F32)
        zero, one = jnp.where(first, a, b), jnp.where(first, b, a)
        zero = jnp.where(first, zero[:, 0:HD], zero[:, HD:])
        one = jnp.where(first, one[:, 0:HD], one[:, HD:])
        return zero, one

    at = 0
    plan = ((dq, HD), (dk, HD), (dv, HD), (vec_ref, 16), (dup, hidden), (do, HD), (ddown, hidden))
    for ref, size in plan:
        zero, one = rows(at, size)
        at += size
        if size == 16:
            ref[...] = zero + one
        else:
            ref[...] = jnp.transpose(jnp.concatenate([zero, one], axis=0))


def qkv_kernel(me_ref, x_ref, bias_ref, w0, w1, w2, w3, w4, out_ref):
    parts = (w0, w1, w2, w3, w4)
    core = me_ref[CORE]
    rows = [x_ref[:, features_of(me_ref, step)] for step in range(4)]
    span = x_ref.shape[0] // 4
    for y in range(4):
        for x in range(2):
            made = bias_ref[y * 2 + x]
            for step in range(4):
                made = made + dims(rows[step], ring_rows(parts, step, y, x, 3 * HD), 1, 1)
            made = made.astype(BF16)
            to = y * 2 + x
            for half in range(2):
                top = made[half * 2 * span : half * 2 * span + span]
                low = made[half * 2 * span + span : (half + 1) * 2 * span]
                packed = jnp.concatenate(
                    [
                        jnp.concatenate(
                            [top[:, i * HD : (i + 1) * HD], low[:, i * HD : (i + 1) * HD]],
                            axis=1,
                        )
                        for i in range(3)
                    ],
                    axis=0,
                )
                out_ref[core ^ half, to] = packed


def attend_kernel(q_ref, kv_ref, ctx_ref, lse_ref, *, rows):
    chunk = q_ref.shape[0] * rows
    length = kv_ref.shape[0] * rows
    queries = q_ref[:, 0:rows].reshape(chunk, 2 * HD) * jnp.bfloat16(0.125)
    keys = kv_ref[:, rows : 2 * rows].reshape(length, 2 * HD)
    values = kv_ref[:, 2 * rows : 3 * rows].reshape(length, 2 * HD)
    lane = lax.broadcasted_iota(jnp.int32, (chunk, 2 * HD), 1)
    parts = []
    for s in range(2):
        mine = (lane < HD) if s == 0 else (lane >= HD)
        picked = jnp.where(mine, queries, jnp.bfloat16(0))
        scores = dims(picked, keys, 1, 1)
        top = jnp.max(scores, axis=1, keepdims=True)
        weights = jnp.exp(scores - top)
        total = jnp.sum(weights, axis=1, keepdims=True)
        mixed = dims(weights.astype(BF16), values, 1, 0)
        parts.append(mixed / total)
        lse = jnp.broadcast_to(top + jnp.log(total), (chunk, 128))
        lse_ref[s] = jnp.transpose(lse)[0:8]
    ctx = jnp.where(lane < HD, parts[0], parts[1])
    ctx_ref[...] = ctx.astype(BF16).reshape(ctx_ref.shape)


def attend_back_kernel(
    q_ref, kv_ref, ctx_ref, dctx_ref, lse_ref, dq_ref, dkv_ref, dk_acc, dv_acc, *, rows
):
    step = pl.program_id(0)
    chunk = q_ref.shape[0] * rows
    length = kv_ref.shape[0] * rows
    queries = q_ref[:, 0:rows].reshape(chunk, 2 * HD) * jnp.bfloat16(0.125)
    grads = dctx_ref[...].reshape(chunk, 2 * HD)
    context = ctx_ref[...].reshape(chunk, 2 * HD)
    keys = kv_ref[:, rows : 2 * rows].reshape(length, 2 * HD)
    values = kv_ref[:, 2 * rows : 3 * rows].reshape(length, 2 * HD)
    lane = lax.broadcasted_iota(jnp.int32, (chunk, 2 * HD), 1)
    long_lane = lax.broadcasted_iota(jnp.int32, (length, 2 * HD), 1)
    both = grads.astype(F32) * context.astype(F32)

    @pl.when(step == 0)
    def _():
        dk_acc[...] = jnp.zeros_like(dk_acc)
        dv_acc[...] = jnp.zeros_like(dv_acc)

    dq_parts, dk_parts, dv_parts = [], [], []
    for s in range(2):
        mine = (lane < HD) if s == 0 else (lane >= HD)
        q_mine = jnp.where(mine, queries, jnp.bfloat16(0))
        g_mine = jnp.where(mine, grads, jnp.bfloat16(0))
        delta = jnp.sum(jnp.where(mine, both, 0.0), axis=1, keepdims=True)
        delta = jnp.transpose(jnp.broadcast_to(delta, (chunk, 128)))[0:1]
        scores = dims(keys, q_mine, 1, 1)
        exact = jnp.exp(scores - lse_ref[s, 0:1])
        grad_probs = dims(values, g_mine, 1, 1)
        grad_scores = (exact * (grad_probs - delta)).astype(BF16)
        dq_parts.append(dims(grad_scores, keys, 0, 0))
        dk_parts.append(dims(grad_scores, queries, 1, 0))
        dv_parts.append(dims(exact.astype(BF16), grads, 1, 0))
    dq = jnp.where(lane < HD, dq_parts[0], dq_parts[1]) * 0.125
    dq_ref[...] = dq.astype(BF16).reshape(dq_ref.shape)
    dk_acc[...] += jnp.where(long_lane < HD, dk_parts[0], dk_parts[1])
    dv_acc[...] += jnp.where(long_lane < HD, dv_parts[0], dv_parts[1])

    @pl.when(step == pl.num_programs(0) - 1)
    def _():
        shape = (kv_ref.shape[0], rows, 2 * HD)
        dkv_ref[:, 0:rows] = dk_acc[...].astype(BF16).reshape(shape)
        dkv_ref[:, rows : 2 * rows] = dv_acc[...].astype(BF16).reshape(shape)


def unpack_rows(top, low):
    return jnp.concatenate([top[:, 0:HD], top[:, HD:], low[:, 0:HD], low[:, HD:]], axis=0)


def out_rows(parts, step):
    return jnp.concatenate(
        [ring_rows(parts, step, y, x, HD) for y in range(4) for x in range(2)], axis=0
    )


def out_kernel(me_ref, recv_ref, w0, w1, w2, w3, w4, ctx_ref, own_ref, other_ref, acc):
    core = me_ref[CORE]
    parts = (w0, w1, w2, w3, w4)
    pieces = [unpack_rows(recv_ref[core, at], recv_ref[1 - core, at]) for at in range(8)]
    ctx = jnp.concatenate(pieces, axis=1)
    ctx_ref[...] = ctx
    for step in range(4):
        acc[:, features_of(me_ref, step)] = dims(ctx, out_rows(parts, step), 1, 0)
    half = ctx.shape[0] // 2
    own_ref[...] = acc[0:half]
    other_ref[...] = acc[half:].astype(BF16)


def wide_down(ref, me):
    return jnp.concatenate(
        [ref[s ^ me[SEQ], 0, 0, away(me, Z, z)] for z in range(4) for s in range(2)], axis=1
    )


def ffn_kernel(
    me_ref, n_ref, w0, w1, w2, w3, w4, wdown_ref, bias_ref,
    active_ref, slope_ref, own_ref, other_ref, acc,
):
    step = pl.program_id(0)
    parts = (w0, w1, w2, w3, w4)
    hidden = bias_ref.shape[2]
    pre = bias_ref[0]
    for turn in range(4):
        rows = n_ref[:, features_of(me_ref, turn)]
        pre = pre + dims(rows, ring_rows(parts, turn, 0, 0, hidden), 1, 1)
    cdf = 0.5 * (1.0 + lax.erf(pre * 0.7071067811865476))
    pdf = jnp.exp(-0.5 * pre * pre) * 0.3989422804014327
    active = (pre * cdf).astype(BF16)
    active_ref[...] = active
    slope_ref[...] = (cdf + pre * pdf).astype(BF16)
    made = dims(active, wide_down(wdown_ref, me_ref), 1, 0)

    @pl.when(step == 0)
    def _():
        acc[...] = made

    @pl.when(step > 0)
    def _():
        acc[...] += made

    @pl.when(step == pl.num_programs(0) - 1)
    def _():
        half = acc.shape[0] // 2
        own_ref[...] = acc[0:half]
        other_ref[...] = acc[half:].astype(BF16)


def ffn_back_kernel(
    me_ref, n_ref, g_ref, w0, w1, w2, w3, w4, wdown_ref, active_ref, slope_ref,
    d0, d1, d2, d3, d4, ddown_ref, bias_ref, own_ref, other_ref, acc,
):
    step = pl.program_id(0)
    parts, messages = (w0, w1, w2, w3, w4), (d0, d1, d2, d3, d4)
    grads = g_ref[...]
    active = active_ref[...]
    hidden = active.shape[1]
    grad = dims(active, grads, 0, 0).astype(BF16)
    for z in range(4):
        for s in range(2):
            at = (z * 2 + s) * 128
            ddown_ref[s ^ me_ref[SEQ], 0, 0, away(me_ref, Z, z)] = grad[:, at : at + 128]
    grad_pre = dims(grads, wide_down(wdown_ref, me_ref), 1, 1) * slope_ref[...].astype(F32)
    bias_ref[0] = jnp.sum(grad_pre, axis=0, keepdims=True)
    low = grad_pre.astype(BF16)

    @pl.when(step == 0)
    def _():
        acc[...] = jnp.zeros_like(acc)

    for turn in range(4):
        at = features_of(me_ref, turn)
        put(messages, turn, 0, 0, slice(0, hidden), dims(low, n_ref[:, at], 0, 0))
        acc[:, at] += dims(low, ring_rows(parts, turn, 0, 0, hidden), 1, 0)

    @pl.when(step == pl.num_programs(0) - 1)
    def _():
        half = acc.shape[0] // 2
        own_ref[...] = acc[0:half]
        other_ref[...] = acc[half:].astype(BF16)


def out_back_kernel(
    me_ref, g_ref, ctx_ref, w0, w1, w2, w3, w4, u0, u1, u2, u3, u4,
    dctx_ref, d0, d1, d2, d3, d4,
):
    core = me_ref[CORE]
    parts, messages = (w0, w1, w2, w3, w4), (d0, d1, d2, d3, d4)
    span = g_ref.shape[0] // 4
    ctx = ctx_ref[...]
    made = None
    for step in range(4):
        grads = g_ref[:, features_of(me_ref, step)]
        part = dims(grads, out_rows(parts, step), 1, 1)
        made = part if made is None else made + part
        grad = dims(ctx, grads, 0, 0)
        for y in range(4):
            for x in range(2):
                at = (y * 2 + x) * HD
                put(messages, step, y, x, slice(0, HD), grad[at : at + HD])
    made = made.astype(BF16)
    for to in range(8):
        piece = made[:, to * HD : (to + 1) * HD]
        for half in range(2):
            base = half * 2 * span
            dctx_ref[core ^ half, to] = jnp.concatenate(
                [piece[base : base + span], piece[base + span : base + 2 * span]], axis=1
            )


def qkv_back_kernel(
    me_ref, recv_ref, x_ref, vec_ref, w0, w1, w2, w3, w4,
    d0, d1, d2, d3, d4, own_ref, other_ref, acc,
):
    core = me_ref[CORE]
    parts, grads = (w0, w1, w2, w3, w4), (d0, d1, d2, d3, d4)
    rows = [x_ref[:, features_of(me_ref, step)] for step in range(4)]
    span = x_ref.shape[0] // 4
    half = x_ref.shape[0] // 2

    sums = []
    totals = [None] * 4
    for y in range(4):
        for x in range(2):
            at = y * 2 + x
            top, low = recv_ref[core, at], recv_ref[1 - core, at]
            made = jnp.concatenate(
                [
                    unpack_rows(
                        top[i * span : (i + 1) * span], low[i * span : (i + 1) * span]
                    )
                    for i in range(3)
                ],
                axis=1,
            )
            sums.append(jnp.sum(made.astype(F32), axis=0, keepdims=True))
            for step in range(4):
                put(grads, step, y, x, slice(0, 3 * HD), dims(made, rows[step], 0, 0))
                part = dims(made, ring_rows(parts, step, y, x, 3 * HD), 1, 0)
                totals[step] = part if totals[step] is None else totals[step] + part
    for step in range(4):
        acc[:, features_of(me_ref, step)] = totals[step]
    own_ref[...] = acc[0:half]
    other_ref[...] = acc[half:].astype(BF16)
    zeros = jnp.zeros((14, 2 * HD), F32)
    twos = []
    for z in range(4):
        a, b = sums[2 * z], sums[2 * z + 1]
        bias_q = jnp.concatenate([a[:, 0:HD], b[:, 0:HD]], axis=1)
        bias_v = jnp.concatenate([a[:, 2 * HD :], b[:, 2 * HD :]], axis=1)
        twos.append(jnp.concatenate([bias_q, bias_v, zeros], axis=0))
    for step in range(4):
        z_abs = lax.rem(me_ref[Z] + step, 4)
        two = twos[3]
        for z in range(3):
            two = jnp.where(z_abs == z, twos[z], two)
        block = jnp.concatenate(
            [vec_ref[z_abs, s] + jnp.where(core == s, two, 0.0) for s in range(2)], axis=1
        )
        for y in range(4):
            for x in range(2):
                put(grads, step, y, x, slice(3 * HD, 3 * HD + 16), block)


def norm_forward(hidden, gain, shift):
    centre = jnp.mean(hidden, axis=-1, keepdims=True)
    centered = hidden - centre
    inverse = lax.rsqrt(jnp.mean(centered * centered, axis=-1, keepdims=True) + EPS)
    normed = centered * inverse
    return (normed * gain + shift, normed, inverse)


def norm_backward(grad_in, normed, inverse, gain):
    scaled = grad_in * gain
    inner_term = (
        scaled
        - jnp.mean(scaled, axis=-1, keepdims=True)
        - normed * jnp.mean(scaled * normed, axis=-1, keepdims=True)
    )
    return (
        inverse * inner_term,
        jnp.sum(grad_in * normed, axis=0),
        jnp.sum(grad_in, axis=0),
    )


def sds(shape, dtype=BF16):
    return jax.ShapeDtypeStruct(shape, dtype)


def took(us):
    return pl.CostEstimate(flops=int(us * 1.15e9), bytes_accessed=1 << 20, transcendentals=0)


def local(
    tokens, w_query, w_key, w_value, w_out, w_up, w_down,
    b_query, b_value, b_out, b_up, b_down,
    gain_attn, shift_attn, gain_mlp, shift_mlp, cotangent,
):
    core = lax.axis_index("core")
    me_z, me_s = lax.axis_index("z"), lax.axis_index("seq")
    me_y, me_x = lax.axis_index("y"), lax.axis_index("xhi")
    first_core = core == 0
    me = jnp.stack([core, me_z, me_s, me_y, me_x]).astype(jnp.int32)
    seqs, span, width = tokens.shape
    rows = seqs * span
    hidden = w_up.shape[1] // 2

    at = jnp.arange(width, dtype=jnp.int32)
    z_of, c_of, s_of, i_of = at // 256, (at // 128) % 2, (at // 64) % 2, at % 64
    stored = z_of * 256 + s_of * 128 + c_of * 64 + i_of
    order = (stored[:, None] == at[None, :]).astype(BF16)

    small = jnp.stack(
        [b_query, b_value, b_out, b_down, gain_attn, shift_attn, gain_mlp, shift_mlp]
    )
    small = jnp.concatenate([small, b_up.reshape(4, HD), jnp.zeros((4, HD), BF16)], axis=0)
    shard_rows = 4 * HD + 2 * hidden + 16
    with jax.named_scope("split"):
        keep, give = pl.pallas_call(
            split_kernel,
            out_shape=(sds((shard_rows, HD)),) * 2,
            in_specs=[smem()] + [vmem()] * 7,
            out_specs=(vmem(), vmem()),
            compiler_params=params(),
            cost_estimate=took(2),
        )(me, w_query, w_key, w_value, w_out.T, w_up, w_down.T, small)
    got = other_core(give)
    shard = jnp.where(
        first_core,
        jnp.concatenate([keep, got], axis=1),
        jnp.concatenate([got, keep], axis=1),
    )
    at_o, at_up, at_down, at_vec = 3 * HD, 4 * HD, 4 * HD + hidden, 4 * HD + 2 * hidden
    qkv_shard = jnp.concatenate([shard[0:at_o], shard[at_vec:]], axis=0)
    up_shard = jnp.concatenate([shard[at_up:at_down], shard[at_o:at_up]])
    sixteen = lambda part: jnp.broadcast_to(part[None], (16,) + part.shape)
    qkv_block = plane_gather(sixteen(qkv_shard))
    qkv_block, up_shard = tie(qkv_block, up_shard)
    *near, head, tail = ring_finish(qkv_block, *ring_begin(qkv_block, "z"), "z")
    up_block = plane_gather(sixteen(up_shard))

    both_in = jnp.concatenate([tokens.reshape(rows, width), cotangent.reshape(rows, width)], axis=0)
    both_in = dims(both_in, order, 1, 0)
    mine = both_in[0:rows]
    grad_final = both_in[rows:]
    mine_low = mine.astype(BF16)
    x_rows = jnp.concatenate([mine_low, other_core(mine_low)], axis=0)

    x_rows, down_shard = tie(x_rows, shard[at_down:at_vec])
    down_block = direct_gather(direct_gather(down_shard, "z"), "y")
    down_begun = ring_begin(down_block, "x")
    head, tail, up_block, *down_begun = tie(head, tail, up_block, *down_begun)
    qkv_parts = (*near, head, tail)
    up_begun = ring_begin(up_block, "z")

    fours = jnp.arange(4, dtype=jnp.int32)
    turn = ((fours[:, None] - me_z) % 4 == fours[None, :]).astype(F32)
    ring = [p[:, 0, 0, 3 * HD :, :].reshape(-1) for p in qkv_parts]
    vec = jnp.concatenate([ring[0], ring[1], ring[3], ring[4], ring[2]])
    vec = vec.reshape(4, 4096).astype(F32)
    vec = jnp.dot(turn, vec, precision=HIGHEST).reshape(4, 2, 16, 2 * HD)
    feature = lambda i: vec[:, :, i, :].reshape(width)
    chosen = jnp.where(first_core, vec[:, 0], vec[:, 1])
    chosen = chosen.reshape(4, 16, 2, HD).transpose(0, 2, 1, 3).reshape(8, 16 * HD)
    zeros = jnp.zeros((8, HD), F32)
    bias_qkv = jnp.concatenate([chosen[:, 0:HD], zeros, chosen[:, HD : 2 * HD]], axis=1)
    bias_qkv = bias_qkv[:, None, :]
    bias_up = chosen[:, 8 * HD : 12 * HD][:, None, :]
    gain_one, gain_two = feature(4), feature(6)

    with jax.named_scope("project"):
        packed = pl.pallas_call(
            qkv_kernel,
            out_shape=sds((2, 8, 3 * span, 2 * HD)),
            in_specs=[smem()] + [vmem()] * 7,
            out_specs=vmem(),
            compiler_params=params(),
            cost_estimate=took(5),
        )(me, x_rows, bias_qkv, *qkv_parts)

    def exchange(block):
        flat = block.reshape((16,) + block.shape[2:])
        return lax.all_to_all(flat, PLANE, 0, 0, tiled=False)

    packed, *down_begun = tie(packed, *down_begun)
    *down_near, head, tail = ring_finish(down_block, *down_begun, "x")
    qkv, *up_halves = tie(exchange(packed), *ring_halves(*up_begun, "z"))
    up_parts = (up_block, *up_begun, *ring_forward(*up_halves, "z"))
    per = Q_BLOCKS
    chunk = per * span
    steps = 16 // per
    length = 16 * span
    with jax.named_scope("attend"):
        ctx_heads, lse = pl.pallas_call(
            functools.partial(attend_kernel, rows=span),
            grid=(steps,),
            out_shape=(sds((16, span, 2 * HD)), sds((2, 8, length), F32)),
            in_specs=[
                pl.BlockSpec((per, 3 * span, 2 * HD), lambda i: (i, 0, 0)),
                pl.BlockSpec((16, 3 * span, 2 * HD), lambda i: (0, 0, 0)),
            ],
            out_specs=(
                pl.BlockSpec((per, span, 2 * HD), lambda i: (i, 0, 0)),
                pl.BlockSpec((2, 8, chunk), lambda i: (0, 0, i)),
            ),
            compiler_params=params("arbitrary"),
            cost_estimate=took(11),
        )(qkv, qkv)
    ctx_heads, head, tail = tie(ctx_heads, head, tail)
    wdown = ring_join(*down_near, head, tail, "x")
    recv = lax.all_to_all(ctx_heads, PLANE, 0, 0, tiled=False)
    recv, wdown = tie(recv, wdown)
    recv = recv.reshape(2, 8, span, 2 * HD)
    out_block = hidden // HD
    out_specs = [
        pl.BlockSpec((p.shape[0], 4, 2, HD, 2 * HD), lambda i: (0, 0, 0, out_block, 0))
        for p in up_parts
    ]
    message_shapes = [sds(p.shape) for p in up_parts]
    with jax.named_scope("out_project"):
        ctx, own, other = pl.pallas_call(
            out_kernel,
            out_shape=(sds((2 * rows, 8 * HD)), sds((rows, width), F32), sds((rows, width))),
            grid=(1,),
            in_specs=[smem(), vmem()] + out_specs,
            out_specs=(vmem(), vmem(), vmem()),
            scratch_shapes=[pltpu.VMEM((2 * rows, width), F32)],
            compiler_params=params("arbitrary"),
            cost_estimate=took(3),
        )(me, recv, *up_parts)
    attended = own + other_core(other).astype(F32)
    resid_one = mine + attended + feature(2)
    normed_one, norm_first, inverse_first = norm_forward(resid_one, gain_one, feature(5))
    normed_low = normed_one.astype(BF16)
    n_rows = jnp.concatenate([normed_low, other_core(normed_low)], axis=0)

    up_specs = [
        pl.BlockSpec(
            (p.shape[0], 1, 1, hidden, 2 * HD), lambda t, at: (0, t // 2, t % 2, 0, 0)
        )
        for p in up_parts
    ]
    down_spec = pl.BlockSpec(
        (2, 1, 1, 4, hidden, 2 * HD),
        lambda t, at: (0, (t % 2) ^ at[XHI], away(at, Y, t // 2), 0, 0, 0),
    )
    whole_spec = pl.BlockSpec((2 * rows, width), lambda t, at: (0, 0))
    cols_spec = pl.BlockSpec((2 * rows, hidden), lambda t, at: (0, t))
    half_spec = pl.BlockSpec((rows, width), lambda t, at: (0, 0))
    bias_spec = pl.BlockSpec((1, 1, hidden), lambda t, at: (t, 0, 0))
    with jax.named_scope("feed_forward"):
        active, slope, own, other = pl.pallas_call(
            ffn_kernel,
            grid_spec=pltpu.PrefetchScalarGridSpec(
                num_scalar_prefetch=1,
                grid=(8,),
                in_specs=[whole_spec] + up_specs + [down_spec, bias_spec],
                out_specs=(cols_spec, cols_spec, half_spec, half_spec),
                scratch_shapes=[pltpu.VMEM((2 * rows, width), F32)],
            ),
            out_shape=(
                sds((2 * rows, 8 * hidden)),
                sds((2 * rows, 8 * hidden)),
                sds((rows, width), F32),
                sds((rows, width)),
            ),
            compiler_params=params("arbitrary"),
            cost_estimate=took(14),
        )(me, n_rows, *up_parts, wdown, bias_up)
    mixed = own + other_core(other).astype(F32)
    resid_two = normed_one + mixed + feature(3)
    final, norm_second, inverse_second = norm_forward(resid_two, gain_two, feature(7))
    output = dims(final.astype(BF16), order, 1, 1).astype(BF16)
    grad_two, part_gain_mlp, part_shift_mlp = norm_backward(
        grad_final, norm_second, inverse_second, gain_two
    )
    grad_low = grad_two.astype(BF16)
    g_rows = jnp.concatenate([grad_low, other_core(grad_low)], axis=0)
    with jax.named_scope("feed_forward_back"):
        *grad_up, grad_down, part_up, own, other = pl.pallas_call(
            ffn_back_kernel,
            grid_spec=pltpu.PrefetchScalarGridSpec(
                num_scalar_prefetch=1,
                grid=(8,),
                in_specs=[whole_spec] * 2 + up_specs + [down_spec, cols_spec, cols_spec],
                out_specs=(*up_specs, down_spec, bias_spec, half_spec, half_spec),
                scratch_shapes=[pltpu.VMEM((2 * rows, width), F32)],
            ),
            out_shape=(
                *message_shapes,
                sds(wdown.shape),
                sds((8, 1, hidden), F32),
                sds((rows, width), F32),
                sds((rows, width)),
            ),
            compiler_params=params("arbitrary"),
            cost_estimate=took(20),
        )(me, n_rows, g_rows, *up_parts, wdown, active, slope)
    grad_mid = grad_two + (own + other_core(other).astype(F32))
    grad_one, part_gain_attn, part_shift_attn = norm_backward(
        grad_mid, norm_first, inverse_first, gain_one
    )
    grad_low = grad_one.astype(BF16)
    g_rows = jnp.concatenate([grad_low, other_core(grad_low)], axis=0)
    with jax.named_scope("out_project_back"):
        dctx, *grad_up = pl.pallas_call(
            out_back_kernel,
            grid=(1,),
            out_shape=(sds((2, 8, span, 2 * HD)), *message_shapes),
            in_specs=[smem(), vmem(), vmem()]
            + out_specs
            + [pl.BlockSpec(memory_space=pl.ANY)] * 5,
            out_specs=(vmem(), *out_specs),
            input_output_aliases={8 + i: 1 + i for i in range(5)},
            compiler_params=params("arbitrary"),
            cost_estimate=took(4),
        )(me, g_rows, ctx, *up_parts, *grad_up)
    dctx, grad_down = tie(exchange(dctx), grad_down)
    down_begun = reduce_start(cross_messages(grad_down), "x")
    up_begun = reduce_start(grad_up, "z")
    with jax.named_scope("attend_back"):
        dq, dkv = pl.pallas_call(
            functools.partial(attend_back_kernel, rows=span),
            grid=(steps,),
            out_shape=(sds((16, span, 2 * HD)), sds((16, 2 * span, 2 * HD))),
            in_specs=[
                pl.BlockSpec((per, 3 * span, 2 * HD), lambda i: (i, 0, 0)),
                pl.BlockSpec((16, 3 * span, 2 * HD), lambda i: (0, 0, 0)),
                pl.BlockSpec((per, span, 2 * HD), lambda i: (i, 0, 0)),
                pl.BlockSpec((per, span, 2 * HD), lambda i: (i, 0, 0)),
                pl.BlockSpec((2, 8, chunk), lambda i: (0, 0, i)),
            ],
            out_specs=(
                pl.BlockSpec((per, span, 2 * HD), lambda i: (i, 0, 0)),
                pl.BlockSpec((16, 2 * span, 2 * HD), lambda i: (0, 0, 0)),
            ),
            scratch_shapes=[pltpu.VMEM((length, 2 * HD), F32)] * 2,
            compiler_params=params("arbitrary"),
            cost_estimate=took(18),
        )(qkv, qkv, ctx_heads, dctx, lse)
    dq, *up_begun = tie(dq, *up_begun)
    dqkv = exchange(jnp.concatenate([dq, dkv], axis=1)[None])
    *up_middle, down_first, down_second = tie(*reduce_middle(up_begun, "z"), *down_begun[1:3])
    up_sent = reduce_send(up_middle, "z")
    down_begun = (down_begun[0], down_first, down_second) + down_begun[3:5]
    down_sent = reduce_send(reduce_middle(down_begun, "x"), "x")
    up_sum = reduce_join(up_sent)
    dqkv, up_sum = tie(dqkv, up_sum)
    dqkv = dqkv.reshape(2, 8, 3 * span, 2 * HD)
    ups = part_up.reshape(4, 2, 4, HD).transpose(0, 2, 1, 3).reshape(4, 1, 4, 2 * HD)
    nothing = jnp.zeros_like(ups)
    ups = jnp.concatenate(
        [jnp.where(first_core, ups, nothing), jnp.where(first_core, nothing, ups)], axis=1
    )
    six = jnp.stack(
        [
            jnp.sum(grad_one, axis=0), jnp.sum(grad_two, axis=0),
            part_gain_attn, part_shift_attn, part_gain_mlp, part_shift_mlp,
        ]
    ).reshape(6, 4, 2, 2 * HD).transpose(1, 2, 0, 3)
    vec_rows = jnp.concatenate(
        [jnp.zeros((4, 2, 2, 2 * HD), F32), six, ups, jnp.zeros((4, 2, 4, 2 * HD), F32)], axis=2
    )
    with jax.named_scope("project_back"):
        part, far = sds((2, 4, 2, 3 * HD + 16, 2 * HD)), sds((1, 4, 2, 3 * HD + 16, 2 * HD))
        *grad_qkv, own, other = pl.pallas_call(
            qkv_back_kernel,
            out_shape=(
                part, part, part, far, far, sds((rows, width), F32), sds((rows, width)),
            ),
            in_specs=[smem()] + [vmem()] * 8,
            out_specs=(vmem(),) * 7,
            scratch_shapes=[pltpu.VMEM((2 * rows, width), F32)],
            compiler_params=params(),
            cost_estimate=took(8),
        )(me, dqkv, x_rows, vec_rows, *qkv_parts)
    own, other, *sent = tie(own, other, *down_sent)
    down_sum = reduce_join(sent)
    input_sum = own + other_core(other).astype(F32)
    grad_tokens = lax.dot_general(
        grad_one + input_sum, order.astype(F32), (((1,), (1,)), ((), ())),
        precision=lax.Precision.HIGH,
    )
    down_begun = reduce_start(ring_messages(down_sum), "y")
    begun = tie(*reduce_start(grad_qkv, "z"), *down_begun, grad_tokens)
    qkv_sum = reduce_end(reduce_middle(begun[0:5], "z"), "z")
    down_begun, grad_tokens = begun[5:10], begun[10]
    down_sum = reduce_end(reduce_middle(down_begun, "y"), "y")
    got_up = plane_reduce(up_sum).astype(BF16)
    got_down = direct_reduce(down_sum, "z")
    got_qkv = plane_reduce(qkv_sum)
    final_rows = jnp.concatenate([got_qkv.astype(BF16), got_up, got_down], axis=0)
    swapped = other_core(final_rows)
    with jax.named_scope("join"):
        square = sds((HD, 2 * HD), F32)
        *weights, g_out, g_up, g_down, vecs = pl.pallas_call(
            join_kernel,
            out_shape=(
                square, square, square, square,
                sds((HD, 2 * hidden), F32),
                sds((HD, 2 * hidden), F32),
                sds((16, HD), F32),
            ),
            in_specs=[smem(), vmem(), vmem()],
            out_specs=(vmem(),) * 7,
            compiler_params=params(),
            cost_estimate=took(2),
        )(me, final_rows, swapped)
    return (
        output.reshape(seqs, span, width),
        grad_tokens.reshape(seqs, span, width),
        *weights,
        g_out.T,
        g_up,
        g_down.T,
        vecs[0],
        vecs[1],
        vecs[2],
        vecs[8:12].reshape(4 * HD),
        vecs[3],
        vecs[4],
        vecs[5],
        vecs[6],
        vecs[7],
    )


def solution(mesh):
    fine = Mesh(mesh.devices.reshape(4, 2, 2, 4, 2), ("z", "core", "seq", "y", "xhi"))
    owners, tensor = ("z", "core", "seq"), ("y", "xhi")
    tokens = P(("z", "core"), ("seq", "y", "xhi"), None)
    columns, by_rows, vector = P(owners, tensor), P(tensor, owners), P(owners)
    weights = (columns, columns, columns, by_rows, columns, by_rows)
    return jax.shard_map(
        local,
        mesh=fine,
        in_specs=(tokens,) + weights + (vector,) * 9 + (tokens,),
        out_specs=(tokens, tokens) + weights + (vector,) * 9,
        check_vma=False,
    )
```

```python
import functools

import jax
import jax.numpy as jnp
from jax import lax
from jax.experimental import pallas as pl
from jax.experimental.pallas import tpu as pltpu
from jax.sharding import Mesh, PartitionSpec as P

HD = 64
EPS = 1e-05
F32 = jnp.float32
BF16 = jnp.bfloat16
HIGHEST = lax.Precision.HIGHEST
VMEM_LIMIT = 56 * 1024 * 1024
Q_BLOCKS = 4
PLANE = ("seq", "y", "xhi")


def dims(a, b, ca, cb):
    return lax.dot_general(a, b, (((ca,), (cb,)), ((), ())), preferred_element_type=F32)


def shift4(by):
    return [(i, (i + by) % 4) for i in range(4)]


def flip(seq_too, xhi_too):
    return [
        (seq * 2 + xhi, (seq ^ seq_too) * 2 + (xhi ^ xhi_too))
        for seq in range(2)
        for xhi in range(2)
    ]


def links(axis):
    if axis == "x":
        return ("seq", "xhi"), flip(1, 0), flip(1, 1)
    return axis, shift4(-1), shift4(1)


def halves(block):
    half = block.shape[0] // 2
    return block[0:half], block[half:]


def ring_begin(block, axis):
    names, one, two = links(axis)
    return lax.ppermute(block, names, one), lax.ppermute(block, names, two)


def ring_halves(first, second, axis):
    if axis == "x":
        return halves(second)[0], halves(first)[1]
    return halves(first)[0], halves(second)[1]


def ring_forward(head, tail, axis):
    names, one, two = links(axis)
    return lax.ppermute(head, names, one), lax.ppermute(tail, names, two)


def ring_finish(block, first, second, axis):
    head, tail = ring_forward(*ring_halves(first, second, axis), axis)
    return block, first, second, head, tail


def ring_join(block, first, second, head, tail, axis):
    if axis == "x":
        whole = jnp.concatenate([block, head, tail, first, second], axis=0)
        return whole.reshape((2, 2) + block.shape)
    whole = jnp.concatenate([block, first, head, tail, second], axis=0)
    return whole.reshape((4,) + block.shape)


def ring_gather(block, axis):
    return ring_join(*ring_finish(block, *ring_begin(block, axis), axis), axis)


def direct_gather(block, axis):
    parts = [block] + [lax.ppermute(block, axis, shift4(-i)) for i in (1, 2, 3)]
    return jnp.stack(parts)


def add(*terms):
    total = terms[0].astype(F32)
    for term in terms[1:]:
        total = total + term.astype(F32)
    return total.astype(BF16)


def ring_messages(block):
    first_head, first_tail = halves(block[1])
    far_head, far_tail = halves(block[2])
    second_head, second_tail = halves(block[3])
    return (
        block[0],
        jnp.concatenate([far_head, first_tail], axis=0),
        jnp.concatenate([second_head, far_tail], axis=0),
        first_head,
        second_tail,
    )


def cross_messages(block):
    first_head, first_tail = halves(block[1, 0])
    far_head, far_tail = halves(block[0, 1])
    second_head, second_tail = halves(block[1, 1])
    return (
        block[0, 0],
        jnp.concatenate([far_head, first_head], axis=0),
        jnp.concatenate([far_tail, second_tail], axis=0),
        first_tail,
        second_head,
    )


def reduce_ways(axis):
    names, one, two = links(axis)
    return (names, one, two) if axis == "x" else (names, two, one)


def reduce_start(messages, axis):
    names, to_first, to_second = reduce_ways(axis)
    own, a, b, first, second = messages
    return own, lax.ppermute(a, names, to_first), lax.ppermute(b, names, to_second), first, second


def reduce_middle(begun, axis):
    own, a, b, first, second = begun
    (a_head, a_tail), (b_head, b_tail) = halves(a), halves(b)
    if axis == "x":
        return own, a_tail, b_tail, add(first, b_head), add(second, a_head)
    return own, b_head, a_tail, add(first, a_head), add(second, b_tail)


def reduce_send(middle, axis):
    names, to_first, to_second = reduce_ways(axis)
    own, near_head, near_tail, first, second = middle
    first = lax.ppermute(first, names, to_first)
    second = lax.ppermute(second, names, to_second)
    if axis == "x":
        first, second = second, first
    return own, near_head, near_tail, first, second


def reduce_join(sent):
    own, near_head, near_tail, far_head, far_tail = sent
    head, tail = halves(own)
    return jnp.concatenate([add(head, near_head, far_head), add(tail, near_tail, far_tail)], axis=0)


def reduce_end(middle, axis):
    return reduce_join(reduce_send(middle, axis))


def tie(*values):
    return lax.optimization_barrier(values)


def direct_reduce(block, axis):
    parts = [block[0]] + [lax.ppermute(block[i], axis, shift4(i)) for i in (1, 2, 3)]
    return add(*parts)


def plane_gather(copies):
    got = lax.all_to_all(copies, PLANE, 0, 0, tiled=False)
    return got.reshape((2, 4, 2) + copies.shape[1:])


def plane_reduce(block):
    flat = block.reshape((16,) + block.shape[-2:])
    got = lax.all_to_all(flat, PLANE, 0, 0, tiled=False)
    return jnp.sum(got.astype(F32), axis=0)


def other_core(block):
    return lax.ppermute(block, "core", [(0, 1), (1, 0)])


def params(*semantics):
    return pltpu.CompilerParams(
        vmem_limit_bytes=VMEM_LIMIT,
        dimension_semantics=semantics if semantics else None,
    )


def vmem():
    return pl.BlockSpec(memory_space=pltpu.VMEM)


def smem():
    return pl.BlockSpec(memory_space=pltpu.SMEM)


CORE, Z, SEQ, Y, XHI = range(5)


def away(me, axis, at):
    return lax.rem(at + 4 - me[axis], 4)


def ring_rows(parts, step, y, x, size):
    if step == 2:
        a, b = parts[3][0, y, x, 0:size], parts[4][0, y, x, 0:size]
    else:
        ref = parts[{0: 0, 1: 1, 3: 2}[step]]
        a, b = ref[0, y, x, 0:size], ref[1, y, x, 0:size]
    return jnp.concatenate([a, b], axis=1)


def features_of(me, step):
    return pl.ds(pl.multiple_of(lax.rem(me[Z] + step, 4) * 256, 256), 256)


def put(messages, step, y, x, rows, value):
    for s in range(2):
        name, at = {
            (0, 0): (0, 0), (0, 1): (0, 1), (1, 0): (3, 0), (1, 1): (1, 1),
            (2, 0): (1, 0), (2, 1): (2, 1), (3, 0): (2, 0), (3, 1): (4, 0),
        }[step, s]
        messages[name][at, y, x, rows] = value[:, s * 128 : (s + 1) * 128].astype(BF16)


def split_kernel(me_ref, wq, wk, wv, wo, wup, wdown, small, keep_ref, give_ref):
    first = me_ref[CORE] == 0
    at = 0
    for ref in (wq, wk, wv, wo, wup, wdown):
        value = jnp.transpose(ref[...].astype(F32))
        half = value.shape[0] // 2
        a, b = value[0:half], value[half:]
        keep_ref[at : at + half] = jnp.where(first, a, b).astype(BF16)
        give_ref[at : at + half] = jnp.where(first, b, a).astype(BF16)
        at += half
    keep_ref[at:] = small[...]
    give_ref[at:] = small[...]


def join_kernel(me_ref, mine_ref, other_ref, dq, dk, dv, do, dup, ddown, vec_ref):
    first = me_ref[CORE] == 0
    hidden = ddown.shape[1] // 2

    def rows(start, size):
        a = mine_ref[start : start + size].astype(F32)
        b = other_ref[start : start + size].astype(F32)
        zero, one = jnp.where(first, a, b), jnp.where(first, b, a)
        zero = jnp.where(first, zero[:, 0:HD], zero[:, HD:])
        one = jnp.where(first, one[:, 0:HD], one[:, HD:])
        return zero, one

    at = 0
    plan = ((dq, HD), (dk, HD), (dv, HD), (vec_ref, 16), (dup, hidden), (do, HD), (ddown, hidden))
    for ref, size in plan:
        zero, one = rows(at, size)
        at += size
        if size == 16:
            ref[...] = zero + one
        else:
            ref[...] = jnp.transpose(jnp.concatenate([zero, one], axis=0))


def qkv_kernel(me_ref, x_ref, bias_ref, w0, w1, w2, w3, w4, out_ref):
    parts = (w0, w1, w2, w3, w4)
    core = me_ref[CORE]
    rows = [x_ref[:, features_of(me_ref, step)] for step in range(4)]
    span = x_ref.shape[0] // 4
    for y in range(4):
        for x in range(2):
            made = bias_ref[y * 2 + x]
            for step in range(4):
                made = made + dims(rows[step], ring_rows(parts, step, y, x, 3 * HD), 1, 1)
            made = made.astype(BF16)
            to = y * 2 + x
            for half in range(2):
                top = made[half * 2 * span : half * 2 * span + span]
                low = made[half * 2 * span + span : (half + 1) * 2 * span]
                packed = jnp.concatenate(
                    [
                        jnp.concatenate(
                            [top[:, i * HD : (i + 1) * HD], low[:, i * HD : (i + 1) * HD]],
                            axis=1,
                        )
                        for i in range(3)
                    ],
                    axis=0,
                )
                out_ref[core ^ half, to] = packed


def attend_kernel(q_ref, kv_ref, ctx_ref, lse_ref, *, rows):
    chunk = q_ref.shape[0] * rows
    length = kv_ref.shape[0] * rows
    queries = q_ref[:, 0:rows].reshape(chunk, 2 * HD) * jnp.bfloat16(0.125)
    keys = kv_ref[:, rows : 2 * rows].reshape(length, 2 * HD)
    values = kv_ref[:, 2 * rows : 3 * rows].reshape(length, 2 * HD)
    lane = lax.broadcasted_iota(jnp.int32, (chunk, 2 * HD), 1)
    parts = []
    for s in range(2):
        mine = (lane < HD) if s == 0 else (lane >= HD)
        picked = jnp.where(mine, queries, jnp.bfloat16(0))
        scores = dims(picked, keys, 1, 1)
        top = jnp.max(scores, axis=1, keepdims=True)
        weights = jnp.exp(scores - top)
        total = jnp.sum(weights, axis=1, keepdims=True)
        mixed = dims(weights.astype(BF16), values, 1, 0)
        parts.append(mixed / total)
        lse = jnp.broadcast_to(top + jnp.log(total), (chunk, 128))
        lse_ref[s] = jnp.transpose(lse)[0:8]
    ctx = jnp.where(lane < HD, parts[0], parts[1])
    ctx_ref[...] = ctx.astype(BF16).reshape(ctx_ref.shape)


def attend_back_kernel(
    q_ref, kv_ref, ctx_ref, dctx_ref, lse_ref, dq_ref, dkv_ref, dk_acc, dv_acc, *, rows
):
    step = pl.program_id(0)
    chunk = q_ref.shape[0] * rows
    length = kv_ref.shape[0] * rows
    queries = q_ref[:, 0:rows].reshape(chunk, 2 * HD) * jnp.bfloat16(0.125)
    grads = dctx_ref[...].reshape(chunk, 2 * HD)
    context = ctx_ref[...].reshape(chunk, 2 * HD)
    keys = kv_ref[:, rows : 2 * rows].reshape(length, 2 * HD)
    values = kv_ref[:, 2 * rows : 3 * rows].reshape(length, 2 * HD)
    lane = lax.broadcasted_iota(jnp.int32, (chunk, 2 * HD), 1)
    long_lane = lax.broadcasted_iota(jnp.int32, (length, 2 * HD), 1)
    both = grads.astype(F32) * context.astype(F32)

    @pl.when(step == 0)
    def _():
        dk_acc[...] = jnp.zeros_like(dk_acc)
        dv_acc[...] = jnp.zeros_like(dv_acc)

    dq_parts, dk_parts, dv_parts = [], [], []
    for s in range(2):
        mine = (lane < HD) if s == 0 else (lane >= HD)
        q_mine = jnp.where(mine, queries, jnp.bfloat16(0))
        g_mine = jnp.where(mine, grads, jnp.bfloat16(0))
        delta = jnp.sum(jnp.where(mine, both, 0.0), axis=1, keepdims=True)
        delta = jnp.transpose(jnp.broadcast_to(delta, (chunk, 128)))[0:1]
        scores = dims(keys, q_mine, 1, 1)
        exact = jnp.exp(scores - lse_ref[s, 0:1])
        grad_probs = dims(values, g_mine, 1, 1)
        grad_scores = (exact * (grad_probs - delta)).astype(BF16)
        dq_parts.append(dims(grad_scores, keys, 0, 0))
        dk_parts.append(dims(grad_scores, queries, 1, 0))
        dv_parts.append(dims(exact.astype(BF16), grads, 1, 0))
    dq = jnp.where(lane < HD, dq_parts[0], dq_parts[1]) * 0.125
    dq_ref[...] = dq.astype(BF16).reshape(dq_ref.shape)
    dk_acc[...] += jnp.where(long_lane < HD, dk_parts[0], dk_parts[1])
    dv_acc[...] += jnp.where(long_lane < HD, dv_parts[0], dv_parts[1])

    @pl.when(step == pl.num_programs(0) - 1)
    def _():
        shape = (kv_ref.shape[0], rows, 2 * HD)
        dkv_ref[:, 0:rows] = dk_acc[...].astype(BF16).reshape(shape)
        dkv_ref[:, rows : 2 * rows] = dv_acc[...].astype(BF16).reshape(shape)


def unpack_rows(top, low):
    return jnp.concatenate([top[:, 0:HD], top[:, HD:], low[:, 0:HD], low[:, HD:]], axis=0)


def out_rows(parts, step):
    return jnp.concatenate(
        [ring_rows(parts, step, y, x, HD) for y in range(4) for x in range(2)], axis=0
    )


def out_kernel(me_ref, recv_ref, w0, w1, w2, w3, w4, ctx_ref, own_ref, other_ref, acc):
    core = me_ref[CORE]
    parts = (w0, w1, w2, w3, w4)
    pieces = [unpack_rows(recv_ref[core, at], recv_ref[1 - core, at]) for at in range(8)]
    ctx = jnp.concatenate(pieces, axis=1)
    ctx_ref[...] = ctx
    for step in range(4):
        acc[:, features_of(me_ref, step)] = dims(ctx, out_rows(parts, step), 1, 0)
    half = ctx.shape[0] // 2
    own_ref[...] = acc[0:half]
    other_ref[...] = acc[half:].astype(BF16)


def wide_down(ref, me):
    return jnp.concatenate(
        [ref[s ^ me[SEQ], 0, 0, away(me, Z, z)] for z in range(4) for s in range(2)], axis=1
    )


def ffn_kernel(
    me_ref, n_ref, w0, w1, w2, w3, w4, wdown_ref, bias_ref,
    active_ref, slope_ref, own_ref, other_ref, acc,
):
    step = pl.program_id(0)
    parts = (w0, w1, w2, w3, w4)
    hidden = bias_ref.shape[2]
    pre = bias_ref[0]
    for turn in range(4):
        rows = n_ref[:, features_of(me_ref, turn)]
        pre = pre + dims(rows, ring_rows(parts, turn, 0, 0, hidden), 1, 1)
    cdf = 0.5 * (1.0 + lax.erf(pre * 0.7071067811865476))
    pdf = jnp.exp(-0.5 * pre * pre) * 0.3989422804014327
    active = (pre * cdf).astype(BF16)
    active_ref[...] = active
    slope_ref[...] = (cdf + pre * pdf).astype(BF16)
    made = dims(active, wide_down(wdown_ref, me_ref), 1, 0)

    @pl.when(step == 0)
    def _():
        acc[...] = made

    @pl.when(step > 0)
    def _():
        acc[...] += made

    @pl.when(step == pl.num_programs(0) - 1)
    def _():
        half = acc.shape[0] // 2
        own_ref[...] = acc[0:half]
        other_ref[...] = acc[half:].astype(BF16)


def ffn_back_kernel(
    me_ref, n_ref, g_ref, w0, w1, w2, w3, w4, wdown_ref, active_ref, slope_ref,
    d0, d1, d2, d3, d4, ddown_ref, bias_ref, own_ref, other_ref, acc,
):
    step = pl.program_id(0)
    parts, messages = (w0, w1, w2, w3, w4), (d0, d1, d2, d3, d4)
    grads = g_ref[...]
    active = active_ref[...]
    hidden = active.shape[1]
    grad = dims(active, grads, 0, 0).astype(BF16)
    for z in range(4):
        for s in range(2):
            at = (z * 2 + s) * 128
            ddown_ref[s ^ me_ref[SEQ], 0, 0, away(me_ref, Z, z)] = grad[:, at : at + 128]
    grad_pre = dims(grads, wide_down(wdown_ref, me_ref), 1, 1) * slope_ref[...].astype(F32)
    bias_ref[0] = jnp.sum(grad_pre, axis=0, keepdims=True)
    low = grad_pre.astype(BF16)

    @pl.when(step == 0)
    def _():
        acc[...] = jnp.zeros_like(acc)

    for turn in range(4):
        at = features_of(me_ref, turn)
        put(messages, turn, 0, 0, slice(0, hidden), dims(low, n_ref[:, at], 0, 0))
        acc[:, at] += dims(low, ring_rows(parts, turn, 0, 0, hidden), 1, 0)

    @pl.when(step == pl.num_programs(0) - 1)
    def _():
        half = acc.shape[0] // 2
        own_ref[...] = acc[0:half]
        other_ref[...] = acc[half:].astype(BF16)


def out_back_kernel(
    me_ref, g_ref, ctx_ref, w0, w1, w2, w3, w4, u0, u1, u2, u3, u4,
    dctx_ref, d0, d1, d2, d3, d4,
):
    core = me_ref[CORE]
    parts, messages = (w0, w1, w2, w3, w4), (d0, d1, d2, d3, d4)
    span = g_ref.shape[0] // 4
    ctx = ctx_ref[...]
    made = None
    for step in range(4):
        grads = g_ref[:, features_of(me_ref, step)]
        part = dims(grads, out_rows(parts, step), 1, 1)
        made = part if made is None else made + part
        grad = dims(ctx, grads, 0, 0)
        for y in range(4):
            for x in range(2):
                at = (y * 2 + x) * HD
                put(messages, step, y, x, slice(0, HD), grad[at : at + HD])
    made = made.astype(BF16)
    for to in range(8):
        piece = made[:, to * HD : (to + 1) * HD]
        for half in range(2):
            base = half * 2 * span
            dctx_ref[core ^ half, to] = jnp.concatenate(
                [piece[base : base + span], piece[base + span : base + 2 * span]], axis=1
            )


def qkv_back_kernel(
    me_ref, recv_ref, x_ref, vec_ref, w0, w1, w2, w3, w4,
    d0, d1, d2, d3, d4, own_ref, other_ref, acc,
):
    core = me_ref[CORE]
    parts, grads = (w0, w1, w2, w3, w4), (d0, d1, d2, d3, d4)
    rows = [x_ref[:, features_of(me_ref, step)] for step in range(4)]
    span = x_ref.shape[0] // 4
    half = x_ref.shape[0] // 2

    sums = []
    totals = [None] * 4
    for y in range(4):
        for x in range(2):
            at = y * 2 + x
            top, low = recv_ref[core, at], recv_ref[1 - core, at]
            made = jnp.concatenate(
                [
                    unpack_rows(
                        top[i * span : (i + 1) * span], low[i * span : (i + 1) * span]
                    )
                    for i in range(3)
                ],
                axis=1,
            )
            sums.append(jnp.sum(made.astype(F32), axis=0, keepdims=True))
            for step in range(4):
                put(grads, step, y, x, slice(0, 3 * HD), dims(made, rows[step], 0, 0))
                part = dims(made, ring_rows(parts, step, y, x, 3 * HD), 1, 0)
                totals[step] = part if totals[step] is None else totals[step] + part
    for step in range(4):
        acc[:, features_of(me_ref, step)] = totals[step]
    own_ref[...] = acc[0:half]
    other_ref[...] = acc[half:].astype(BF16)
    zeros = jnp.zeros((14, 2 * HD), F32)
    twos = []
    for z in range(4):
        a, b = sums[2 * z], sums[2 * z + 1]
        bias_q = jnp.concatenate([a[:, 0:HD], b[:, 0:HD]], axis=1)
        bias_v = jnp.concatenate([a[:, 2 * HD :], b[:, 2 * HD :]], axis=1)
        twos.append(jnp.concatenate([bias_q, bias_v, zeros], axis=0))
    for step in range(4):
        z_abs = lax.rem(me_ref[Z] + step, 4)
        two = twos[3]
        for z in range(3):
            two = jnp.where(z_abs == z, twos[z], two)
        block = jnp.concatenate(
            [vec_ref[z_abs, s] + jnp.where(core == s, two, 0.0) for s in range(2)], axis=1
        )
        for y in range(4):
            for x in range(2):
                put(grads, step, y, x, slice(3 * HD, 3 * HD + 16), block)


def norm_forward(hidden, gain, shift):
    centre = jnp.mean(hidden, axis=-1, keepdims=True)
    centered = hidden - centre
    inverse = lax.rsqrt(jnp.mean(centered * centered, axis=-1, keepdims=True) + EPS)
    normed = centered * inverse
    return (normed * gain + shift, normed, inverse)


def norm_backward(grad_in, normed, inverse, gain):
    scaled = grad_in * gain
    inner_term = (
        scaled
        - jnp.mean(scaled, axis=-1, keepdims=True)
        - normed * jnp.mean(scaled * normed, axis=-1, keepdims=True)
    )
    return (
        inverse * inner_term,
        jnp.sum(grad_in * normed, axis=0),
        jnp.sum(grad_in, axis=0),
    )


def sds(shape, dtype=BF16):
    return jax.ShapeDtypeStruct(shape, dtype)


def took(us):
    return pl.CostEstimate(flops=int(us * 1.15e9), bytes_accessed=1 << 20, transcendentals=0)


def local(
    tokens, w_query, w_key, w_value, w_out, w_up, w_down,
    b_query, b_value, b_out, b_up, b_down,
    gain_attn, shift_attn, gain_mlp, shift_mlp, cotangent,
):
    core = lax.axis_index("core")
    me_z, me_s = lax.axis_index("z"), lax.axis_index("seq")
    me_y, me_x = lax.axis_index("y"), lax.axis_index("xhi")
    first_core = core == 0
    me = jnp.stack([core, me_z, me_s, me_y, me_x]).astype(jnp.int32)
    seqs, span, width = tokens.shape
    rows = seqs * span
    hidden = w_up.shape[1] // 2

    at = jnp.arange(width, dtype=jnp.int32)
    z_of, c_of, s_of, i_of = at // 256, (at // 128) % 2, (at // 64) % 2, at % 64
    stored = z_of * 256 + s_of * 128 + c_of * 64 + i_of
    order = (stored[:, None] == at[None, :]).astype(BF16)

    small = jnp.stack(
        [b_query, b_value, b_out, b_down, gain_attn, shift_attn, gain_mlp, shift_mlp]
    )
    small = jnp.concatenate([small, b_up.reshape(4, HD), jnp.zeros((4, HD), BF16)], axis=0)
    shard_rows = 4 * HD + 2 * hidden + 16
    with jax.named_scope("split"):
        keep, give = pl.pallas_call(
            split_kernel,
            out_shape=(sds((shard_rows, HD)),) * 2,
            in_specs=[smem()] + [vmem()] * 7,
            out_specs=(vmem(), vmem()),
            compiler_params=params(),
            cost_estimate=took(2),
        )(me, w_query, w_key, w_value, w_out.T, w_up, w_down.T, small)
    got = other_core(give)
    shard = jnp.where(
        first_core,
        jnp.concatenate([keep, got], axis=1),
        jnp.concatenate([got, keep], axis=1),
    )
    at_o, at_up, at_down, at_vec = 3 * HD, 4 * HD, 4 * HD + hidden, 4 * HD + 2 * hidden
    qkv_shard = jnp.concatenate([shard[0:at_o], shard[at_vec:]], axis=0)
    up_shard = jnp.concatenate([shard[at_up:at_down], shard[at_o:at_up]])
    sixteen = lambda part: jnp.broadcast_to(part[None], (16,) + part.shape)
    qkv_block = plane_gather(sixteen(qkv_shard))
    qkv_block, up_shard = tie(qkv_block, up_shard)
    *near, head, tail = ring_finish(qkv_block, *ring_begin(qkv_block, "z"), "z")
    up_block = plane_gather(sixteen(up_shard))

    both_in = jnp.concatenate([tokens.reshape(rows, width), cotangent.reshape(rows, width)], axis=0)
    both_in = dims(both_in, order, 1, 0)
    mine = both_in[0:rows]
    grad_final = both_in[rows:]
    mine_low = mine.astype(BF16)
    x_rows = jnp.concatenate([mine_low, other_core(mine_low)], axis=0)

    x_rows, down_shard = tie(x_rows, shard[at_down:at_vec])
    down_block = direct_gather(direct_gather(down_shard, "z"), "y")
    down_begun = ring_begin(down_block, "x")
    head, tail, up_block, *down_begun = tie(head, tail, up_block, *down_begun)
    qkv_parts = (*near, head, tail)
    up_begun = ring_begin(up_block, "z")

    fours = jnp.arange(4, dtype=jnp.int32)
    turn = ((fours[:, None] - me_z) % 4 == fours[None, :]).astype(F32)
    ring = [p[:, 0, 0, 3 * HD :, :].reshape(-1) for p in qkv_parts]
    vec = jnp.concatenate([ring[0], ring[1], ring[3], ring[4], ring[2]])
    vec = vec.reshape(4, 4096).astype(F32)
    vec = jnp.dot(turn, vec, precision=HIGHEST).reshape(4, 2, 16, 2 * HD)
    feature = lambda i: vec[:, :, i, :].reshape(width)
    chosen = jnp.where(first_core, vec[:, 0], vec[:, 1])
    chosen = chosen.reshape(4, 16, 2, HD).transpose(0, 2, 1, 3).reshape(8, 16 * HD)
    zeros = jnp.zeros((8, HD), F32)
    bias_qkv = jnp.concatenate([chosen[:, 0:HD], zeros, chosen[:, HD : 2 * HD]], axis=1)
    bias_qkv = bias_qkv[:, None, :]
    bias_up = chosen[:, 8 * HD : 12 * HD][:, None, :]
    gain_one, gain_two = feature(4), feature(6)

    with jax.named_scope("project"):
        packed = pl.pallas_call(
            qkv_kernel,
            out_shape=sds((2, 8, 3 * span, 2 * HD)),
            in_specs=[smem()] + [vmem()] * 7,
            out_specs=vmem(),
            compiler_params=params(),
            cost_estimate=took(5),
        )(me, x_rows, bias_qkv, *qkv_parts)

    def exchange(block):
        flat = block.reshape((16,) + block.shape[2:])
        return lax.all_to_all(flat, PLANE, 0, 0, tiled=False)

    packed, *down_begun = tie(packed, *down_begun)
    *down_near, head, tail = ring_finish(down_block, *down_begun, "x")
    qkv, *up_halves = tie(exchange(packed), *ring_halves(*up_begun, "z"))
    up_parts = (up_block, *up_begun, *ring_forward(*up_halves, "z"))
    per = Q_BLOCKS
    chunk = per * span
    steps = 16 // per
    length = 16 * span
    with jax.named_scope("attend"):
        ctx_heads, lse = pl.pallas_call(
            functools.partial(attend_kernel, rows=span),
            grid=(steps,),
            out_shape=(sds((16, span, 2 * HD)), sds((2, 8, length), F32)),
            in_specs=[
                pl.BlockSpec((per, 3 * span, 2 * HD), lambda i: (i, 0, 0)),
                pl.BlockSpec((16, 3 * span, 2 * HD), lambda i: (0, 0, 0)),
            ],
            out_specs=(
                pl.BlockSpec((per, span, 2 * HD), lambda i: (i, 0, 0)),
                pl.BlockSpec((2, 8, chunk), lambda i: (0, 0, i)),
            ),
            compiler_params=params("arbitrary"),
            cost_estimate=took(11),
        )(qkv, qkv)
    ctx_heads, head, tail = tie(ctx_heads, head, tail)
    wdown = ring_join(*down_near, head, tail, "x")
    recv = lax.all_to_all(ctx_heads, PLANE, 0, 0, tiled=False)
    recv, wdown = tie(recv, wdown)
    recv = recv.reshape(2, 8, span, 2 * HD)
    out_block = hidden // HD
    out_specs = [
        pl.BlockSpec((p.shape[0], 4, 2, HD, 2 * HD), lambda i: (0, 0, 0, out_block, 0))
        for p in up_parts
    ]
    message_shapes = [sds(p.shape) for p in up_parts]
    with jax.named_scope("out_project"):
        ctx, own, other = pl.pallas_call(
            out_kernel,
            out_shape=(sds((2 * rows, 8 * HD)), sds((rows, width), F32), sds((rows, width))),
            grid=(1,),
            in_specs=[smem(), vmem()] + out_specs,
            out_specs=(vmem(), vmem(), vmem()),
            scratch_shapes=[pltpu.VMEM((2 * rows, width), F32)],
            compiler_params=params("arbitrary"),
            cost_estimate=took(3),
        )(me, recv, *up_parts)
    attended = own + other_core(other).astype(F32)
    resid_one = mine + attended + feature(2)
    normed_one, norm_first, inverse_first = norm_forward(resid_one, gain_one, feature(5))
    normed_low = normed_one.astype(BF16)
    n_rows = jnp.concatenate([normed_low, other_core(normed_low)], axis=0)

    up_specs = [
        pl.BlockSpec(
            (p.shape[0], 1, 1, hidden, 2 * HD), lambda t, at: (0, t // 2, t % 2, 0, 0)
        )
        for p in up_parts
    ]
    down_spec = pl.BlockSpec(
        (2, 1, 1, 4, hidden, 2 * HD),
        lambda t, at: (0, (t % 2) ^ at[XHI], away(at, Y, t // 2), 0, 0, 0),
    )
    whole_spec = pl.BlockSpec((2 * rows, width), lambda t, at: (0, 0))
    cols_spec = pl.BlockSpec((2 * rows, hidden), lambda t, at: (0, t))
    half_spec = pl.BlockSpec((rows, width), lambda t, at: (0, 0))
    bias_spec = pl.BlockSpec((1, 1, hidden), lambda t, at: (t, 0, 0))
    with jax.named_scope("feed_forward"):
        active, slope, own, other = pl.pallas_call(
            ffn_kernel,
            grid_spec=pltpu.PrefetchScalarGridSpec(
                num_scalar_prefetch=1,
                grid=(8,),
                in_specs=[whole_spec] + up_specs + [down_spec, bias_spec],
                out_specs=(cols_spec, cols_spec, half_spec, half_spec),
                scratch_shapes=[pltpu.VMEM((2 * rows, width), F32)],
            ),
            out_shape=(
                sds((2 * rows, 8 * hidden)),
                sds((2 * rows, 8 * hidden)),
                sds((rows, width), F32),
                sds((rows, width)),
            ),
            compiler_params=params("arbitrary"),
            cost_estimate=took(14),
        )(me, n_rows, *up_parts, wdown, bias_up)
    mixed = own + other_core(other).astype(F32)
    resid_two = normed_one + mixed + feature(3)
    final, norm_second, inverse_second = norm_forward(resid_two, gain_two, feature(7))
    output = dims(final.astype(BF16), order, 1, 1).astype(BF16)
    grad_two, part_gain_mlp, part_shift_mlp = norm_backward(
        grad_final, norm_second, inverse_second, gain_two
    )
    grad_low = grad_two.astype(BF16)
    g_rows = jnp.concatenate([grad_low, other_core(grad_low)], axis=0)
    with jax.named_scope("feed_forward_back"):
        *grad_up, grad_down, part_up, own, other = pl.pallas_call(
            ffn_back_kernel,
            grid_spec=pltpu.PrefetchScalarGridSpec(
                num_scalar_prefetch=1,
                grid=(8,),
                in_specs=[whole_spec] * 2 + up_specs + [down_spec, cols_spec, cols_spec],
                out_specs=(*up_specs, down_spec, bias_spec, half_spec, half_spec),
                scratch_shapes=[pltpu.VMEM((2 * rows, width), F32)],
            ),
            out_shape=(
                *message_shapes,
                sds(wdown.shape),
                sds((8, 1, hidden), F32),
                sds((rows, width), F32),
                sds((rows, width)),
            ),
            compiler_params=params("arbitrary"),
            cost_estimate=took(20),
        )(me, n_rows, g_rows, *up_parts, wdown, active, slope)
    grad_mid = grad_two + (own + other_core(other).astype(F32))
    grad_one, part_gain_attn, part_shift_attn = norm_backward(
        grad_mid, norm_first, inverse_first, gain_one
    )
    grad_low = grad_one.astype(BF16)
    g_rows = jnp.concatenate([grad_low, other_core(grad_low)], axis=0)
    with jax.named_scope("out_project_back"):
        dctx, *grad_up = pl.pallas_call(
            out_back_kernel,
            grid=(1,),
            out_shape=(sds((2, 8, span, 2 * HD)), *message_shapes),
            in_specs=[smem(), vmem(), vmem()]
            + out_specs
            + [pl.BlockSpec(memory_space=pl.ANY)] * 5,
            out_specs=(vmem(), *out_specs),
            input_output_aliases={8 + i: 1 + i for i in range(5)},
            compiler_params=params("arbitrary"),
            cost_estimate=took(4),
        )(me, g_rows, ctx, *up_parts, *grad_up)
    dctx, grad_down = tie(dctx, grad_down)
    dctx, *messages = tie(exchange(dctx), *cross_messages(grad_down))
    down_begun = reduce_start(messages, "x")
    up_begun = reduce_start(grad_up, "z")
    with jax.named_scope("attend_back"):
        dq, dkv = pl.pallas_call(
            functools.partial(attend_back_kernel, rows=span),
            grid=(steps,),
            out_shape=(sds((16, span, 2 * HD)), sds((16, 2 * span, 2 * HD))),
            in_specs=[
                pl.BlockSpec((per, 3 * span, 2 * HD), lambda i: (i, 0, 0)),
                pl.BlockSpec((16, 3 * span, 2 * HD), lambda i: (0, 0, 0)),
                pl.BlockSpec((per, span, 2 * HD), lambda i: (i, 0, 0)),
                pl.BlockSpec((per, span, 2 * HD), lambda i: (i, 0, 0)),
                pl.BlockSpec((2, 8, chunk), lambda i: (0, 0, i)),
            ],
            out_specs=(
                pl.BlockSpec((per, span, 2 * HD), lambda i: (i, 0, 0)),
                pl.BlockSpec((16, 2 * span, 2 * HD), lambda i: (0, 0, 0)),
            ),
            scratch_shapes=[pltpu.VMEM((length, 2 * HD), F32)] * 2,
            compiler_params=params("arbitrary"),
            cost_estimate=took(18),
        )(qkv, qkv, ctx_heads, dctx, lse)
    dq, *up_begun = tie(dq, *up_begun)
    dqkv = exchange(jnp.concatenate([dq, dkv], axis=1)[None])
    *up_middle, down_first, down_second = tie(*reduce_middle(up_begun, "z"), *down_begun[1:3])
    up_sent = reduce_send(up_middle, "z")
    down_begun = (down_begun[0], down_first, down_second) + down_begun[3:5]
    down_sent = reduce_send(reduce_middle(down_begun, "x"), "x")
    up_sum = reduce_join(up_sent)
    dqkv, up_sum = tie(dqkv, up_sum)
    dqkv = dqkv.reshape(2, 8, 3 * span, 2 * HD)
    ups = part_up.reshape(4, 2, 4, HD).transpose(0, 2, 1, 3).reshape(4, 1, 4, 2 * HD)
    nothing = jnp.zeros_like(ups)
    ups = jnp.concatenate(
        [jnp.where(first_core, ups, nothing), jnp.where(first_core, nothing, ups)], axis=1
    )
    six = jnp.stack(
        [
            jnp.sum(grad_one, axis=0), jnp.sum(grad_two, axis=0),
            part_gain_attn, part_shift_attn, part_gain_mlp, part_shift_mlp,
        ]
    ).reshape(6, 4, 2, 2 * HD).transpose(1, 2, 0, 3)
    vec_rows = jnp.concatenate(
        [jnp.zeros((4, 2, 2, 2 * HD), F32), six, ups, jnp.zeros((4, 2, 4, 2 * HD), F32)], axis=2
    )
    with jax.named_scope("project_back"):
        part, far = sds((2, 4, 2, 3 * HD + 16, 2 * HD)), sds((1, 4, 2, 3 * HD + 16, 2 * HD))
        *grad_qkv, own, other = pl.pallas_call(
            qkv_back_kernel,
            out_shape=(
                part, part, part, far, far, sds((rows, width), F32), sds((rows, width)),
            ),
            in_specs=[smem()] + [vmem()] * 8,
            out_specs=(vmem(),) * 7,
            scratch_shapes=[pltpu.VMEM((2 * rows, width), F32)],
            compiler_params=params(),
            cost_estimate=took(8),
        )(me, dqkv, x_rows, vec_rows, *qkv_parts)
    own, other, *sent = tie(own, other, *down_sent)
    down_sum = reduce_join(sent)
    input_sum = own + other_core(other).astype(F32)
    grad_tokens = lax.dot_general(
        grad_one + input_sum, order.astype(F32), (((1,), (1,)), ((), ())),
        precision=lax.Precision.HIGH,
    )
    down_begun = reduce_start(ring_messages(down_sum), "y")
    begun = tie(*reduce_start(grad_qkv, "z"), *down_begun, grad_tokens)
    qkv_sum = reduce_end(reduce_middle(begun[0:5], "z"), "z")
    down_begun, grad_tokens = begun[5:10], begun[10]
    down_sum = reduce_end(reduce_middle(down_begun, "y"), "y")
    got_up = plane_reduce(up_sum).astype(BF16)
    got_down = direct_reduce(down_sum, "z")
    got_qkv = plane_reduce(qkv_sum)
    final_rows = jnp.concatenate([got_qkv.astype(BF16), got_up, got_down], axis=0)
    swapped = other_core(final_rows)
    with jax.named_scope("join"):
        square = sds((HD, 2 * HD), F32)
        *weights, g_out, g_up, g_down, vecs = pl.pallas_call(
            join_kernel,
            out_shape=(
                square, square, square, square,
                sds((HD, 2 * hidden), F32),
                sds((HD, 2 * hidden), F32),
                sds((16, HD), F32),
            ),
            in_specs=[smem(), vmem(), vmem()],
            out_specs=(vmem(),) * 7,
            compiler_params=params(),
            cost_estimate=took(2),
        )(me, final_rows, swapped)
    return (
        output.reshape(seqs, span, width),
        grad_tokens.reshape(seqs, span, width),
        *weights,
        g_out.T,
        g_up,
        g_down.T,
        vecs[0],
        vecs[1],
        vecs[2],
        vecs[8:12].reshape(4 * HD),
        vecs[3],
        vecs[4],
        vecs[5],
        vecs[6],
        vecs[7],
    )


def solution(mesh):
    fine = Mesh(mesh.devices.reshape(4, 2, 2, 4, 2), ("z", "core", "seq", "y", "xhi"))
    owners, tensor = ("z", "core", "seq"), ("y", "xhi")
    tokens = P(("z", "core"), ("seq", "y", "xhi"), None)
    columns, by_rows, vector = P(owners, tensor), P(tensor, owners), P(owners)
    weights = (columns, columns, columns, by_rows, columns, by_rows)
    return jax.shard_map(
        local,
        mesh=fine,
        in_specs=(tokens,) + weights + (vector,) * 9 + (tokens,),
        out_specs=(tokens, tokens) + weights + (vector,) * 9,
        check_vma=False,
    )
```
